32 devices in a mesh: ctx: 8 (over z, y), mp: 4 (over x, core).
Axes of the slice: x: 2, y: 2, z: 4, core: 2. Of those that a mesh axis runs over, the one named last changes fastest.
Arguments:
- projected: bfloat16 [1024, 3, 8192], P('ctx', None, 'mp'), may hold values from -6 to 6
- short_weight: float32 [3, 3, 8192], P(None, None, 'mp'), may hold values from -3 to 3
- filter_taps: float32 [64, 512], P('mp'), may hold values from -1 to 1
- tap_blocks: int32 [64, 4], P('mp'), may hold values 0 or 1
- skip_bias: float32 [8192], P('mp'), may hold values from -3 to 3
- norm_gain: float32 [8192], P('mp'), may hold values from 0.1 to 1.9
- seq_lengths: int32 [32], replicated, may hold values from 1 to 512, 1024 in all
Outputs:
- output: bfloat16 [1024, 8192], P('ctx', 'mp')
The draws below stay inside these ranges and needn't reach their ends.
Inputs may be any that keep to these rules, and one draw needn't show every extreme that they name: `seq_lengths`: sum to 1024; the longest is exactly 512.
All inputs are finite; a program needn't handle non-finite values. No bound on the sum of `tap_blocks` on one device may be relied on, other than what follows from the above.
Results may differ from the reference program's by a relative error of at most 0.0075.
Values may be sent and summed in bfloat16 or wider, within the bound.
No kernel may reach another device: no remote copies, remote signals or barrier semaphores. Data moves between devices by JAX's collectives and lax.ppermute only.
A program may use at most 64 MiB of HBM per device.

```python
import math
import jax
import jax.numpy as jnp
import numpy as np
from jax import lax

D = 8192
GROUP = 128
BLK = 128
NSEQ = 32
LAGS = 4
FL = 512
GROUPS = 64
TOKENS = 1024
MOST = 512


def draw_filter_taps(key, part):
    key = jax.random.fold_in(key, 11)
    ramp = jnp.arange(GROUPS, dtype=jnp.float32) / max(GROUPS - 1, 1)
    scale = 3.0 ** ramp / math.sqrt(FL)
    base = jnp.clip(jax.random.normal(key, (GROUPS, FL), jnp.float32), -4.0, 4.0)
    return (base * scale[:, None]).astype(jnp.float32)


def touch_ends(array, rng, smallest, high):
    shape = array.shape
    index_at = [jax.random.randint(jax.random.fold_in(rng, axis), (), 0, shape[axis]) for axis in range(len(shape))]
    array = array.at[tuple(index_at)].set(smallest)
    longest = shape.index(max(shape))
    index_at[longest] = (index_at[longest] + 1) % shape[longest]
    return array.at[tuple(index_at)].set(high)


def steps_of(rng, extent, pieces, least, top_value):
    gain = 1.0
    for position, parts in pieces:
        draws = jax.random.uniform(jax.random.fold_in(jax.random.fold_in(rng, 6), position), (parts,), jnp.float32, least / len(pieces), top_value / len(pieces))
        gain = gain * jnp.repeat(jnp.exp(draws), extent[position] // parts).reshape((-1,) + (1,) * (len(extent) - 1 - position))
    return gain


def split_up(number_of, total, reach, lean):
    weights = [(1 << 20) // math.isqrt(grade ** lean) + 1 for grade in range(2, number_of + 1)]
    rest, given = total - reach - (number_of - 1), [1] * (number_of - 1)
    while rest > 0:
        candidates = [i for i in range(number_of - 1) if given[i] < reach]
        pool, remaining = sum([weights[i] for i in candidates]), rest
        for i in candidates:
            extra = min(reach - given[i], max(1, remaining * weights[i] // pool), rest)
            given[i] = given[i] + extra
            rest = rest - extra
    return np.array([reach] + given)


def uneven_parts(rng, number_of, total, limit, lean):
    if number_of == 2:
        one = jax.random.randint(rng, (), max(1, total - limit), min(limit, total - 1) + 1)
        return jnp.stack([one, total - one])
    lengths = jnp.asarray(split_up(number_of, total, limit, lean), jnp.int32)
    twos = (number_of - 1) // 2
    giver, taker = lengths[1:1 + 2 * twos:2], lengths[2:2 + 2 * twos:2]
    slack = jnp.minimum(giver - 1, limit - taker)
    moved = jax.random.randint(jax.random.fold_in(rng, 1), (twos,), 0, 1 << 20) % (slack + 1)
    lengths = lengths.at[1:1 + 2 * twos:2].set(giver - moved).at[2:2 + 2 * twos:2].set(taker + moved)
    return lengths[jax.random.permutation(jax.random.fold_in(rng, 2), number_of)]


def noise(own_key, extent, deviation, most, shards=(), held_as=jnp.bfloat16):
    factor_of = steps_of(own_key, extent, shards, -0.22, 0.18) if shards else 1.0
    entries = jax.random.normal(own_key, extent, jnp.float32) * deviation * factor_of
    return jnp.minimum(jnp.maximum(entries, -most), most).astype(held_as)


def setup_inputs(seed: int = 0) -> dict:
    streams_of = jax.random.split(jax.random.key(seed), 8)
    return {
        "projected": noise(streams_of[0], (TOKENS, 3, D), 1.0, 6.0, ((0, 8), (2, 4))),
        "short_weight": noise(streams_of[1], (3, 3, D), 0.6, 3.0, ((2, 4),), jnp.float32),
        "filter_taps": draw_filter_taps(jax.random.fold_in(streams_of[7], 71), 0),
        "tap_blocks": touch_ends((jax.random.randint(streams_of[3], (GROUPS, LAGS), 0, 4) < 3).astype(jnp.int32), jax.random.fold_in(streams_of[3], 1), 0, 1),
        "skip_bias": noise(streams_of[4], (D,), 0.5, 3.0, ((0, 4),), jnp.float32),
        "norm_gain": jnp.clip(1.0 + 0.18 * jax.random.normal(streams_of[5], (D,), jnp.float32), 0.1, 1.9),
        "seq_lengths": uneven_parts(streams_of[6], NSEQ, TOKENS, MOST, 2).astype(jnp.int32),
    }


norm_eps = 1e-06

def seg_ids(positions, seq_ends):
    counted = lax.optimization_barrier(jnp.sum((seq_ends[None, :] <= positions[:, None]).astype(jnp.int32), axis=1))
    return jnp.where(positions >= 0, counted, -1).astype(jnp.int32)

def build_tables(taps, active):
    filters = taps.shape[0]
    lag_count = taps.shape[1] // BLK
    scaled = (taps * jnp.repeat(active.astype(jnp.float32), BLK, axis=1)).astype(jnp.bfloat16)
    zero_pad = jnp.zeros((filters, BLK), jnp.bfloat16)
    shifted = jnp.concatenate([zero_pad[:, 1:], scaled, zero_pad, jnp.zeros((filters, 1), jnp.bfloat16)], axis=1)
    blocks = shifted.reshape(filters, lag_count + 2, BLK)
    segs = jnp.concatenate([blocks[:, :lag_count + 1], blocks[:, 1:]], axis=2)
    tiled = jnp.broadcast_to(segs[:, :, None, :], (filters, lag_count + 1, BLK + 1, 2 * BLK))
    tiled = tiled.reshape(filters, lag_count + 1, (BLK + 1) * 2 * BLK)[:, :, :BLK * (2 * BLK + 1)]
    hankel = tiled.reshape(filters, lag_count + 1, BLK, 2 * BLK + 1)[:, :, :, :BLK]
    toeplitz = hankel[:, :, :, ::-1]
    return jnp.transpose(toeplitz, (1, 0, 2, 3))

def conv_term(extended, weights, seg_ext, tap_index, length):
    same_seq = (seg_ext[2 - tap_index:2 - tap_index + length] == seg_ext[2:]).astype(jnp.float32)
    return weights[:, tap_index, :][None] * extended[2 - tap_index:2 - tap_index + length].astype(jnp.float32) * same_seq[:, None, None]

def short_conv(extended, weights, seg_ext):
    length = extended.shape[0] - 2
    return conv_term(extended, weights, seg_ext, 0, length) + conv_term(extended, weights, seg_ext, 1, length) + conv_term(extended, weights, seg_ext, 2, length)

def block_conv_ref(product, segments, toeplitz):
    lag_count = toeplitz.shape[0] - 1
    nblocks = product.shape[0] // BLK
    padded = jnp.concatenate([jnp.zeros((lag_count * BLK, product.shape[1]), jnp.bfloat16), product], 0)
    padded = padded.reshape(lag_count + nblocks, BLK, product.shape[1])
    seg_pad = jnp.concatenate([jnp.full((lag_count * BLK,), -1, jnp.int32), segments], 0).reshape(lag_count + nblocks, BLK)
    seg_out = seg_pad[lag_count:]

    def lag_step(totals, lag_index):
        inputs = lax.dynamic_slice_in_dim(padded, lag_count - lag_index, nblocks, 0)
        in_segs = lax.dynamic_slice_in_dim(seg_pad, lag_count - lag_index, nblocks, 0)
        same_seq = seg_out[:, :, None] == in_segs[:, None, :]
        weights = jnp.where(same_seq, toeplitz[lag_index][None], jnp.zeros((), jnp.bfloat16))
        totals = totals + jnp.einsum('nab,nbc->nac', weights.astype(jnp.float32), inputs.astype(jnp.float32))
        return (totals, None)
    totals, _ = lax.scan(lag_step, jnp.zeros((nblocks, BLK, product.shape[1]), jnp.float32), jnp.arange(lag_count + 1, dtype=jnp.int32))
    return totals.reshape(nblocks * BLK, product.shape[1])

def reference(projected, short_weight, filter_taps, tap_blocks, skip_bias, norm_gain, seq_lengths):
    seq_ends = jnp.cumsum(seq_lengths).astype(jnp.int32)
    segments = seg_ids(jnp.arange(TOKENS, dtype=jnp.int32), seq_ends)
    seg_ext = jnp.concatenate([jnp.full((2,), -1, jnp.int32), segments], 0)
    toeplitz = build_tables(filter_taps, tap_blocks)

    def per_group(group_index):
        start = (group_index * GROUP).astype(jnp.int32)
        columns = lax.dynamic_slice_in_dim(projected, start, GROUP, 2)
        extended = jnp.concatenate([jnp.zeros((2, 3, GROUP), jnp.bfloat16), columns], 0)
        weights = lax.dynamic_slice_in_dim(short_weight, start, GROUP, 2)
        features = short_conv(extended, weights, seg_ext)
        product = (features[:, 1] * features[:, 2]).astype(jnp.bfloat16)
        tables = lax.dynamic_index_in_dim(toeplitz, group_index, 1, keepdims=False)
        filtered = block_conv_ref(product, segments, tables)
        bias = lax.dynamic_slice_in_dim(skip_bias, start, GROUP, 0)
        filtered = filtered + bias[None, :] * product.astype(jnp.float32)
        return features[:, 0] * filtered
    gated = lax.map(per_group, jnp.arange(GROUPS, dtype=jnp.int32))
    power = lax.optimization_barrier(jnp.sum(gated * gated, axis=(0, 2)))
    scale = lax.rsqrt(power / D + norm_eps)
    normed = (gated * scale[None, :, None] * norm_gain.reshape(GROUPS, 1, GROUP)).astype(jnp.bfloat16)
    return jnp.transpose(normed, (1, 0, 2)).reshape(TOKENS, D)
```

```python
import functools

import jax
import jax.numpy as jnp
from jax import lax
from jax.experimental import pallas as pl
from jax.experimental.pallas import tpu as pltpu
from jax.sharding import Mesh, PartitionSpec as P

GROUP = 128
BLK = 128
norm_eps = 1e-06

VMEM = pl.BlockSpec(memory_space=pltpu.VMEM)
SMEM = pl.BlockSpec(memory_space=pltpu.SMEM)
SPOTS = ("blk", "half")


def moved(block, pairs):
    return lax.ppermute(block, SPOTS, pairs)


def boundaries(seq_ref, t):
    def step(k, carry):
        end, first, second = carry
        end = end + seq_ref[k]
        return end, first | (t == end).astype(jnp.int32), second | (t - 1 == end).astype(jnp.int32)

    first = (t == 0).astype(jnp.int32)
    second = (t == 1).astype(jnp.int32)
    _, first, second = lax.fori_loop(0, seq_ref.shape[0], step, (jnp.int32(0), first, second))
    return first, second


def counted(seq_ref, t):
    def step(k, carry):
        end, total = carry
        end = end + seq_ref[k]
        return end, total + (end <= t).astype(jnp.int32)

    _, total = lax.fori_loop(
        0, seq_ref.shape[0], step, (jnp.int32(0), jnp.zeros(t.shape, jnp.int32))
    )
    return jnp.where(t >= 0, total, -1)


def products_kernel(
    seq_ref, proj_ref, edge_ref, w_ref, sent_ref, kept_ref, qsent_ref, qkept_ref, x_ref, m1_ref, m2_ref
):
    rows = proj_ref.shape[1]
    width = sent_ref.shape[1]
    half = lax.axis_index("half")
    shard = lax.axis_index("blk") * 2 + half
    t = shard * rows + lax.broadcasted_iota(jnp.int32, (rows, GROUP), 0)
    first, second = boundaries(seq_ref, t)
    m1_ref[...] = 1.0 - first.astype(jnp.float32)
    m2_ref[...] = 1.0 - (first | second).astype(jnp.float32)

    def feature(panel, lanes):
        x = proj_ref[panel, :, lanes].astype(jnp.float32)
        x_ref[panel, 6:8, :] = edge_ref[panel, :, lanes].astype(jnp.float32)
        x_ref[panel, 8:, :] = x
        w = w_ref[panel, :, lanes]
        return (
            w[0:1] * x
            + w[1:2] * x_ref[panel, 7 : rows + 7, :] * m1_ref[...]
            + w[2:3] * x_ref[panel, 6 : rows + 6, :] * m2_ref[...]
        )

    def chunk(c, _):
        there = pl.ds(pl.multiple_of(c * GROUP, GROUP), GROUP)
        for which, p_ref, q_ref in ((1 - half, sent_ref, qsent_ref), (half, kept_ref, qkept_ref)):
            lanes = pl.ds(pl.multiple_of(which * width + c * GROUP, GROUP), GROUP)
            product = feature(1, lanes) * feature(2, lanes)
            p_ref[:, there] = product.astype(p_ref.dtype)
            q_ref[:, there] = feature(0, lanes).astype(q_ref.dtype)
        return 0

    lax.fori_loop(0, width // GROUP, chunk, 0)


def tables_kernel(seq_ref, taps_ref, out_ref, rev_ref, m_ref):
    groups = out_ref.shape[0]
    taps = taps_ref.shape[1]
    span = rev_ref.shape[1]
    width = out_ref.shape[3]
    half = lax.axis_index("half")
    start = lax.axis_index("blk") * (2 * BLK)
    turn = lax.broadcasted_iota(jnp.int32, (taps, span), 0) + lax.broadcasted_iota(
        jnp.int32, (taps, span), 1
    )
    turn = (turn == taps).astype(jnp.bfloat16)
    rev_ref[...] = jnp.dot(taps_ref[...], turn, preferred_element_type=jnp.float32)
    for part in range(2):
        t_in = start - taps + part * BLK + lax.broadcasted_iota(jnp.int32, (8, width), 1)
        t_out = start + part * BLK + lax.broadcasted_iota(jnp.int32, (BLK, GROUP), 0)
        seg_in = counted(seq_ref, t_in)[0:1]
        seg_out = counted(seq_ref, t_out)[:, 0:1]
        m_ref[part] = (seg_in == seg_out).astype(jnp.float32)

    def one(g, _):
        row = rev_ref[pl.ds(half * groups + g, 1), :]
        table = pltpu.roll(
            jnp.broadcast_to(row, (BLK, span)), 0, 1, stride=1, stride_axis=0
        )[:, :width]
        for part in range(2):
            out_ref[g, part] = (table * m_ref[part]).astype(out_ref.dtype)
        return 0

    lax.fori_loop(0, groups, one, 0)


def near_kernel(table_ref, own_ref, pair_ref, back_own_ref, back_pair_ref, bias_ref, acc_ref, win_ref):
    groups = table_ref.shape[0]
    half = lax.axis_index("half")
    own = pl.multiple_of(half * BLK, BLK)
    pair = pl.multiple_of((1 - half) * BLK, BLK)
    win_ref[pl.ds(own, BLK), :] = back_own_ref[...]
    win_ref[pl.ds(pair, BLK), :] = back_pair_ref[...]
    win_ref[pl.ds(2 * BLK + own, BLK), :] = own_ref[...]
    win_ref[pl.ds(2 * BLK + pair, BLK), :] = pair_ref[...]
    for g in range(groups):
        lanes = slice(g * GROUP, (g + 1) * GROUP)
        bias = bias_ref[:, pl.ds(pl.multiple_of(half * groups * GROUP + g * GROUP, GROUP), GROUP)]
        for part in range(2):
            total = jnp.dot(
                table_ref[g, part, :, (2 - part) * BLK :],
                win_ref[: (3 + part) * BLK, lanes],
                preferred_element_type=jnp.float32,
            )
            here = win_ref[(2 + part) * BLK : (3 + part) * BLK, lanes].astype(jnp.float32)
            acc_ref[part * BLK : (part + 1) * BLK, lanes] = total + bias * here


def far_kernel(
    table_ref, acc_ref, far_own_ref, far_pair_ref, qkept_ref, qgot_ref, kept_ref, sent_ref, power_ref, win_ref, sq_ref
):
    groups = table_ref.shape[0]
    half = lax.axis_index("half")
    own = pl.multiple_of(half * BLK, BLK)
    pair = pl.multiple_of((1 - half) * BLK, BLK)
    win_ref[pl.ds(own, BLK), :] = far_own_ref[...]
    win_ref[pl.ds(pair, BLK), :] = far_pair_ref[...]
    for g in range(groups):
        lanes = slice(g * GROUP, (g + 1) * GROUP)
        for part in range(2):
            rows = slice(part * BLK, (part + 1) * BLK)
            acc_ref[rows, lanes] += jnp.dot(
                table_ref[g, part, :, : (2 - part) * BLK],
                win_ref[part * BLK :, lanes],
                preferred_element_type=jnp.float32,
            )
    for spot, q_ref, out_ref in ((own, qkept_ref, kept_ref), (pair, qgot_ref, sent_ref)):
        squares = jnp.zeros((BLK, GROUP), jnp.float32)
        for g in range(groups):
            lanes = slice(g * GROUP, (g + 1) * GROUP)
            gated = q_ref[:, lanes].astype(jnp.float32) * acc_ref[pl.ds(spot, BLK), lanes]
            out_ref[:, lanes] = gated.astype(out_ref.dtype)
            squares = squares + gated * gated
        sq_ref[pl.ds(spot, BLK), :] = squares
    power_ref[...] = lax.dot_general(
        jnp.ones((8, GROUP), jnp.float32),
        sq_ref[...],
        (((1,), (1,)), ((), ())),
        precision=lax.Precision.HIGHEST,
        preferred_element_type=jnp.float32,
    )[0:1]


def norm_kernel(channels, power_ref, kept_ref, got_ref, gain_ref, out_ref):
    half = lax.axis_index("half")
    width = kept_ref.shape[1]
    power = power_ref[:, pl.ds(pl.multiple_of(half * BLK, BLK), BLK)]
    scale = lax.rsqrt(power / channels + norm_eps)
    diagonal = lax.broadcasted_iota(jnp.int32, (BLK, BLK), 0) == lax.broadcasted_iota(
        jnp.int32, (BLK, BLK), 1
    )
    column = jnp.sum(jnp.where(diagonal, scale, 0.0), axis=1, keepdims=True)
    for which, part_ref in ((half, kept_ref), (1 - half, got_ref)):
        for c in range(0, width, GROUP):
            lanes = pl.ds(pl.multiple_of(which * width + c, GROUP), GROUP)
            out_ref[:, lanes] = (
                part_ref[:, c : c + GROUP].astype(jnp.float32) * column * gain_ref[:, lanes]
            ).astype(out_ref.dtype)


def kernel_call(body, outs, in_specs, scratch, flops, moved_bytes):
    return pl.pallas_call(
        body,
        out_shape=outs,
        in_specs=in_specs,
        out_specs=jax.tree.map(lambda _: VMEM, outs),
        scratch_shapes=scratch,
        compiler_params=pltpu.CompilerParams(vmem_limit_bytes=24 << 20),
        cost_estimate=pl.CostEstimate(flops=flops, bytes_accessed=moved_bytes, transcendentals=0),
    )


def shards(blocks, channels, projected, short_weight, filter_taps, tap_blocks, skip_bias, norm_gain, seq_lengths):
    rows = projected.shape[0]
    width = projected.shape[2] // 2
    groups = width // GROUP
    taps = filter_taps.shape[1]
    shape = jax.ShapeDtypeStruct
    half_shape = shape((rows, width), jnp.bfloat16)
    half_wide = shape((rows, width), jnp.float32)

    spots = range(2 * blocks)
    to_next = [(i, i + 1) for i in spots if i + 1 < 2 * blocks]
    to_pair = [(i, i ^ 1) for i in spots]
    ahead = [(i, i + 2) for i in spots if i + 2 < 2 * blocks]
    ahead_pair = [(i, (i ^ 1) + 2) for i in spots if (i ^ 1) + 2 < 2 * blocks]

    panels = jnp.transpose(projected, (1, 0, 2))
    edge = moved(panels[:, rows - 2 :], to_next)

    sent, kept, qsent, qkept = kernel_call(
        products_kernel,
        (half_shape, half_shape, half_shape, half_wide),
        [SMEM, VMEM, VMEM, VMEM],
        [
            pltpu.VMEM((3, rows + 8, GROUP), jnp.float32),
            pltpu.VMEM((rows, GROUP), jnp.float32),
            pltpu.VMEM((rows, GROUP), jnp.float32),
        ],
        60 * rows * width,
        16 * rows * width,
    )(seq_lengths, panels, edge, short_weight)

    pair = moved(sent, to_pair)
    back_own = moved(kept, ahead)
    back_pair = moved(sent, ahead_pair)
    qgot = moved(qsent, to_pair)

    scaled = (filter_taps * jnp.repeat(tap_blocks.astype(jnp.float32), BLK, axis=1)).astype(jnp.bfloat16)
    table = kernel_call(
        tables_kernel,
        shape((groups, 2, BLK, taps + BLK), jnp.bfloat16),
        [SMEM, VMEM],
        [pltpu.VMEM((2 * groups, taps + 2 * BLK), jnp.float32), pltpu.VMEM((2, BLK, taps + BLK), jnp.float32)],
        40 * groups * BLK * taps,
        8 * groups * BLK * taps,
    )(seq_lengths, scaled)

    acc = kernel_call(
        near_kernel,
        shape((2 * rows, width), jnp.float32),
        [VMEM] * 6,
        [pltpu.VMEM((4 * rows, width), jnp.bfloat16)],
        2 * 7 * rows * BLK * width,
        16 * rows * width,
    )(table, kept, pair, back_own, back_pair, skip_bias.reshape(1, -1))

    far_own = moved(back_own, ahead)
    far_pair = moved(back_pair, ahead)
    done, send, power = kernel_call(
        far_kernel,
        (half_wide, half_shape, shape((1, 2 * rows), jnp.float32)),
        [VMEM] * 6,
        [pltpu.VMEM((2 * rows, width), jnp.bfloat16), pltpu.VMEM((2 * rows, GROUP), jnp.float32)],
        2 * 3 * rows * BLK * width,
        24 * rows * width,
    )(table, acc, far_own, far_pair, qkept, qgot)

    back = moved(send, to_pair)
    power = lax.psum(power, ("half", "mp"))
    return kernel_call(
        functools.partial(norm_kernel, channels),
        shape((rows, 2 * width), jnp.bfloat16),
        [VMEM] * 4,
        [],
        8 * rows * width,
        10 * rows * width,
    )(power, done, back, norm_gain.reshape(1, -1))


def solution(mesh):
    blocks = mesh.shape["ctx"] // 2
    grid = Mesh(mesh.devices.reshape(blocks, 2, mesh.shape["mp"]), ("blk", "half", "mp"))
    in_specs = (
        P(SPOTS, None, "mp"),
        P(None, None, "mp"),
        P("mp", None),
        P("mp", None),
        P("mp"),
        P("mp"),
        P(),
    )

    def program(projected, *rest):
        body = functools.partial(shards, blocks, projected.shape[2])
        return jax.shard_map(
            body, mesh=grid, in_specs=in_specs, out_specs=P(SPOTS, "mp"), check_vma=False
        )(projected, *rest)

    return program
```

```python
import functools

import jax
import jax.numpy as jnp
from jax import lax
from jax.experimental import pallas as pl
from jax.experimental.pallas import tpu as pltpu
from jax.sharding import Mesh, PartitionSpec as P

GROUP = 128
BLK = 128
norm_eps = 1e-06

VMEM = pl.BlockSpec(memory_space=pltpu.VMEM)
SMEM = pl.BlockSpec(memory_space=pltpu.SMEM)
SPOTS = ("blk", "half")


def moved(block, pairs):
    return lax.ppermute(block, SPOTS, pairs)


def boundaries(seq_ref, t):
    def step(k, carry):
        end, first, second = carry
        end = end + seq_ref[k]
        return end, first | (t == end).astype(jnp.int32), second | (t - 1 == end).astype(jnp.int32)

    first = (t == 0).astype(jnp.int32)
    second = (t == 1).astype(jnp.int32)
    _, first, second = lax.fori_loop(0, seq_ref.shape[0], step, (jnp.int32(0), first, second))
    return first, second


def counted(seq_ref, t):
    def step(k, carry):
        end, total = carry
        end = end + seq_ref[k]
        return end, total + (end <= t).astype(jnp.int32)

    _, total = lax.fori_loop(
        0, seq_ref.shape[0], step, (jnp.int32(0), jnp.zeros(t.shape, jnp.int32))
    )
    return jnp.where(t >= 0, total, -1)


def products_kernel(
    seq_ref, proj_ref, edge_ref, w_ref, sent_ref, kept_ref, qsent_ref, qkept_ref, x_ref, m1_ref, m2_ref
):
    rows = proj_ref.shape[1]
    width = sent_ref.shape[1]
    half = lax.axis_index("half")
    shard = lax.axis_index("blk") * 2 + half
    t = shard * rows + lax.broadcasted_iota(jnp.int32, (rows, GROUP), 0)
    first, second = boundaries(seq_ref, t)
    m1_ref[...] = 1.0 - first.astype(jnp.float32)
    m2_ref[...] = 1.0 - (first | second).astype(jnp.float32)

    def feature(panel, lanes):
        x = proj_ref[panel, :, lanes].astype(jnp.float32)
        x_ref[panel, 6:8, :] = edge_ref[panel, :, lanes].astype(jnp.float32)
        x_ref[panel, 8:, :] = x
        w = w_ref[panel, :, lanes]
        return (
            w[0:1] * x
            + w[1:2] * x_ref[panel, 7 : rows + 7, :] * m1_ref[...]
            + w[2:3] * x_ref[panel, 6 : rows + 6, :] * m2_ref[...]
        )

    def chunk(c, _):
        there = pl.ds(pl.multiple_of(c * GROUP, GROUP), GROUP)
        for which, p_ref, q_ref in ((1 - half, sent_ref, qsent_ref), (half, kept_ref, qkept_ref)):
            lanes = pl.ds(pl.multiple_of(which * width + c * GROUP, GROUP), GROUP)
            product = feature(1, lanes) * feature(2, lanes)
            p_ref[:, there] = product.astype(p_ref.dtype)
            q_ref[:, there] = feature(0, lanes).astype(q_ref.dtype)
        return 0

    lax.fori_loop(0, width // GROUP, chunk, 0)


def tables_kernel(seq_ref, taps_ref, out_ref, rev_ref, m_ref):
    groups = out_ref.shape[0]
    taps = taps_ref.shape[1]
    span = rev_ref.shape[1]
    width = out_ref.shape[3]
    half = lax.axis_index("half")
    start = lax.axis_index("blk") * (2 * BLK)
    turn = lax.broadcasted_iota(jnp.int32, (taps, span), 0) + lax.broadcasted_iota(
        jnp.int32, (taps, span), 1
    )
    turn = (turn == taps).astype(jnp.bfloat16)
    rev_ref[...] = jnp.dot(taps_ref[...], turn, preferred_element_type=jnp.float32)
    for part in range(2):
        t_in = start - taps + part * BLK + lax.broadcasted_iota(jnp.int32, (8, width), 1)
        t_out = start + part * BLK + lax.broadcasted_iota(jnp.int32, (BLK, GROUP), 0)
        seg_in = counted(seq_ref, t_in)[0:1]
        seg_out = counted(seq_ref, t_out)[:, 0:1]
        m_ref[part] = (seg_in == seg_out).astype(jnp.float32)

    def one(g, _):
        row = rev_ref[pl.ds(half * groups + g, 1), :]
        table = pltpu.roll(
            jnp.broadcast_to(row, (BLK, span)), 0, 1, stride=1, stride_axis=0
        )[:, :width]
        for part in range(2):
            out_ref[g, part] = (table * m_ref[part]).astype(out_ref.dtype)
        return 0

    lax.fori_loop(0, groups, one, 0)


def near_kernel(table_ref, own_ref, pair_ref, back_own_ref, back_pair_ref, bias_ref, acc_ref, win_ref):
    groups = table_ref.shape[0]
    half = lax.axis_index("half")
    own = pl.multiple_of(half * BLK, BLK)
    pair = pl.multiple_of((1 - half) * BLK, BLK)
    win_ref[pl.ds(own, BLK), :] = back_own_ref[...]
    win_ref[pl.ds(pair, BLK), :] = back_pair_ref[...]
    win_ref[pl.ds(2 * BLK + own, BLK), :] = own_ref[...]
    win_ref[pl.ds(2 * BLK + pair, BLK), :] = pair_ref[...]
    for g in range(groups):
        lanes = slice(g * GROUP, (g + 1) * GROUP)
        bias = bias_ref[:, pl.ds(pl.multiple_of(half * groups * GROUP + g * GROUP, GROUP), GROUP)]
        for part in range(2):
            total = jnp.dot(
                table_ref[g, part, :, (2 - part) * BLK :],
                win_ref[: (3 + part) * BLK, lanes],
                preferred_element_type=jnp.float32,
            )
            here = win_ref[(2 + part) * BLK : (3 + part) * BLK, lanes].astype(jnp.float32)
            acc_ref[part * BLK : (part + 1) * BLK, lanes] = total + bias * here


def far_kernel(
    table_ref, acc_ref, far_own_ref, far_pair_ref, qkept_ref, qgot_ref, kept_ref, sent_ref, pkept_ref, psent_ref, win_ref, sq_ref
):
    groups = table_ref.shape[0]
    half = lax.axis_index("half")
    own = pl.multiple_of(half * BLK, BLK)
    pair = pl.multiple_of((1 - half) * BLK, BLK)
    win_ref[pl.ds(own, BLK), :] = far_own_ref[...]
    win_ref[pl.ds(pair, BLK), :] = far_pair_ref[...]
    for g in range(groups):
        lanes = slice(g * GROUP, (g + 1) * GROUP)
        for part in range(2):
            rows = slice(part * BLK, (part + 1) * BLK)
            acc_ref[rows, lanes] += jnp.dot(
                table_ref[g, part, :, : (2 - part) * BLK],
                win_ref[part * BLK :, lanes],
                preferred_element_type=jnp.float32,
            )
    for spot, q_ref, out_ref in ((own, qkept_ref, kept_ref), (pair, qgot_ref, sent_ref)):
        squares = jnp.zeros((BLK, GROUP), jnp.float32)
        for g in range(groups):
            lanes = slice(g * GROUP, (g + 1) * GROUP)
            gated = q_ref[:, lanes].astype(jnp.float32) * acc_ref[pl.ds(spot, BLK), lanes]
            out_ref[:, lanes] = gated.astype(out_ref.dtype)
            squares = squares + gated * gated
        sq_ref[pl.ds(spot, BLK), :] = squares
    for spot, out_ref in ((own, pkept_ref), (pair, psent_ref)):
        out_ref[...] = lax.dot_general(
            jnp.ones((8, GROUP), jnp.float32),
            sq_ref[pl.ds(spot, BLK), :],
            (((1,), (1,)), ((), ())),
            precision=lax.Precision.HIGHEST,
            preferred_element_type=jnp.float32,
        )[0:1]


def norm_kernel(channels, p0_ref, p1_ref, p2_ref, p3_ref, kept_ref, got_ref, gain_ref, out_ref):
    half = lax.axis_index("half")
    width = kept_ref.shape[1]
    power = (p0_ref[...] + p1_ref[...]) + (p2_ref[...] + p3_ref[...])
    scale = lax.rsqrt(power / channels + norm_eps)
    diagonal = lax.broadcasted_iota(jnp.int32, (BLK, BLK), 0) == lax.broadcasted_iota(
        jnp.int32, (BLK, BLK), 1
    )
    column = jnp.sum(jnp.where(diagonal, scale, 0.0), axis=1, keepdims=True)
    for which, part_ref in ((half, kept_ref), (1 - half, got_ref)):
        for c in range(0, width, GROUP):
            lanes = pl.ds(pl.multiple_of(which * width + c, GROUP), GROUP)
            out_ref[:, lanes] = (
                part_ref[:, c : c + GROUP].astype(jnp.float32) * column * gain_ref[:, lanes]
            ).astype(out_ref.dtype)


def kernel_call(body, outs, in_specs, scratch, flops, moved_bytes):
    return pl.pallas_call(
        body,
        out_shape=outs,
        in_specs=in_specs,
        out_specs=jax.tree.map(lambda _: VMEM, outs),
        scratch_shapes=scratch,
        compiler_params=pltpu.CompilerParams(vmem_limit_bytes=24 << 20),
        cost_estimate=pl.CostEstimate(flops=flops, bytes_accessed=moved_bytes, transcendentals=0),
    )


def shards(blocks, channels, projected, short_weight, filter_taps, tap_blocks, skip_bias, norm_gain, seq_lengths):
    rows = projected.shape[0]
    width = projected.shape[2] // 2
    groups = width // GROUP
    taps = filter_taps.shape[1]
    shape = jax.ShapeDtypeStruct
    half_shape = shape((rows, width), jnp.bfloat16)
    half_wide = shape((rows, width), jnp.float32)

    spots = range(2 * blocks)
    to_next = [(i, (i + 1) % (2 * blocks)) for i in spots]
    to_pair = [(i, i ^ 1) for i in spots]
    ahead = [(i, (i + 2) % (2 * blocks)) for i in spots]
    ahead_pair = [(i, ((i ^ 1) + 2) % (2 * blocks)) for i in spots]

    panels = jnp.transpose(projected, (1, 0, 2))
    edge = moved(panels[:, rows - 2 :], to_next)

    sent, kept, qsent, qkept = kernel_call(
        products_kernel,
        (half_shape, half_shape, half_shape, half_wide),
        [SMEM, VMEM, VMEM, VMEM],
        [
            pltpu.VMEM((3, rows + 8, GROUP), jnp.float32),
            pltpu.VMEM((rows, GROUP), jnp.float32),
            pltpu.VMEM((rows, GROUP), jnp.float32),
        ],
        60 * rows * width,
        16 * rows * width,
    )(seq_lengths, panels, edge, short_weight)

    pair = moved(sent, to_pair)
    back_own = moved(kept, ahead)
    back_pair = moved(sent, ahead_pair)
    qgot = moved(qsent, to_pair)

    scaled = (filter_taps * jnp.repeat(tap_blocks.astype(jnp.float32), BLK, axis=1)).astype(jnp.bfloat16)
    table = kernel_call(
        tables_kernel,
        shape((groups, 2, BLK, taps + BLK), jnp.bfloat16),
        [SMEM, VMEM],
        [pltpu.VMEM((2 * groups, taps + 2 * BLK), jnp.float32), pltpu.VMEM((2, BLK, taps + BLK), jnp.float32)],
        40 * groups * BLK * taps,
        8 * groups * BLK * taps,
    )(seq_lengths, scaled)

    acc = kernel_call(
        near_kernel,
        shape((2 * rows, width), jnp.float32),
        [VMEM] * 6,
        [pltpu.VMEM((4 * rows, width), jnp.bfloat16)],
        2 * 7 * rows * BLK * width,
        16 * rows * width,
    )(table, kept, pair, back_own, back_pair, skip_bias.reshape(1, -1))

    far_own = moved(back_own, ahead)
    far_pair = moved(back_pair, ahead)
    done, send, pkept, psent = kernel_call(
        far_kernel,
        (half_wide, half_shape, shape((1, rows), jnp.float32), shape((1, rows), jnp.float32)),
        [VMEM] * 6,
        [pltpu.VMEM((2 * rows, width), jnp.bfloat16), pltpu.VMEM((2 * rows, GROUP), jnp.float32)],
        2 * 3 * rows * BLK * width,
        24 * rows * width,
    )(table, acc, far_own, far_pair, qkept, qgot)

    power = pkept + moved(psent, to_pair)
    powers = [power] + [lax.ppermute(power, "mp", [(i, i ^ k) for i in range(4)]) for k in (1, 2, 3)]
    back = moved(send, to_pair)
    return kernel_call(
        functools.partial(norm_kernel, channels),
        shape((rows, 2 * width), jnp.bfloat16),
        [VMEM] * 7,
        [],
        8 * rows * width,
        10 * rows * width,
    )(*powers, done, back, norm_gain.reshape(1, -1))


def solution(mesh):
    blocks = mesh.shape["ctx"] // 2
    grid = Mesh(mesh.devices.reshape(blocks, 2, mesh.shape["mp"]), ("blk", "half", "mp"))
    in_specs = (
        P(SPOTS, None, "mp"),
        P(None, None, "mp"),
        P("mp", None),
        P("mp", None),
        P("mp"),
        P("mp"),
        P(),
    )

    def program(projected, *rest):
        body = functools.partial(shards, blocks, projected.shape[2])
        return jax.shard_map(
            body, mesh=grid, in_specs=in_specs, out_specs=P(SPOTS, "mp"), check_vma=False
        )(projected, *rest)

    return program
```

```python
import functools

import jax
import jax.numpy as jnp
from jax import lax
from jax.experimental import pallas as pl
from jax.experimental.pallas import tpu as pltpu
from jax.sharding import Mesh, PartitionSpec as P

GROUP = 128
BLK = 128
norm_eps = 1e-06

VMEM = pl.BlockSpec(memory_space=pltpu.VMEM)
SMEM = pl.BlockSpec(memory_space=pltpu.SMEM)
SPOTS = ("blk", "half")


def moved(block, pairs):
    return lax.ppermute(block, SPOTS, pairs)


def boundaries(seq_ref, t):
    def step(k, carry):
        end, first, second = carry
        end = end + seq_ref[k]
        return end, first | (t == end).astype(jnp.int32), second | (t - 1 == end).astype(jnp.int32)

    first = (t == 0).astype(jnp.int32)
    second = (t == 1).astype(jnp.int32)
    _, first, second = lax.fori_loop(0, seq_ref.shape[0], step, (jnp.int32(0), first, second))
    return first, first | second


def row_masks(seq_ref, start, m1_ref, m2_ref):
    rows = lax.broadcasted_iota(jnp.int32, (BLK, GROUP), 0)
    diagonal = rows == lax.broadcasted_iota(jnp.int32, (BLK, GROUP), 1)
    marks = boundaries(seq_ref, start + lax.broadcasted_iota(jnp.int32, (8, GROUP), 1))
    for mark, m_ref in zip(marks, (m1_ref, m2_ref)):
        keep = 1.0 - mark.astype(jnp.float32)[0:1]
        column = jnp.sum(jnp.where(diagonal, keep, 0.0), axis=1, keepdims=True)
        m_ref[...] = jnp.broadcast_to(column, (BLK, GROUP))


def counted(seq_ref, t):
    def step(k, carry):
        end, total = carry
        end = end + seq_ref[k]
        return end, total + (end <= t).astype(jnp.int32)

    _, total = lax.fori_loop(
        0, seq_ref.shape[0], step, (jnp.int32(0), jnp.zeros(t.shape, jnp.int32))
    )
    return jnp.where(t >= 0, total, -1)


def feature(x, x_ref, w, m1_ref, m2_ref):
    rows = x.shape[0]
    return (
        w[0:1] * x
        + w[1:2] * x_ref[7 : rows + 7, :] * m1_ref[...]
        + w[2:3] * x_ref[6 : rows + 6, :] * m2_ref[...]
    )


def products_kernel(
    seq_hbm, panels_hbm, w_hbm, sent_ref, kept_ref, qsent_ref, qkept_ref,
    seq_ref, kv_ref, w_ref, x_ref, m1_ref, m2_ref, sems,
):
    rows, width = qsent_ref.shape
    pieces = kv_ref.shape[0]
    piece = kv_ref.shape[3]
    half = lax.axis_index("half")
    shard = lax.axis_index("blk") * 2 + half
    keep_at = pl.multiple_of(half * width, width)
    send_at = pl.multiple_of((1 - half) * width, width)

    loads = [
        pltpu.make_async_copy(seq_hbm, seq_ref, sems.at[0]),
        pltpu.make_async_copy(w_hbm, w_ref, sems.at[1]),
    ]
    for p in range(pieces):
        at = keep_at if p < pieces // 2 else send_at
        lanes = pl.ds(pl.multiple_of(at + (p % (pieces // 2)) * piece, piece), piece)
        loads.append(pltpu.make_async_copy(panels_hbm.at[1:3, :, lanes], kv_ref.at[p], sems.at[2 + p]))
    asides = [
        pltpu.make_async_copy(panels_hbm.at[0, :, pl.ds(keep_at, width)], qkept_ref, sems.at[2 + pieces]),
        pltpu.make_async_copy(panels_hbm.at[0, :, pl.ds(send_at, width)], qsent_ref, sems.at[3 + pieces]),
    ]
    for load in loads + asides:
        load.start()
    loads[0].wait()
    row_masks(seq_ref, shard * rows, m1_ref, m2_ref)
    x_ref[:, 0:8, :] = jnp.zeros((x_ref.shape[0], 8, GROUP), jnp.float32)
    loads[1].wait()
    asides[0].wait()
    asides[1].wait()
    for p in range(pieces):
        loads[2 + p].wait()
        kept = p < pieces // 2
        out_ref, q_ref, at = (kept_ref, qkept_ref, keep_at) if kept else (sent_ref, qsent_ref, send_at)
        for c in range(0, piece, GROUP):
            base = (p % (pieces // 2)) * piece + c
            there = slice(base, base + GROUP)
            w_lanes = pl.ds(pl.multiple_of(at + base, GROUP), GROUP)
            slot = (c // GROUP) % (x_ref.shape[0] // 2) * 2
            heads, tails, made = [], [], []
            for i in range(2):
                x = kv_ref[p, i, :, c : c + GROUP].astype(jnp.float32)
                x_ref[slot + i, 8:, :] = x
                made.append(feature(x, x_ref.at[slot + i], w_ref[1 + i, :, w_lanes], m1_ref, m2_ref))
                heads.append(x[0:2])
                tails.append(x[rows - 2 :])
            out_ref[:rows, there] = (made[0] * made[1]).astype(out_ref.dtype)
            tails.append(q_ref[rows - 16 :, there].astype(jnp.float32)[14:])
            extra = jnp.concatenate(heads + tails + [jnp.zeros((6, GROUP), jnp.float32)], 0)
            out_ref[rows:, there] = extra.astype(out_ref.dtype)


def edge_marks(seq_ref):
    t = (
        (lax.axis_index("blk") - 2) * (2 * BLK)
        + lax.broadcasted_iota(jnp.int32, (8, GROUP), 1) * BLK
        + lax.broadcasted_iota(jnp.int32, (8, GROUP), 0)
    )
    return [1.0 - mark.astype(jnp.float32) for mark in boundaries(seq_ref, t)]


def first_rows(now, ahead, w_ref, lanes, marks, spot):
    m1, m2 = [mark[:, spot : spot + 1] for mark in marks]
    top = lax.broadcasted_iota(jnp.int32, now.shape, 0) == 0
    made = []
    for i in range(2):
        x0 = pltpu.roll(now, (8 - 2 * i) % 8, 0) if i else now
        x1 = jnp.where(top, pltpu.roll(ahead, 3 - 2 * i, 0), pltpu.roll(now, (9 - 2 * i) % 8, 0))
        x2 = pltpu.roll(ahead, 4 - 2 * i, 0)
        w = w_ref[1 + i, :, lanes]
        made.append(w[0:1] * x0 + w[1:2] * x1 * m1 + w[2:3] * x2 * m2)
    return made[0] * made[1]


def put_first_rows(win_ref, at, rows):
    old = win_ref[at : at + 16, :].astype(jnp.float32)
    new = jnp.concatenate([rows, rows], 0)
    first = lax.broadcasted_iota(jnp.int32, old.shape, 0) < 2
    win_ref[at : at + 16, :] = jnp.where(first, new, old).astype(win_ref.dtype)


def tables_kernel(seq_ref, taps_ref, out_ref, rev_ref, m_ref):
    groups = out_ref.shape[0]
    taps = taps_ref.shape[1]
    span = rev_ref.shape[1]
    width = out_ref.shape[3]
    half = lax.axis_index("half")
    start = lax.axis_index("blk") * (2 * BLK)
    turn = lax.broadcasted_iota(jnp.int32, (taps, span), 0) + lax.broadcasted_iota(
        jnp.int32, (taps, span), 1
    )
    turn = (turn == taps).astype(jnp.bfloat16)
    rev_ref[...] = jnp.dot(taps_ref[...], turn, preferred_element_type=jnp.float32)
    for part in range(2):
        t_in = start - taps + part * BLK + lax.broadcasted_iota(jnp.int32, (8, width), 1)
        t_out = start + part * BLK + lax.broadcasted_iota(jnp.int32, (BLK, GROUP), 0)
        seg_in = counted(seq_ref, t_in)[0:1]
        seg_out = counted(seq_ref, t_out)[:, 0:1]
        m_ref[part] = (seg_in == seg_out).astype(jnp.float32)

    def one(g, _):
        row = rev_ref[pl.ds(half * groups + g, 1), :]
        table = pltpu.roll(
            jnp.broadcast_to(row, (BLK, span)), 0, 1, stride=1, stride_axis=0
        )[:, :width]
        for part in range(2):
            out_ref[g, part] = (table * m_ref[part]).astype(out_ref.dtype)
        return 0

    lax.fori_loop(0, groups, one, 0)


def near_kernel(
    seq_ref, table_ref, own_ref, pair_ref, back_own_ref, back_pair_ref, qkept_ref, qgot_ref, w_ref, bias_ref,
    acc_ref, q_ref, win_ref, extra_ref, x_ref, m1_ref, m2_ref,
):
    groups = table_ref.shape[0]
    width = groups * GROUP
    half = lax.axis_index("half")
    start = lax.axis_index("blk") * (2 * BLK)
    half_lanes = pl.ds(pl.multiple_of(half * width, width), width)
    for spot, message in ((half, back_own_ref), (1 - half, back_pair_ref), (2 + half, own_ref), (3 - half, pair_ref)):
        win_ref[pl.ds(pl.multiple_of(spot * BLK, BLK), BLK), :] = message[:BLK]
        extra_ref[spot] = message[BLK:].astype(jnp.float32)
    marks = edge_marks(seq_ref)
    for spot in (1, 2, 3):
        rows = first_rows(extra_ref[spot, :8], extra_ref[spot - 1, :8], w_ref, half_lanes, marks, spot + 2)
        put_first_rows(win_ref, spot * BLK, rows)
    for g in range(groups):
        lanes = slice(g * GROUP, (g + 1) * GROUP)
        bias = bias_ref[:, pl.ds(pl.multiple_of(half * width + g * GROUP, GROUP), GROUP)]
        for part in range(2):
            total = jnp.dot(
                table_ref[g, part, :, (3 - part) * BLK :],
                win_ref[BLK : (3 + part) * BLK, lanes],
                preferred_element_type=jnp.float32,
            )
            here = win_ref[(2 + part) * BLK : (3 + part) * BLK, lanes].astype(jnp.float32)
            acc_ref[part * BLK : (part + 1) * BLK, lanes] = total + bias * here
    for part, raw_ref in ((half, qkept_ref), (1 - half, qgot_ref)):
        row_masks(seq_ref, start + part * BLK, m1_ref, m2_ref)
        for g in range(groups):
            lanes = slice(g * GROUP, (g + 1) * GROUP)
            w = w_ref[0, :, pl.ds(pl.multiple_of(half * width + g * GROUP, GROUP), GROUP)]
            x = raw_ref[:, lanes].astype(jnp.float32)
            slot = g % 2
            x_ref[slot, 6:8, :] = extra_ref[1 + part, 8:10, lanes]
            x_ref[slot, 8:, :] = x
            q_ref[pl.ds(pl.multiple_of(part * BLK, BLK), BLK), lanes] = feature(
                x, x_ref.at[slot], w, m1_ref, m2_ref
            )


def far_kernel(deep, seq_ref, table_ref, acc_ref, q_ref, w_ref, *refs):
    messages, refs = refs[: 4 + deep], refs[4 + deep :]
    back_own_ref, back_pair_ref, far_own_ref, far_pair_ref = messages[:4]
    kept_ref, sent_ref, power_ref, win_ref, extra_ref, sq_ref = refs
    groups = table_ref.shape[0]
    width = groups * GROUP
    half = lax.axis_index("half")
    half_lanes = pl.ds(pl.multiple_of(half * width, width), width)
    for spot, message in (
        (half, far_own_ref), (1 - half, far_pair_ref), (2 + half, back_own_ref), (3 - half, back_pair_ref)
    ):
        win_ref[pl.ds(pl.multiple_of(spot * BLK, BLK), BLK), :] = message[:BLK]
        extra_ref[spot] = message[BLK:].astype(jnp.float32)
    marks = edge_marks(seq_ref)
    for spot in (1, 2):
        rows = first_rows(extra_ref[spot, :8], extra_ref[spot - 1, :8], w_ref, half_lanes, marks, spot)
        put_first_rows(win_ref, spot * BLK, rows)
    if deep:
        ahead = messages[4][...].astype(jnp.float32)[:8]
        put_first_rows(win_ref, 0, first_rows(extra_ref[0, :8], ahead, w_ref, half_lanes, marks, 0))
    for part in range(2):
        squares = jnp.zeros((BLK, GROUP), jnp.float32)
        rows = slice(part * BLK, (part + 1) * BLK)
        for g in range(groups):
            lanes = slice(g * GROUP, (g + 1) * GROUP)
            filtered = acc_ref[rows, lanes] + jnp.dot(
                table_ref[g, part, :, : (3 - part) * BLK],
                win_ref[part * BLK : 3 * BLK, lanes],
                preferred_element_type=jnp.float32,
            )
            gated = q_ref[rows, lanes] * filtered
            squares = squares + gated * gated

            @pl.when(half == part)
            def _():
                kept_ref[:, lanes] = gated

            @pl.when(half != part)
            def _():
                sent_ref[:, lanes] = gated.astype(sent_ref.dtype)

        sq_ref[rows, :] = squares
    power_ref[...] = lax.dot_general(
        jnp.ones((8, GROUP), jnp.float32),
        sq_ref[...],
        (((1,), (1,)), ((), ())),
        precision=lax.Precision.HIGHEST,
        preferred_element_type=jnp.float32,
    )[0:1]


def norm_kernel(channels, power_ref, power_got_ref, kept_ref, got_ref, gain_ref, out_ref):
    half = lax.axis_index("half")
    width = kept_ref.shape[1]
    mine = pl.ds(pl.multiple_of(half * BLK, BLK), BLK)
    power = power_ref[:, mine] + power_got_ref[:, mine]
    scale = lax.rsqrt(power / channels + norm_eps)
    diagonal = lax.broadcasted_iota(jnp.int32, (BLK, BLK), 0) == lax.broadcasted_iota(
        jnp.int32, (BLK, BLK), 1
    )
    column = jnp.sum(jnp.where(diagonal, scale, 0.0), axis=1, keepdims=True)
    for which, part_ref in ((half, kept_ref), (1 - half, got_ref)):
        for c in range(0, width, GROUP):
            lanes = pl.ds(pl.multiple_of(which * width + c, GROUP), GROUP)
            out_ref[:, lanes] = (
                part_ref[:, c : c + GROUP].astype(jnp.float32) * column * gain_ref[:, lanes]
            ).astype(out_ref.dtype)


def kernel_call(body, outs, in_specs, scratch, flops, moved_bytes):
    return pl.pallas_call(
        body,
        out_shape=outs,
        in_specs=in_specs,
        out_specs=jax.tree.map(lambda _: VMEM, outs),
        scratch_shapes=scratch,
        compiler_params=pltpu.CompilerParams(vmem_limit_bytes=24 << 20),
        cost_estimate=pl.CostEstimate(flops=flops, bytes_accessed=moved_bytes, transcendentals=0),
    )


def shards(blocks, whole_tokens, channels, projected, short_weight, filter_taps, tap_blocks, skip_bias, norm_gain, seq_lengths):
    rows = projected.shape[0]
    width = projected.shape[2] // 2
    groups = width // GROUP
    taps = filter_taps.shape[1]
    shape = jax.ShapeDtypeStruct
    half_shape = shape((rows, width), jnp.bfloat16)
    half_wide = shape((rows, width), jnp.float32)

    spots = range(2 * blocks)
    to_pair = [(i, i ^ 1) for i in spots]
    ahead = [(i, (i + 2) % (2 * blocks)) for i in spots]
    ahead_pair = [(i, ((i ^ 1) + 2) % (2 * blocks)) for i in spots]

    panels = jnp.transpose(projected, (1, 0, 2))
    message = shape((rows + 16, width), jnp.bfloat16)
    any_space = pl.BlockSpec(memory_space=pl.ANY)
    pieces = 4
    row_mask = pltpu.VMEM((rows, GROUP), jnp.float32)

    sent, kept, qsent, qkept = kernel_call(
        products_kernel,
        (message, message, half_shape, half_shape),
        [any_space] * 3,
        [
            pltpu.SMEM(seq_lengths.shape, jnp.int32),
            pltpu.VMEM((pieces, 2, rows, 2 * width // pieces), jnp.bfloat16),
            pltpu.VMEM(short_weight.shape, jnp.float32),
            pltpu.VMEM((4, rows + 8, GROUP), jnp.float32),
            row_mask,
            row_mask,
            pltpu.SemaphoreType.DMA((4 + pieces,)),
        ],
        40 * rows * width,
        16 * rows * width,
    )(seq_lengths, panels, short_weight)

    back_own = moved(kept, ahead)
    back_pair = moved(sent, ahead_pair)

    filter_taps, _ = lax.optimization_barrier((filter_taps, kept))
    scaled = (filter_taps * jnp.repeat(tap_blocks.astype(jnp.float32), BLK, axis=1)).astype(jnp.bfloat16)
    table = kernel_call(
        tables_kernel,
        shape((groups, 2, BLK, taps + BLK), jnp.bfloat16),
        [SMEM, VMEM],
        [pltpu.VMEM((2 * groups, taps + 2 * BLK), jnp.float32), pltpu.VMEM((2, BLK, taps + BLK), jnp.float32)],
        40 * groups * BLK * taps,
        8 * groups * BLK * taps,
    )(seq_lengths, scaled)

    table, back_own = lax.optimization_barrier((table, back_own))
    far_own = moved(back_own, ahead)
    far_pair = moved(back_pair, ahead)
    sent_late, qsent, back_pair = lax.optimization_barrier((sent, qsent, back_pair))
    pair = moved(sent_late, to_pair)
    qgot = moved(qsent, to_pair)
    extras = ()
    if whole_tokens // 2 > taps:
        half = lax.axis_index("half")
        straight = moved(kept[rows:], [(i, (i + 6) % (2 * blocks)) for i in spots])
        across = moved(sent[rows:], [(i, ((i ^ 1) + 6) % (2 * blocks)) for i in spots])
        extras = (jnp.where(half == 1, straight, across),)

    acc, q = kernel_call(
        near_kernel,
        (shape((2 * rows, width), jnp.float32), shape((2 * rows, width), jnp.float32)),
        [SMEM] + [VMEM] * 9,
        [
            pltpu.VMEM((4 * rows, width), jnp.bfloat16),
            pltpu.VMEM((4, 16, width), jnp.float32),
            pltpu.VMEM((2, rows + 8, GROUP), jnp.float32),
            row_mask,
            row_mask,
        ],
        2 * 5 * rows * BLK * width,
        16 * rows * width,
    )(seq_lengths, table, kept, pair, back_own, back_pair, qkept, qgot, short_weight, skip_bias.reshape(1, -1))

    done, send, power = kernel_call(
        functools.partial(far_kernel, len(extras)),
        (half_wide, half_shape, shape((1, 2 * rows), jnp.float32)),
        [SMEM] + [VMEM] * (8 + len(extras)),
        [
            pltpu.VMEM((4 * rows, width), jnp.bfloat16),
            pltpu.VMEM((4, 16, width), jnp.float32),
            pltpu.VMEM((2 * rows, GROUP), jnp.float32),
        ],
        2 * 5 * rows * BLK * width,
        24 * rows * width,
    )(seq_lengths, table, acc, q, short_weight, back_own, back_pair, far_own, far_pair, *extras)

    back = moved(send, to_pair)
    peers = lax.axis_size("mp")
    shares = [lax.ppermute(power, "mp", [(i, i ^ k) for i in range(peers)]) for k in range(1, peers)]
    power = sum(shares, power)
    return kernel_call(
        functools.partial(norm_kernel, channels),
        shape((rows, 2 * width), jnp.bfloat16),
        [VMEM] * 5,
        [],
        8 * rows * width,
        10 * rows * width,
    )(power, moved(power, to_pair), done, back, norm_gain.reshape(1, -1))


def solution(mesh):
    blocks = mesh.shape["ctx"] // 2
    grid = Mesh(mesh.devices.reshape(blocks, 2, mesh.shape["mp"]), ("blk", "half", "mp"))
    in_specs = (
        P(SPOTS, None, "mp"),
        P(None, None, "mp"),
        P("mp", None),
        P("mp", None),
        P("mp"),
        P("mp"),
        P(),
    )

    def program(projected, *rest):
        body = functools.partial(shards, blocks, projected.shape[0], projected.shape[2])
        return jax.shard_map(
            body, mesh=grid, in_specs=in_specs, out_specs=P(SPOTS, "mp"), check_vma=False
        )(projected, *rest)

    return program
```

```python
import functools

import jax
import jax.numpy as jnp
from jax import lax
from jax.experimental import pallas as pl
from jax.experimental.pallas import tpu as pltpu
from jax.sharding import Mesh, PartitionSpec as P

GROUP = 128
BLK = 128
norm_eps = 1e-06

VMEM = pl.BlockSpec(memory_space=pltpu.VMEM)
SMEM = pl.BlockSpec(memory_space=pltpu.SMEM)
SPOTS = ("blk", "half")


def moved(block, pairs):
    return lax.ppermute(block, SPOTS, pairs)


def boundaries(seq_ref, t):
    def step(k, carry):
        end, first, second = carry
        end = end + seq_ref[k]
        return end, first | (t == end).astype(jnp.int32), second | (t - 1 == end).astype(jnp.int32)

    first = (t == 0).astype(jnp.int32)
    second = (t == 1).astype(jnp.int32)
    _, first, second = lax.fori_loop(0, seq_ref.shape[0], step, (jnp.int32(0), first, second), unroll=True)
    return first, first | second


def row_masks(seq_ref, start, m1_ref, m2_ref):
    rows = lax.broadcasted_iota(jnp.int32, (BLK, GROUP), 0)
    diagonal = rows == lax.broadcasted_iota(jnp.int32, (BLK, GROUP), 1)
    marks = boundaries(seq_ref, start + lax.broadcasted_iota(jnp.int32, (8, GROUP), 1))
    for mark, m_ref in zip(marks, (m1_ref, m2_ref)):
        keep = 1.0 - mark.astype(jnp.float32)[0:1]
        column = jnp.sum(jnp.where(diagonal, keep, 0.0), axis=1, keepdims=True)
        m_ref[...] = jnp.broadcast_to(column, (BLK, GROUP))


def counted(seq_ref, t):
    def step(k, carry):
        end, total = carry
        end = end + seq_ref[k]
        return end, total + (end <= t).astype(jnp.int32)

    _, total = lax.fori_loop(
        0, seq_ref.shape[0], step, (jnp.int32(0), jnp.zeros(t.shape, jnp.int32)), unroll=True
    )
    return jnp.where(t >= 0, total, -1)


def feature(x, x_ref, w, m1_ref, m2_ref):
    rows = x.shape[0]
    return (
        w[0:1] * x
        + w[1:2] * x_ref[7 : rows + 7, :] * m1_ref[...]
        + w[2:3] * x_ref[6 : rows + 6, :] * m2_ref[...]
    )


def products_kernel(
    seq_hbm, panels_hbm, w_hbm, sent_ref, kept_ref, qsent_ref, qkept_ref,
    seq_ref, kv_ref, w_ref, x_ref, m1_ref, m2_ref, sems,
):
    rows, width = qsent_ref.shape
    pieces = kv_ref.shape[0]
    piece = kv_ref.shape[3]
    half = lax.axis_index("half")
    shard = lax.axis_index("blk") * 2 + half
    keep_at = pl.multiple_of(half * width, width)
    send_at = pl.multiple_of((1 - half) * width, width)

    loads = [
        pltpu.make_async_copy(seq_hbm, seq_ref, sems.at[0]),
        pltpu.make_async_copy(w_hbm, w_ref, sems.at[1]),
    ]
    for p in range(pieces):
        at = keep_at if p < pieces // 2 else send_at
        lanes = pl.ds(pl.multiple_of(at + (p % (pieces // 2)) * piece, piece), piece)
        loads.append(pltpu.make_async_copy(panels_hbm.at[1:3, :, lanes], kv_ref.at[p], sems.at[2 + p]))
    asides = [
        pltpu.make_async_copy(panels_hbm.at[0, :, pl.ds(keep_at, width)], qkept_ref, sems.at[2 + pieces]),
        pltpu.make_async_copy(panels_hbm.at[0, :, pl.ds(send_at, width)], qsent_ref, sems.at[3 + pieces]),
    ]
    for load in loads + asides:
        load.start()
    loads[0].wait()
    row_masks(seq_ref, shard * rows, m1_ref, m2_ref)
    x_ref[:, 0:8, :] = jnp.zeros((x_ref.shape[0], 8, GROUP), jnp.float32)
    loads[1].wait()
    asides[0].wait()
    asides[1].wait()
    for p in range(pieces):
        loads[2 + p].wait()
        kept = p < pieces // 2
        out_ref, q_ref, at = (kept_ref, qkept_ref, keep_at) if kept else (sent_ref, qsent_ref, send_at)
        for c in range(0, piece, GROUP):
            base = (p % (pieces // 2)) * piece + c
            there = slice(base, base + GROUP)
            w_lanes = pl.ds(pl.multiple_of(at + base, GROUP), GROUP)
            slot = (c // GROUP) % (x_ref.shape[0] // 2) * 2
            heads, tails, made = [], [], []
            for i in range(2):
                x = kv_ref[p, i, :, c : c + GROUP].astype(jnp.float32)
                x_ref[slot + i, 8:, :] = x
                made.append(feature(x, x_ref.at[slot + i], w_ref[1 + i, :, w_lanes], m1_ref, m2_ref))
                heads.append(x[0:2])
                tails.append(x[rows - 2 :])
            out_ref[:rows, there] = (made[0] * made[1]).astype(out_ref.dtype)
            tails.append(q_ref[rows - 16 :, there].astype(jnp.float32)[14:])
            extra = jnp.concatenate(heads + tails + [jnp.zeros((6, GROUP), jnp.float32)], 0)
            out_ref[rows:, there] = extra.astype(out_ref.dtype)


def edge_marks(seq_ref):
    t = (
        (lax.axis_index("blk") - 2) * (2 * BLK)
        + lax.broadcasted_iota(jnp.int32, (8, GROUP), 1) * BLK
        + lax.broadcasted_iota(jnp.int32, (8, GROUP), 0)
    )
    return [1.0 - mark.astype(jnp.float32) for mark in boundaries(seq_ref, t)]


def first_rows(now, ahead, w_ref, lanes, marks, spot):
    m1, m2 = [mark[:, spot : spot + 1] for mark in marks]
    top = lax.broadcasted_iota(jnp.int32, now.shape, 0) == 0
    made = []
    for i in range(2):
        x0 = pltpu.roll(now, (8 - 2 * i) % 8, 0) if i else now
        x1 = jnp.where(top, pltpu.roll(ahead, 3 - 2 * i, 0), pltpu.roll(now, (9 - 2 * i) % 8, 0))
        x2 = pltpu.roll(ahead, 4 - 2 * i, 0)
        w = w_ref[1 + i, :, lanes]
        made.append(w[0:1] * x0 + w[1:2] * x1 * m1 + w[2:3] * x2 * m2)
    return made[0] * made[1]


def put_first_rows(win_ref, at, rows):
    old = win_ref[at : at + 16, :].astype(jnp.float32)
    new = jnp.concatenate([rows, rows], 0)
    first = lax.broadcasted_iota(jnp.int32, old.shape, 0) < 2
    win_ref[at : at + 16, :] = jnp.where(first, new, old).astype(win_ref.dtype)


def tables_kernel(seq_ref, taps_ref, out_ref, rev_ref, m_ref):
    groups = out_ref.shape[0]
    taps = taps_ref.shape[1]
    span = rev_ref.shape[1]
    width = out_ref.shape[3]
    half = lax.axis_index("half")
    start = lax.axis_index("blk") * (2 * BLK)
    turn = lax.broadcasted_iota(jnp.int32, (taps, span), 0) + lax.broadcasted_iota(
        jnp.int32, (taps, span), 1
    )
    turn = (turn == taps).astype(jnp.bfloat16)
    rev_ref[...] = jnp.dot(taps_ref[...], turn, preferred_element_type=jnp.float32)
    for part in range(2):
        t_in = start - taps + part * BLK + lax.broadcasted_iota(jnp.int32, (8, width), 1)
        t_out = start + part * BLK + lax.broadcasted_iota(jnp.int32, (BLK, GROUP), 0)
        seg_in = counted(seq_ref, t_in)[0:1]
        seg_out = counted(seq_ref, t_out)[:, 0:1]
        m_ref[part] = (seg_in == seg_out).astype(jnp.float32)

    def one(g, _):
        row = rev_ref[pl.ds(half * groups + g, 1), :]
        table = pltpu.roll(
            jnp.broadcast_to(row, (BLK, span)), 0, 1, stride=1, stride_axis=0
        )[:, :width]
        for part in range(2):
            out_ref[g, part] = (table * m_ref[part]).astype(out_ref.dtype)
        return 0

    lax.fori_loop(0, groups, one, 0)


def near_kernel(
    seq_ref, table_ref, own_ref, pair_ref, back_own_ref, back_pair_ref, qkept_ref, qgot_ref, w_ref, bias_ref,
    acc_ref, q_ref, marks_ref, win_ref, extra_ref, x_ref, m1_ref, m2_ref,
):
    groups = table_ref.shape[0]
    width = groups * GROUP
    half = lax.axis_index("half")
    start = lax.axis_index("blk") * (2 * BLK)
    half_lanes = pl.ds(pl.multiple_of(half * width, width), width)
    for spot, message in ((half, back_own_ref), (1 - half, back_pair_ref), (2 + half, own_ref), (3 - half, pair_ref)):
        win_ref[pl.ds(pl.multiple_of(spot * BLK, BLK), BLK), :] = message[:BLK]
        extra_ref[spot] = message[BLK:].astype(jnp.float32)
    marks = edge_marks(seq_ref)
    marks_ref[0], marks_ref[1] = marks
    for spot in (1, 2, 3):
        rows = first_rows(extra_ref[spot, :8], extra_ref[spot - 1, :8], w_ref, half_lanes, marks, spot + 2)
        put_first_rows(win_ref, spot * BLK, rows)
    for g in range(groups):
        lanes = slice(g * GROUP, (g + 1) * GROUP)
        bias = bias_ref[:, pl.ds(pl.multiple_of(half * width + g * GROUP, GROUP), GROUP)]
        for part in range(2):
            total = jnp.dot(
                table_ref[g, part, :, (3 - part) * BLK :],
                win_ref[BLK : (3 + part) * BLK, lanes],
                preferred_element_type=jnp.float32,
            )
            here = win_ref[(2 + part) * BLK : (3 + part) * BLK, lanes].astype(jnp.float32)
            acc_ref[part * BLK : (part + 1) * BLK, lanes] = total + bias * here
    for part, raw_ref in ((half, qkept_ref), (1 - half, qgot_ref)):
        row_masks(seq_ref, start + part * BLK, m1_ref, m2_ref)
        for g in range(groups):
            lanes = slice(g * GROUP, (g + 1) * GROUP)
            w = w_ref[0, :, pl.ds(pl.multiple_of(half * width + g * GROUP, GROUP), GROUP)]
            x = raw_ref[:, lanes].astype(jnp.float32)
            slot = g % 2
            x_ref[slot, 6:8, :] = extra_ref[1 + part, 8:10, lanes]
            x_ref[slot, 8:, :] = x
            q_ref[pl.ds(pl.multiple_of(part * BLK, BLK), BLK), lanes] = feature(
                x, x_ref.at[slot], w, m1_ref, m2_ref
            )


def far_kernel(deep, table_ref, acc_ref, q_ref, w_ref, marks_ref, *refs):
    messages, refs = refs[: 4 + deep], refs[4 + deep :]
    back_own_ref, back_pair_ref, far_own_ref, far_pair_ref = messages[:4]
    kept_ref, sent_ref, power_ref, win_ref, extra_ref, gated_ref = refs
    groups = table_ref.shape[0]
    width = groups * GROUP
    half = lax.axis_index("half")
    half_lanes = pl.ds(pl.multiple_of(half * width, width), width)
    for spot, message in (
        (half, far_own_ref), (1 - half, far_pair_ref), (2 + half, back_own_ref), (3 - half, back_pair_ref)
    ):
        win_ref[pl.ds(pl.multiple_of(spot * BLK, BLK), BLK), :] = message[:BLK]
        extra_ref[spot] = message[BLK:].astype(jnp.float32)
    marks = [marks_ref[0], marks_ref[1]]
    for spot in (1, 2):
        rows = first_rows(extra_ref[spot, :8], extra_ref[spot - 1, :8], w_ref, half_lanes, marks, spot)
        put_first_rows(win_ref, spot * BLK, rows)
    if deep:
        ahead = messages[4][...].astype(jnp.float32)[:8]
        put_first_rows(win_ref, 0, first_rows(extra_ref[0, :8], ahead, w_ref, half_lanes, marks, 0))
    power = []
    for part in range(2):
        squares = jnp.zeros((BLK, GROUP), jnp.float32)
        rows = slice(part * BLK, (part + 1) * BLK)
        for g in range(groups):
            lanes = slice(g * GROUP, (g + 1) * GROUP)
            filtered = acc_ref[rows, lanes] + jnp.dot(
                table_ref[g, part, :, : (3 - part) * BLK],
                win_ref[part * BLK : 3 * BLK, lanes],
                preferred_element_type=jnp.float32,
            )
            gated = q_ref[rows, lanes] * filtered
            squares = squares + gated * gated
            gated_ref[rows, lanes] = gated
        power.append(
            lax.dot_general(
                jnp.ones((8, GROUP), jnp.float32),
                squares,
                (((1,), (1,)), ((), ())),
                precision=lax.Precision.HIGHEST,
                preferred_element_type=jnp.float32,
            )[0:1]
        )
    power_ref[...] = jnp.concatenate(power, 1)
    kept_ref[...] = gated_ref[pl.ds(pl.multiple_of(half * BLK, BLK), BLK), :]
    sent_ref[...] = gated_ref[pl.ds(pl.multiple_of((1 - half) * BLK, BLK), BLK), :].astype(sent_ref.dtype)


def norm_kernel(channels, *refs):
    half = lax.axis_index("half")
    *power_refs, kept_ref, got_ref, gain_ref, out_ref = refs
    width = kept_ref.shape[1]
    mine = pl.ds(pl.multiple_of(half * BLK, BLK), BLK)
    power = sum(ref[:, mine] for ref in power_refs)
    scale = lax.rsqrt(power / channels + norm_eps)
    diagonal = lax.broadcasted_iota(jnp.int32, (BLK, BLK), 0) == lax.broadcasted_iota(
        jnp.int32, (BLK, BLK), 1
    )
    column = jnp.sum(jnp.where(diagonal, scale, 0.0), axis=1, keepdims=True)
    for which, part_ref in ((half, kept_ref), (1 - half, got_ref)):
        for c in range(0, width, GROUP):
            lanes = pl.ds(pl.multiple_of(which * width + c, GROUP), GROUP)
            out_ref[:, lanes] = (
                part_ref[:, c : c + GROUP].astype(jnp.float32) * column * gain_ref[:, lanes]
            ).astype(out_ref.dtype)


def kernel_call(body, outs, in_specs, scratch, flops, moved_bytes, vmem=24 << 20):
    return pl.pallas_call(
        body,
        out_shape=outs,
        in_specs=in_specs,
        out_specs=jax.tree.map(lambda _: VMEM, outs),
        scratch_shapes=scratch,
        compiler_params=pltpu.CompilerParams(vmem_limit_bytes=vmem),
        cost_estimate=pl.CostEstimate(flops=flops, bytes_accessed=moved_bytes, transcendentals=0),
    )


def shards(blocks, whole_tokens, channels, projected, short_weight, filter_taps, tap_blocks, skip_bias, norm_gain, seq_lengths):
    rows = projected.shape[0]
    width = projected.shape[2] // 2
    groups = width // GROUP
    taps = filter_taps.shape[1]
    shape = jax.ShapeDtypeStruct
    half_shape = shape((rows, width), jnp.bfloat16)
    half_wide = shape((rows, width), jnp.float32)

    spots = range(2 * blocks)
    to_pair = [(i, i ^ 1) for i in spots]
    ahead = [(i, (i + 2) % (2 * blocks)) for i in spots]
    ahead_pair = [(i, ((i ^ 1) + 2) % (2 * blocks)) for i in spots]

    panels = jnp.transpose(projected, (1, 0, 2))
    message = shape((rows + 16, width), jnp.bfloat16)
    hbm = pl.BlockSpec(memory_space=pltpu.HBM)
    pieces = 4
    row_mask = pltpu.VMEM((rows, GROUP), jnp.float32)

    sent, kept, qsent, qkept = kernel_call(
        products_kernel,
        (message, message, half_shape, half_shape),
        [hbm] * 3,
        [
            pltpu.SMEM(seq_lengths.shape, jnp.int32),
            pltpu.VMEM((pieces, 2, rows, 2 * width // pieces), jnp.bfloat16),
            pltpu.VMEM(short_weight.shape, jnp.float32),
            pltpu.VMEM((4, rows + 8, GROUP), jnp.float32),
            row_mask,
            row_mask,
            pltpu.SemaphoreType.DMA((4 + pieces,)),
        ],
        40 * rows * width,
        16 * rows * width,
        60 << 20,
    )(seq_lengths, panels, short_weight)

    back_own = moved(kept, ahead)
    back_pair = moved(sent, ahead_pair)
    pair = moved(sent, to_pair)

    filter_taps, _ = lax.optimization_barrier((filter_taps, kept))
    scaled = (filter_taps * jnp.repeat(tap_blocks.astype(jnp.float32), BLK, axis=1)).astype(jnp.bfloat16)
    table = kernel_call(
        tables_kernel,
        shape((groups, 2, BLK, taps + BLK), jnp.bfloat16),
        [SMEM, VMEM],
        [pltpu.VMEM((2 * groups, taps + 2 * BLK), jnp.float32), pltpu.VMEM((2, BLK, taps + BLK), jnp.float32)],
        40 * groups * BLK * taps,
        8 * groups * BLK * taps,
    )(seq_lengths, scaled)

    table, back_own = lax.optimization_barrier((table, back_own))
    far_own = moved(back_own, ahead)
    table, back_pair, qsent = lax.optimization_barrier((table, back_pair, qsent))
    far_pair = moved(back_pair, ahead)
    qgot = moved(qsent, to_pair)
    extras = ()
    if whole_tokens // 2 > taps:
        half = lax.axis_index("half")
        straight = moved(kept[rows:], [(i, (i + 6) % (2 * blocks)) for i in spots])
        across = moved(sent[rows:], [(i, ((i ^ 1) + 6) % (2 * blocks)) for i in spots])
        extras = (jnp.where(half == 1, straight, across),)

    acc, q, marks = kernel_call(
        near_kernel,
        (
            shape((2 * rows, width), jnp.float32),
            shape((2 * rows, width), jnp.float32),
            shape((2, 8, GROUP), jnp.float32),
        ),
        [SMEM] + [VMEM] * 9,
        [
            pltpu.VMEM((4 * rows, width), jnp.bfloat16),
            pltpu.VMEM((4, 16, width), jnp.float32),
            pltpu.VMEM((2, rows + 8, GROUP), jnp.float32),
            row_mask,
            row_mask,
        ],
        2 * 5 * rows * BLK * width,
        16 * rows * width,
    )(seq_lengths, table, kept, pair, back_own, back_pair, qkept, qgot, short_weight, skip_bias.reshape(1, -1))

    done, send, power = kernel_call(
        functools.partial(far_kernel, len(extras)),
        (half_wide, half_shape, shape((1, 2 * rows), jnp.float32)),
        [VMEM] * (9 + len(extras)),
        [
            pltpu.VMEM((4 * rows, width), jnp.bfloat16),
            pltpu.VMEM((4, 16, width), jnp.float32),
            pltpu.VMEM((2 * rows, width), jnp.float32),
        ],
        2 * 5 * rows * BLK * width,
        24 * rows * width,
    )(table, acc, q, short_weight, marks, back_own, back_pair, far_own, far_pair, *extras)

    back = moved(send, to_pair)
    peers = lax.axis_size("mp")
    powers = [power] + [
        lax.ppermute(power, SPOTS + ("mp",), [(i, i ^ k) for i in range(2 * blocks * peers)])
        for k in range(1, 2 * peers)
    ]
    return kernel_call(
        functools.partial(norm_kernel, channels),
        shape((rows, 2 * width), jnp.bfloat16),
        [VMEM] * (3 + len(powers)),
        [],
        8 * rows * width,
        10 * rows * width,
    )(*powers, done, back, norm_gain.reshape(1, -1))


def solution(mesh):
    blocks = mesh.shape["ctx"] // 2
    grid = Mesh(mesh.devices.reshape(blocks, 2, mesh.shape["mp"]), ("blk", "half", "mp"))
    in_specs = (
        P(SPOTS, None, "mp"),
        P(None, None, "mp"),
        P("mp", None),
        P("mp", None),
        P("mp"),
        P("mp"),
        P(),
    )

    def program(projected, *rest):
        body = functools.partial(shards, blocks, projected.shape[0], projected.shape[2])
        return jax.shard_map(
            body, mesh=grid, in_specs=in_specs, out_specs=P(SPOTS, "mp"), check_vma=False
        )(projected, *rest)

    return program
```

```python
import functools

import jax
import jax.numpy as jnp
from jax import lax
from jax.experimental import pallas as pl
from jax.experimental.pallas import tpu as pltpu
from jax.sharding import Mesh, PartitionSpec as P

GROUP = 128
BLK = 128
norm_eps = 1e-06

VMEM = pl.BlockSpec(memory_space=pltpu.VMEM)
SMEM = pl.BlockSpec(memory_space=pltpu.SMEM)
SPOTS = ("blk", "half")


def moved(block, pairs):
    return lax.ppermute(block, SPOTS, pairs)


def boundaries(seq_ref, t):
    def step(k, carry):
        end, first, second = carry
        end = end + seq_ref[k]
        return end, first | (t == end).astype(jnp.int32), second | (t - 1 == end).astype(jnp.int32)

    first = (t == 0).astype(jnp.int32)
    second = (t == 1).astype(jnp.int32)
    _, first, second = lax.fori_loop(0, seq_ref.shape[0], step, (jnp.int32(0), first, second), unroll=True)
    return first, first | second


def row_masks(seq_ref, start, m1_ref, m2_ref):
    rows = lax.broadcasted_iota(jnp.int32, (BLK, GROUP), 0)
    diagonal = rows == lax.broadcasted_iota(jnp.int32, (BLK, GROUP), 1)
    marks = boundaries(seq_ref, start + lax.broadcasted_iota(jnp.int32, (8, GROUP), 1))
    for mark, m_ref in zip(marks, (m1_ref, m2_ref)):
        keep = 1.0 - mark.astype(jnp.float32)[0:1]
        column = jnp.sum(jnp.where(diagonal, keep, 0.0), axis=1, keepdims=True)
        m_ref[...] = jnp.broadcast_to(column, (BLK, GROUP))


def counted(seq_ref, t):
    def step(k, carry):
        end, total = carry
        end = end + seq_ref[k]
        return end, total + (end <= t).astype(jnp.int32)

    _, total = lax.fori_loop(
        0, seq_ref.shape[0], step, (jnp.int32(0), jnp.zeros(t.shape, jnp.int32)), unroll=True
    )
    return jnp.where(t >= 0, total, -1)


def feature(x, x_ref, w, m1_ref, m2_ref):
    rows = x.shape[0]
    return (
        w[0:1] * x
        + w[1:2] * x_ref[7 : rows + 7, :] * m1_ref[...]
        + w[2:3] * x_ref[6 : rows + 6, :] * m2_ref[...]
    )


def products_kernel(
    seq_hbm, panels_hbm, w_hbm, sent_ref, kept_ref, qsent_ref, qkept_ref,
    seq_ref, kv_ref, w_ref, x_ref, m1_ref, m2_ref, sems,
):
    rows, width = qsent_ref.shape
    pieces = kv_ref.shape[0]
    piece = kv_ref.shape[3]
    half = lax.axis_index("half")
    shard = lax.axis_index("blk") * 2 + half
    keep_at = pl.multiple_of(half * width, width)
    send_at = pl.multiple_of((1 - half) * width, width)

    loads = [
        pltpu.make_async_copy(seq_hbm, seq_ref, sems.at[0]),
        pltpu.make_async_copy(w_hbm, w_ref, sems.at[1]),
    ]
    for p in range(pieces):
        at = keep_at if p < pieces // 2 else send_at
        lanes = pl.ds(pl.multiple_of(at + (p % (pieces // 2)) * piece, piece), piece)
        loads.append(pltpu.make_async_copy(panels_hbm.at[1:3, :, lanes], kv_ref.at[p], sems.at[2 + p]))
    asides = [
        pltpu.make_async_copy(panels_hbm.at[0, :, pl.ds(keep_at, width)], qkept_ref, sems.at[2 + pieces]),
        pltpu.make_async_copy(panels_hbm.at[0, :, pl.ds(send_at, width)], qsent_ref, sems.at[3 + pieces]),
    ]
    for load in loads + asides:
        load.start()
    loads[0].wait()
    row_masks(seq_ref, shard * rows, m1_ref, m2_ref)
    x_ref[:, 0:8, :] = jnp.zeros((x_ref.shape[0], 8, GROUP), jnp.float32)
    loads[1].wait()
    asides[0].wait()
    asides[1].wait()
    for p in range(pieces):
        loads[2 + p].wait()
        kept = p < pieces // 2
        out_ref, q_ref, at = (kept_ref, qkept_ref, keep_at) if kept else (sent_ref, qsent_ref, send_at)
        for c in range(0, piece, GROUP):
            base = (p % (pieces // 2)) * piece + c
            there = slice(base, base + GROUP)
            w_lanes = pl.ds(pl.multiple_of(at + base, GROUP), GROUP)
            slot = (c // GROUP) % (x_ref.shape[0] // 2) * 2
            heads, tails, made = [], [], []
            for i in range(2):
                x = kv_ref[p, i, :, c : c + GROUP].astype(jnp.float32)
                x_ref[slot + i, 8:, :] = x
                made.append(feature(x, x_ref.at[slot + i], w_ref[1 + i, :, w_lanes], m1_ref, m2_ref))
                heads.append(x[0:2])
                tails.append(x[rows - 2 :])
            out_ref[:rows, there] = (made[0] * made[1]).astype(out_ref.dtype)
            tails.append(q_ref[rows - 16 :, there].astype(jnp.float32)[14:])
            extra = jnp.concatenate(heads + tails + [jnp.zeros((6, GROUP), jnp.float32)], 0)
            out_ref[rows:, there] = extra.astype(out_ref.dtype)


def edge_marks(seq_ref):
    t = (
        (lax.axis_index("blk") - 2) * (2 * BLK)
        + lax.broadcasted_iota(jnp.int32, (8, GROUP), 1) * BLK
        + lax.broadcasted_iota(jnp.int32, (8, GROUP), 0)
    )
    return [1.0 - mark.astype(jnp.float32) for mark in boundaries(seq_ref, t)]


def first_rows(now, ahead, w_ref, lanes, marks, spot):
    m1, m2 = [mark[:, spot : spot + 1] for mark in marks]
    top = lax.broadcasted_iota(jnp.int32, now.shape, 0) == 0
    made = []
    for i in range(2):
        x0 = pltpu.roll(now, (8 - 2 * i) % 8, 0) if i else now
        x1 = jnp.where(top, pltpu.roll(ahead, 3 - 2 * i, 0), pltpu.roll(now, (9 - 2 * i) % 8, 0))
        x2 = pltpu.roll(ahead, 4 - 2 * i, 0)
        w = w_ref[1 + i, :, lanes]
        made.append(w[0:1] * x0 + w[1:2] * x1 * m1 + w[2:3] * x2 * m2)
    return made[0] * made[1]


def put_first_rows(win_ref, at, rows):
    old = win_ref[at : at + 16, :].astype(jnp.float32)
    new = jnp.concatenate([rows, rows], 0)
    first = lax.broadcasted_iota(jnp.int32, old.shape, 0) < 2
    win_ref[at : at + 16, :] = jnp.where(first, new, old).astype(win_ref.dtype)


def reaches_past(seq_ref, block):
    first = block * (2 * BLK)

    def step(k, carry):
        end, start = carry
        end = end + seq_ref[k]
        return end, jnp.where(end <= first, end, start)

    _, start = lax.fori_loop(0, seq_ref.shape[0], step, (jnp.int32(0), jnp.int32(0)), unroll=True)
    return first - 2 * BLK - start > BLK


def tables_kernel(seq_ref, taps_ref, out_ref, next_ref, rev_ref, m_ref):
    groups = out_ref.shape[0]
    taps = taps_ref.shape[1]
    span = out_ref.shape[3]
    half = lax.axis_index("half")
    start = lax.axis_index("blk") * (2 * BLK)
    turn = lax.broadcasted_iota(jnp.int32, (taps, span), 0) + lax.broadcasted_iota(
        jnp.int32, (taps, span), 1
    )
    turn = (turn == taps).astype(jnp.bfloat16)
    rev_ref[...] = jnp.dot(taps_ref[...], turn, preferred_element_type=jnp.float32)
    seg_in = counted(seq_ref, start - taps + lax.broadcasted_iota(jnp.int32, (8, span), 1))[0:1]
    for part in range(3):
        t_out = start + part * BLK + lax.broadcasted_iota(jnp.int32, (BLK, GROUP), 0)
        seg_out = counted(seq_ref, t_out)[:, 0:1]
        if part < 2:
            m_ref[part] = (seg_in == seg_out).astype(jnp.float32)
        else:
            m_ref[2, :, : 2 * BLK] = (seg_in[:, 2 * BLK : 4 * BLK] == seg_out).astype(jnp.float32)

    def one(g, _):
        row = rev_ref[pl.ds(half * groups + g, 1), :]
        table = pltpu.roll(jnp.broadcast_to(row, (BLK, span)), 0, 1, stride=1, stride_axis=0)
        out_ref[g, 0] = (table * m_ref[0]).astype(out_ref.dtype)
        later = jnp.concatenate([table[:, span - BLK :], table[:, : span - BLK]], 1)
        out_ref[g, 1] = (later * m_ref[1]).astype(out_ref.dtype)
        next_ref[g] = (table[:, : 2 * BLK] * m_ref[2, :, : 2 * BLK]).astype(next_ref.dtype)
        return 0

    lax.fori_loop(0, groups, one, 0)


def fill(win_ref, extra_ref, spot, message):
    win_ref[pl.ds(pl.multiple_of(spot * BLK, BLK), BLK), :] = message[:BLK]
    extra_ref[spot] = message[BLK:].astype(jnp.float32)


def relay_kernel(seq_ref, next_ref, back_own_ref, back_pair_ref, w_ref, out_ref, win_ref, extra_ref):
    groups = next_ref.shape[0]
    width = groups * GROUP
    half = lax.axis_index("half")
    half_lanes = pl.ds(pl.multiple_of(half * width, width), width)
    fill(win_ref, extra_ref, half, back_own_ref)
    fill(win_ref, extra_ref, 1 - half, back_pair_ref)
    marks = edge_marks(seq_ref)
    rows = first_rows(extra_ref[1, :8], extra_ref[0, :8], w_ref, half_lanes, marks, 3)
    put_first_rows(win_ref, BLK, rows)
    out_ref[BLK:] = extra_ref[1].astype(out_ref.dtype)
    summed = reaches_past(seq_ref, lax.axis_index("blk") + 1)

    @pl.when(summed)
    def _():
        for g in range(groups):
            lanes = slice(g * GROUP, (g + 1) * GROUP)
            total = jnp.dot(next_ref[g], win_ref[:, lanes], preferred_element_type=jnp.float32)
            out_ref[:BLK, lanes] = total.astype(out_ref.dtype)

    @pl.when(jnp.logical_not(summed))
    def _():
        out_ref[:BLK] = win_ref[BLK:]


def gate_rows(seq_ref, raw_ref, tail, w_ref, part, q_ref, x_ref, m1_ref, m2_ref):
    width = raw_ref.shape[1]
    half = lax.axis_index("half")
    row_masks(seq_ref, lax.axis_index("blk") * (2 * BLK) + part * BLK, m1_ref, m2_ref)
    for c in range(0, width, GROUP):
        lanes = slice(c, c + GROUP)
        w = w_ref[0, :, pl.ds(pl.multiple_of(half * width + c, GROUP), GROUP)]
        x = raw_ref[:, lanes].astype(jnp.float32)
        slot = (c // GROUP) % 2
        x_ref[slot, 6:8, :] = tail(lanes)
        x_ref[slot, 8:, :] = x
        q_ref[:, lanes] = feature(x, x_ref.at[slot], w, m1_ref, m2_ref)


def near_kernel(
    seq_ref, table_ref, own_ref, pair_ref, back_own_ref, back_pair_ref, qkept_ref, w_ref, bias_ref,
    acc_ref, q_ref, marks_ref, win_ref, extra_ref, x_ref, m1_ref, m2_ref,
):
    groups = table_ref.shape[0]
    width = groups * GROUP
    half = lax.axis_index("half")
    block = lax.axis_index("blk")
    half_lanes = pl.ds(pl.multiple_of(half * width, width), width)
    for spot, message in ((half, back_own_ref), (1 - half, back_pair_ref), (2 + half, own_ref), (3 - half, pair_ref)):
        fill(win_ref, extra_ref, spot, message)
    marks = edge_marks(seq_ref)
    marks_ref[0], marks_ref[1] = marks
    marks_ref[2] = jnp.full((8, GROUP), reaches_past(seq_ref, block).astype(jnp.float32))
    for spot in (1, 2, 3):
        rows = first_rows(extra_ref[spot, :8], extra_ref[spot - 1, :8], w_ref, half_lanes, marks, spot + 2)
        put_first_rows(win_ref, spot * BLK, rows)
    for g in range(groups):
        lanes = slice(g * GROUP, (g + 1) * GROUP)
        bias = bias_ref[:, pl.ds(pl.multiple_of(half * width + g * GROUP, GROUP), GROUP)]
        for part in range(2):
            total = jnp.dot(
                table_ref[g, part, :, 3 * BLK : (5 + part) * BLK],
                win_ref[BLK : (3 + part) * BLK, lanes],
                preferred_element_type=jnp.float32,
            )
            here = win_ref[(2 + part) * BLK : (3 + part) * BLK, lanes].astype(jnp.float32)
            acc_ref[part * BLK : (part + 1) * BLK, lanes] = total + bias * here
    gate_rows(
        seq_ref, qkept_ref, lambda lanes: extra_ref[1 + half, 8:10, lanes], w_ref, half, q_ref, x_ref, m1_ref, m2_ref
    )


def pair_gate_kernel(seq_ref, raw_ref, own_ref, back_own_ref, w_ref, q_ref, x_ref, m1_ref, m2_ref):
    half = lax.axis_index("half")

    def tail(lanes):
        back = back_own_ref[BLK:, lanes].astype(jnp.float32)
        own = own_ref[BLK:, lanes].astype(jnp.float32)
        return jnp.where(half == 1, back, own)[8:10]

    gate_rows(seq_ref, raw_ref, tail, w_ref, 1 - half, q_ref, x_ref, m1_ref, m2_ref)


def far_kernel(short, table_ref, acc_ref, qown_ref, qpair_ref, w_ref, marks_ref, *refs):
    *messages, kept_ref, sent_ref, power_ref, win_ref, extra_ref = refs
    groups = table_ref.shape[0]
    width = groups * GROUP
    half = lax.axis_index("half")
    half_lanes = pl.ds(pl.multiple_of(half * width, width), width)
    marks = [marks_ref[0], marks_ref[1]]
    back_own_ref, back_pair_ref, far_ref, *others = messages
    low = 1 if short else 0
    fill(win_ref, extra_ref, 2 + half, back_own_ref)
    fill(win_ref, extra_ref, 3 - half, back_pair_ref)
    if short:
        summed = marks_ref[2, 0:1, 0:1]
        payload = far_ref[:BLK].astype(jnp.float32)
        win_ref[BLK : 2 * BLK, :] = (payload * (1.0 - summed)).astype(win_ref.dtype)
        extra_ref[1] = far_ref[BLK:].astype(jnp.float32)
    else:
        fill(win_ref, extra_ref, half, far_ref)
        fill(win_ref, extra_ref, 1 - half, others[0])
        ahead = others[1][...].astype(jnp.float32)[:8]
        put_first_rows(win_ref, 0, first_rows(extra_ref[0, :8], ahead, w_ref, half_lanes, marks, 0))
        rows = first_rows(extra_ref[1, :8], extra_ref[0, :8], w_ref, half_lanes, marks, 1)
        put_first_rows(win_ref, BLK, rows)
    rows = first_rows(extra_ref[2, :8], extra_ref[1, :8], w_ref, half_lanes, marks, 2)
    put_first_rows(win_ref, 2 * BLK, rows)
    power = []
    for part, q_ref, out_ref in ((half, qown_ref, kept_ref), (1 - half, qpair_ref, sent_ref)):
        squares = jnp.zeros((BLK, GROUP), jnp.float32)
        rows = pl.ds(pl.multiple_of(part * BLK, BLK), BLK)
        for g in range(groups):
            lanes = slice(g * GROUP, (g + 1) * GROUP)
            filtered = acc_ref[rows, lanes] + jnp.dot(
                table_ref[g, part, :, low * BLK : 3 * BLK],
                win_ref[low * BLK : 3 * BLK, lanes],
                preferred_element_type=jnp.float32,
            )
            if short:
                weight = summed * (part == 0).astype(jnp.float32)
                filtered = filtered + weight * far_ref[:BLK, lanes].astype(jnp.float32)
            gated = q_ref[:, lanes] * filtered
            squares = squares + gated * gated
            out_ref[:, lanes] = gated.astype(out_ref.dtype)
        power.append(
            lax.dot_general(
                jnp.ones((8, GROUP), jnp.float32),
                squares,
                (((1,), (1,)), ((), ())),
                precision=lax.Precision.HIGHEST,
                preferred_element_type=jnp.float32,
            )[0:1]
        )
    own, pair = power
    power_ref[:, :BLK] = jnp.where(half == 0, own, pair)
    power_ref[:, BLK:] = jnp.where(half == 0, pair, own)


def norm_kernel(channels, *refs):
    half = lax.axis_index("half")
    *power_refs, kept_ref, got_ref, gain_ref, out_ref = refs
    width = kept_ref.shape[1]
    mine = pl.ds(pl.multiple_of(half * BLK, BLK), BLK)
    power = sum(ref[:, mine] for ref in power_refs)
    scale = lax.rsqrt(power / channels + norm_eps)
    diagonal = lax.broadcasted_iota(jnp.int32, (BLK, BLK), 0) == lax.broadcasted_iota(
        jnp.int32, (BLK, BLK), 1
    )
    column = jnp.sum(jnp.where(diagonal, scale, 0.0), axis=1, keepdims=True)
    for which, part_ref in ((half, kept_ref), (1 - half, got_ref)):
        for c in range(0, width, GROUP):
            lanes = pl.ds(pl.multiple_of(which * width + c, GROUP), GROUP)
            out_ref[:, lanes] = (
                part_ref[:, c : c + GROUP].astype(jnp.float32) * column * gain_ref[:, lanes]
            ).astype(out_ref.dtype)


def kernel_call(body, outs, in_specs, scratch, flops, moved_bytes, vmem=24 << 20):
    return pl.pallas_call(
        body,
        out_shape=outs,
        in_specs=in_specs,
        out_specs=jax.tree.map(lambda _: VMEM, outs),
        scratch_shapes=scratch,
        compiler_params=pltpu.CompilerParams(vmem_limit_bytes=vmem),
        cost_estimate=pl.CostEstimate(flops=flops, bytes_accessed=moved_bytes, transcendentals=0),
    )


def shards(blocks, whole_tokens, channels, projected, short_weight, filter_taps, tap_blocks, skip_bias, norm_gain, seq_lengths):
    rows = projected.shape[0]
    width = projected.shape[2] // 2
    groups = width // GROUP
    taps = filter_taps.shape[1]
    shape = jax.ShapeDtypeStruct
    half_shape = shape((rows, width), jnp.bfloat16)
    half_wide = shape((rows, width), jnp.float32)

    spots = range(2 * blocks)
    to_pair = [(i, i ^ 1) for i in spots]
    ahead = [(i, (i + 2) % (2 * blocks)) for i in spots]
    ahead_pair = [(i, ((i ^ 1) + 2) % (2 * blocks)) for i in spots]

    panels = jnp.transpose(projected, (1, 0, 2))
    message = shape((rows + 16, width), jnp.bfloat16)
    hbm = pl.BlockSpec(memory_space=pltpu.HBM)
    pieces = 4
    row_mask = pltpu.VMEM((rows, GROUP), jnp.float32)

    sent, kept, qsent, qkept = kernel_call(
        products_kernel,
        (message, message, half_shape, half_shape),
        [hbm] * 3,
        [
            pltpu.SMEM(seq_lengths.shape, jnp.int32),
            pltpu.VMEM((pieces, 2, rows, 2 * width // pieces), jnp.bfloat16),
            pltpu.VMEM(short_weight.shape, jnp.float32),
            pltpu.VMEM((4, rows + 8, GROUP), jnp.float32),
            row_mask,
            row_mask,
            pltpu.SemaphoreType.DMA((4 + pieces,)),
        ],
        40 * rows * width,
        16 * rows * width,
        60 << 20,
    )(seq_lengths, panels, short_weight)

    back_own = moved(kept, ahead)
    back_pair = moved(sent, ahead_pair)
    pair = moved(sent, to_pair)

    filter_taps, _ = lax.optimization_barrier((filter_taps, kept))
    scaled = (filter_taps * jnp.repeat(tap_blocks.astype(jnp.float32), BLK, axis=1)).astype(jnp.bfloat16)
    span = taps + 2 * BLK
    table, table_next = kernel_call(
        tables_kernel,
        (shape((groups, 2, BLK, span), jnp.bfloat16), shape((groups, BLK, 2 * BLK), jnp.bfloat16)),
        [SMEM, VMEM],
        [pltpu.VMEM((2 * groups, span), jnp.float32), pltpu.VMEM((3, BLK, span), jnp.float32)],
        40 * groups * BLK * taps,
        8 * groups * BLK * taps,
    )(seq_lengths, scaled)
    table, table_next, back_own = lax.optimization_barrier((table, table_next, back_own))
    table, back_pair, qsent = lax.optimization_barrier((table, back_pair, qsent))
    qgot = moved(qsent, to_pair)

    window = pltpu.VMEM((4 * rows, width), jnp.bfloat16)
    extras = pltpu.VMEM((4, 16, width), jnp.float32)
    shifted = pltpu.VMEM((2, rows + 8, GROUP), jnp.float32)
    short = whole_tokens // 2 <= 4 * BLK
    if short:
        relayed = kernel_call(
            relay_kernel,
            message,
            [SMEM] + [VMEM] * 4,
            [pltpu.VMEM((2 * rows, width), jnp.bfloat16), pltpu.VMEM((2, 16, width), jnp.float32)],
            2 * 2 * rows * BLK * width,
            8 * rows * width,
        )(seq_lengths, table_next, back_own, back_pair, short_weight)
        far = (moved(relayed, ahead),)
    else:
        straight = moved(kept[rows:], [(i, (i + 6) % (2 * blocks)) for i in spots])
        across = moved(sent[rows:], [(i, ((i ^ 1) + 6) % (2 * blocks)) for i in spots])
        deep = jnp.where(lax.axis_index("half") == 1, straight, across)
        far = (moved(back_own, ahead), moved(back_pair, ahead), deep)

    acc, qown, marks = kernel_call(
        near_kernel,
        (shape((2 * rows, width), jnp.float32), half_wide, shape((3, 8, GROUP), jnp.float32)),
        [SMEM] + [VMEM] * 8,
        [window, extras, shifted, row_mask, row_mask],
        2 * 5 * rows * BLK * width,
        16 * rows * width,
    )(seq_lengths, table, kept, pair, back_own, back_pair, qkept, short_weight, skip_bias.reshape(1, -1))

    qpair = kernel_call(
        pair_gate_kernel,
        half_wide,
        [SMEM] + [VMEM] * 4,
        [shifted, row_mask, row_mask],
        10 * rows * width,
        8 * rows * width,
    )(seq_lengths, qgot, kept, back_own, short_weight)

    done, send, power = kernel_call(
        functools.partial(far_kernel, short),
        (half_wide, half_shape, shape((1, 2 * rows), jnp.float32)),
        [VMEM] * (8 + len(far)),
        [window, extras],
        2 * 5 * rows * BLK * width,
        24 * rows * width,
    )(table, acc, qown, qpair, short_weight, marks, back_own, back_pair, *far)

    back = moved(send, to_pair)
    peers = lax.axis_size("mp")
    shares = [lax.ppermute(power, "mp", [(i, i ^ k) for i in range(peers)]) for k in range(1, peers)]
    power = sum(shares, power)
    return kernel_call(
        functools.partial(norm_kernel, channels),
        shape((rows, 2 * width), jnp.bfloat16),
        [VMEM] * 5,
        [],
        8 * rows * width,
        10 * rows * width,
    )(power, moved(power, to_pair), done, back, norm_gain.reshape(1, -1))


def solution(mesh):
    blocks = mesh.shape["ctx"] // 2
    grid = Mesh(mesh.devices.reshape(blocks, 2, mesh.shape["mp"]), ("blk", "half", "mp"))
    in_specs = (
        P(SPOTS, None, "mp"),
        P(None, None, "mp"),
        P("mp", None),
        P("mp", None),
        P("mp"),
        P("mp"),
        P(),
    )

    def program(projected, *rest):
        body = functools.partial(shards, blocks, projected.shape[0], projected.shape[2])
        return jax.shard_map(
            body, mesh=grid, in_specs=in_specs, out_specs=P(SPOTS, "mp"), check_vma=False
        )(projected, *rest)

    return program
```

```python
import functools

import jax
import jax.numpy as jnp
from jax import lax
from jax.experimental import pallas as pl
from jax.experimental.pallas import tpu as pltpu
from jax.sharding import Mesh, PartitionSpec as P

GROUP = 128
BLK = 128
norm_eps = 1e-06

VMEM = pl.BlockSpec(memory_space=pltpu.VMEM)
SMEM = pl.BlockSpec(memory_space=pltpu.SMEM)
SPOTS = ("blk", "half")


def moved(block, pairs):
    return lax.ppermute(block, SPOTS, pairs)


def boundaries(seq_ref, t):
    def step(k, carry):
        end, first, second = carry
        end = end + seq_ref[k]
        return end, first | (t == end).astype(jnp.int32), second | (t - 1 == end).astype(jnp.int32)

    first = (t == 0).astype(jnp.int32)
    second = (t == 1).astype(jnp.int32)
    _, first, second = lax.fori_loop(0, seq_ref.shape[0], step, (jnp.int32(0), first, second), unroll=True)
    return first, first | second


def row_masks(seq_ref, start, m1_ref, m2_ref):
    rows = lax.broadcasted_iota(jnp.int32, (BLK, GROUP), 0)
    diagonal = rows == lax.broadcasted_iota(jnp.int32, (BLK, GROUP), 1)
    marks = boundaries(seq_ref, start + lax.broadcasted_iota(jnp.int32, (8, GROUP), 1))
    for mark, m_ref in zip(marks, (m1_ref, m2_ref)):
        keep = 1.0 - mark.astype(jnp.float32)[0:1]
        column = jnp.sum(jnp.where(diagonal, keep, 0.0), axis=1, keepdims=True)
        m_ref[...] = jnp.broadcast_to(column, (BLK, GROUP))


def counted(seq_ref, t):
    def step(k, carry):
        end, total = carry
        end = end + seq_ref[k]
        return end, total + (end <= t).astype(jnp.int32)

    _, total = lax.fori_loop(
        0, seq_ref.shape[0], step, (jnp.int32(0), jnp.zeros(t.shape, jnp.int32)), unroll=True
    )
    return jnp.where(t >= 0, total, -1)


def feature(x, x_ref, w, m1_ref, m2_ref):
    rows = x.shape[0]
    return (
        w[0:1] * x
        + w[1:2] * x_ref[7 : rows + 7, :] * m1_ref[...]
        + w[2:3] * x_ref[6 : rows + 6, :] * m2_ref[...]
    )


def products_kernel(
    seq_hbm, panels_hbm, w_hbm, sent_ref, kept_ref, seq_ref, kv_ref, q_ref, w_ref, x_ref, m1_ref, m2_ref, sems
):
    width = kept_ref.shape[1]
    rows = kv_ref.shape[2]
    pieces = kv_ref.shape[0]
    piece = kv_ref.shape[3]
    half = lax.axis_index("half")
    shard = lax.axis_index("blk") * 2 + half
    keep_at = pl.multiple_of(half * width, width)
    send_at = pl.multiple_of((1 - half) * width, width)

    loads = [pltpu.make_async_copy(seq_hbm, seq_ref, sems.at[0])]
    for p in range(pieces):
        at = keep_at if p < pieces // 2 else send_at
        lanes = pl.ds(pl.multiple_of(at + (p % (pieces // 2)) * piece, piece), piece)
        loads.append(pltpu.make_async_copy(panels_hbm.at[1:3, :, lanes], kv_ref.at[p], sems.at[1 + p]))
    loads.append(pltpu.make_async_copy(w_hbm, w_ref, sems.at[1 + pieces]))
    loads.append(pltpu.make_async_copy(panels_hbm.at[0, rows - 16 :, :], q_ref, sems.at[2 + pieces]))
    for load in loads:
        load.start()
    x_ref[:, 0:8, :] = jnp.zeros((x_ref.shape[0], 8, GROUP), jnp.float32)
    loads[0].wait()
    row_masks(seq_ref, shard * rows, m1_ref, m2_ref)
    loads[1 + pieces].wait()
    loads[2 + pieces].wait()
    for p in range(pieces):
        loads[1 + p].wait()
        out_ref, at = (kept_ref, keep_at) if p < pieces // 2 else (sent_ref, send_at)
        for c in range(0, piece, GROUP):
            base = (p % (pieces // 2)) * piece + c
            there = slice(base, base + GROUP)
            lanes = pl.ds(pl.multiple_of(at + base, GROUP), GROUP)
            slot = (c // GROUP) % (x_ref.shape[0] // 2) * 2
            heads, tails, made = [], [], []
            for i in range(2):
                x = kv_ref[p, i, :, c : c + GROUP].astype(jnp.float32)
                x_ref[slot + i, 8:, :] = x
                made.append(feature(x, x_ref.at[slot + i], w_ref[1 + i, :, lanes], m1_ref, m2_ref))
                heads.append(x[0:2])
                tails.append(x[rows - 2 :])
            out_ref[:rows, there] = (made[0] * made[1]).astype(out_ref.dtype)
            tails.append(q_ref[:, lanes].astype(jnp.float32)[14:])
            extra = jnp.concatenate(heads + tails + [jnp.zeros((6, GROUP), jnp.float32)], 0)
            out_ref[rows:, there] = extra.astype(out_ref.dtype)


def edge_marks(seq_ref):
    t = (
        (lax.axis_index("blk") - 2) * (2 * BLK)
        + lax.broadcasted_iota(jnp.int32, (8, GROUP), 1) * BLK
        + lax.broadcasted_iota(jnp.int32, (8, GROUP), 0)
    )
    return [1.0 - mark.astype(jnp.float32) for mark in boundaries(seq_ref, t)]


def first_rows(now, ahead, w_ref, marks, spot):
    m1, m2 = [mark[:, spot : spot + 1] for mark in marks]
    top = lax.broadcasted_iota(jnp.int32, now.shape, 0) == 0
    made = []
    for i in range(2):
        x0 = pltpu.roll(now, (8 - 2 * i) % 8, 0) if i else now
        x1 = jnp.where(top, pltpu.roll(ahead, 3 - 2 * i, 0), pltpu.roll(now, (9 - 2 * i) % 8, 0))
        x2 = pltpu.roll(ahead, 4 - 2 * i, 0)
        w = w_ref[1 + i]
        made.append(w[0:1] * x0 + w[1:2] * x1 * m1 + w[2:3] * x2 * m2)
    return made[0] * made[1]


def put_first_rows(win_ref, at, rows):
    old = win_ref[at : at + 16, :].astype(jnp.float32)
    new = jnp.concatenate([rows, rows], 0)
    first = lax.broadcasted_iota(jnp.int32, old.shape, 0) < 2
    win_ref[at : at + 16, :] = jnp.where(first, new, old).astype(win_ref.dtype)


def reaches_past(seq_ref, block):
    first = block * (2 * BLK)

    def step(k, carry):
        end, start = carry
        end = end + seq_ref[k]
        return end, jnp.where(end <= first, end, start)

    _, start = lax.fori_loop(0, seq_ref.shape[0], step, (jnp.int32(0), jnp.int32(0)), unroll=True)
    return first - 2 * BLK - start > BLK


def tables_kernel(seq_ref, taps_ref, w_ref, out_ref, next_ref, w_half_ref, rev_ref, m_ref):
    groups = out_ref.shape[0]
    taps = taps_ref.shape[1]
    span = out_ref.shape[3]
    half = lax.axis_index("half")
    start = lax.axis_index("blk") * (2 * BLK)
    width = w_half_ref.shape[2]
    w_half_ref[...] = w_ref[:, :, pl.ds(pl.multiple_of(half * width, width), width)]
    turn = lax.broadcasted_iota(jnp.int32, (taps, span), 0) + lax.broadcasted_iota(
        jnp.int32, (taps, span), 1
    )
    turn = (turn == taps).astype(jnp.bfloat16)
    rev_ref[...] = jnp.dot(taps_ref[...], turn, preferred_element_type=jnp.float32)
    seg_in = counted(seq_ref, start - taps + lax.broadcasted_iota(jnp.int32, (8, span), 1))[0:1]
    for part in range(3):
        t_out = start + part * BLK + lax.broadcasted_iota(jnp.int32, (BLK, GROUP), 0)
        seg_out = counted(seq_ref, t_out)[:, 0:1]
        if part < 2:
            m_ref[part] = (seg_in == seg_out).astype(jnp.float32)
        else:
            m_ref[2, :, : 2 * BLK] = (seg_in[:, 2 * BLK : 4 * BLK] == seg_out).astype(jnp.float32)

    def one(g, _):
        row = rev_ref[pl.ds(half * groups + g, 1), :]
        table = pltpu.roll(jnp.broadcast_to(row, (BLK, span)), 0, 1, stride=1, stride_axis=0)
        out_ref[g, 0] = (table * m_ref[0]).astype(out_ref.dtype)
        later = jnp.concatenate([table[:, span - BLK :], table[:, : span - BLK]], 1)
        out_ref[g, 1] = (later * m_ref[1]).astype(out_ref.dtype)
        next_ref[g] = (table[:, : 2 * BLK] * m_ref[2, :, : 2 * BLK]).astype(next_ref.dtype)
        return 0

    lax.fori_loop(0, groups, one, 0)


def fill(win_ref, extra_ref, spot, message):
    win_ref[pl.ds(pl.multiple_of(spot * BLK, BLK), BLK), :] = message[:BLK]
    extra_ref[spot] = message[BLK:].astype(jnp.float32)


def relay_kernel(seq_ref, next_ref, back_own_ref, back_pair_ref, w_ref, out_ref, win_ref, extra_ref):
    groups = next_ref.shape[0]
    width = groups * GROUP
    half = lax.axis_index("half")
    fill(win_ref, extra_ref, half, back_own_ref)
    fill(win_ref, extra_ref, 1 - half, back_pair_ref)
    marks = edge_marks(seq_ref)
    rows = first_rows(extra_ref[1, :8], extra_ref[0, :8], w_ref, marks, 3)
    put_first_rows(win_ref, BLK, rows)
    out_ref[BLK:] = extra_ref[1].astype(out_ref.dtype)
    summed = reaches_past(seq_ref, lax.axis_index("blk") + 1)

    @pl.when(summed)
    def _():
        for g in range(groups):
            lanes = slice(g * GROUP, (g + 1) * GROUP)
            total = jnp.dot(next_ref[g], win_ref[:, lanes], preferred_element_type=jnp.float32)
            out_ref[:BLK, lanes] = total.astype(out_ref.dtype)

    @pl.when(jnp.logical_not(summed))
    def _():
        out_ref[:BLK] = win_ref[BLK:]


def gate_rows(seq_ref, raw_ref, tail, w_ref, part, q_ref, x_ref, m1_ref, m2_ref):
    width = raw_ref.shape[1]
    row_masks(seq_ref, lax.axis_index("blk") * (2 * BLK) + part * BLK, m1_ref, m2_ref)
    for c in range(0, width, GROUP):
        lanes = slice(c, c + GROUP)
        w = w_ref[0, :, lanes]
        x = raw_ref[:, lanes].astype(jnp.float32)
        slot = (c // GROUP) % 2
        x_ref[slot, 6:8, :] = tail(lanes)
        x_ref[slot, 8:, :] = x
        q_ref[:, lanes] = feature(x, x_ref.at[slot], w, m1_ref, m2_ref)


def near_kernel(
    seq_ref, table_ref, own_ref, pair_ref, back_own_ref, back_pair_ref, qkept_ref, w_ref, bias_ref,
    acc_ref, q_ref, marks_ref, win_ref, extra_ref, x_ref, m1_ref, m2_ref,
):
    groups = table_ref.shape[0]
    width = groups * GROUP
    half = lax.axis_index("half")
    block = lax.axis_index("blk")
    for spot, message in ((half, back_own_ref), (1 - half, back_pair_ref), (2 + half, own_ref), (3 - half, pair_ref)):
        fill(win_ref, extra_ref, spot, message)
    marks = edge_marks(seq_ref)
    marks_ref[0], marks_ref[1] = marks
    marks_ref[2] = jnp.full((8, GROUP), reaches_past(seq_ref, block).astype(jnp.float32))
    for spot in (1, 2, 3):
        rows = first_rows(extra_ref[spot, :8], extra_ref[spot - 1, :8], w_ref, marks, spot + 2)
        put_first_rows(win_ref, spot * BLK, rows)
    for g in range(groups):
        lanes = slice(g * GROUP, (g + 1) * GROUP)
        bias = bias_ref[:, pl.ds(pl.multiple_of(half * width + g * GROUP, GROUP), GROUP)]
        for part in range(2):
            total = jnp.dot(
                table_ref[g, part, :, 3 * BLK : (5 + part) * BLK],
                win_ref[BLK : (3 + part) * BLK, lanes],
                preferred_element_type=jnp.float32,
            )
            here = win_ref[(2 + part) * BLK : (3 + part) * BLK, lanes].astype(jnp.float32)
            acc_ref[part * BLK : (part + 1) * BLK, lanes] = total + bias * here
    gate_rows(
        seq_ref, qkept_ref, lambda lanes: extra_ref[1 + half, 8:10, lanes], w_ref, half, q_ref, x_ref, m1_ref, m2_ref
    )


def pair_gate_kernel(seq_ref, raw_ref, own_ref, back_own_ref, w_ref, q_ref, x_ref, m1_ref, m2_ref):
    half = lax.axis_index("half")

    def tail(lanes):
        back = back_own_ref[BLK:, lanes].astype(jnp.float32)
        own = own_ref[BLK:, lanes].astype(jnp.float32)
        return jnp.where(half == 1, back, own)[8:10]

    gate_rows(seq_ref, raw_ref, tail, w_ref, 1 - half, q_ref, x_ref, m1_ref, m2_ref)


def far_kernel(short, table_ref, acc_ref, qown_ref, qpair_ref, w_ref, marks_ref, *refs):
    *messages, kept_ref, sent_ref, power_ref, win_ref, extra_ref = refs
    groups = table_ref.shape[0]
    width = groups * GROUP
    half = lax.axis_index("half")
    marks = [marks_ref[0], marks_ref[1]]
    back_own_ref, back_pair_ref, far_ref, *others = messages
    low = 1 if short else 0
    fill(win_ref, extra_ref, 2 + half, back_own_ref)
    fill(win_ref, extra_ref, 3 - half, back_pair_ref)
    if short:
        summed = marks_ref[2, 0:1, 0:1]
        payload = far_ref[:BLK].astype(jnp.float32)
        win_ref[BLK : 2 * BLK, :] = (payload * (1.0 - summed)).astype(win_ref.dtype)
        extra_ref[1] = far_ref[BLK:].astype(jnp.float32)
    else:
        fill(win_ref, extra_ref, half, far_ref)
        fill(win_ref, extra_ref, 1 - half, others[0])
        ahead = others[1][...].astype(jnp.float32)[:8]
        put_first_rows(win_ref, 0, first_rows(extra_ref[0, :8], ahead, w_ref, marks, 0))
        rows = first_rows(extra_ref[1, :8], extra_ref[0, :8], w_ref, marks, 1)
        put_first_rows(win_ref, BLK, rows)
    rows = first_rows(extra_ref[2, :8], extra_ref[1, :8], w_ref, marks, 2)
    put_first_rows(win_ref, 2 * BLK, rows)
    for at, part, q_ref, out_ref in ((0, half, qown_ref, kept_ref), (BLK, 1 - half, qpair_ref, sent_ref)):
        squares = jnp.zeros((BLK, GROUP), jnp.float32)
        rows = pl.ds(pl.multiple_of(part * BLK, BLK), BLK)
        for g in range(groups):
            lanes = slice(g * GROUP, (g + 1) * GROUP)
            filtered = acc_ref[rows, lanes] + jnp.dot(
                table_ref[g, part, :, low * BLK : 3 * BLK],
                win_ref[low * BLK : 3 * BLK, lanes],
                preferred_element_type=jnp.float32,
            )
            if short:
                weight = summed * (part == 0).astype(jnp.float32)
                filtered = filtered + weight * far_ref[:BLK, lanes].astype(jnp.float32)
            gated = q_ref[:, lanes] * filtered
            squares = squares + gated * gated
            out_ref[:, lanes] = gated.astype(out_ref.dtype)
        power_ref[:, at : at + BLK] = lax.dot_general(
            jnp.ones((8, GROUP), jnp.float32),
            squares,
            (((1,), (1,)), ((), ())),
            precision=lax.Precision.HIGHEST,
            preferred_element_type=jnp.float32,
        )[0:1]


def norm_kernel(channels, power_ref, power_got_ref, kept_ref, got_ref, gain_ref, out_ref):
    half = lax.axis_index("half")
    width = kept_ref.shape[1]
    power = power_ref[:, :BLK] + power_got_ref[:, BLK:]
    scale = lax.rsqrt(power / channels + norm_eps)
    diagonal = lax.broadcasted_iota(jnp.int32, (BLK, BLK), 0) == lax.broadcasted_iota(
        jnp.int32, (BLK, BLK), 1
    )
    column = jnp.sum(jnp.where(diagonal, scale, 0.0), axis=1, keepdims=True)
    for which, part_ref in ((half, kept_ref), (1 - half, got_ref)):
        for c in range(0, width, GROUP):
            lanes = pl.ds(pl.multiple_of(which * width + c, GROUP), GROUP)
            out_ref[:, lanes] = (
                part_ref[:, c : c + GROUP].astype(jnp.float32) * column * gain_ref[:, lanes]
            ).astype(out_ref.dtype)


def kernel_call(body, outs, in_specs, scratch, flops, moved_bytes, vmem=24 << 20):
    return pl.pallas_call(
        body,
        out_shape=outs,
        in_specs=in_specs,
        out_specs=jax.tree.map(lambda _: VMEM, outs),
        scratch_shapes=scratch,
        compiler_params=pltpu.CompilerParams(vmem_limit_bytes=vmem),
        cost_estimate=pl.CostEstimate(flops=flops, bytes_accessed=moved_bytes, transcendentals=0),
    )


def shards(blocks, whole_tokens, channels, projected, short_weight, filter_taps, tap_blocks, skip_bias, norm_gain, seq_lengths):
    rows = projected.shape[0]
    width = projected.shape[2] // 2
    groups = width // GROUP
    taps = filter_taps.shape[1]
    shape = jax.ShapeDtypeStruct
    half_shape = shape((rows, width), jnp.bfloat16)
    half_wide = shape((rows, width), jnp.float32)

    spots = range(2 * blocks)
    to_pair = [(i, i ^ 1) for i in spots]
    ahead = [(i, (i + 2) % (2 * blocks)) for i in spots]
    ahead_pair = [(i, ((i ^ 1) + 2) % (2 * blocks)) for i in spots]

    panels = jnp.transpose(projected, (1, 0, 2))
    message = shape((rows + 16, width), jnp.bfloat16)
    hbm = pl.BlockSpec(memory_space=pltpu.HBM)
    pieces = 4
    row_mask = pltpu.VMEM((rows, GROUP), jnp.float32)

    sent, kept = kernel_call(
        products_kernel,
        (message, message),
        [hbm] * 3,
        [
            pltpu.SMEM(seq_lengths.shape, jnp.int32),
            pltpu.VMEM((pieces, 2, rows, 2 * width // pieces), jnp.bfloat16),
            pltpu.VMEM((16, 2 * width), jnp.bfloat16),
            pltpu.VMEM(short_weight.shape, jnp.float32),
            pltpu.VMEM((4, rows + 8, GROUP), jnp.float32),
            row_mask,
            row_mask,
            pltpu.SemaphoreType.DMA((3 + pieces,)),
        ],
        40 * rows * width,
        16 * rows * width,
        60 << 20,
    )(seq_lengths, panels, short_weight)

    back_own = moved(kept, ahead)
    back_pair = moved(sent, ahead_pair)
    filter_taps, query, _ = lax.optimization_barrier((filter_taps, panels[0], kept))
    half = lax.axis_index("half")
    qkept = lax.dynamic_slice_in_dim(query, half * width, width, 1)
    qsent = lax.dynamic_slice_in_dim(query, (1 - half) * width, width, 1)
    scaled = (filter_taps * jnp.repeat(tap_blocks.astype(jnp.float32), BLK, axis=1)).astype(jnp.bfloat16)
    scaled, sent_late = lax.optimization_barrier((scaled, sent))
    pair = moved(sent_late, to_pair)
    span = taps + 2 * BLK
    table, table_next, w_half = kernel_call(
        tables_kernel,
        (
            shape((groups, 2, BLK, span), jnp.bfloat16),
            shape((groups, BLK, 2 * BLK), jnp.bfloat16),
            shape((3, 3, width), jnp.float32),
        ),
        [SMEM, VMEM, VMEM],
        [pltpu.VMEM((2 * groups, span), jnp.float32), pltpu.VMEM((3, BLK, span), jnp.float32)],
        40 * groups * BLK * taps,
        8 * groups * BLK * taps,
    )(seq_lengths, scaled, short_weight)
    table, table_next, back_own = lax.optimization_barrier((table, table_next, back_own))
    table, back_pair, qsent, qkept = lax.optimization_barrier((table, back_pair, qsent, qkept))
    qgot = moved(qsent, to_pair)

    window = pltpu.VMEM((4 * rows, width), jnp.bfloat16)
    extras = pltpu.VMEM((4, 16, width), jnp.float32)
    shifted = pltpu.VMEM((2, rows + 8, GROUP), jnp.float32)
    short = whole_tokens // 2 <= 4 * BLK
    if short:
        relayed = kernel_call(
            relay_kernel,
            message,
            [SMEM] + [VMEM] * 4,
            [pltpu.VMEM((2 * rows, width), jnp.bfloat16), pltpu.VMEM((2, 16, width), jnp.float32)],
            2 * 2 * rows * BLK * width,
            8 * rows * width,
        )(seq_lengths, table_next, back_own, back_pair, w_half)
        far = (moved(relayed, ahead),)
    else:
        straight = moved(kept[rows:], [(i, (i + 6) % (2 * blocks)) for i in spots])
        across = moved(sent[rows:], [(i, ((i ^ 1) + 6) % (2 * blocks)) for i in spots])
        deep = jnp.where(half == 1, straight, across)
        far = (moved(back_own, ahead), moved(back_pair, ahead), deep)

    acc, qown, marks = kernel_call(
        near_kernel,
        (shape((2 * rows, width), jnp.float32), half_wide, shape((3, 8, GROUP), jnp.float32)),
        [SMEM] + [VMEM] * 8,
        [window, extras, shifted, row_mask, row_mask],
        2 * 5 * rows * BLK * width,
        16 * rows * width,
    )(seq_lengths, table, kept, pair, back_own, back_pair, qkept, w_half, skip_bias.reshape(1, -1))

    qpair = kernel_call(
        pair_gate_kernel,
        half_wide,
        [SMEM] + [VMEM] * 4,
        [shifted, row_mask, row_mask],
        10 * rows * width,
        8 * rows * width,
    )(seq_lengths, qgot, kept, back_own, w_half)

    done, send, power = kernel_call(
        functools.partial(far_kernel, short),
        (half_wide, half_shape, shape((1, 2 * rows), jnp.float32)),
        [VMEM] * (8 + len(far)),
        [window, extras],
        2 * 5 * rows * BLK * width,
        24 * rows * width,
    )(table, acc, qown, qpair, w_half, marks, back_own, back_pair, *far)

    back = moved(send, to_pair)
    peers = lax.axis_size("mp")
    shares = [lax.ppermute(power, "mp", [(i, i ^ k) for i in range(peers)]) for k in range(1, peers)]
    power = sum(shares, power)
    return kernel_call(
        functools.partial(norm_kernel, channels),
        shape((rows, 2 * width), jnp.bfloat16),
        [VMEM] * 5,
        [],
        8 * rows * width,
        10 * rows * width,
    )(power, moved(power, to_pair), done, back, norm_gain.reshape(1, -1))


def solution(mesh):
    blocks = mesh.shape["ctx"] // 2
    grid = Mesh(mesh.devices.reshape(blocks, 2, mesh.shape["mp"]), ("blk", "half", "mp"))
    in_specs = (
        P(SPOTS, None, "mp"),
        P(None, None, "mp"),
        P("mp", None),
        P("mp", None),
        P("mp"),
        P("mp"),
        P(),
    )

    def program(projected, *rest):
        body = functools.partial(shards, blocks, projected.shape[0], projected.shape[2])
        return jax.shard_map(
            body, mesh=grid, in_specs=in_specs, out_specs=P(SPOTS, "mp"), check_vma=False
        )(projected, *rest)

    return program
```

```python
import functools

import jax
import jax.numpy as jnp
from jax import lax
from jax.experimental import pallas as pl
from jax.experimental.pallas import tpu as pltpu
from jax.sharding import Mesh, PartitionSpec as P

GROUP = 128
BLK = 128
norm_eps = 1e-06

VMEM = pl.BlockSpec(memory_space=pltpu.VMEM)
SMEM = pl.BlockSpec(memory_space=pltpu.SMEM)
SPOTS = ("blk", "half")


def moved(block, pairs):
    return lax.ppermute(block, SPOTS, pairs)


def boundaries(seq_ref, t):
    def step(k, carry):
        end, first, second = carry
        end = end + seq_ref[k]
        return end, first | (t == end).astype(jnp.int32), second | (t - 1 == end).astype(jnp.int32)

    first = (t == 0).astype(jnp.int32)
    second = (t == 1).astype(jnp.int32)
    _, first, second = lax.fori_loop(0, seq_ref.shape[0], step, (jnp.int32(0), first, second), unroll=True)
    return first, first | second


def row_masks(seq_ref, start, m1_ref, m2_ref):
    rows = lax.broadcasted_iota(jnp.int32, (BLK, GROUP), 0)
    diagonal = rows == lax.broadcasted_iota(jnp.int32, (BLK, GROUP), 1)
    marks = boundaries(seq_ref, start + lax.broadcasted_iota(jnp.int32, (8, GROUP), 1))
    for mark, m_ref in zip(marks, (m1_ref, m2_ref)):
        keep = 1.0 - mark.astype(jnp.float32)[0:1]
        column = jnp.sum(jnp.where(diagonal, keep, 0.0), axis=1, keepdims=True)
        m_ref[...] = jnp.broadcast_to(column, (BLK, GROUP))


def counted(seq_ref, t):
    def step(k, carry):
        end, total = carry
        end = end + seq_ref[k]
        return end, total + (end <= t).astype(jnp.int32)

    _, total = lax.fori_loop(
        0, seq_ref.shape[0], step, (jnp.int32(0), jnp.zeros(t.shape, jnp.int32)), unroll=True
    )
    return jnp.where(t >= 0, total, -1)


def feature(x, x_ref, w, m1_ref, m2_ref):
    rows = x.shape[0]
    return (
        w[0:1] * x
        + w[1:2] * x_ref[7 : rows + 7, :] * m1_ref[...]
        + w[2:3] * x_ref[6 : rows + 6, :] * m2_ref[...]
    )


def products_kernel(
    seq_hbm, panels_hbm, w_hbm, sent_ref, kept_ref, seq_ref, kv_ref, q_ref, w_ref, x_ref, m1_ref, m2_ref, sems
):
    width = kept_ref.shape[1]
    rows = kv_ref.shape[2]
    pieces = kv_ref.shape[0]
    piece = kv_ref.shape[3]
    half = lax.axis_index("half")
    shard = lax.axis_index("blk") * 2 + half
    keep_at = pl.multiple_of(half * width, width)
    send_at = pl.multiple_of((1 - half) * width, width)

    loads = [pltpu.make_async_copy(seq_hbm, seq_ref, sems.at[0])]
    for p in range(pieces):
        at = keep_at if p < pieces // 2 else send_at
        lanes = pl.ds(pl.multiple_of(at + (p % (pieces // 2)) * piece, piece), piece)
        loads.append(pltpu.make_async_copy(panels_hbm.at[1:3, :, lanes], kv_ref.at[p], sems.at[1 + p]))
    loads.append(pltpu.make_async_copy(w_hbm, w_ref, sems.at[1 + pieces]))
    loads.append(pltpu.make_async_copy(panels_hbm.at[0, rows - 16 :, :], q_ref, sems.at[2 + pieces]))
    for load in loads:
        load.start()
    x_ref[:, 0:8, :] = jnp.zeros((x_ref.shape[0], 8, GROUP), jnp.float32)
    loads[0].wait()
    row_masks(seq_ref, shard * rows, m1_ref, m2_ref)
    loads[1 + pieces].wait()
    loads[2 + pieces].wait()
    for p in range(pieces):
        loads[1 + p].wait()
        out_ref, at = (kept_ref, keep_at) if p < pieces // 2 else (sent_ref, send_at)
        for c in range(0, piece, GROUP):
            base = (p % (pieces // 2)) * piece + c
            there = slice(base, base + GROUP)
            lanes = pl.ds(pl.multiple_of(at + base, GROUP), GROUP)
            slot = (c // GROUP) % (x_ref.shape[0] // 2) * 2
            heads, tails, made = [], [], []
            for i in range(2):
                x = kv_ref[p, i, :, c : c + GROUP].astype(jnp.float32)
                x_ref[slot + i, 8:, :] = x
                made.append(feature(x, x_ref.at[slot + i], w_ref[1 + i, :, lanes], m1_ref, m2_ref))
                heads.append(x[0:2])
                tails.append(x[rows - 2 :])
            out_ref[:rows, there] = (made[0] * made[1]).astype(out_ref.dtype)
            tails.append(q_ref[:, lanes].astype(jnp.float32)[14:])
            extra = jnp.concatenate(heads + tails + [jnp.zeros((6, GROUP), jnp.float32)], 0)
            out_ref[rows:, there] = extra.astype(out_ref.dtype)


def edge_marks(seq_ref):
    t = (
        (lax.axis_index("blk") - 2) * (2 * BLK)
        + lax.broadcasted_iota(jnp.int32, (8, GROUP), 1) * BLK
        + lax.broadcasted_iota(jnp.int32, (8, GROUP), 0)
    )
    return [1.0 - mark.astype(jnp.float32) for mark in boundaries(seq_ref, t)]


def first_rows(now, ahead, w_ref, marks, spot):
    m1, m2 = [mark[:, spot : spot + 1] for mark in marks]
    top = lax.broadcasted_iota(jnp.int32, now.shape, 0) == 0
    made = []
    for i in range(2):
        x0 = pltpu.roll(now, (8 - 2 * i) % 8, 0) if i else now
        x1 = jnp.where(top, pltpu.roll(ahead, 3 - 2 * i, 0), pltpu.roll(now, (9 - 2 * i) % 8, 0))
        x2 = pltpu.roll(ahead, 4 - 2 * i, 0)
        w = w_ref[1 + i]
        made.append(w[0:1] * x0 + w[1:2] * x1 * m1 + w[2:3] * x2 * m2)
    return made[0] * made[1]


def put_first_rows(win_ref, at, rows):
    old = win_ref[at : at + 16, :].astype(jnp.float32)
    new = jnp.concatenate([rows, rows], 0)
    first = lax.broadcasted_iota(jnp.int32, old.shape, 0) < 2
    win_ref[at : at + 16, :] = jnp.where(first, new, old).astype(win_ref.dtype)


def reaches_past(seq_ref, block):
    first = block * (2 * BLK)

    def step(k, carry):
        end, start = carry
        end = end + seq_ref[k]
        return end, jnp.where(end <= first, end, start)

    _, start = lax.fori_loop(0, seq_ref.shape[0], step, (jnp.int32(0), jnp.int32(0)), unroll=True)
    return first - 2 * BLK - start > BLK


def tables_kernel(seq_ref, taps_ref, w_ref, out_ref, next_ref, w_half_ref, rev_ref, m_ref):
    groups = out_ref.shape[0]
    taps = taps_ref.shape[1]
    span = out_ref.shape[3]
    half = lax.axis_index("half")
    start = lax.axis_index("blk") * (2 * BLK)
    width = w_half_ref.shape[2]
    w_half_ref[...] = w_ref[:, :, pl.ds(pl.multiple_of(half * width, width), width)]
    turn = lax.broadcasted_iota(jnp.int32, (taps, span), 0) + lax.broadcasted_iota(
        jnp.int32, (taps, span), 1
    )
    turn = (turn == taps).astype(jnp.bfloat16)
    rev_ref[...] = jnp.dot(taps_ref[...], turn, preferred_element_type=jnp.float32)
    seg_in = counted(seq_ref, start - taps + lax.broadcasted_iota(jnp.int32, (8, span), 1))[0:1]
    for part in range(3):
        t_out = start + part * BLK + lax.broadcasted_iota(jnp.int32, (BLK, GROUP), 0)
        seg_out = counted(seq_ref, t_out)[:, 0:1]
        if part < 2:
            m_ref[part] = (seg_in == seg_out).astype(jnp.float32)
        else:
            m_ref[2, :, : 2 * BLK] = (seg_in[:, 2 * BLK : 4 * BLK] == seg_out).astype(jnp.float32)

    def one(g, _):
        row = rev_ref[pl.ds(half * groups + g, 1), :]
        table = pltpu.roll(jnp.broadcast_to(row, (BLK, span)), 0, 1, stride=1, stride_axis=0)
        out_ref[g, 0] = (table * m_ref[0]).astype(out_ref.dtype)
        later = jnp.concatenate([table[:, span - BLK :], table[:, : span - BLK]], 1)
        out_ref[g, 1] = (later * m_ref[1]).astype(out_ref.dtype)
        next_ref[g] = (table[:, : 2 * BLK] * m_ref[2, :, : 2 * BLK]).astype(next_ref.dtype)
        return 0

    lax.fori_loop(0, groups, one, 0)


def fill(win_ref, extra_ref, spot, message):
    win_ref[pl.ds(pl.multiple_of(spot * BLK, BLK), BLK), :] = message[:BLK]
    extra_ref[spot] = message[BLK:].astype(jnp.float32)


def relay_kernel(seq_ref, next_ref, back_own_ref, back_pair_ref, w_ref, out_ref, win_ref, extra_ref):
    groups = next_ref.shape[0]
    width = groups * GROUP
    half = lax.axis_index("half")
    fill(win_ref, extra_ref, half, back_own_ref)
    fill(win_ref, extra_ref, 1 - half, back_pair_ref)
    marks = edge_marks(seq_ref)
    rows = first_rows(extra_ref[1, :8], extra_ref[0, :8], w_ref, marks, 3)
    put_first_rows(win_ref, BLK, rows)
    out_ref[BLK:] = extra_ref[1].astype(out_ref.dtype)
    summed = reaches_past(seq_ref, lax.axis_index("blk") + 1)

    @pl.when(summed)
    def _():
        for g in range(groups):
            lanes = slice(g * GROUP, (g + 1) * GROUP)
            total = jnp.dot(next_ref[g], win_ref[:, lanes], preferred_element_type=jnp.float32)
            out_ref[:BLK, lanes] = total.astype(out_ref.dtype)

    @pl.when(jnp.logical_not(summed))
    def _():
        out_ref[:BLK] = win_ref[BLK:]


def gate_rows(seq_ref, raw_ref, tail, w_ref, part, q_ref, x_ref, m1_ref, m2_ref):
    width = raw_ref.shape[1]
    row_masks(seq_ref, lax.axis_index("blk") * (2 * BLK) + part * BLK, m1_ref, m2_ref)
    for c in range(0, width, GROUP):
        lanes = slice(c, c + GROUP)
        w = w_ref[0, :, lanes]
        x = raw_ref[:, lanes].astype(jnp.float32)
        slot = (c // GROUP) % 2
        x_ref[slot, 6:8, :] = tail(lanes)
        x_ref[slot, 8:, :] = x
        q_ref[:, lanes] = feature(x, x_ref.at[slot], w, m1_ref, m2_ref)


def near_kernel(
    seq_ref, table_ref, own_ref, pair_ref, back_own_ref, back_pair_ref, qkept_ref, w_ref, bias_ref,
    acc_ref, q_ref, marks_ref, win_ref, extra_ref, x_ref, m1_ref, m2_ref,
):
    groups = table_ref.shape[0]
    width = groups * GROUP
    half = lax.axis_index("half")
    block = lax.axis_index("blk")
    for spot, message in ((half, back_own_ref), (1 - half, back_pair_ref), (2 + half, own_ref), (3 - half, pair_ref)):
        fill(win_ref, extra_ref, spot, message)
    marks = edge_marks(seq_ref)
    marks_ref[0], marks_ref[1] = marks
    marks_ref[2] = jnp.full((8, GROUP), reaches_past(seq_ref, block).astype(jnp.float32))
    for spot in (1, 2, 3):
        rows = first_rows(extra_ref[spot, :8], extra_ref[spot - 1, :8], w_ref, marks, spot + 2)
        put_first_rows(win_ref, spot * BLK, rows)
    for g in range(groups):
        lanes = slice(g * GROUP, (g + 1) * GROUP)
        bias = bias_ref[:, pl.ds(pl.multiple_of(half * width + g * GROUP, GROUP), GROUP)]
        for part in range(2):
            total = jnp.dot(
                table_ref[g, part, :, 3 * BLK : (5 + part) * BLK],
                win_ref[BLK : (3 + part) * BLK, lanes],
                preferred_element_type=jnp.float32,
            )
            here = win_ref[(2 + part) * BLK : (3 + part) * BLK, lanes].astype(jnp.float32)
            acc_ref[part * BLK : (part + 1) * BLK, lanes] = total + bias * here
    gate_rows(
        seq_ref, qkept_ref, lambda lanes: extra_ref[1 + half, 8:10, lanes], w_ref, half, q_ref, x_ref, m1_ref, m2_ref
    )


def pair_gate_kernel(seq_ref, raw_ref, own_ref, back_own_ref, w_ref, q_ref, x_ref, m1_ref, m2_ref):
    half = lax.axis_index("half")

    def tail(lanes):
        back = back_own_ref[BLK:, lanes].astype(jnp.float32)
        own = own_ref[BLK:, lanes].astype(jnp.float32)
        return jnp.where(half == 1, back, own)[8:10]

    gate_rows(seq_ref, raw_ref, tail, w_ref, 1 - half, q_ref, x_ref, m1_ref, m2_ref)


def far_kernel(short, table_ref, acc_ref, qown_ref, qpair_ref, w_ref, marks_ref, *refs):
    *messages, kept_ref, sent_ref, power_ref, win_ref, extra_ref = refs
    groups = table_ref.shape[0]
    width = groups * GROUP
    half = lax.axis_index("half")
    marks = [marks_ref[0], marks_ref[1]]
    back_own_ref, back_pair_ref, far_ref, *others = messages
    low = 1 if short else 0
    fill(win_ref, extra_ref, 2 + half, back_own_ref)
    fill(win_ref, extra_ref, 3 - half, back_pair_ref)
    if short:
        summed = marks_ref[2, 0:1, 0:1]
        payload = far_ref[:BLK].astype(jnp.float32)
        win_ref[BLK : 2 * BLK, :] = (payload * (1.0 - summed)).astype(win_ref.dtype)
        extra_ref[1] = far_ref[BLK:].astype(jnp.float32)
    else:
        fill(win_ref, extra_ref, half, far_ref)
        fill(win_ref, extra_ref, 1 - half, others[0])
        ahead = others[1][...].astype(jnp.float32)[:8]
        put_first_rows(win_ref, 0, first_rows(extra_ref[0, :8], ahead, w_ref, marks, 0))
        rows = first_rows(extra_ref[1, :8], extra_ref[0, :8], w_ref, marks, 1)
        put_first_rows(win_ref, BLK, rows)
    rows = first_rows(extra_ref[2, :8], extra_ref[1, :8], w_ref, marks, 2)
    put_first_rows(win_ref, 2 * BLK, rows)
    for at, part, q_ref, out_ref in ((0, half, qown_ref, kept_ref), (BLK, 1 - half, qpair_ref, sent_ref)):
        squares = jnp.zeros((BLK, GROUP), jnp.float32)
        rows = pl.ds(pl.multiple_of(part * BLK, BLK), BLK)
        for g in range(groups):
            lanes = slice(g * GROUP, (g + 1) * GROUP)
            filtered = acc_ref[rows, lanes] + jnp.dot(
                table_ref[g, part, :, low * BLK : 3 * BLK],
                win_ref[low * BLK : 3 * BLK, lanes],
                preferred_element_type=jnp.float32,
            )
            if short:
                weight = summed * (part == 0).astype(jnp.float32)
                filtered = filtered + weight * far_ref[:BLK, lanes].astype(jnp.float32)
            gated = q_ref[:, lanes] * filtered
            squares = squares + gated * gated
            out_ref[:, lanes] = gated.astype(out_ref.dtype)
        power_ref[:, at : at + BLK] = lax.dot_general(
            jnp.ones((8, GROUP), jnp.float32),
            squares,
            (((1,), (1,)), ((), ())),
            precision=lax.Precision.HIGHEST,
            preferred_element_type=jnp.float32,
        )[0:1]


def norm_kernel(channels, power_ref, power_got_ref, kept_ref, got_ref, gain_ref, out_ref):
    half = lax.axis_index("half")
    width = kept_ref.shape[1]
    power = power_ref[:, :BLK] + power_got_ref[:, BLK:]
    scale = lax.rsqrt(power / channels + norm_eps)
    diagonal = lax.broadcasted_iota(jnp.int32, (BLK, BLK), 0) == lax.broadcasted_iota(
        jnp.int32, (BLK, BLK), 1
    )
    column = jnp.sum(jnp.where(diagonal, scale, 0.0), axis=1, keepdims=True)
    for which, part_ref in ((half, kept_ref), (1 - half, got_ref)):
        for c in range(0, width, GROUP):
            lanes = pl.ds(pl.multiple_of(which * width + c, GROUP), GROUP)
            out_ref[:, lanes] = (
                part_ref[:, c : c + GROUP].astype(jnp.float32) * column * gain_ref[:, lanes]
            ).astype(out_ref.dtype)


def kernel_call(body, outs, in_specs, scratch, flops, moved_bytes, vmem=24 << 20):
    return pl.pallas_call(
        body,
        out_shape=outs,
        in_specs=in_specs,
        out_specs=jax.tree.map(lambda _: VMEM, outs),
        scratch_shapes=scratch,
        compiler_params=pltpu.CompilerParams(vmem_limit_bytes=vmem),
        cost_estimate=pl.CostEstimate(flops=flops, bytes_accessed=moved_bytes, transcendentals=0),
    )


def shards(blocks, whole_tokens, channels, projected, short_weight, filter_taps, tap_blocks, skip_bias, norm_gain, seq_lengths):
    rows = projected.shape[0]
    width = projected.shape[2] // 2
    groups = width // GROUP
    taps = filter_taps.shape[1]
    shape = jax.ShapeDtypeStruct
    half_shape = shape((rows, width), jnp.bfloat16)
    half_wide = shape((rows, width), jnp.float32)

    spots = range(2 * blocks)
    to_pair = [(i, i ^ 1) for i in spots]
    ahead = [(i, (i + 2) % (2 * blocks)) for i in spots]

    panels = jnp.transpose(projected, (1, 0, 2))
    message = shape((rows + 16, width), jnp.bfloat16)
    hbm = pl.BlockSpec(memory_space=pltpu.HBM)
    pieces = 4
    row_mask = pltpu.VMEM((rows, GROUP), jnp.float32)

    sent, kept = kernel_call(
        products_kernel,
        (message, message),
        [hbm] * 3,
        [
            pltpu.SMEM(seq_lengths.shape, jnp.int32),
            pltpu.VMEM((pieces, 2, rows, 2 * width // pieces), jnp.bfloat16),
            pltpu.VMEM((16, 2 * width), jnp.bfloat16),
            pltpu.VMEM(short_weight.shape, jnp.float32),
            pltpu.VMEM((4, rows + 8, GROUP), jnp.float32),
            row_mask,
            row_mask,
            pltpu.SemaphoreType.DMA((3 + pieces,)),
        ],
        40 * rows * width,
        16 * rows * width,
        60 << 20,
    )(seq_lengths, panels, short_weight)

    pair = moved(sent, to_pair)
    back_own = moved(kept, ahead)
    back_pair = moved(pair, ahead)
    filter_taps, query, _ = lax.optimization_barrier((filter_taps, panels[0], kept))
    half = lax.axis_index("half")
    qkept = lax.dynamic_slice_in_dim(query, half * width, width, 1)
    qsent = lax.dynamic_slice_in_dim(query, (1 - half) * width, width, 1)
    scaled = (filter_taps * jnp.repeat(tap_blocks.astype(jnp.float32), BLK, axis=1)).astype(jnp.bfloat16)
    pair, qsent = lax.optimization_barrier((pair, qsent))
    qgot = moved(qsent, to_pair)
    span = taps + 2 * BLK
    table, table_next, w_half = kernel_call(
        tables_kernel,
        (
            shape((groups, 2, BLK, span), jnp.bfloat16),
            shape((groups, BLK, 2 * BLK), jnp.bfloat16),
            shape((3, 3, width), jnp.float32),
        ),
        [SMEM, VMEM, VMEM],
        [pltpu.VMEM((2 * groups, span), jnp.float32), pltpu.VMEM((3, BLK, span), jnp.float32)],
        40 * groups * BLK * taps,
        8 * groups * BLK * taps,
    )(seq_lengths, scaled, short_weight)
    table, table_next, back_own = lax.optimization_barrier((table, table_next, back_own))
    table, back_pair, qkept, qgot = lax.optimization_barrier((table, back_pair, qkept, qgot))

    window = pltpu.VMEM((4 * rows, width), jnp.bfloat16)
    extras = pltpu.VMEM((4, 16, width), jnp.float32)
    shifted = pltpu.VMEM((2, rows + 8, GROUP), jnp.float32)
    short = whole_tokens // 2 <= 4 * BLK
    if short:
        relayed = kernel_call(
            relay_kernel,
            message,
            [SMEM] + [VMEM] * 4,
            [pltpu.VMEM((2 * rows, width), jnp.bfloat16), pltpu.VMEM((2, 16, width), jnp.float32)],
            2 * 2 * rows * BLK * width,
            8 * rows * width,
        )(seq_lengths, table_next, back_own, back_pair, w_half)
        far = (moved(relayed, ahead),)
    else:
        straight = moved(kept[rows:], [(i, (i + 6) % (2 * blocks)) for i in spots])
        across = moved(sent[rows:], [(i, ((i ^ 1) + 6) % (2 * blocks)) for i in spots])
        deep = jnp.where(half == 1, straight, across)
        far = (moved(back_own, ahead), moved(back_pair, ahead), deep)

    acc, qown, marks = kernel_call(
        near_kernel,
        (shape((2 * rows, width), jnp.float32), half_wide, shape((3, 8, GROUP), jnp.float32)),
        [SMEM] + [VMEM] * 8,
        [window, extras, shifted, row_mask, row_mask],
        2 * 5 * rows * BLK * width,
        16 * rows * width,
    )(seq_lengths, table, kept, pair, back_own, back_pair, qkept, w_half, skip_bias.reshape(1, -1))

    qpair = kernel_call(
        pair_gate_kernel,
        half_wide,
        [SMEM] + [VMEM] * 4,
        [shifted, row_mask, row_mask],
        10 * rows * width,
        8 * rows * width,
    )(seq_lengths, qgot, kept, back_own, w_half)

    done, send, power = kernel_call(
        functools.partial(far_kernel, short),
        (half_wide, half_shape, shape((1, 2 * rows), jnp.float32)),
        [VMEM] * (8 + len(far)),
        [window, extras],
        2 * 5 * rows * BLK * width,
        24 * rows * width,
    )(table, acc, qown, qpair, w_half, marks, back_own, back_pair, *far)

    back = moved(send, to_pair)
    peers = lax.axis_size("mp")
    shares = [lax.ppermute(power, "mp", [(i, i ^ k) for i in range(peers)]) for k in range(1, peers)]
    power = sum(shares, power)
    return kernel_call(
        functools.partial(norm_kernel, channels),
        shape((rows, 2 * width), jnp.bfloat16),
        [VMEM] * 5,
        [],
        8 * rows * width,
        10 * rows * width,
    )(power, moved(power, to_pair), done, back, norm_gain.reshape(1, -1))


def solution(mesh):
    blocks = mesh.shape["ctx"] // 2
    grid = Mesh(mesh.devices.reshape(blocks, 2, mesh.shape["mp"]), ("blk", "half", "mp"))
    in_specs = (
        P(SPOTS, None, "mp"),
        P(None, None, "mp"),
        P("mp", None),
        P("mp", None),
        P("mp"),
        P("mp"),
        P(),
    )

    def program(projected, *rest):
        body = functools.partial(shards, blocks, projected.shape[0], projected.shape[2])
        return jax.shard_map(
            body, mesh=grid, in_specs=in_specs, out_specs=P(SPOTS, "mp"), check_vma=False
        )(projected, *rest)

    return program
```

```python
import functools

import jax
import jax.numpy as jnp
from jax import lax
from jax.experimental import pallas as pl
from jax.experimental.pallas import tpu as pltpu
from jax.sharding import Mesh, PartitionSpec as P

GROUP = 128
BLK = 128
norm_eps = 1e-06

VMEM = pl.BlockSpec(memory_space=pltpu.VMEM)
SMEM = pl.BlockSpec(memory_space=pltpu.SMEM)
SPOTS = ("blk", "half")


def moved(block, pairs):
    return lax.ppermute(block, SPOTS, pairs)


def boundaries(seq_ref, t):
    def step(k, carry):
        end, first, second = carry
        end = end + seq_ref[k]
        return end, first | (t == end).astype(jnp.int32), second | (t - 1 == end).astype(jnp.int32)

    first = (t == 0).astype(jnp.int32)
    second = (t == 1).astype(jnp.int32)
    _, first, second = lax.fori_loop(0, seq_ref.shape[0], step, (jnp.int32(0), first, second), unroll=True)
    return first, first | second


def row_masks(seq_ref, start, m1_ref, m2_ref):
    rows = lax.broadcasted_iota(jnp.int32, (BLK, GROUP), 0)
    diagonal = rows == lax.broadcasted_iota(jnp.int32, (BLK, GROUP), 1)
    marks = boundaries(seq_ref, start + lax.broadcasted_iota(jnp.int32, (8, GROUP), 1))
    for mark, m_ref in zip(marks, (m1_ref, m2_ref)):
        keep = 1.0 - mark.astype(jnp.float32)[0:1]
        column = jnp.sum(jnp.where(diagonal, keep, 0.0), axis=1, keepdims=True)
        m_ref[...] = jnp.broadcast_to(column, (BLK, GROUP))


def counted(seq_ref, t):
    def step(k, carry):
        end, total = carry
        end = end + seq_ref[k]
        return end, total + (end <= t).astype(jnp.int32)

    _, total = lax.fori_loop(
        0, seq_ref.shape[0], step, (jnp.int32(0), jnp.zeros(t.shape, jnp.int32)), unroll=True
    )
    return jnp.where(t >= 0, total, -1)


def feature(x, x_ref, w, m1_ref, m2_ref):
    rows = x.shape[0]
    return (
        w[0:1] * x
        + w[1:2] * x_ref[7 : rows + 7, :] * m1_ref[...]
        + w[2:3] * x_ref[6 : rows + 6, :] * m2_ref[...]
    )


def products_kernel(
    seq_hbm, panels_hbm, w_hbm, sent_ref, kept_ref, seq_ref, kv_ref, q_ref, w_ref, x_ref, m1_ref, m2_ref, sems
):
    width = kept_ref.shape[1]
    rows = kv_ref.shape[2]
    pieces = kv_ref.shape[0]
    piece = kv_ref.shape[3]
    half = lax.axis_index("half")
    shard = lax.axis_index("blk") * 2 + half
    keep_at = pl.multiple_of(half * width, width)
    send_at = pl.multiple_of((1 - half) * width, width)

    loads = [pltpu.make_async_copy(seq_hbm, seq_ref, sems.at[0])]
    for p in range(pieces):
        at = keep_at if p < pieces // 2 else send_at
        lanes = pl.ds(pl.multiple_of(at + (p % (pieces // 2)) * piece, piece), piece)
        loads.append(pltpu.make_async_copy(panels_hbm.at[1:3, :, lanes], kv_ref.at[p], sems.at[1 + p]))
    loads.append(pltpu.make_async_copy(w_hbm, w_ref, sems.at[1 + pieces]))
    loads.append(pltpu.make_async_copy(panels_hbm.at[0, rows - 16 :, :], q_ref, sems.at[2 + pieces]))
    for load in loads:
        load.start()
    x_ref[:, 0:8, :] = jnp.zeros((x_ref.shape[0], 8, GROUP), jnp.float32)
    loads[0].wait()
    row_masks(seq_ref, shard * rows, m1_ref, m2_ref)
    loads[1 + pieces].wait()
    loads[2 + pieces].wait()
    for p in range(pieces):
        loads[1 + p].wait()
        out_ref, at = (kept_ref, keep_at) if p < pieces // 2 else (sent_ref, send_at)
        for c in range(0, piece, GROUP):
            base = (p % (pieces // 2)) * piece + c
            there = slice(base, base + GROUP)
            lanes = pl.ds(pl.multiple_of(at + base, GROUP), GROUP)
            slot = (c // GROUP) % (x_ref.shape[0] // 2) * 2
            heads, tails, made = [], [], []
            for i in range(2):
                x = kv_ref[p, i, :, c : c + GROUP].astype(jnp.float32)
                x_ref[slot + i, 8:, :] = x
                made.append(feature(x, x_ref.at[slot + i], w_ref[1 + i, :, lanes], m1_ref, m2_ref))
                heads.append(x[0:2])
                tails.append(x[rows - 2 :])
            out_ref[:rows, there] = (made[0] * made[1]).astype(out_ref.dtype)
            tails.append(q_ref[:, lanes].astype(jnp.float32)[14:])
            extra = jnp.concatenate(heads + tails + [jnp.zeros((6, GROUP), jnp.float32)], 0)
            out_ref[rows:, there] = extra.astype(out_ref.dtype)


def edge_marks(seq_ref):
    t = (
        (lax.axis_index("blk") - 2) * (2 * BLK)
        + lax.broadcasted_iota(jnp.int32, (8, GROUP), 1) * BLK
        + lax.broadcasted_iota(jnp.int32, (8, GROUP), 0)
    )
    return [1.0 - mark.astype(jnp.float32) for mark in boundaries(seq_ref, t)]


def first_rows(now, ahead, w_ref, marks, spot):
    m1, m2 = [mark[:, spot : spot + 1] for mark in marks]
    top = lax.broadcasted_iota(jnp.int32, now.shape, 0) == 0
    made = []
    for i in range(2):
        x0 = pltpu.roll(now, (8 - 2 * i) % 8, 0) if i else now
        x1 = jnp.where(top, pltpu.roll(ahead, 3 - 2 * i, 0), pltpu.roll(now, (9 - 2 * i) % 8, 0))
        x2 = pltpu.roll(ahead, 4 - 2 * i, 0)
        w = w_ref[1 + i]
        made.append(w[0:1] * x0 + w[1:2] * x1 * m1 + w[2:3] * x2 * m2)
    return made[0] * made[1]


def put_first_rows(win_ref, at, rows):
    old = win_ref[at : at + 16, :].astype(jnp.float32)
    new = jnp.concatenate([rows, rows], 0)
    first = lax.broadcasted_iota(jnp.int32, old.shape, 0) < 2
    win_ref[at : at + 16, :] = jnp.where(first, new, old).astype(win_ref.dtype)


def reaches_past(seq_ref, block):
    first = block * (2 * BLK)

    def step(k, carry):
        end, start = carry
        end = end + seq_ref[k]
        return end, jnp.where(end <= first, end, start)

    _, start = lax.fori_loop(0, seq_ref.shape[0], step, (jnp.int32(0), jnp.int32(0)), unroll=True)
    return first - 2 * BLK - start > BLK


def tables_kernel(seq_ref, taps_ref, w_ref, out_ref, next_ref, w_half_ref, rev_ref, m_ref):
    groups = out_ref.shape[0]
    taps = taps_ref.shape[1]
    span = out_ref.shape[3]
    half = lax.axis_index("half")
    start = lax.axis_index("blk") * (2 * BLK)
    width = w_half_ref.shape[2]
    w_half_ref[...] = w_ref[:, :, pl.ds(pl.multiple_of(half * width, width), width)]
    turn = lax.broadcasted_iota(jnp.int32, (taps, span), 0) + lax.broadcasted_iota(
        jnp.int32, (taps, span), 1
    )
    turn = (turn == taps).astype(jnp.bfloat16)
    rev_ref[...] = jnp.dot(taps_ref[...], turn, preferred_element_type=jnp.float32)
    seg_in = counted(seq_ref, start - taps + lax.broadcasted_iota(jnp.int32, (8, span), 1))[0:1]
    for part in range(3):
        t_out = start + part * BLK + lax.broadcasted_iota(jnp.int32, (BLK, GROUP), 0)
        seg_out = counted(seq_ref, t_out)[:, 0:1]
        if part < 2:
            m_ref[part] = (seg_in == seg_out).astype(jnp.float32)
        else:
            m_ref[2, :, : 2 * BLK] = (seg_in[:, 2 * BLK : 4 * BLK] == seg_out).astype(jnp.float32)

    def one(g, _):
        row = rev_ref[pl.ds(half * groups + g, 1), :]
        table = pltpu.roll(jnp.broadcast_to(row, (BLK, span)), 0, 1, stride=1, stride_axis=0)
        out_ref[g, 0] = (table * m_ref[0]).astype(out_ref.dtype)
        later = jnp.concatenate([table[:, span - BLK :], table[:, : span - BLK]], 1)
        out_ref[g, 1] = (later * m_ref[1]).astype(out_ref.dtype)
        next_ref[g] = (table[:, : 2 * BLK] * m_ref[2, :, : 2 * BLK]).astype(next_ref.dtype)
        return 0

    lax.fori_loop(0, groups, one, 0)


def fill(win_ref, extra_ref, spot, message):
    win_ref[pl.ds(pl.multiple_of(spot * BLK, BLK), BLK), :] = message[:BLK]
    extra_ref[spot] = message[BLK:].astype(jnp.float32)


def relay_kernel(seq_ref, next_ref, back_own_ref, back_pair_ref, w_ref, out_ref, win_ref, extra_ref):
    groups = next_ref.shape[0]
    width = groups * GROUP
    half = lax.axis_index("half")
    fill(win_ref, extra_ref, half, back_own_ref)
    fill(win_ref, extra_ref, 1 - half, back_pair_ref)
    marks = edge_marks(seq_ref)
    rows = first_rows(extra_ref[1, :8], extra_ref[0, :8], w_ref, marks, 3)
    put_first_rows(win_ref, BLK, rows)
    out_ref[BLK:] = extra_ref[1].astype(out_ref.dtype)
    summed = reaches_past(seq_ref, lax.axis_index("blk") + 1)

    @pl.when(summed)
    def _():
        for g in range(groups):
            lanes = slice(g * GROUP, (g + 1) * GROUP)
            total = jnp.dot(next_ref[g], win_ref[:, lanes], preferred_element_type=jnp.float32)
            out_ref[:BLK, lanes] = total.astype(out_ref.dtype)

    @pl.when(jnp.logical_not(summed))
    def _():
        out_ref[:BLK] = win_ref[BLK:]


def gate_rows(seq_ref, raw_ref, tail, w_ref, part, q_ref, x_ref, m1_ref, m2_ref):
    width = raw_ref.shape[1]
    row_masks(seq_ref, lax.axis_index("blk") * (2 * BLK) + part * BLK, m1_ref, m2_ref)
    for c in range(0, width, GROUP):
        lanes = slice(c, c + GROUP)
        w = w_ref[0, :, lanes]
        x = raw_ref[:, lanes].astype(jnp.float32)
        slot = (c // GROUP) % 2
        x_ref[slot, 6:8, :] = tail(lanes)
        x_ref[slot, 8:, :] = x
        q_ref[:, lanes] = feature(x, x_ref.at[slot], w, m1_ref, m2_ref)


def near_kernel(
    seq_ref, table_ref, own_ref, pair_ref, back_own_ref, back_pair_ref, qkept_ref, w_ref, bias_ref,
    acc_ref, q_ref, marks_ref, win_ref, extra_ref, x_ref, m1_ref, m2_ref,
):
    groups = table_ref.shape[0]
    width = groups * GROUP
    half = lax.axis_index("half")
    block = lax.axis_index("blk")
    for spot, message in ((half, back_own_ref), (1 - half, back_pair_ref), (2 + half, own_ref), (3 - half, pair_ref)):
        fill(win_ref, extra_ref, spot, message)
    marks = edge_marks(seq_ref)
    marks_ref[0], marks_ref[1] = marks
    marks_ref[2] = jnp.full((8, GROUP), reaches_past(seq_ref, block).astype(jnp.float32))
    for spot in (1, 2, 3):
        rows = first_rows(extra_ref[spot, :8], extra_ref[spot - 1, :8], w_ref, marks, spot + 2)
        put_first_rows(win_ref, spot * BLK, rows)
    for g in range(groups):
        lanes = slice(g * GROUP, (g + 1) * GROUP)
        bias = bias_ref[:, pl.ds(pl.multiple_of(half * width + g * GROUP, GROUP), GROUP)]
        for part in range(2):
            total = jnp.dot(
                table_ref[g, part, :, 3 * BLK : (5 + part) * BLK],
                win_ref[BLK : (3 + part) * BLK, lanes],
                preferred_element_type=jnp.float32,
            )
            here = win_ref[(2 + part) * BLK : (3 + part) * BLK, lanes].astype(jnp.float32)
            acc_ref[part * BLK : (part + 1) * BLK, lanes] = total + bias * here
    gate_rows(
        seq_ref, qkept_ref, lambda lanes: extra_ref[1 + half, 8:10, lanes], w_ref, half, q_ref, x_ref, m1_ref, m2_ref
    )


def pair_gate_kernel(seq_ref, raw_ref, own_ref, back_own_ref, w_ref, q_ref, x_ref, m1_ref, m2_ref):
    half = lax.axis_index("half")

    def tail(lanes):
        back = back_own_ref[BLK:, lanes].astype(jnp.float32)
        own = own_ref[BLK:, lanes].astype(jnp.float32)
        return jnp.where(half == 1, back, own)[8:10]

    gate_rows(seq_ref, raw_ref, tail, w_ref, 1 - half, q_ref, x_ref, m1_ref, m2_ref)


def far_kernel(short, table_ref, acc_ref, qown_ref, qpair_ref, w_ref, marks_ref, *refs):
    *messages, kept_ref, sent_ref, power_ref, win_ref, extra_ref = refs
    groups = table_ref.shape[0]
    width = groups * GROUP
    half = lax.axis_index("half")
    marks = [marks_ref[0], marks_ref[1]]
    back_own_ref, back_pair_ref, far_ref, *others = messages
    low = 1 if short else 0
    fill(win_ref, extra_ref, 2 + half, back_own_ref)
    fill(win_ref, extra_ref, 3 - half, back_pair_ref)
    if short:
        summed = marks_ref[2, 0:1, 0:1]
        payload = far_ref[:BLK].astype(jnp.float32)
        win_ref[BLK : 2 * BLK, :] = (payload * (1.0 - summed)).astype(win_ref.dtype)
        extra_ref[1] = far_ref[BLK:].astype(jnp.float32)
    else:
        fill(win_ref, extra_ref, half, far_ref)
        fill(win_ref, extra_ref, 1 - half, others[0])
        ahead = others[1][...].astype(jnp.float32)[:8]
        put_first_rows(win_ref, 0, first_rows(extra_ref[0, :8], ahead, w_ref, marks, 0))
        rows = first_rows(extra_ref[1, :8], extra_ref[0, :8], w_ref, marks, 1)
        put_first_rows(win_ref, BLK, rows)
    rows = first_rows(extra_ref[2, :8], extra_ref[1, :8], w_ref, marks, 2)
    put_first_rows(win_ref, 2 * BLK, rows)
    for at, part, q_ref, out_ref in ((0, half, qown_ref, kept_ref), (BLK, 1 - half, qpair_ref, sent_ref)):
        squares = jnp.zeros((BLK, GROUP), jnp.float32)
        rows = pl.ds(pl.multiple_of(part * BLK, BLK), BLK)
        for g in range(groups):
            lanes = slice(g * GROUP, (g + 1) * GROUP)
            filtered = acc_ref[rows, lanes] + jnp.dot(
                table_ref[g, part, :, low * BLK : 3 * BLK],
                win_ref[low * BLK : 3 * BLK, lanes],
                preferred_element_type=jnp.float32,
            )
            if short:
                weight = summed * (part == 0).astype(jnp.float32)
                filtered = filtered + weight * far_ref[:BLK, lanes].astype(jnp.float32)
            gated = q_ref[:, lanes] * filtered
            squares = squares + gated * gated
            out_ref[:, lanes] = gated.astype(out_ref.dtype)
        power_ref[:, at : at + BLK] = lax.dot_general(
            jnp.ones((8, GROUP), jnp.float32),
            squares,
            (((1,), (1,)), ((), ())),
            precision=lax.Precision.HIGHEST,
            preferred_element_type=jnp.float32,
        )[0:1]


def norm_kernel(channels, power_ref, power_got_ref, kept_ref, got_ref, gain_ref, out_ref):
    half = lax.axis_index("half")
    width = kept_ref.shape[1]
    power = power_ref[:, :BLK] + power_got_ref[:, BLK:]
    scale = lax.rsqrt(power / channels + norm_eps)
    diagonal = lax.broadcasted_iota(jnp.int32, (BLK, BLK), 0) == lax.broadcasted_iota(
        jnp.int32, (BLK, BLK), 1
    )
    column = jnp.sum(jnp.where(diagonal, scale, 0.0), axis=1, keepdims=True)
    for which, part_ref in ((half, kept_ref), (1 - half, got_ref)):
        for c in range(0, width, GROUP):
            lanes = pl.ds(pl.multiple_of(which * width + c, GROUP), GROUP)
            out_ref[:, lanes] = (
                part_ref[:, c : c + GROUP].astype(jnp.float32) * column * gain_ref[:, lanes]
            ).astype(out_ref.dtype)


def kernel_call(body, outs, in_specs, scratch, flops, moved_bytes, vmem=24 << 20):
    return pl.pallas_call(
        body,
        out_shape=outs,
        in_specs=in_specs,
        out_specs=jax.tree.map(lambda _: VMEM, outs),
        scratch_shapes=scratch,
        compiler_params=pltpu.CompilerParams(vmem_limit_bytes=vmem),
        cost_estimate=pl.CostEstimate(flops=flops, bytes_accessed=moved_bytes, transcendentals=0),
    )


def shards(blocks, whole_tokens, channels, projected, short_weight, filter_taps, tap_blocks, skip_bias, norm_gain, seq_lengths):
    rows = projected.shape[0]
    width = projected.shape[2] // 2
    groups = width // GROUP
    taps = filter_taps.shape[1]
    shape = jax.ShapeDtypeStruct
    half_shape = shape((rows, width), jnp.bfloat16)
    half_wide = shape((rows, width), jnp.float32)

    spots = range(2 * blocks)
    to_pair = [(i, i ^ 1) for i in spots]
    ahead = [(i, (i + 2) % (2 * blocks)) for i in spots]

    panels = jnp.transpose(projected, (1, 0, 2))
    message = shape((rows + 16, width), jnp.bfloat16)
    hbm = pl.BlockSpec(memory_space=pltpu.HBM)
    pieces = 4
    row_mask = pltpu.VMEM((rows, GROUP), jnp.float32)

    sent, kept = kernel_call(
        products_kernel,
        (message, message),
        [hbm] * 3,
        [
            pltpu.SMEM(seq_lengths.shape, jnp.int32),
            pltpu.VMEM((pieces, 2, rows, 2 * width // pieces), jnp.bfloat16),
            pltpu.VMEM((16, 2 * width), jnp.bfloat16),
            pltpu.VMEM(short_weight.shape, jnp.float32),
            pltpu.VMEM((4, rows + 8, GROUP), jnp.float32),
            row_mask,
            row_mask,
            pltpu.SemaphoreType.DMA((3 + pieces,)),
        ],
        40 * rows * width,
        16 * rows * width,
        60 << 20,
    )(seq_lengths, panels, short_weight)

    pair = moved(sent, to_pair)
    back_own = moved(kept, ahead)
    back_pair = moved(pair, ahead)
    filter_taps, query, _ = lax.optimization_barrier((filter_taps, panels[0], kept))
    half = lax.axis_index("half")
    qkept = lax.dynamic_slice_in_dim(query, half * width, width, 1)
    qsent = lax.dynamic_slice_in_dim(query, (1 - half) * width, width, 1)
    scaled = (filter_taps * jnp.repeat(tap_blocks.astype(jnp.float32), BLK, axis=1)).astype(jnp.bfloat16)
    pair, qsent = lax.optimization_barrier((pair, qsent))
    qgot = moved(qsent, to_pair)
    span = taps + 2 * BLK
    table, table_next, w_half = kernel_call(
        tables_kernel,
        (
            shape((groups, 2, BLK, span), jnp.bfloat16),
            shape((groups, BLK, 2 * BLK), jnp.bfloat16),
            shape((3, 3, width), jnp.float32),
        ),
        [SMEM, VMEM, VMEM],
        [pltpu.VMEM((2 * groups, span), jnp.float32), pltpu.VMEM((3, BLK, span), jnp.float32)],
        40 * groups * BLK * taps,
        8 * groups * BLK * taps,
    )(seq_lengths, scaled, short_weight)
    table, table_next, back_own = lax.optimization_barrier((table, table_next, back_own))
    table, back_pair, qkept, qgot = lax.optimization_barrier((table, back_pair, qkept, qgot))

    window = pltpu.VMEM((4 * rows, width), jnp.bfloat16)
    extras = pltpu.VMEM((4, 16, width), jnp.float32)
    shifted = pltpu.VMEM((2, rows + 8, GROUP), jnp.float32)
    short = whole_tokens // 2 <= 4 * BLK
    if short:
        relayed = kernel_call(
            relay_kernel,
            message,
            [SMEM] + [VMEM] * 4,
            [pltpu.VMEM((2 * rows, width), jnp.bfloat16), pltpu.VMEM((2, 16, width), jnp.float32)],
            2 * 2 * rows * BLK * width,
            8 * rows * width,
        )(seq_lengths, table_next, back_own, back_pair, w_half)
        far = (moved(relayed, [(i, j) for i, j in ahead if 2 <= i < j]),)
    else:
        straight = moved(kept[rows:], [(i, (i + 6) % (2 * blocks)) for i in spots])
        across = moved(sent[rows:], [(i, ((i ^ 1) + 6) % (2 * blocks)) for i in spots])
        deep = jnp.where(half == 1, straight, across)
        far = (moved(back_own, ahead), moved(back_pair, ahead), deep)

    acc, qown, marks = kernel_call(
        near_kernel,
        (shape((2 * rows, width), jnp.float32), half_wide, shape((3, 8, GROUP), jnp.float32)),
        [SMEM] + [VMEM] * 8,
        [window, extras, shifted, row_mask, row_mask],
        2 * 5 * rows * BLK * width,
        16 * rows * width,
    )(seq_lengths, table, kept, pair, back_own, back_pair, qkept, w_half, skip_bias.reshape(1, -1))

    qpair = kernel_call(
        pair_gate_kernel,
        half_wide,
        [SMEM] + [VMEM] * 4,
        [shifted, row_mask, row_mask],
        10 * rows * width,
        8 * rows * width,
    )(seq_lengths, qgot, kept, back_own, w_half)

    done, send, power = kernel_call(
        functools.partial(far_kernel, short),
        (half_wide, half_shape, shape((1, 2 * rows), jnp.float32)),
        [VMEM] * (8 + len(far)),
        [window, extras],
        2 * 5 * rows * BLK * width,
        24 * rows * width,
    )(table, acc, qown, qpair, w_half, marks, back_own, back_pair, *far)

    back = moved(send, to_pair)
    peers = lax.axis_size("mp")
    shares = [lax.ppermute(power, "mp", [(i, i ^ k) for i in range(peers)]) for k in range(1, peers)]
    power = sum(shares, power)
    return kernel_call(
        functools.partial(norm_kernel, channels),
        shape((rows, 2 * width), jnp.bfloat16),
        [VMEM] * 5,
        [],
        8 * rows * width,
        10 * rows * width,
    )(power, moved(power, to_pair), done, back, norm_gain.reshape(1, -1))


def solution(mesh):
    blocks = mesh.shape["ctx"] // 2
    grid = Mesh(mesh.devices.reshape(blocks, 2, mesh.shape["mp"]), ("blk", "half", "mp"))
    in_specs = (
        P(SPOTS, None, "mp"),
        P(None, None, "mp"),
        P("mp", None),
        P("mp", None),
        P("mp"),
        P("mp"),
        P(),
    )

    def program(projected, *rest):
        body = functools.partial(shards, blocks, projected.shape[0], projected.shape[2])
        return jax.shard_map(
            body, mesh=grid, in_specs=in_specs, out_specs=P(SPOTS, "mp"), check_vma=False
        )(projected, *rest)

    return program
```

```python
import functools

import jax
import jax.numpy as jnp
from jax import lax
from jax.experimental import pallas as pl
from jax.experimental.pallas import tpu as pltpu
from jax.sharding import Mesh, PartitionSpec as P

GROUP = 128
BLK = 128
norm_eps = 1e-06

VMEM = pl.BlockSpec(memory_space=pltpu.VMEM)
SMEM = pl.BlockSpec(memory_space=pltpu.SMEM)
SPOTS = ("blk", "half")


def moved(block, pairs):
    return lax.ppermute(block, SPOTS, pairs)


def boundaries(seq_ref, t):
    def step(k, carry):
        end, first, second = carry
        end = end + seq_ref[k]
        return end, first | (t == end).astype(jnp.int32), second | (t - 1 == end).astype(jnp.int32)

    first = (t == 0).astype(jnp.int32)
    second = (t == 1).astype(jnp.int32)
    _, first, second = lax.fori_loop(0, seq_ref.shape[0], step, (jnp.int32(0), first, second), unroll=True)
    return first, first | second


def row_masks(seq_ref, start, m1_ref, m2_ref):
    rows = lax.broadcasted_iota(jnp.int32, (BLK, GROUP), 0)
    diagonal = rows == lax.broadcasted_iota(jnp.int32, (BLK, GROUP), 1)
    marks = boundaries(seq_ref, start + lax.broadcasted_iota(jnp.int32, (8, GROUP), 1))
    for mark, m_ref in zip(marks, (m1_ref, m2_ref)):
        keep = 1.0 - mark.astype(jnp.float32)[0:1]
        column = jnp.sum(jnp.where(diagonal, keep, 0.0), axis=1, keepdims=True)
        m_ref[...] = jnp.broadcast_to(column, (BLK, GROUP))


def counted(seq_ref, t):
    def step(k, carry):
        end, total = carry
        end = end + seq_ref[k]
        return end, total + (end <= t).astype(jnp.int32)

    _, total = lax.fori_loop(
        0, seq_ref.shape[0], step, (jnp.int32(0), jnp.zeros(t.shape, jnp.int32)), unroll=True
    )
    return jnp.where(t >= 0, total, -1)


def feature(x, x_ref, w, m1_ref, m2_ref):
    rows = x.shape[0]
    return (
        w[0:1] * x
        + w[1:2] * x_ref[7 : rows + 7, :] * m1_ref[...]
        + w[2:3] * x_ref[6 : rows + 6, :] * m2_ref[...]
    )


def products_kernel(seq_hbm, panels_hbm, w_hbm, kept_ref, *refs):
    *sent_refs, seq_ref, kv_ref, q_ref, w_ref, x_ref, m1_ref, m2_ref, sems = refs
    width = kept_ref.shape[1]
    rows = kv_ref.shape[2]
    pieces = kv_ref.shape[0]
    piece = kv_ref.shape[3]
    half = lax.axis_index("half")
    shard = lax.axis_index("blk") * 2 + half
    keep_at = pl.multiple_of(half * width, width)
    send_at = pl.multiple_of((1 - half) * width, width)

    loads = [pltpu.make_async_copy(seq_hbm, seq_ref, sems.at[0])]
    for p in range(pieces):
        at = keep_at if p < pieces // 2 else send_at
        lanes = pl.ds(pl.multiple_of(at + (p % (pieces // 2)) * piece, piece), piece)
        loads.append(pltpu.make_async_copy(panels_hbm.at[1:3, :, lanes], kv_ref.at[p], sems.at[1 + p]))
    loads.append(pltpu.make_async_copy(w_hbm, w_ref, sems.at[1 + pieces]))
    loads.append(pltpu.make_async_copy(panels_hbm.at[0, rows - 16 :, :], q_ref, sems.at[2 + pieces]))
    for load in loads:
        load.start()
    x_ref[:, 0:8, :] = jnp.zeros((x_ref.shape[0], 8, GROUP), jnp.float32)
    loads[0].wait()
    row_masks(seq_ref, shard * rows, m1_ref, m2_ref)
    loads[1 + pieces].wait()
    loads[2 + pieces].wait()
    for p in range(pieces):
        loads[1 + p].wait()
        out_ref, at = (kept_ref, keep_at) if p < pieces // 2 else (sent_refs[p - pieces // 2], send_at)
        for c in range(0, piece, GROUP):
            base = (p % (pieces // 2)) * piece + c
            there = slice(base, base + GROUP) if p < pieces // 2 else slice(c, c + GROUP)
            lanes = pl.ds(pl.multiple_of(at + base, GROUP), GROUP)
            slot = (c // GROUP) % (x_ref.shape[0] // 2) * 2
            heads, tails, made = [], [], []
            for i in range(2):
                x = kv_ref[p, i, :, c : c + GROUP].astype(jnp.float32)
                x_ref[slot + i, 8:, :] = x
                made.append(feature(x, x_ref.at[slot + i], w_ref[1 + i, :, lanes], m1_ref, m2_ref))
                heads.append(x[0:2])
                tails.append(x[rows - 2 :])
            out_ref[:rows, there] = (made[0] * made[1]).astype(out_ref.dtype)
            tails.append(q_ref[:, lanes].astype(jnp.float32)[14:])
            extra = jnp.concatenate(heads + tails + [jnp.zeros((6, GROUP), jnp.float32)], 0)
            out_ref[rows:, there] = extra.astype(out_ref.dtype)


def edge_marks(seq_ref):
    t = (
        (lax.axis_index("blk") - 2) * (2 * BLK)
        + lax.broadcasted_iota(jnp.int32, (8, GROUP), 1) * BLK
        + lax.broadcasted_iota(jnp.int32, (8, GROUP), 0)
    )
    return [1.0 - mark.astype(jnp.float32) for mark in boundaries(seq_ref, t)]


def first_rows(now, ahead, w_ref, marks, spot, lanes=slice(None)):
    m1, m2 = [mark[:, spot : spot + 1] for mark in marks]
    top = lax.broadcasted_iota(jnp.int32, now.shape, 0) == 0
    made = []
    for i in range(2):
        x0 = pltpu.roll(now, (8 - 2 * i) % 8, 0) if i else now
        x1 = jnp.where(top, pltpu.roll(ahead, 3 - 2 * i, 0), pltpu.roll(now, (9 - 2 * i) % 8, 0))
        x2 = pltpu.roll(ahead, 4 - 2 * i, 0)
        w = w_ref[1 + i, :, lanes]
        made.append(w[0:1] * x0 + w[1:2] * x1 * m1 + w[2:3] * x2 * m2)
    return made[0] * made[1]


def put_first_rows(win_ref, at, rows):
    old = win_ref[at : at + 16, :].astype(jnp.float32)
    new = jnp.concatenate([rows, rows], 0)
    first = lax.broadcasted_iota(jnp.int32, old.shape, 0) < 2
    win_ref[at : at + 16, :] = jnp.where(first, new, old).astype(win_ref.dtype)


def reaches_past(seq_ref, block):
    first = block * (2 * BLK)

    def step(k, carry):
        end, start = carry
        end = end + seq_ref[k]
        return end, jnp.where(end <= first, end, start)

    _, start = lax.fori_loop(0, seq_ref.shape[0], step, (jnp.int32(0), jnp.int32(0)), unroll=True)
    return first - 2 * BLK - start > BLK


def tables_kernel(seq_ref, taps_ref, w_ref, out_ref, next_ref, w_half_ref, rev_ref, m_ref):
    groups = out_ref.shape[0]
    taps = taps_ref.shape[1]
    span = out_ref.shape[3]
    half = lax.axis_index("half")
    start = lax.axis_index("blk") * (2 * BLK)
    width = w_half_ref.shape[2]
    w_half_ref[...] = w_ref[:, :, pl.ds(pl.multiple_of(half * width, width), width)]
    turn = lax.broadcasted_iota(jnp.int32, (taps, span), 0) + lax.broadcasted_iota(
        jnp.int32, (taps, span), 1
    )
    turn = (turn == taps).astype(jnp.bfloat16)
    rev_ref[...] = jnp.dot(taps_ref[...], turn, preferred_element_type=jnp.float32)
    seg_in = counted(seq_ref, start - taps + lax.broadcasted_iota(jnp.int32, (8, span), 1))[0:1]
    for part in range(3):
        t_out = start + part * BLK + lax.broadcasted_iota(jnp.int32, (BLK, GROUP), 0)
        seg_out = counted(seq_ref, t_out)[:, 0:1]
        if part < 2:
            m_ref[part] = (seg_in == seg_out).astype(jnp.float32)
        else:
            m_ref[2, :, : 2 * BLK] = (seg_in[:, 2 * BLK : 4 * BLK] == seg_out).astype(jnp.float32)

    def one(g, _):
        row = rev_ref[pl.ds(half * groups + g, 1), :]
        table = pltpu.roll(jnp.broadcast_to(row, (BLK, span)), 0, 1, stride=1, stride_axis=0)
        out_ref[g, 0] = (table * m_ref[0]).astype(out_ref.dtype)
        later = jnp.concatenate([table[:, span - BLK :], table[:, : span - BLK]], 1)
        out_ref[g, 1] = (later * m_ref[1]).astype(out_ref.dtype)
        next_ref[g] = (table[:, : 2 * BLK] * m_ref[2, :, : 2 * BLK]).astype(next_ref.dtype)
        return 0

    lax.fori_loop(0, groups, one, 0)


def fill(win_ref, extra_ref, spot, *pieces):
    at = 0
    for piece in pieces:
        lanes = slice(at, at + piece.shape[1])
        win_ref[pl.ds(pl.multiple_of(spot * BLK, BLK), BLK), lanes] = piece[:BLK]
        extra_ref[spot, :, lanes] = piece[BLK:].astype(jnp.float32)
        at += piece.shape[1]


def relay_kernel(piece, seq_ref, next_ref, back_own_ref, back_pair_ref, w_ref, out_ref, win_ref, extra_ref):
    width = out_ref.shape[1]
    half = lax.axis_index("half")
    lanes = slice(piece * width, (piece + 1) * width)
    fill(win_ref, extra_ref, half, back_own_ref.at[:, lanes])
    fill(win_ref, extra_ref, 1 - half, back_pair_ref)
    marks = edge_marks(seq_ref)
    rows = first_rows(extra_ref[1, :8], extra_ref[0, :8], w_ref, marks, 3, lanes)
    put_first_rows(win_ref, BLK, rows)
    out_ref[BLK:] = extra_ref[1].astype(out_ref.dtype)
    summed = reaches_past(seq_ref, lax.axis_index("blk") + 1)

    @pl.when(summed)
    def _():
        for c in range(0, width, GROUP):
            total = jnp.dot(
                next_ref[(piece * width + c) // GROUP],
                win_ref[:, c : c + GROUP],
                preferred_element_type=jnp.float32,
            )
            out_ref[:BLK, c : c + GROUP] = total.astype(out_ref.dtype)

    @pl.when(jnp.logical_not(summed))
    def _():
        out_ref[:BLK] = win_ref[BLK:]


def gate_rows(seq_ref, raw_ref, tail, w_ref, part, q_ref, x_ref, m1_ref, m2_ref):
    width = raw_ref.shape[1]
    row_masks(seq_ref, lax.axis_index("blk") * (2 * BLK) + part * BLK, m1_ref, m2_ref)
    for c in range(0, width, GROUP):
        lanes = slice(c, c + GROUP)
        w = w_ref[0, :, lanes]
        x = raw_ref[:, lanes].astype(jnp.float32)
        slot = (c // GROUP) % 2
        x_ref[slot, 6:8, :] = tail(lanes)
        x_ref[slot, 8:, :] = x
        q_ref[:, lanes] = feature(x, x_ref.at[slot], w, m1_ref, m2_ref)


def near_kernel(
    seq_ref, table_ref, own_ref, back_own_ref, pair_a_ref, pair_b_ref, back_a_ref, back_b_ref, qkept_ref, w_ref, bias_ref,
    acc_ref, q_ref, marks_ref, win_ref, extra_ref, x_ref, m1_ref, m2_ref,
):
    groups = table_ref.shape[0]
    width = groups * GROUP
    half = lax.axis_index("half")
    block = lax.axis_index("blk")
    fill(win_ref, extra_ref, half, back_own_ref)
    fill(win_ref, extra_ref, 1 - half, back_a_ref, back_b_ref)
    fill(win_ref, extra_ref, 2 + half, own_ref)
    fill(win_ref, extra_ref, 3 - half, pair_a_ref, pair_b_ref)
    marks = edge_marks(seq_ref)
    marks_ref[0], marks_ref[1] = marks
    marks_ref[2] = jnp.full((8, GROUP), reaches_past(seq_ref, block).astype(jnp.float32))
    for spot in (1, 2, 3):
        rows = first_rows(extra_ref[spot, :8], extra_ref[spot - 1, :8], w_ref, marks, spot + 2)
        put_first_rows(win_ref, spot * BLK, rows)
    for g in range(groups):
        lanes = slice(g * GROUP, (g + 1) * GROUP)
        bias = bias_ref[:, pl.ds(pl.multiple_of(half * width + g * GROUP, GROUP), GROUP)]
        for part in range(2):
            total = jnp.dot(
                table_ref[g, part, :, 3 * BLK : (5 + part) * BLK],
                win_ref[BLK : (3 + part) * BLK, lanes],
                preferred_element_type=jnp.float32,
            )
            here = win_ref[(2 + part) * BLK : (3 + part) * BLK, lanes].astype(jnp.float32)
            acc_ref[part * BLK : (part + 1) * BLK, lanes] = total + bias * here
    gate_rows(
        seq_ref, qkept_ref, lambda lanes: extra_ref[1 + half, 8:10, lanes], w_ref, half, q_ref, x_ref, m1_ref, m2_ref
    )


def pair_gate_kernel(seq_ref, raw_ref, own_ref, back_own_ref, w_ref, q_ref, x_ref, m1_ref, m2_ref):
    half = lax.axis_index("half")

    def tail(lanes):
        back = back_own_ref[BLK:, lanes].astype(jnp.float32)
        own = own_ref[BLK:, lanes].astype(jnp.float32)
        return jnp.where(half == 1, back, own)[8:10]

    gate_rows(seq_ref, raw_ref, tail, w_ref, 1 - half, q_ref, x_ref, m1_ref, m2_ref)


def far_kernel(short, table_ref, acc_ref, qown_ref, qpair_ref, w_ref, marks_ref, *refs):
    *messages, kept_ref, sent_ref, power_ref, win_ref, extra_ref = refs
    groups = table_ref.shape[0]
    width = groups * GROUP
    half = lax.axis_index("half")
    marks = [marks_ref[0], marks_ref[1]]
    back_own_ref, back_a_ref, back_b_ref, *far_refs = messages
    low = 1 if short else 0
    fill(win_ref, extra_ref, 2 + half, back_own_ref)
    fill(win_ref, extra_ref, 3 - half, back_a_ref, back_b_ref)
    if short:
        summed = marks_ref[2, 0:1, 0:1]
        fill(win_ref, extra_ref, 1, *far_refs)
        payload = win_ref[BLK : 2 * BLK, :].astype(jnp.float32)
        win_ref[BLK : 2 * BLK, :] = (payload * (1.0 - summed)).astype(win_ref.dtype)
    else:
        fill(win_ref, extra_ref, half, far_refs[0])
        fill(win_ref, extra_ref, 1 - half, far_refs[1], far_refs[2])
        ahead = far_refs[3][...].astype(jnp.float32)[:8]
        put_first_rows(win_ref, 0, first_rows(extra_ref[0, :8], ahead, w_ref, marks, 0))
        rows = first_rows(extra_ref[1, :8], extra_ref[0, :8], w_ref, marks, 1)
        put_first_rows(win_ref, BLK, rows)
    rows = first_rows(extra_ref[2, :8], extra_ref[1, :8], w_ref, marks, 2)
    put_first_rows(win_ref, 2 * BLK, rows)
    for at, part, q_ref, out_ref in ((0, half, qown_ref, kept_ref), (BLK, 1 - half, qpair_ref, sent_ref)):
        squares = jnp.zeros((BLK, GROUP), jnp.float32)
        rows = pl.ds(pl.multiple_of(part * BLK, BLK), BLK)
        for g in range(groups):
            lanes = slice(g * GROUP, (g + 1) * GROUP)
            filtered = acc_ref[rows, lanes] + jnp.dot(
                table_ref[g, part, :, low * BLK : 3 * BLK],
                win_ref[low * BLK : 3 * BLK, lanes],
                preferred_element_type=jnp.float32,
            )
            if short:
                weight = summed * (part == 0).astype(jnp.float32)
                at_far = g * GROUP % far_refs[0].shape[1]
                far_ref = far_refs[g * GROUP // far_refs[0].shape[1]]
                filtered = filtered + weight * far_ref[:BLK, at_far : at_far + GROUP].astype(jnp.float32)
            gated = q_ref[:, lanes] * filtered
            squares = squares + gated * gated
            out_ref[:, lanes] = gated.astype(out_ref.dtype)
        power_ref[:, at : at + BLK] = lax.dot_general(
            jnp.ones((8, GROUP), jnp.float32),
            squares,
            (((1,), (1,)), ((), ())),
            precision=lax.Precision.HIGHEST,
            preferred_element_type=jnp.float32,
        )[0:1]


def norm_kernel(channels, power_ref, power_got_ref, kept_ref, got_ref, gain_ref, out_ref):
    half = lax.axis_index("half")
    width = kept_ref.shape[1]
    power = power_ref[:, :BLK] + power_got_ref[:, BLK:]
    scale = lax.rsqrt(power / channels + norm_eps)
    diagonal = lax.broadcasted_iota(jnp.int32, (BLK, BLK), 0) == lax.broadcasted_iota(
        jnp.int32, (BLK, BLK), 1
    )
    column = jnp.sum(jnp.where(diagonal, scale, 0.0), axis=1, keepdims=True)
    for which, part_ref in ((half, kept_ref), (1 - half, got_ref)):
        for c in range(0, width, GROUP):
            lanes = pl.ds(pl.multiple_of(which * width + c, GROUP), GROUP)
            out_ref[:, lanes] = (
                part_ref[:, c : c + GROUP].astype(jnp.float32) * column * gain_ref[:, lanes]
            ).astype(out_ref.dtype)


def kernel_call(body, outs, in_specs, scratch, flops, moved_bytes, vmem=24 << 20):
    return pl.pallas_call(
        body,
        out_shape=outs,
        in_specs=in_specs,
        out_specs=jax.tree.map(lambda _: VMEM, outs),
        scratch_shapes=scratch,
        compiler_params=pltpu.CompilerParams(vmem_limit_bytes=vmem),
        cost_estimate=pl.CostEstimate(flops=flops, bytes_accessed=moved_bytes, transcendentals=0),
    )


def shards(blocks, whole_tokens, channels, projected, short_weight, filter_taps, tap_blocks, skip_bias, norm_gain, seq_lengths):
    rows = projected.shape[0]
    width = projected.shape[2] // 2
    groups = width // GROUP
    taps = filter_taps.shape[1]
    shape = jax.ShapeDtypeStruct
    half_shape = shape((rows, width), jnp.bfloat16)
    half_wide = shape((rows, width), jnp.float32)

    spots = range(2 * blocks)
    to_pair = [(i, i ^ 1) for i in spots]
    ahead = [(i, (i + 2) % (2 * blocks)) for i in spots]

    panels = jnp.transpose(projected, (1, 0, 2))
    message = shape((rows + 16, width), jnp.bfloat16)
    small = shape((rows + 16, width // 2), jnp.bfloat16)
    hbm = pl.BlockSpec(memory_space=pltpu.HBM)
    pieces = 4
    row_mask = pltpu.VMEM((rows, GROUP), jnp.float32)

    kept, *sent = kernel_call(
        products_kernel,
        (message, small, small),
        [hbm] * 3,
        [
            pltpu.SMEM(seq_lengths.shape, jnp.int32),
            pltpu.VMEM((pieces, 2, rows, 2 * width // pieces), jnp.bfloat16),
            pltpu.VMEM((16, 2 * width), jnp.bfloat16),
            pltpu.VMEM(short_weight.shape, jnp.float32),
            pltpu.VMEM((4, rows + 8, GROUP), jnp.float32),
            row_mask,
            row_mask,
            pltpu.SemaphoreType.DMA((3 + pieces,)),
        ],
        40 * rows * width,
        16 * rows * width,
        60 << 20,
    )(seq_lengths, panels, short_weight)

    back_own = moved(kept, ahead)
    pair = [moved(piece, to_pair) for piece in sent]

    filter_taps, _ = lax.optimization_barrier((filter_taps, kept))
    scaled = (filter_taps * jnp.repeat(tap_blocks.astype(jnp.float32), BLK, axis=1)).astype(jnp.bfloat16)
    span = taps + 2 * BLK
    table, table_next, w_half = kernel_call(
        tables_kernel,
        (
            shape((groups, 2, BLK, span), jnp.bfloat16),
            shape((groups, BLK, 2 * BLK), jnp.bfloat16),
            shape((3, 3, width), jnp.float32),
        ),
        [SMEM, VMEM, VMEM],
        [pltpu.VMEM((2 * groups, span), jnp.float32), pltpu.VMEM((3, BLK, span), jnp.float32)],
        40 * groups * BLK * taps,
        8 * groups * BLK * taps,
    )(seq_lengths, scaled, short_weight)
    table, table_next, pair[0] = lax.optimization_barrier((table, table_next, pair[0]))
    back_pair = [moved(piece, ahead) for piece in pair]

    half = lax.axis_index("half")
    query, pair[0] = lax.optimization_barrier((panels[0], pair[0]))
    qkept = lax.dynamic_slice_in_dim(query, half * width, width, 1)
    qsent = lax.dynamic_slice_in_dim(query, (1 - half) * width, width, 1)
    qgot = moved(qsent, to_pair)

    window = pltpu.VMEM((4 * rows, width), jnp.bfloat16)
    extras = pltpu.VMEM((4, 16, width), jnp.float32)
    shifted = pltpu.VMEM((2, rows + 8, GROUP), jnp.float32)
    short = whole_tokens // 2 <= 4 * BLK
    if short:
        onward = [(i, i if i < 2 else i + 2 if i + 2 < 2 * blocks else 2 + i % 2) for i in spots]
        far = []
        for piece in range(2):
            relayed = kernel_call(
                functools.partial(relay_kernel, piece),
                small,
                [SMEM] + [VMEM] * 4,
                [pltpu.VMEM((2 * rows, width // 2), jnp.bfloat16), pltpu.VMEM((2, 16, width // 2), jnp.float32)],
                2 * rows * BLK * width,
                4 * rows * width,
            )(seq_lengths, table_next, back_own, back_pair[piece], w_half)
            far.append(moved(relayed, onward))
    else:
        across = jnp.concatenate([piece[rows:] for piece in sent], 1)
        across = moved(across, [(i, ((i ^ 1) + 6) % (2 * blocks)) for i in spots])
        straight = moved(kept[rows:], [(i, (i + 6) % (2 * blocks)) for i in spots])
        deep = jnp.where(half == 1, straight, across)
        far = [moved(piece, ahead) for piece in (back_own, *back_pair)] + [deep]

    acc, qown, marks = kernel_call(
        near_kernel,
        (shape((2 * rows, width), jnp.float32), half_wide, shape((3, 8, GROUP), jnp.float32)),
        [SMEM] + [VMEM] * 10,
        [window, extras, shifted, row_mask, row_mask],
        2 * 5 * rows * BLK * width,
        16 * rows * width,
    )(seq_lengths, table, kept, back_own, *pair, *back_pair, qkept, w_half, skip_bias.reshape(1, -1))

    qpair = kernel_call(
        pair_gate_kernel,
        half_wide,
        [SMEM] + [VMEM] * 4,
        [shifted, row_mask, row_mask],
        10 * rows * width,
        8 * rows * width,
    )(seq_lengths, qgot, kept, back_own, w_half)

    done, send, power = kernel_call(
        functools.partial(far_kernel, short),
        (half_wide, half_shape, shape((1, 2 * rows), jnp.float32)),
        [VMEM] * (9 + len(far)),
        [window, extras],
        2 * 5 * rows * BLK * width,
        24 * rows * width,
    )(table, acc, qown, qpair, w_half, marks, back_own, *back_pair, *far)

    back = moved(send, to_pair)
    peers = lax.axis_size("mp")
    shares = [lax.ppermute(power, "mp", [(i, i ^ k) for i in range(peers)]) for k in range(1, peers)]
    power = sum(shares, power)
    return kernel_call(
        functools.partial(norm_kernel, channels),
        shape((rows, 2 * width), jnp.bfloat16),
        [VMEM] * 5,
        [],
        8 * rows * width,
        10 * rows * width,
    )(power, moved(power, to_pair), done, back, norm_gain.reshape(1, -1))


def solution(mesh):
    blocks = mesh.shape["ctx"] // 2
    grid = Mesh(mesh.devices.reshape(blocks, 2, mesh.shape["mp"]), ("blk", "half", "mp"))
    in_specs = (
        P(SPOTS, None, "mp"),
        P(None, None, "mp"),
        P("mp", None),
        P("mp", None),
        P("mp"),
        P("mp"),
        P(),
    )

    def program(projected, *rest):
        body = functools.partial(shards, blocks, projected.shape[0], projected.shape[2])
        return jax.shard_map(
            body, mesh=grid, in_specs=in_specs, out_specs=P(SPOTS, "mp"), check_vma=False
        )(projected, *rest)

    return program
```

```python
import functools

import jax
import jax.numpy as jnp
from jax import lax
from jax.experimental import pallas as pl
from jax.experimental.pallas import tpu as pltpu
from jax.sharding import Mesh, PartitionSpec as P

GROUP = 128
BLK = 128
norm_eps = 1e-06

VMEM = pl.BlockSpec(memory_space=pltpu.VMEM)
SMEM = pl.BlockSpec(memory_space=pltpu.SMEM)
SPOTS = ("blk", "half")


def moved(block, pairs):
    return lax.ppermute(block, SPOTS, pairs)


def boundaries(seq_ref, t):
    def step(k, carry):
        end, first, second = carry
        end = end + seq_ref[k]
        return end, first | (t == end).astype(jnp.int32), second | (t - 1 == end).astype(jnp.int32)

    first = (t == 0).astype(jnp.int32)
    second = (t == 1).astype(jnp.int32)
    _, first, second = lax.fori_loop(0, seq_ref.shape[0], step, (jnp.int32(0), first, second), unroll=True)
    return first, first | second


def row_masks(seq_ref, start, m1_ref, m2_ref):
    rows = lax.broadcasted_iota(jnp.int32, (BLK, GROUP), 0)
    diagonal = rows == lax.broadcasted_iota(jnp.int32, (BLK, GROUP), 1)
    marks = boundaries(seq_ref, start + lax.broadcasted_iota(jnp.int32, (8, GROUP), 1))
    for mark, m_ref in zip(marks, (m1_ref, m2_ref)):
        keep = 1.0 - mark.astype(jnp.float32)[0:1]
        column = jnp.sum(jnp.where(diagonal, keep, 0.0), axis=1, keepdims=True)
        m_ref[...] = jnp.broadcast_to(column, (BLK, GROUP))


def counted(seq_ref, t):
    def step(k, carry):
        end, total = carry
        end = end + seq_ref[k]
        return end, total + (end <= t).astype(jnp.int32)

    _, total = lax.fori_loop(
        0, seq_ref.shape[0], step, (jnp.int32(0), jnp.zeros(t.shape, jnp.int32)), unroll=True
    )
    return jnp.where(t >= 0, total, -1)


def feature(x, x_ref, w, m1_ref, m2_ref):
    rows = x.shape[0]
    return (
        w[0:1] * x
        + w[1:2] * x_ref[7 : rows + 7, :] * m1_ref[...]
        + w[2:3] * x_ref[6 : rows + 6, :] * m2_ref[...]
    )


def products_kernel(seq_hbm, panels_hbm, w_hbm, kept_ref, *refs):
    *sent_refs, seq_ref, kv_ref, q_ref, w_ref, x_ref, m1_ref, m2_ref, sems = refs
    width = kept_ref.shape[1]
    rows = kv_ref.shape[2]
    pieces = kv_ref.shape[0]
    piece = kv_ref.shape[3]
    half = lax.axis_index("half")
    shard = lax.axis_index("blk") * 2 + half
    keep_at = pl.multiple_of(half * width, width)
    send_at = pl.multiple_of((1 - half) * width, width)

    loads = [pltpu.make_async_copy(seq_hbm, seq_ref, sems.at[0])]
    for p in range(pieces):
        at = keep_at if p < pieces // 2 else send_at
        lanes = pl.ds(pl.multiple_of(at + (p % (pieces // 2)) * piece, piece), piece)
        loads.append(pltpu.make_async_copy(panels_hbm.at[1:3, :, lanes], kv_ref.at[p], sems.at[1 + p]))
    loads.append(pltpu.make_async_copy(w_hbm, w_ref, sems.at[1 + pieces]))
    loads.append(pltpu.make_async_copy(panels_hbm.at[0, rows - 16 :, :], q_ref, sems.at[2 + pieces]))
    for load in loads:
        load.start()
    x_ref[:, 0:8, :] = jnp.zeros((x_ref.shape[0], 8, GROUP), jnp.float32)
    loads[0].wait()
    row_masks(seq_ref, shard * rows, m1_ref, m2_ref)
    loads[1 + pieces].wait()
    loads[2 + pieces].wait()
    for p in range(pieces):
        loads[1 + p].wait()
        out_ref, at = (kept_ref, keep_at) if p < pieces // 2 else (sent_refs[p - pieces // 2], send_at)
        for c in range(0, piece, GROUP):
            base = (p % (pieces // 2)) * piece + c
            there = slice(base, base + GROUP) if p < pieces // 2 else slice(c, c + GROUP)
            lanes = pl.ds(pl.multiple_of(at + base, GROUP), GROUP)
            slot = (c // GROUP) % (x_ref.shape[0] // 2) * 2
            heads, tails, made = [], [], []
            for i in range(2):
                x = kv_ref[p, i, :, c : c + GROUP].astype(jnp.float32)
                x_ref[slot + i, 8:, :] = x
                made.append(feature(x, x_ref.at[slot + i], w_ref[1 + i, :, lanes], m1_ref, m2_ref))
                heads.append(x[0:2])
                tails.append(x[rows - 2 :])
            out_ref[:rows, there] = (made[0] * made[1]).astype(out_ref.dtype)
            tails.append(q_ref[:, lanes].astype(jnp.float32)[14:])
            extra = jnp.concatenate(heads + tails + [jnp.zeros((6, GROUP), jnp.float32)], 0)
            out_ref[rows:, there] = extra.astype(out_ref.dtype)


def edge_marks(seq_ref):
    t = (
        (lax.axis_index("blk") - 2) * (2 * BLK)
        + lax.broadcasted_iota(jnp.int32, (8, GROUP), 1) * BLK
        + lax.broadcasted_iota(jnp.int32, (8, GROUP), 0)
    )
    return [1.0 - mark.astype(jnp.float32) for mark in boundaries(seq_ref, t)]


def first_rows(now, ahead, w_ref, marks, spot, lanes=slice(None)):
    m1, m2 = [mark[:, spot : spot + 1] for mark in marks]
    top = lax.broadcasted_iota(jnp.int32, now.shape, 0) == 0
    made = []
    for i in range(2):
        x0 = pltpu.roll(now, (8 - 2 * i) % 8, 0) if i else now
        x1 = jnp.where(top, pltpu.roll(ahead, 3 - 2 * i, 0), pltpu.roll(now, (9 - 2 * i) % 8, 0))
        x2 = pltpu.roll(ahead, 4 - 2 * i, 0)
        w = w_ref[1 + i, :, lanes]
        made.append(w[0:1] * x0 + w[1:2] * x1 * m1 + w[2:3] * x2 * m2)
    return made[0] * made[1]


def put_first_rows(win_ref, at, rows):
    old = win_ref[at : at + 16, :].astype(jnp.float32)
    new = jnp.concatenate([rows, rows], 0)
    first = lax.broadcasted_iota(jnp.int32, old.shape, 0) < 2
    win_ref[at : at + 16, :] = jnp.where(first, new, old).astype(win_ref.dtype)


def reaches_past(seq_ref, block):
    first = block * (2 * BLK)

    def step(k, carry):
        end, start = carry
        end = end + seq_ref[k]
        return end, jnp.where(end <= first, end, start)

    _, start = lax.fori_loop(0, seq_ref.shape[0], step, (jnp.int32(0), jnp.int32(0)), unroll=True)
    return first - 2 * BLK - start > BLK


def tables_kernel(seq_ref, taps_ref, w_ref, out_ref, next_ref, w_half_ref, rev_ref, m_ref):
    groups = out_ref.shape[0]
    taps = taps_ref.shape[1]
    span = out_ref.shape[3]
    half = lax.axis_index("half")
    start = lax.axis_index("blk") * (2 * BLK)
    width = w_half_ref.shape[2]
    w_half_ref[...] = w_ref[:, :, pl.ds(pl.multiple_of(half * width, width), width)]
    turn = lax.broadcasted_iota(jnp.int32, (taps, span), 0) + lax.broadcasted_iota(
        jnp.int32, (taps, span), 1
    )
    turn = (turn == taps).astype(jnp.bfloat16)
    rev_ref[...] = jnp.dot(taps_ref[...], turn, preferred_element_type=jnp.float32)
    seg_in = counted(seq_ref, start - taps + lax.broadcasted_iota(jnp.int32, (8, span), 1))[0:1]
    for part in range(3):
        t_out = start + part * BLK + lax.broadcasted_iota(jnp.int32, (BLK, GROUP), 0)
        seg_out = counted(seq_ref, t_out)[:, 0:1]
        if part < 2:
            m_ref[part] = (seg_in == seg_out).astype(jnp.float32)
        else:
            m_ref[2, :, : 2 * BLK] = (seg_in[:, 2 * BLK : 4 * BLK] == seg_out).astype(jnp.float32)

    def one(g, _):
        row = rev_ref[pl.ds(half * groups + g, 1), :]
        table = pltpu.roll(jnp.broadcast_to(row, (BLK, span)), 0, 1, stride=1, stride_axis=0)
        out_ref[g, 0] = (table * m_ref[0]).astype(out_ref.dtype)
        later = jnp.concatenate([table[:, span - BLK :], table[:, : span - BLK]], 1)
        out_ref[g, 1] = (later * m_ref[1]).astype(out_ref.dtype)
        next_ref[g] = (table[:, : 2 * BLK] * m_ref[2, :, : 2 * BLK]).astype(next_ref.dtype)
        return 0

    lax.fori_loop(0, groups, one, 0)


def fill(win_ref, extra_ref, spot, *pieces):
    at = 0
    for piece in pieces:
        lanes = slice(at, at + piece.shape[1])
        win_ref[pl.ds(pl.multiple_of(spot * BLK, BLK), BLK), lanes] = piece[:BLK]
        extra_ref[spot, :, lanes] = piece[BLK:].astype(jnp.float32)
        at += piece.shape[1]


def relay_kernel(piece, seq_ref, next_ref, back_own_ref, back_pair_ref, w_ref, out_ref, win_ref, extra_ref):
    width = out_ref.shape[1]
    half = lax.axis_index("half")
    lanes = slice(piece * width, (piece + 1) * width)
    fill(win_ref, extra_ref, half, back_own_ref.at[:, lanes])
    fill(win_ref, extra_ref, 1 - half, back_pair_ref)
    marks = edge_marks(seq_ref)
    rows = first_rows(extra_ref[1, :8], extra_ref[0, :8], w_ref, marks, 3, lanes)
    put_first_rows(win_ref, BLK, rows)
    out_ref[BLK:] = extra_ref[1].astype(out_ref.dtype)
    summed = reaches_past(seq_ref, lax.axis_index("blk") + 1)

    @pl.when(summed)
    def _():
        for c in range(0, width, GROUP):
            total = jnp.dot(
                next_ref[(piece * width + c) // GROUP],
                win_ref[:, c : c + GROUP],
                preferred_element_type=jnp.float32,
            )
            out_ref[:BLK, c : c + GROUP] = total.astype(out_ref.dtype)

    @pl.when(jnp.logical_not(summed))
    def _():
        out_ref[:BLK] = win_ref[BLK:]


def gate_rows(seq_ref, raw_ref, tail, w_ref, part, q_ref, x_ref, m1_ref, m2_ref):
    width = raw_ref.shape[1]
    row_masks(seq_ref, lax.axis_index("blk") * (2 * BLK) + part * BLK, m1_ref, m2_ref)
    for c in range(0, width, GROUP):
        lanes = slice(c, c + GROUP)
        w = w_ref[0, :, lanes]
        x = raw_ref[:, lanes].astype(jnp.float32)
        slot = (c // GROUP) % 2
        x_ref[slot, 6:8, :] = tail(lanes)
        x_ref[slot, 8:, :] = x
        q_ref[:, lanes] = feature(x, x_ref.at[slot], w, m1_ref, m2_ref)


def near_kernel(
    seq_ref, table_ref, own_ref, back_own_ref, pair_a_ref, pair_b_ref, back_a_ref, back_b_ref, qkept_ref, w_ref, bias_ref,
    acc_ref, q_ref, marks_ref, win_ref, extra_ref, x_ref, m1_ref, m2_ref,
):
    groups = table_ref.shape[0]
    width = groups * GROUP
    half = lax.axis_index("half")
    block = lax.axis_index("blk")
    fill(win_ref, extra_ref, half, back_own_ref)
    fill(win_ref, extra_ref, 1 - half, back_a_ref, back_b_ref)
    fill(win_ref, extra_ref, 2 + half, own_ref)
    fill(win_ref, extra_ref, 3 - half, pair_a_ref, pair_b_ref)
    marks = edge_marks(seq_ref)
    marks_ref[0], marks_ref[1] = marks
    marks_ref[2] = jnp.full((8, GROUP), reaches_past(seq_ref, block).astype(jnp.float32))
    for spot in (1, 2, 3):
        rows = first_rows(extra_ref[spot, :8], extra_ref[spot - 1, :8], w_ref, marks, spot + 2)
        put_first_rows(win_ref, spot * BLK, rows)
    for g in range(groups):
        lanes = slice(g * GROUP, (g + 1) * GROUP)
        bias = bias_ref[:, pl.ds(pl.multiple_of(half * width + g * GROUP, GROUP), GROUP)]
        for part in range(2):
            total = jnp.dot(
                table_ref[g, part, :, 3 * BLK : (5 + part) * BLK],
                win_ref[BLK : (3 + part) * BLK, lanes],
                preferred_element_type=jnp.float32,
            )
            here = win_ref[(2 + part) * BLK : (3 + part) * BLK, lanes].astype(jnp.float32)
            acc_ref[part * BLK : (part + 1) * BLK, lanes] = total + bias * here
    gate_rows(
        seq_ref, qkept_ref, lambda lanes: extra_ref[1 + half, 8:10, lanes], w_ref, half, q_ref, x_ref, m1_ref, m2_ref
    )


def pair_gate_kernel(seq_ref, raw_ref, own_ref, back_own_ref, w_ref, q_ref, x_ref, m1_ref, m2_ref):
    half = lax.axis_index("half")

    def tail(lanes):
        back = back_own_ref[BLK:, lanes].astype(jnp.float32)
        own = own_ref[BLK:, lanes].astype(jnp.float32)
        return jnp.where(half == 1, back, own)[8:10]

    gate_rows(seq_ref, raw_ref, tail, w_ref, 1 - half, q_ref, x_ref, m1_ref, m2_ref)


def far_kernel(short, table_ref, acc_ref, qown_ref, qpair_ref, w_ref, marks_ref, *refs):
    *messages, kept_ref, sent_ref, power_ref, win_ref, extra_ref = refs
    groups = table_ref.shape[0]
    width = groups * GROUP
    half = lax.axis_index("half")
    marks = [marks_ref[0], marks_ref[1]]
    back_own_ref, back_a_ref, back_b_ref, *far_refs = messages
    low = 1 if short else 0
    fill(win_ref, extra_ref, 2 + half, back_own_ref)
    fill(win_ref, extra_ref, 3 - half, back_a_ref, back_b_ref)
    if short:
        summed = marks_ref[2, 0:1, 0:1]
        fill(win_ref, extra_ref, 1, *far_refs)
        payload = win_ref[BLK : 2 * BLK, :].astype(jnp.float32)
        win_ref[BLK : 2 * BLK, :] = (payload * (1.0 - summed)).astype(win_ref.dtype)
    else:
        fill(win_ref, extra_ref, half, far_refs[0])
        fill(win_ref, extra_ref, 1 - half, far_refs[1], far_refs[2])
        ahead = far_refs[3][...].astype(jnp.float32)[:8]
        put_first_rows(win_ref, 0, first_rows(extra_ref[0, :8], ahead, w_ref, marks, 0))
        rows = first_rows(extra_ref[1, :8], extra_ref[0, :8], w_ref, marks, 1)
        put_first_rows(win_ref, BLK, rows)
    rows = first_rows(extra_ref[2, :8], extra_ref[1, :8], w_ref, marks, 2)
    put_first_rows(win_ref, 2 * BLK, rows)
    for at, part, q_ref, out_ref in ((0, half, qown_ref, kept_ref), (BLK, 1 - half, qpair_ref, sent_ref)):
        squares = jnp.zeros((BLK, GROUP), jnp.float32)
        rows = pl.ds(pl.multiple_of(part * BLK, BLK), BLK)
        for g in range(groups):
            lanes = slice(g * GROUP, (g + 1) * GROUP)
            filtered = acc_ref[rows, lanes] + jnp.dot(
                table_ref[g, part, :, low * BLK : 3 * BLK],
                win_ref[low * BLK : 3 * BLK, lanes],
                preferred_element_type=jnp.float32,
            )
            if short:
                weight = summed * (part == 0).astype(jnp.float32)
                at_far = g * GROUP % far_refs[0].shape[1]
                far_ref = far_refs[g * GROUP // far_refs[0].shape[1]]
                filtered = filtered + weight * far_ref[:BLK, at_far : at_far + GROUP].astype(jnp.float32)
            gated = q_ref[:, lanes] * filtered
            squares = squares + gated * gated
            out_ref[:, lanes] = gated.astype(out_ref.dtype)
        power_ref[:, at : at + BLK] = lax.dot_general(
            jnp.ones((8, GROUP), jnp.float32),
            squares,
            (((1,), (1,)), ((), ())),
            precision=lax.Precision.HIGHEST,
            preferred_element_type=jnp.float32,
        )[0:1]


def norm_kernel(channels, power_ref, power_got_ref, kept_ref, got_ref, gain_ref, out_ref):
    half = lax.axis_index("half")
    width = kept_ref.shape[1]
    power = power_ref[:, :BLK] + power_got_ref[:, BLK:]
    scale = lax.rsqrt(power / channels + norm_eps)
    diagonal = lax.broadcasted_iota(jnp.int32, (BLK, BLK), 0) == lax.broadcasted_iota(
        jnp.int32, (BLK, BLK), 1
    )
    column = jnp.sum(jnp.where(diagonal, scale, 0.0), axis=1, keepdims=True)
    for which, part_ref in ((half, kept_ref), (1 - half, got_ref)):
        for c in range(0, width, GROUP):
            lanes = pl.ds(pl.multiple_of(which * width + c, GROUP), GROUP)
            out_ref[:, lanes] = (
                part_ref[:, c : c + GROUP].astype(jnp.float32) * column * gain_ref[:, lanes]
            ).astype(out_ref.dtype)


def kernel_call(body, outs, in_specs, scratch, flops, moved_bytes, vmem=24 << 20):
    return pl.pallas_call(
        body,
        out_shape=outs,
        in_specs=in_specs,
        out_specs=jax.tree.map(lambda _: VMEM, outs),
        scratch_shapes=scratch,
        compiler_params=pltpu.CompilerParams(vmem_limit_bytes=vmem),
        cost_estimate=pl.CostEstimate(flops=flops, bytes_accessed=moved_bytes, transcendentals=0),
    )


def shards(blocks, whole_tokens, channels, projected, short_weight, filter_taps, tap_blocks, skip_bias, norm_gain, seq_lengths):
    rows = projected.shape[0]
    width = projected.shape[2] // 2
    groups = width // GROUP
    taps = filter_taps.shape[1]
    shape = jax.ShapeDtypeStruct
    half_shape = shape((rows, width), jnp.bfloat16)
    half_wide = shape((rows, width), jnp.float32)

    spots = range(2 * blocks)
    to_pair = [(i, i ^ 1) for i in spots]
    ahead = [(i, (i + 2) % (2 * blocks)) for i in spots]

    panels = jnp.transpose(projected, (1, 0, 2))
    message = shape((rows + 16, width), jnp.bfloat16)
    small = shape((rows + 16, width // 2), jnp.bfloat16)
    hbm = pl.BlockSpec(memory_space=pltpu.HBM)
    pieces = 4
    row_mask = pltpu.VMEM((rows, GROUP), jnp.float32)

    kept, *sent = kernel_call(
        products_kernel,
        (message, small, small),
        [hbm] * 3,
        [
            pltpu.SMEM(seq_lengths.shape, jnp.int32),
            pltpu.VMEM((pieces, 2, rows, 2 * width // pieces), jnp.bfloat16),
            pltpu.VMEM((16, 2 * width), jnp.bfloat16),
            pltpu.VMEM(short_weight.shape, jnp.float32),
            pltpu.VMEM((4, rows + 8, GROUP), jnp.float32),
            row_mask,
            row_mask,
            pltpu.SemaphoreType.DMA((3 + pieces,)),
        ],
        40 * rows * width,
        16 * rows * width,
        60 << 20,
    )(seq_lengths, panels, short_weight)

    back_own = moved(kept, ahead)
    pair = [moved(piece, to_pair) for piece in sent]

    filter_taps, _ = lax.optimization_barrier((filter_taps, kept))
    scaled = (filter_taps * jnp.repeat(tap_blocks.astype(jnp.float32), BLK, axis=1)).astype(jnp.bfloat16)
    scaled, pair[0] = lax.optimization_barrier((scaled, pair[0]))
    span = taps + 2 * BLK
    table, table_next, w_half = kernel_call(
        tables_kernel,
        (
            shape((groups, 2, BLK, span), jnp.bfloat16),
            shape((groups, BLK, 2 * BLK), jnp.bfloat16),
            shape((3, 3, width), jnp.float32),
        ),
        [SMEM, VMEM, VMEM],
        [pltpu.VMEM((2 * groups, span), jnp.float32), pltpu.VMEM((3, BLK, span), jnp.float32)],
        40 * groups * BLK * taps,
        8 * groups * BLK * taps,
    )(seq_lengths, scaled, short_weight)
    table, table_next, pair[1] = lax.optimization_barrier((table, table_next, pair[1]))
    back_pair = [moved(piece, ahead) for piece in pair]

    half = lax.axis_index("half")
    query, pair[1] = lax.optimization_barrier((panels, pair[1]))
    qkept = lax.dynamic_slice(query, (0, 0, half * width), (1, rows, width))[0]
    qsent = lax.dynamic_slice(query, (0, 0, (1 - half) * width), (1, rows, width))[0]
    qgot = moved(qsent, to_pair)

    window = pltpu.VMEM((4 * rows, width), jnp.bfloat16)
    extras = pltpu.VMEM((4, 16, width), jnp.float32)
    shifted = pltpu.VMEM((2, rows + 8, GROUP), jnp.float32)
    short = whole_tokens // 2 <= 4 * BLK
    if short:
        far = []
        for piece in range(2):
            relayed = kernel_call(
                functools.partial(relay_kernel, piece),
                small,
                [SMEM] + [VMEM] * 4,
                [pltpu.VMEM((2 * rows, width // 2), jnp.bfloat16), pltpu.VMEM((2, 16, width // 2), jnp.float32)],
                2 * rows * BLK * width,
                4 * rows * width,
            )(seq_lengths, table_next, back_own, back_pair[piece], w_half)
            far.append(moved(relayed, ahead))
    else:
        across = jnp.concatenate([piece[rows:] for piece in sent], 1)
        across = moved(across, [(i, ((i ^ 1) + 6) % (2 * blocks)) for i in spots])
        straight = moved(kept[rows:], [(i, (i + 6) % (2 * blocks)) for i in spots])
        deep = jnp.where(half == 1, straight, across)
        far = [moved(piece, ahead) for piece in (back_own, *back_pair)] + [deep]

    acc, qown, marks = kernel_call(
        near_kernel,
        (shape((2 * rows, width), jnp.float32), half_wide, shape((3, 8, GROUP), jnp.float32)),
        [SMEM] + [VMEM] * 10,
        [window, extras, shifted, row_mask, row_mask],
        2 * 5 * rows * BLK * width,
        16 * rows * width,
    )(seq_lengths, table, kept, back_own, *pair, *back_pair, qkept, w_half, skip_bias.reshape(1, -1))

    qpair = kernel_call(
        pair_gate_kernel,
        half_wide,
        [SMEM] + [VMEM] * 4,
        [shifted, row_mask, row_mask],
        10 * rows * width,
        8 * rows * width,
    )(seq_lengths, qgot, kept, back_own, w_half)

    done, send, power = kernel_call(
        functools.partial(far_kernel, short),
        (half_wide, half_shape, shape((1, 2 * rows), jnp.float32)),
        [VMEM] * (9 + len(far)),
        [window, extras],
        2 * 5 * rows * BLK * width,
        24 * rows * width,
    )(table, acc, qown, qpair, w_half, marks, back_own, *back_pair, *far)

    back = moved(send, to_pair)
    peers = lax.axis_size("mp")
    shares = [lax.ppermute(power, "mp", [(i, i ^ k) for i in range(peers)]) for k in range(1, peers)]
    power = sum(shares, power)
    return kernel_call(
        functools.partial(norm_kernel, channels),
        shape((rows, 2 * width), jnp.bfloat16),
        [VMEM] * 5,
        [],
        8 * rows * width,
        10 * rows * width,
    )(power, moved(power, to_pair), done, back, norm_gain.reshape(1, -1))


def solution(mesh):
    blocks = mesh.shape["ctx"] // 2
    grid = Mesh(mesh.devices.reshape(blocks, 2, mesh.shape["mp"]), ("blk", "half", "mp"))
    in_specs = (
        P(SPOTS, None, "mp"),
        P(None, None, "mp"),
        P("mp", None),
        P("mp", None),
        P("mp"),
        P("mp"),
        P(),
    )

    def program(projected, *rest):
        body = functools.partial(shards, blocks, projected.shape[0], projected.shape[2])
        return jax.shard_map(
            body, mesh=grid, in_specs=in_specs, out_specs=P(SPOTS, "mp"), check_vma=False
        )(projected, *rest)

    return program
```

```python
import functools

import jax
import jax.numpy as jnp
from jax import lax
from jax.experimental import pallas as pl
from jax.experimental.pallas import tpu as pltpu
from jax.sharding import Mesh, PartitionSpec as P

GROUP = 128
BLK = 128
norm_eps = 1e-06

VMEM = pl.BlockSpec(memory_space=pltpu.VMEM)
SMEM = pl.BlockSpec(memory_space=pltpu.SMEM)
SPOTS = ("blk", "half")


def moved(block, pairs):
    return lax.ppermute(block, SPOTS, pairs)


def boundaries(seq_ref, t):
    def step(k, carry):
        end, first, second = carry
        end = end + seq_ref[k]
        return end, first | (t == end).astype(jnp.int32), second | (t - 1 == end).astype(jnp.int32)

    first = (t == 0).astype(jnp.int32)
    second = (t == 1).astype(jnp.int32)
    _, first, second = lax.fori_loop(0, seq_ref.shape[0], step, (jnp.int32(0), first, second), unroll=True)
    return first, first | second


def row_masks(seq_ref, start, m1_ref, m2_ref):
    rows = lax.broadcasted_iota(jnp.int32, (BLK, GROUP), 0)
    diagonal = rows == lax.broadcasted_iota(jnp.int32, (BLK, GROUP), 1)
    marks = boundaries(seq_ref, start + lax.broadcasted_iota(jnp.int32, (8, GROUP), 1))
    for mark, m_ref in zip(marks, (m1_ref, m2_ref)):
        keep = 1.0 - mark.astype(jnp.float32)[0:1]
        column = jnp.sum(jnp.where(diagonal, keep, 0.0), axis=1, keepdims=True)
        m_ref[...] = jnp.broadcast_to(column, (BLK, GROUP))


def counted(seq_ref, t):
    def step(k, carry):
        end, total = carry
        end = end + seq_ref[k]
        return end, total + (end <= t).astype(jnp.int32)

    _, total = lax.fori_loop(
        0, seq_ref.shape[0], step, (jnp.int32(0), jnp.zeros(t.shape, jnp.int32)), unroll=True
    )
    return jnp.where(t >= 0, total, -1)


def feature(x, x_ref, w, m1_ref, m2_ref):
    rows = x.shape[0]
    return (
        w[0:1] * x
        + w[1:2] * x_ref[7 : rows + 7, :] * m1_ref[...]
        + w[2:3] * x_ref[6 : rows + 6, :] * m2_ref[...]
    )


def products_kernel(seq_hbm, panels_hbm, w_hbm, kept_ref, *refs):
    *sent_refs, seq_ref, kv_ref, q_ref, w_ref, x_ref, m1_ref, m2_ref, sems = refs
    width = kept_ref.shape[1]
    rows = kv_ref.shape[2]
    pieces = kv_ref.shape[0]
    piece = kv_ref.shape[3]
    half = lax.axis_index("half")
    shard = lax.axis_index("blk") * 2 + half
    keep_at = pl.multiple_of(half * width, width)
    send_at = pl.multiple_of((1 - half) * width, width)

    loads = [pltpu.make_async_copy(seq_hbm, seq_ref, sems.at[0])]
    for p in range(pieces):
        at = keep_at if p < pieces // 2 else send_at
        lanes = pl.ds(pl.multiple_of(at + (p % (pieces // 2)) * piece, piece), piece)
        loads.append(pltpu.make_async_copy(panels_hbm.at[1:3, :, lanes], kv_ref.at[p], sems.at[1 + p]))
    loads.append(pltpu.make_async_copy(w_hbm, w_ref, sems.at[1 + pieces]))
    loads.append(pltpu.make_async_copy(panels_hbm.at[0, rows - 16 :, :], q_ref, sems.at[2 + pieces]))
    for load in loads:
        load.start()
    x_ref[:, 0:8, :] = jnp.zeros((x_ref.shape[0], 8, GROUP), jnp.float32)
    loads[0].wait()
    row_masks(seq_ref, shard * rows, m1_ref, m2_ref)
    loads[1 + pieces].wait()
    loads[2 + pieces].wait()
    for p in range(pieces):
        loads[1 + p].wait()
        out_ref, at = (kept_ref, keep_at) if p < pieces // 2 else (sent_refs[p - pieces // 2], send_at)
        for c in range(0, piece, GROUP):
            base = (p % (pieces // 2)) * piece + c
            there = slice(base, base + GROUP) if p < pieces // 2 else slice(c, c + GROUP)
            lanes = pl.ds(pl.multiple_of(at + base, GROUP), GROUP)
            slot = (c // GROUP) % (x_ref.shape[0] // 2) * 2
            heads, tails, made = [], [], []
            for i in range(2):
                x = kv_ref[p, i, :, c : c + GROUP].astype(jnp.float32)
                x_ref[slot + i, 8:, :] = x
                made.append(feature(x, x_ref.at[slot + i], w_ref[1 + i, :, lanes], m1_ref, m2_ref))
                heads.append(x[0:2])
                tails.append(x[rows - 2 :])
            out_ref[:rows, there] = (made[0] * made[1]).astype(out_ref.dtype)
            tails.append(q_ref[:, lanes].astype(jnp.float32)[14:])
            extra = jnp.concatenate(heads + tails + [jnp.zeros((6, GROUP), jnp.float32)], 0)
            out_ref[rows:, there] = extra.astype(out_ref.dtype)


def edge_marks(seq_ref):
    t = (
        (lax.axis_index("blk") - 2) * (2 * BLK)
        + lax.broadcasted_iota(jnp.int32, (8, GROUP), 1) * BLK
        + lax.broadcasted_iota(jnp.int32, (8, GROUP), 0)
    )
    return [1.0 - mark.astype(jnp.float32) for mark in boundaries(seq_ref, t)]


def first_rows(now, ahead, w_ref, marks, spot, lanes=slice(None)):
    m1, m2 = [mark[:, spot : spot + 1] for mark in marks]
    top = lax.broadcasted_iota(jnp.int32, now.shape, 0) == 0
    made = []
    for i in range(2):
        x0 = pltpu.roll(now, (8 - 2 * i) % 8, 0) if i else now
        x1 = jnp.where(top, pltpu.roll(ahead, 3 - 2 * i, 0), pltpu.roll(now, (9 - 2 * i) % 8, 0))
        x2 = pltpu.roll(ahead, 4 - 2 * i, 0)
        w = w_ref[1 + i, :, lanes]
        made.append(w[0:1] * x0 + w[1:2] * x1 * m1 + w[2:3] * x2 * m2)
    return made[0] * made[1]


def put_first_rows(win_ref, at, rows):
    old = win_ref[at : at + 16, :].astype(jnp.float32)
    new = jnp.concatenate([rows, rows], 0)
    first = lax.broadcasted_iota(jnp.int32, old.shape, 0) < 2
    win_ref[at : at + 16, :] = jnp.where(first, new, old).astype(win_ref.dtype)


def reaches_past(seq_ref, block):
    first = block * (2 * BLK)

    def step(k, carry):
        end, start = carry
        end = end + seq_ref[k]
        return end, jnp.where(end <= first, end, start)

    _, start = lax.fori_loop(0, seq_ref.shape[0], step, (jnp.int32(0), jnp.int32(0)), unroll=True)
    return first - 2 * BLK - start > BLK


def tables_kernel(seq_ref, taps_ref, w_ref, out_ref, next_ref, w_half_ref, rev_ref, m_ref):
    groups = out_ref.shape[0]
    taps = taps_ref.shape[1]
    span = out_ref.shape[3]
    half = lax.axis_index("half")
    start = lax.axis_index("blk") * (2 * BLK)
    width = w_half_ref.shape[2]
    w_half_ref[...] = w_ref[:, :, pl.ds(pl.multiple_of(half * width, width), width)]
    turn = lax.broadcasted_iota(jnp.int32, (taps, span), 0) + lax.broadcasted_iota(
        jnp.int32, (taps, span), 1
    )
    turn = (turn == taps).astype(jnp.bfloat16)
    rev_ref[...] = jnp.dot(taps_ref[...], turn, preferred_element_type=jnp.float32)
    seg_in = counted(seq_ref, start - taps + lax.broadcasted_iota(jnp.int32, (8, span), 1))[0:1]
    for part in range(3):
        t_out = start + part * BLK + lax.broadcasted_iota(jnp.int32, (BLK, GROUP), 0)
        seg_out = counted(seq_ref, t_out)[:, 0:1]
        if part < 2:
            m_ref[part] = (seg_in == seg_out).astype(jnp.float32)
        else:
            m_ref[2, :, : 2 * BLK] = (seg_in[:, 2 * BLK : 4 * BLK] == seg_out).astype(jnp.float32)

    def one(g, _):
        row = rev_ref[pl.ds(half * groups + g, 1), :]
        table = pltpu.roll(jnp.broadcast_to(row, (BLK, span)), 0, 1, stride=1, stride_axis=0)
        out_ref[g, 0] = (table * m_ref[0]).astype(out_ref.dtype)
        later = jnp.concatenate([table[:, span - BLK :], table[:, : span - BLK]], 1)
        out_ref[g, 1] = (later * m_ref[1]).astype(out_ref.dtype)
        next_ref[g] = (table[:, : 2 * BLK] * m_ref[2, :, : 2 * BLK]).astype(next_ref.dtype)
        return 0

    lax.fori_loop(0, groups, one, 0)


def fill(win_ref, extra_ref, spot, *pieces):
    at = 0
    for piece in pieces:
        lanes = slice(at, at + piece.shape[1])
        win_ref[pl.ds(pl.multiple_of(spot * BLK, BLK), BLK), lanes] = piece[:BLK]
        extra_ref[spot, :, lanes] = piece[BLK:].astype(jnp.float32)
        at += piece.shape[1]


def relay_kernel(piece, seq_ref, next_ref, back_own_ref, back_pair_ref, w_ref, out_ref, win_ref, extra_ref):
    width = out_ref.shape[1]
    half = lax.axis_index("half")
    lanes = slice(piece * width, (piece + 1) * width)
    fill(win_ref, extra_ref, half, back_own_ref.at[:, lanes])
    fill(win_ref, extra_ref, 1 - half, back_pair_ref)
    marks = edge_marks(seq_ref)
    rows = first_rows(extra_ref[1, :8], extra_ref[0, :8], w_ref, marks, 3, lanes)
    put_first_rows(win_ref, BLK, rows)
    out_ref[BLK:] = extra_ref[1].astype(out_ref.dtype)
    summed = reaches_past(seq_ref, lax.axis_index("blk") + 1)

    @pl.when(summed)
    def _():
        for c in range(0, width, GROUP):
            total = jnp.dot(
                next_ref[(piece * width + c) // GROUP],
                win_ref[:, c : c + GROUP],
                preferred_element_type=jnp.float32,
            )
            out_ref[:BLK, c : c + GROUP] = total.astype(out_ref.dtype)

    @pl.when(jnp.logical_not(summed))
    def _():
        out_ref[:BLK] = win_ref[BLK:]


def gate_rows(seq_ref, raw_ref, tail, w_ref, part, q_ref, x_ref, m1_ref, m2_ref):
    width = raw_ref.shape[1]
    row_masks(seq_ref, lax.axis_index("blk") * (2 * BLK) + part * BLK, m1_ref, m2_ref)
    for c in range(0, width, GROUP):
        lanes = slice(c, c + GROUP)
        w = w_ref[0, :, lanes]
        x = raw_ref[:, lanes].astype(jnp.float32)
        slot = (c // GROUP) % 2
        x_ref[slot, 6:8, :] = tail(lanes)
        x_ref[slot, 8:, :] = x
        q_ref[:, lanes] = feature(x, x_ref.at[slot], w, m1_ref, m2_ref)


def near_kernel(
    seq_ref, table_ref, own_ref, back_own_ref, pair_a_ref, pair_b_ref, back_a_ref, back_b_ref, qkept_ref, w_ref, bias_ref,
    acc_ref, q_ref, marks_ref, win_ref, extra_ref, x_ref, m1_ref, m2_ref,
):
    groups = table_ref.shape[0]
    width = groups * GROUP
    half = lax.axis_index("half")
    block = lax.axis_index("blk")
    fill(win_ref, extra_ref, half, back_own_ref)
    fill(win_ref, extra_ref, 1 - half, back_a_ref, back_b_ref)
    fill(win_ref, extra_ref, 2 + half, own_ref)
    fill(win_ref, extra_ref, 3 - half, pair_a_ref, pair_b_ref)
    marks = edge_marks(seq_ref)
    marks_ref[0], marks_ref[1] = marks
    marks_ref[2] = jnp.full((8, GROUP), reaches_past(seq_ref, block).astype(jnp.float32))
    for spot in (1, 2, 3):
        rows = first_rows(extra_ref[spot, :8], extra_ref[spot - 1, :8], w_ref, marks, spot + 2)
        put_first_rows(win_ref, spot * BLK, rows)
    for g in range(groups):
        lanes = slice(g * GROUP, (g + 1) * GROUP)
        bias = bias_ref[:, pl.ds(pl.multiple_of(half * width + g * GROUP, GROUP), GROUP)]
        for part in range(2):
            total = jnp.dot(
                table_ref[g, part, :, 3 * BLK : (5 + part) * BLK],
                win_ref[BLK : (3 + part) * BLK, lanes],
                preferred_element_type=jnp.float32,
            )
            here = win_ref[(2 + part) * BLK : (3 + part) * BLK, lanes].astype(jnp.float32)
            acc_ref[part * BLK : (part + 1) * BLK, lanes] = total + bias * here
    gate_rows(
        seq_ref, qkept_ref, lambda lanes: extra_ref[1 + half, 8:10, lanes], w_ref, half, q_ref, x_ref, m1_ref, m2_ref
    )


def pair_gate_kernel(seq_ref, raw_ref, own_ref, back_own_ref, w_ref, q_ref, x_ref, m1_ref, m2_ref):
    half = lax.axis_index("half")

    def tail(lanes):
        back = back_own_ref[BLK:, lanes].astype(jnp.float32)
        own = own_ref[BLK:, lanes].astype(jnp.float32)
        return jnp.where(half == 1, back, own)[8:10]

    gate_rows(seq_ref, raw_ref, tail, w_ref, 1 - half, q_ref, x_ref, m1_ref, m2_ref)


def far_kernel(short, table_ref, acc_ref, qown_ref, qpair_ref, w_ref, marks_ref, *refs):
    *messages, kept_ref, sent_ref, power_ref, win_ref, extra_ref = refs
    groups = table_ref.shape[0]
    width = groups * GROUP
    half = lax.axis_index("half")
    marks = [marks_ref[0], marks_ref[1]]
    back_own_ref, back_a_ref, back_b_ref, *far_refs = messages
    low = 1 if short else 0
    fill(win_ref, extra_ref, 2 + half, back_own_ref)
    fill(win_ref, extra_ref, 3 - half, back_a_ref, back_b_ref)
    if short:
        summed = marks_ref[2, 0:1, 0:1]
        fill(win_ref, extra_ref, 1, *far_refs)
        payload = win_ref[BLK : 2 * BLK, :].astype(jnp.float32)
        win_ref[BLK : 2 * BLK, :] = (payload * (1.0 - summed)).astype(win_ref.dtype)
    else:
        fill(win_ref, extra_ref, half, far_refs[0])
        fill(win_ref, extra_ref, 1 - half, far_refs[1], far_refs[2])
        ahead = far_refs[3][...].astype(jnp.float32)[:8]
        put_first_rows(win_ref, 0, first_rows(extra_ref[0, :8], ahead, w_ref, marks, 0))
        rows = first_rows(extra_ref[1, :8], extra_ref[0, :8], w_ref, marks, 1)
        put_first_rows(win_ref, BLK, rows)
    rows = first_rows(extra_ref[2, :8], extra_ref[1, :8], w_ref, marks, 2)
    put_first_rows(win_ref, 2 * BLK, rows)
    for at, part, q_ref, out_ref in ((0, half, qown_ref, kept_ref), (BLK, 1 - half, qpair_ref, sent_ref)):
        squares = jnp.zeros((BLK, GROUP), jnp.float32)
        rows = pl.ds(pl.multiple_of(part * BLK, BLK), BLK)
        for g in range(groups):
            lanes = slice(g * GROUP, (g + 1) * GROUP)
            filtered = acc_ref[rows, lanes] + jnp.dot(
                table_ref[g, part, :, low * BLK : 3 * BLK],
                win_ref[low * BLK : 3 * BLK, lanes],
                preferred_element_type=jnp.float32,
            )
            if short:
                weight = summed * (part == 0).astype(jnp.float32)
                at_far = g * GROUP % far_refs[0].shape[1]
                far_ref = far_refs[g * GROUP // far_refs[0].shape[1]]
                filtered = filtered + weight * far_ref[:BLK, at_far : at_far + GROUP].astype(jnp.float32)
            gated = q_ref[:, lanes] * filtered
            squares = squares + gated * gated
            out_ref[:, lanes] = gated.astype(out_ref.dtype)
        power_ref[:, at : at + BLK] = lax.dot_general(
            jnp.ones((8, GROUP), jnp.float32),
            squares,
            (((1,), (1,)), ((), ())),
            precision=lax.Precision.HIGHEST,
            preferred_element_type=jnp.float32,
        )[0:1]


def norm_kernel(channels, power_ref, power_got_ref, kept_ref, got_ref, gain_ref, out_ref):
    half = lax.axis_index("half")
    width = kept_ref.shape[1]
    power = power_ref[:, :BLK] + power_got_ref[:, BLK:]
    scale = lax.rsqrt(power / channels + norm_eps)
    diagonal = lax.broadcasted_iota(jnp.int32, (BLK, BLK), 0) == lax.broadcasted_iota(
        jnp.int32, (BLK, BLK), 1
    )
    column = jnp.sum(jnp.where(diagonal, scale, 0.0), axis=1, keepdims=True)
    for which, part_ref in ((half, kept_ref), (1 - half, got_ref)):
        for c in range(0, width, GROUP):
            lanes = pl.ds(pl.multiple_of(which * width + c, GROUP), GROUP)
            out_ref[:, lanes] = (
                part_ref[:, c : c + GROUP].astype(jnp.float32) * column * gain_ref[:, lanes]
            ).astype(out_ref.dtype)


def kernel_call(body, outs, in_specs, scratch, flops, moved_bytes, vmem=24 << 20):
    return pl.pallas_call(
        body,
        out_shape=outs,
        in_specs=in_specs,
        out_specs=jax.tree.map(lambda _: VMEM, outs),
        scratch_shapes=scratch,
        compiler_params=pltpu.CompilerParams(vmem_limit_bytes=vmem),
        cost_estimate=pl.CostEstimate(flops=flops, bytes_accessed=moved_bytes, transcendentals=0),
    )


def shards(blocks, whole_tokens, channels, projected, short_weight, filter_taps, tap_blocks, skip_bias, norm_gain, seq_lengths):
    rows = projected.shape[0]
    width = projected.shape[2] // 2
    groups = width // GROUP
    taps = filter_taps.shape[1]
    shape = jax.ShapeDtypeStruct
    half_shape = shape((rows, width), jnp.bfloat16)
    half_wide = shape((rows, width), jnp.float32)

    spots = range(2 * blocks)
    to_pair = [(i, i ^ 1) for i in spots]
    ahead = [(i, (i + 2) % (2 * blocks)) for i in spots]

    panels = jnp.transpose(projected, (1, 0, 2))
    message = shape((rows + 16, width), jnp.bfloat16)
    small = shape((rows + 16, width // 2), jnp.bfloat16)
    hbm = pl.BlockSpec(memory_space=pltpu.HBM)
    pieces = 4
    row_mask = pltpu.VMEM((rows, GROUP), jnp.float32)

    kept, *sent = kernel_call(
        products_kernel,
        (message, small, small),
        [hbm] * 3,
        [
            pltpu.SMEM(seq_lengths.shape, jnp.int32),
            pltpu.VMEM((pieces, 2, rows, 2 * width // pieces), jnp.bfloat16),
            pltpu.VMEM((16, 2 * width), jnp.bfloat16),
            pltpu.VMEM(short_weight.shape, jnp.float32),
            pltpu.VMEM((4, rows + 8, GROUP), jnp.float32),
            row_mask,
            row_mask,
            pltpu.SemaphoreType.DMA((3 + pieces,)),
        ],
        40 * rows * width,
        16 * rows * width,
        60 << 20,
    )(seq_lengths, panels, short_weight)

    back_own = moved(kept, ahead)
    pair = [moved(piece, to_pair) for piece in sent]

    filter_taps, _ = lax.optimization_barrier((filter_taps, kept))
    scaled = (filter_taps * jnp.repeat(tap_blocks.astype(jnp.float32), BLK, axis=1)).astype(jnp.bfloat16)
    span = taps + 2 * BLK
    table, table_next, w_half = kernel_call(
        tables_kernel,
        (
            shape((groups, 2, BLK, span), jnp.bfloat16),
            shape((groups, BLK, 2 * BLK), jnp.bfloat16),
            shape((3, 3, width), jnp.float32),
        ),
        [SMEM, VMEM, VMEM],
        [pltpu.VMEM((2 * groups, span), jnp.float32), pltpu.VMEM((3, BLK, span), jnp.float32)],
        40 * groups * BLK * taps,
        8 * groups * BLK * taps,
    )(seq_lengths, scaled, short_weight)
    table, table_next, pair[0] = lax.optimization_barrier((table, table_next, pair[0]))

    half = lax.axis_index("half")
    query, _ = lax.optimization_barrier((panels, pair[0]))
    qkept = lax.dynamic_slice(query, (0, 0, half * width), (1, rows, width))[0]
    qsent = lax.dynamic_slice(query, (0, 0, (1 - half) * width), (1, rows, width))[0]
    qkept, qsent, pair[1] = lax.optimization_barrier((qkept, qsent, pair[1]))
    qgot = moved(qsent, to_pair)
    back_pair = [moved(piece, ahead) for piece in pair]

    window = pltpu.VMEM((4 * rows, width), jnp.bfloat16)
    extras = pltpu.VMEM((4, 16, width), jnp.float32)
    shifted = pltpu.VMEM((2, rows + 8, GROUP), jnp.float32)
    short = whole_tokens // 2 <= 4 * BLK
    if short:
        onward = [(i, i ^ 1 if i < 2 else i + 2 if i + 2 < 2 * blocks else 2 + i % 2) for i in spots]
        far = []
        for piece in range(2):
            relayed = kernel_call(
                functools.partial(relay_kernel, piece),
                small,
                [SMEM] + [VMEM] * 4,
                [pltpu.VMEM((2 * rows, width // 2), jnp.bfloat16), pltpu.VMEM((2, 16, width // 2), jnp.float32)],
                2 * rows * BLK * width,
                4 * rows * width,
            )(seq_lengths, table_next, back_own, back_pair[piece], w_half)
            far.append(moved(relayed, onward))
    else:
        across = jnp.concatenate([piece[rows:] for piece in sent], 1)
        across = moved(across, [(i, ((i ^ 1) + 6) % (2 * blocks)) for i in spots])
        straight = moved(kept[rows:], [(i, (i + 6) % (2 * blocks)) for i in spots])
        deep = jnp.where(half == 1, straight, across)
        far = [moved(piece, ahead) for piece in (back_own, *back_pair)] + [deep]

    acc, qown, marks = kernel_call(
        near_kernel,
        (shape((2 * rows, width), jnp.float32), half_wide, shape((3, 8, GROUP), jnp.float32)),
        [SMEM] + [VMEM] * 10,
        [window, extras, shifted, row_mask, row_mask],
        2 * 5 * rows * BLK * width,
        16 * rows * width,
    )(seq_lengths, table, kept, back_own, *pair, *back_pair, qkept, w_half, skip_bias.reshape(1, -1))

    qpair = kernel_call(
        pair_gate_kernel,
        half_wide,
        [SMEM] + [VMEM] * 4,
        [shifted, row_mask, row_mask],
        10 * rows * width,
        8 * rows * width,
    )(seq_lengths, qgot, kept, back_own, w_half)

    done, send, power = kernel_call(
        functools.partial(far_kernel, short),
        (half_wide, half_shape, shape((1, 2 * rows), jnp.float32)),
        [VMEM] * (9 + len(far)),
        [window, extras],
        2 * 5 * rows * BLK * width,
        24 * rows * width,
    )(table, acc, qown, qpair, w_half, marks, back_own, *back_pair, *far)

    back = moved(send, to_pair)
    peers = lax.axis_size("mp")
    shares = [lax.ppermute(power, "mp", [(i, i ^ k) for i in range(peers)]) for k in range(1, peers)]
    power = sum(shares, power)
    return kernel_call(
        functools.partial(norm_kernel, channels),
        shape((rows, 2 * width), jnp.bfloat16),
        [VMEM] * 5,
        [],
        8 * rows * width,
        10 * rows * width,
    )(power, moved(power, to_pair), done, back, norm_gain.reshape(1, -1))


def solution(mesh):
    blocks = mesh.shape["ctx"] // 2
    grid = Mesh(mesh.devices.reshape(blocks, 2, mesh.shape["mp"]), ("blk", "half", "mp"))
    in_specs = (
        P(SPOTS, None, "mp"),
        P(None, None, "mp"),
        P("mp", None),
        P("mp", None),
        P("mp"),
        P("mp"),
        P(),
    )

    def program(projected, *rest):
        body = functools.partial(shards, blocks, projected.shape[0], projected.shape[2])
        return jax.shard_map(
            body, mesh=grid, in_specs=in_specs, out_specs=P(SPOTS, "mp"), check_vma=False
        )(projected, *rest)

    return program
```

```python
import functools

import jax
import jax.numpy as jnp
from jax import lax
from jax.experimental import pallas as pl
from jax.experimental.pallas import tpu as pltpu
from jax.sharding import Mesh, PartitionSpec as P

GROUP = 128
BLK = 128
norm_eps = 1e-06

VMEM = pl.BlockSpec(memory_space=pltpu.VMEM)
SMEM = pl.BlockSpec(memory_space=pltpu.SMEM)
SPOTS = ("blk", "half")


def moved(block, pairs):
    return lax.ppermute(block, SPOTS, pairs)


def boundaries(seq_ref, t):
    def step(k, carry):
        end, first, second = carry
        end = end + seq_ref[k]
        return end, first | (t == end).astype(jnp.int32), second | (t - 1 == end).astype(jnp.int32)

    first = (t == 0).astype(jnp.int32)
    second = (t == 1).astype(jnp.int32)
    _, first, second = lax.fori_loop(0, seq_ref.shape[0], step, (jnp.int32(0), first, second), unroll=True)
    return first, first | second


def row_masks(seq_ref, start, m1_ref, m2_ref):
    rows = lax.broadcasted_iota(jnp.int32, (BLK, GROUP), 0)
    diagonal = rows == lax.broadcasted_iota(jnp.int32, (BLK, GROUP), 1)
    marks = boundaries(seq_ref, start + lax.broadcasted_iota(jnp.int32, (8, GROUP), 1))
    for mark, m_ref in zip(marks, (m1_ref, m2_ref)):
        keep = 1.0 - mark.astype(jnp.float32)[0:1]
        column = jnp.sum(jnp.where(diagonal, keep, 0.0), axis=1, keepdims=True)
        m_ref[...] = jnp.broadcast_to(column, (BLK, GROUP))


def counted(seq_ref, t):
    def step(k, carry):
        end, total = carry
        end = end + seq_ref[k]
        return end, total + (end <= t).astype(jnp.int32)

    _, total = lax.fori_loop(
        0, seq_ref.shape[0], step, (jnp.int32(0), jnp.zeros(t.shape, jnp.int32)), unroll=True
    )
    return jnp.where(t >= 0, total, -1)


def feature(x, x_ref, w, m1_ref, m2_ref):
    rows = x.shape[0]
    return (
        w[0:1] * x
        + w[1:2] * x_ref[7 : rows + 7, :] * m1_ref[...]
        + w[2:3] * x_ref[6 : rows + 6, :] * m2_ref[...]
    )


def products_kernel(seq_hbm, panels_hbm, w_hbm, kept_ref, *refs):
    *sent_refs, seq_ref, kv_ref, q_ref, w_ref, x_ref, m1_ref, m2_ref, sems = refs
    width = kept_ref.shape[1]
    rows = kv_ref.shape[2]
    pieces = kv_ref.shape[0]
    piece = kv_ref.shape[3]
    half = lax.axis_index("half")
    shard = lax.axis_index("blk") * 2 + half
    keep_at = pl.multiple_of(half * width, width)
    send_at = pl.multiple_of((1 - half) * width, width)

    loads = [pltpu.make_async_copy(seq_hbm, seq_ref, sems.at[0])]
    for p in range(pieces):
        at = keep_at if p < pieces // 2 else send_at
        lanes = pl.ds(pl.multiple_of(at + (p % (pieces // 2)) * piece, piece), piece)
        loads.append(pltpu.make_async_copy(panels_hbm.at[1:3, :, lanes], kv_ref.at[p], sems.at[1 + p]))
    loads.append(pltpu.make_async_copy(w_hbm, w_ref, sems.at[1 + pieces]))
    loads.append(pltpu.make_async_copy(panels_hbm.at[0, rows - 16 :, :], q_ref, sems.at[2 + pieces]))
    for load in loads:
        load.start()
    x_ref[:, 0:8, :] = jnp.zeros((x_ref.shape[0], 8, GROUP), jnp.float32)
    loads[0].wait()
    row_masks(seq_ref, shard * rows, m1_ref, m2_ref)
    loads[1 + pieces].wait()
    loads[2 + pieces].wait()
    for p in range(pieces):
        loads[1 + p].wait()
        out_ref, at = (kept_ref, keep_at) if p < pieces // 2 else (sent_refs[p - pieces // 2], send_at)
        for c in range(0, piece, GROUP):
            base = (p % (pieces // 2)) * piece + c
            there = slice(base, base + GROUP) if p < pieces // 2 else slice(c, c + GROUP)
            lanes = pl.ds(pl.multiple_of(at + base, GROUP), GROUP)
            slot = (c // GROUP) % (x_ref.shape[0] // 2) * 2
            heads, tails, made = [], [], []
            for i in range(2):
                x = kv_ref[p, i, :, c : c + GROUP].astype(jnp.float32)
                x_ref[slot + i, 8:, :] = x
                made.append(feature(x, x_ref.at[slot + i], w_ref[1 + i, :, lanes], m1_ref, m2_ref))
                heads.append(x[0:2])
                tails.append(x[rows - 2 :])
            out_ref[:rows, there] = (made[0] * made[1]).astype(out_ref.dtype)
            across = pl.ds(pl.multiple_of(keep_at + send_at - at + base, GROUP), GROUP)
            for place in (lanes, across):
                tails.append(q_ref[:, place].astype(jnp.float32)[14:])
            extra = jnp.concatenate(heads + tails + [jnp.zeros((4, GROUP), jnp.float32)], 0)
            out_ref[rows:, there] = extra.astype(out_ref.dtype)


def edge_marks(seq_ref):
    t = (
        (lax.axis_index("blk") - 2) * (2 * BLK)
        + lax.broadcasted_iota(jnp.int32, (8, GROUP), 1) * BLK
        + lax.broadcasted_iota(jnp.int32, (8, GROUP), 0)
    )
    return [1.0 - mark.astype(jnp.float32) for mark in boundaries(seq_ref, t)]


def first_rows(now, ahead, w_ref, marks, spot, lanes=slice(None)):
    m1, m2 = [mark[:, spot : spot + 1] for mark in marks]
    top = lax.broadcasted_iota(jnp.int32, now.shape, 0) == 0
    made = []
    for i in range(2):
        x0 = pltpu.roll(now, (8 - 2 * i) % 8, 0) if i else now
        x1 = jnp.where(top, pltpu.roll(ahead, 3 - 2 * i, 0), pltpu.roll(now, (9 - 2 * i) % 8, 0))
        x2 = pltpu.roll(ahead, 4 - 2 * i, 0)
        w = w_ref[1 + i, :, lanes]
        made.append(w[0:1] * x0 + w[1:2] * x1 * m1 + w[2:3] * x2 * m2)
    return made[0] * made[1]


def put_first_rows(win_ref, at, rows):
    old = win_ref[at : at + 16, :].astype(jnp.float32)
    new = jnp.concatenate([rows, rows], 0)
    first = lax.broadcasted_iota(jnp.int32, old.shape, 0) < 2
    win_ref[at : at + 16, :] = jnp.where(first, new, old).astype(win_ref.dtype)


def reaches_past(seq_ref, block):
    first = block * (2 * BLK)

    def step(k, carry):
        end, start = carry
        end = end + seq_ref[k]
        return end, jnp.where(end <= first, end, start)

    _, start = lax.fori_loop(0, seq_ref.shape[0], step, (jnp.int32(0), jnp.int32(0)), unroll=True)
    return first - 2 * BLK - start > BLK


def tables_kernel(seq_ref, taps_ref, w_ref, out_ref, next_ref, w_half_ref, wq_ref, rev_ref, m_ref):
    groups = out_ref.shape[0]
    taps = taps_ref.shape[1]
    span = out_ref.shape[3]
    half = lax.axis_index("half")
    start = lax.axis_index("blk") * (2 * BLK)
    width = w_half_ref.shape[2]
    w_half_ref[...] = w_ref[:, :, pl.ds(pl.multiple_of(half * width, width), width)]
    wq_ref[...] = w_ref[0]
    turn = lax.broadcasted_iota(jnp.int32, (taps, span), 0) + lax.broadcasted_iota(
        jnp.int32, (taps, span), 1
    )
    turn = (turn == taps).astype(jnp.bfloat16)
    rev_ref[...] = jnp.dot(taps_ref[...], turn, preferred_element_type=jnp.float32)
    seg_in = counted(seq_ref, start - taps + lax.broadcasted_iota(jnp.int32, (8, span), 1))[0:1]
    for part in range(3):
        t_out = start + part * BLK + lax.broadcasted_iota(jnp.int32, (BLK, GROUP), 0)
        seg_out = counted(seq_ref, t_out)[:, 0:1]
        if part < 2:
            m_ref[part] = (seg_in == seg_out).astype(jnp.float32)
        else:
            m_ref[2, :, : 2 * BLK] = (seg_in[:, 2 * BLK : 4 * BLK] == seg_out).astype(jnp.float32)

    def one(g, _):
        row = rev_ref[pl.ds(half * groups + g, 1), :]
        table = pltpu.roll(jnp.broadcast_to(row, (BLK, span)), 0, 1, stride=1, stride_axis=0)
        out_ref[g, 0] = (table * m_ref[0]).astype(out_ref.dtype)
        later = jnp.concatenate([table[:, span - BLK :], table[:, : span - BLK]], 1)
        out_ref[g, 1] = (later * m_ref[1]).astype(out_ref.dtype)
        next_ref[g] = (table[:, : 2 * BLK] * m_ref[2, :, : 2 * BLK]).astype(next_ref.dtype)
        return 0

    lax.fori_loop(0, groups, one, 0)


def fill(win_ref, extra_ref, spot, *pieces):
    at = 0
    for piece in pieces:
        lanes = slice(at, at + piece.shape[1])
        win_ref[pl.ds(pl.multiple_of(spot * BLK, BLK), BLK), lanes] = piece[:BLK]
        extra_ref[spot, :, lanes] = piece[BLK:].astype(jnp.float32)
        at += piece.shape[1]


def relay_kernel(piece, seq_ref, next_ref, back_own_ref, back_pair_ref, w_ref, out_ref, win_ref, extra_ref):
    width = out_ref.shape[1]
    half = lax.axis_index("half")
    lanes = slice(piece * width, (piece + 1) * width)
    fill(win_ref, extra_ref, half, back_own_ref.at[:, lanes])
    fill(win_ref, extra_ref, 1 - half, back_pair_ref)
    marks = edge_marks(seq_ref)
    rows = first_rows(extra_ref[1, :8], extra_ref[0, :8], w_ref, marks, 3, lanes)
    put_first_rows(win_ref, BLK, rows)
    out_ref[BLK:] = extra_ref[1].astype(out_ref.dtype)
    summed = reaches_past(seq_ref, lax.axis_index("blk") + 1)

    @pl.when(summed)
    def _():
        for c in range(0, width, GROUP):
            total = jnp.dot(
                next_ref[(piece * width + c) // GROUP],
                win_ref[:, c : c + GROUP],
                preferred_element_type=jnp.float32,
            )
            out_ref[:BLK, c : c + GROUP] = total.astype(out_ref.dtype)

    @pl.when(jnp.logical_not(summed))
    def _():
        out_ref[:BLK] = win_ref[BLK:]


def query_kernel(
    seq_ref, raw_ref, pair_a_ref, pair_b_ref, back_a_ref, back_b_ref, w_ref, q_ref, x_ref, m1_ref, m2_ref
):
    piece = pair_a_ref.shape[1]
    half = lax.axis_index("half")
    row_masks(seq_ref, (lax.axis_index("blk") * 2 + half) * BLK, m1_ref, m2_ref)
    for c in range(0, 4 * piece, GROUP):
        turned = c // (2 * piece)
        inside = c % (2 * piece)
        at = jnp.where(half == turned, 0, 2 * piece) + inside
        lanes = pl.ds(pl.multiple_of(at, GROUP), GROUP)
        there = slice(inside % piece, inside % piece + GROUP)
        pair_ref, back_ref = (pair_a_ref, back_a_ref) if inside < piece else (pair_b_ref, back_b_ref)
        pair = pair_ref[BLK:, there].astype(jnp.float32)
        back = back_ref[BLK:, there].astype(jnp.float32)
        x = raw_ref[:, lanes].astype(jnp.float32)
        slot = (c // GROUP) % 2
        x_ref[slot, 6:8, :] = jnp.where(half == 1, pair, back)[8 + 2 * turned : 10 + 2 * turned]
        x_ref[slot, 8:, :] = x
        q_ref[:, c : c + GROUP] = feature(x, x_ref.at[slot], w_ref[:, lanes], m1_ref, m2_ref)


def near_kernel(
    seq_ref, table_ref, own_ref, back_own_ref, pair_a_ref, pair_b_ref, back_a_ref, back_b_ref, w_ref, bias_ref,
    acc_ref, marks_ref, win_ref, extra_ref,
):
    groups = table_ref.shape[0]
    width = groups * GROUP
    half = lax.axis_index("half")
    block = lax.axis_index("blk")
    fill(win_ref, extra_ref, half, back_own_ref)
    fill(win_ref, extra_ref, 1 - half, back_a_ref, back_b_ref)
    fill(win_ref, extra_ref, 2 + half, own_ref)
    fill(win_ref, extra_ref, 3 - half, pair_a_ref, pair_b_ref)
    marks = edge_marks(seq_ref)
    marks_ref[0], marks_ref[1] = marks
    marks_ref[2] = jnp.full((8, GROUP), reaches_past(seq_ref, block).astype(jnp.float32))
    for spot in (1, 2, 3):
        rows = first_rows(extra_ref[spot, :8], extra_ref[spot - 1, :8], w_ref, marks, spot + 2)
        put_first_rows(win_ref, spot * BLK, rows)
    for g in range(groups):
        lanes = slice(g * GROUP, (g + 1) * GROUP)
        bias = bias_ref[:, pl.ds(pl.multiple_of(half * width + g * GROUP, GROUP), GROUP)]
        for part in range(2):
            total = jnp.dot(
                table_ref[g, part, :, 3 * BLK : (5 + part) * BLK],
                win_ref[BLK : (3 + part) * BLK, lanes],
                preferred_element_type=jnp.float32,
            )
            here = win_ref[(2 + part) * BLK : (3 + part) * BLK, lanes].astype(jnp.float32)
            acc_ref[part * BLK : (part + 1) * BLK, lanes] = total + bias * here


def far_kernel(short, piece, table_ref, acc_ref, q_ref, w_ref, marks_ref, back_own_ref, back_pair_ref, *refs):
    *far_refs, kept_ref, sent_ref, squares_ref, win_ref, extra_ref = refs
    width = kept_ref.shape[1]
    half = lax.axis_index("half")
    lanes = slice(piece * width, (piece + 1) * width)
    marks = [marks_ref[0], marks_ref[1]]
    low = 1 if short else 0
    fill(win_ref, extra_ref, 2 + half, back_own_ref.at[:, lanes])
    fill(win_ref, extra_ref, 3 - half, back_pair_ref)
    if short:
        summed = marks_ref[2, 0:1, 0:1]
        fill(win_ref, extra_ref, 1, far_refs[0])
        payload = win_ref[BLK : 2 * BLK, :].astype(jnp.float32)
        win_ref[BLK : 2 * BLK, :] = (payload * (1.0 - summed)).astype(win_ref.dtype)
    else:
        fill(win_ref, extra_ref, half, far_refs[0].at[:, lanes])
        fill(win_ref, extra_ref, 1 - half, far_refs[1 + piece])
        ahead = far_refs[3][:, lanes].astype(jnp.float32)[:8]
        put_first_rows(win_ref, 0, first_rows(extra_ref[0, :8], ahead, w_ref, marks, 0, lanes))
        rows = first_rows(extra_ref[1, :8], extra_ref[0, :8], w_ref, marks, 1, lanes)
        put_first_rows(win_ref, BLK, rows)
    rows = first_rows(extra_ref[2, :8], extra_ref[1, :8], w_ref, marks, 2, lanes)
    put_first_rows(win_ref, 2 * BLK, rows)
    squares = jnp.zeros((BLK, GROUP), jnp.float32)
    for part, own in ((1 - half, False), (half, True)):
        rows = pl.ds(pl.multiple_of(part * BLK, BLK), BLK)
        for c in range(0, width, GROUP):
            here = slice(c, c + GROUP)
            whole = slice(piece * width + c, piece * width + c + GROUP)
            filtered = acc_ref[rows, whole] + jnp.dot(
                table_ref[(piece * width + c) // GROUP, part, :, low * BLK : 3 * BLK],
                win_ref[low * BLK : 3 * BLK, here],
                preferred_element_type=jnp.float32,
            )
            if short:
                weight = summed * (part == 0).astype(jnp.float32)
                filtered = filtered + weight * far_refs[0][:BLK, here].astype(jnp.float32)
            if own:
                gated = q_ref[:, whole] * filtered
                kept_ref[:, here] = gated
                squares = squares + gated * gated
            else:
                sent_ref[:, here] = filtered.astype(sent_ref.dtype)
    squares_ref[...] = squares


def gate_kernel(piece, q_ref, got_ref, gated_ref, squares_ref):
    width = got_ref.shape[1]
    squares = jnp.zeros((BLK, GROUP), jnp.float32)
    for c in range(0, width, GROUP):
        at = (2 + piece) * width + c
        gated = q_ref[:, at : at + GROUP] * got_ref[:, c : c + GROUP].astype(jnp.float32)
        gated_ref[:, c : c + GROUP] = gated
        squares = squares + gated * gated
    squares_ref[...] = squares


def last_gate_kernel(piece, q_ref, got_ref, *refs):
    *other_refs, gated_ref, power_ref, squares_ref = refs
    gate_kernel(piece, q_ref, got_ref, gated_ref, squares_ref)
    power_ref[...] = lax.dot_general(
        jnp.ones((8, GROUP), jnp.float32),
        sum([ref[...] for ref in other_refs], squares_ref[...]),
        (((1,), (1,)), ((), ())),
        precision=lax.Precision.HIGHEST,
        preferred_element_type=jnp.float32,
    )[0:1]


def norm_kernel(channels, pieces, *refs):
    part_refs, (*power_refs, gain_ref, out_ref) = refs[:pieces], refs[pieces:]
    half = lax.axis_index("half")
    width = part_refs[0].shape[1]
    power = sum([ref[...] for ref in power_refs[1:]], power_refs[0][...])
    scale = lax.rsqrt(power / channels + norm_eps)
    diagonal = lax.broadcasted_iota(jnp.int32, (BLK, BLK), 0) == lax.broadcasted_iota(
        jnp.int32, (BLK, BLK), 1
    )
    column = jnp.sum(jnp.where(diagonal, scale, 0.0), axis=1, keepdims=True)
    for p, part_ref in enumerate(part_refs):
        which = half if p < pieces // 2 else 1 - half
        for c in range(0, width, GROUP):
            at = (which * (pieces // 2) + p % (pieces // 2)) * width + c
            lanes = pl.ds(pl.multiple_of(at, GROUP), GROUP)
            out_ref[:, lanes] = (part_ref[:, c : c + GROUP] * column * gain_ref[:, lanes]).astype(out_ref.dtype)


def kernel_call(body, outs, in_specs, scratch, flops, moved_bytes, vmem=24 << 20):
    return pl.pallas_call(
        body,
        out_shape=outs,
        in_specs=in_specs,
        out_specs=jax.tree.map(lambda _: VMEM, outs),
        scratch_shapes=scratch,
        compiler_params=pltpu.CompilerParams(vmem_limit_bytes=vmem),
        cost_estimate=pl.CostEstimate(flops=flops, bytes_accessed=moved_bytes, transcendentals=0),
    )


def shards(blocks, whole_tokens, channels, projected, short_weight, filter_taps, tap_blocks, skip_bias, norm_gain, seq_lengths):
    rows = projected.shape[0]
    width = projected.shape[2] // 2
    groups = width // GROUP
    taps = filter_taps.shape[1]
    shape = jax.ShapeDtypeStruct
    piece_shape = shape((rows, width // 2), jnp.bfloat16)
    piece_wide = shape((rows, width // 2), jnp.float32)
    squares = shape((rows, GROUP), jnp.float32)

    spots = range(2 * blocks)
    to_pair = [(i, i ^ 1) for i in spots]
    ahead = [(i, (i + 2) % (2 * blocks)) for i in spots]

    panels = jnp.transpose(projected, (1, 0, 2))
    message = shape((rows + 16, width), jnp.bfloat16)
    small = shape((rows + 16, width // 2), jnp.bfloat16)
    hbm = pl.BlockSpec(memory_space=pltpu.HBM)
    pieces = 4
    row_mask = pltpu.VMEM((rows, GROUP), jnp.float32)

    kept, *sent = kernel_call(
        products_kernel,
        (message, small, small),
        [hbm] * 3,
        [
            pltpu.SMEM(seq_lengths.shape, jnp.int32),
            pltpu.VMEM((pieces, 2, rows, 2 * width // pieces), jnp.bfloat16),
            pltpu.VMEM((16, 2 * width), jnp.bfloat16),
            pltpu.VMEM(short_weight.shape, jnp.float32),
            pltpu.VMEM((4, rows + 8, GROUP), jnp.float32),
            row_mask,
            row_mask,
            pltpu.SemaphoreType.DMA((3 + pieces,)),
        ],
        40 * rows * width,
        16 * rows * width,
        60 << 20,
    )(seq_lengths, panels, short_weight)

    back_own = moved(kept, ahead)
    filter_taps, _ = lax.optimization_barrier((filter_taps, kept))
    scaled = (filter_taps * jnp.repeat(tap_blocks.astype(jnp.float32), BLK, axis=1)).astype(jnp.bfloat16)
    scaled, *sent = lax.optimization_barrier((scaled, *sent))
    pair = [moved(piece, to_pair) for piece in sent]
    span = taps + 2 * BLK
    table, table_next, w_half, w_query = kernel_call(
        tables_kernel,
        (
            shape((groups, 2, BLK, span), jnp.bfloat16),
            shape((groups, BLK, 2 * BLK), jnp.bfloat16),
            shape((3, 3, width), jnp.float32),
            shape((3, 2 * width), jnp.float32),
        ),
        [SMEM, VMEM, VMEM],
        [pltpu.VMEM((2 * groups, span), jnp.float32), pltpu.VMEM((3, BLK, span), jnp.float32)],
        40 * groups * BLK * taps,
        8 * groups * BLK * taps,
    )(seq_lengths, scaled, short_weight)
    table, table_next, pair[1] = lax.optimization_barrier((table, table_next, pair[1]))

    query, _ = lax.optimization_barrier((panels, table_next))
    query = query[0]
    back_pair = [moved(piece, ahead) for piece in pair]

    window = pltpu.VMEM((4 * rows, width), jnp.bfloat16)
    extras = pltpu.VMEM((4, 16, width), jnp.float32)
    shifted = pltpu.VMEM((2, rows + 8, GROUP), jnp.float32)
    short = whole_tokens // 2 <= 4 * BLK
    if short:
        onward = [(i, i ^ 1 if i < 2 else i + 2 if i + 2 < 2 * blocks else 2 + i % 2) for i in spots]
        far = []
        for piece in range(2):
            relayed = kernel_call(
                functools.partial(relay_kernel, piece),
                small,
                [SMEM] + [VMEM] * 4,
                [pltpu.VMEM((2 * rows, width // 2), jnp.bfloat16), pltpu.VMEM((2, 16, width // 2), jnp.float32)],
                2 * rows * BLK * width,
                4 * rows * width,
            )(seq_lengths, table_next, back_own, back_pair[piece], w_half)
            far.append(moved(relayed, onward))
    else:
        across = jnp.concatenate([piece[rows:] for piece in sent], 1)
        across = moved(across, [(i, ((i ^ 1) + 6) % (2 * blocks)) for i in spots])
        straight = moved(kept[rows:], [(i, (i + 6) % (2 * blocks)) for i in spots])
        deep = jnp.where(lax.axis_index("half") == 1, straight, across)
        far = [moved(piece, ahead) for piece in (back_own, *back_pair)] + [deep]

    acc, marks = kernel_call(
        near_kernel,
        (shape((2 * rows, width), jnp.float32), shape((3, 8, GROUP), jnp.float32)),
        [SMEM] + [VMEM] * 9,
        [window, extras],
        2 * 5 * rows * BLK * width,
        16 * rows * width,
    )(seq_lengths, table, kept, back_own, *pair, *back_pair, w_half, skip_bias.reshape(1, -1))

    q = kernel_call(
        query_kernel,
        shape((rows, 2 * width), jnp.float32),
        [SMEM] + [VMEM] * 6,
        [pltpu.VMEM((2, rows + 8, GROUP), jnp.float32), row_mask, row_mask],
        20 * rows * width,
        12 * rows * width,
    )(seq_lengths, query, *pair, *back_pair, w_query)

    own, got, parts = [], [], []
    for piece in range(2):
        needed = far[piece : piece + 1] if short else far
        if parts:
            acc, _ = lax.optimization_barrier((acc, parts[0]))
        done, send, part = kernel_call(
            functools.partial(far_kernel, short, piece),
            (piece_wide, piece_shape, squares),
            [VMEM] * (7 + len(needed)),
            [pltpu.VMEM((4 * rows, width // 2), jnp.bfloat16), pltpu.VMEM((4, 16, width // 2), jnp.float32)],
            2 * 3 * rows * BLK * width,
            12 * rows * width,
        )(table, acc, q, w_half, marks, back_own, back_pair[piece], *needed)
        own.append(done)
        parts.append(part)
        got.append(moved(send, to_pair))
    first, part = kernel_call(
        functools.partial(gate_kernel, 0), (piece_wide, squares), [VMEM] * 2, [], rows * width, 5 * rows * width
    )(q, got[0])
    second, power = kernel_call(
        functools.partial(last_gate_kernel, 1),
        (piece_wide, shape((1, rows), jnp.float32)),
        [VMEM] * 5,
        [pltpu.VMEM((rows, GROUP), jnp.float32)],
        rows * width,
        5 * rows * width,
    )(q, got[1], *parts, part)

    peers = lax.axis_size("mp")
    powers = [power] + [lax.ppermute(power, "mp", [(i, i ^ k) for i in range(peers)]) for k in range(1, peers)]
    results = (*own, first, second)
    return kernel_call(
        functools.partial(norm_kernel, channels, len(results)),
        shape((rows, 2 * width), jnp.bfloat16),
        [VMEM] * (len(results) + len(powers) + 1),
        [],
        8 * rows * width,
        10 * rows * width,
    )(*results, *powers, norm_gain.reshape(1, -1))


def solution(mesh):
    blocks = mesh.shape["ctx"] // 2
    grid = Mesh(mesh.devices.reshape(blocks, 2, mesh.shape["mp"]), ("blk", "half", "mp"))
    in_specs = (
        P(SPOTS, None, "mp"),
        P(None, None, "mp"),
        P("mp", None),
        P("mp", None),
        P("mp"),
        P("mp"),
        P(),
    )

    def program(projected, *rest):
        body = functools.partial(shards, blocks, projected.shape[0], projected.shape[2])
        return jax.shard_map(
            body, mesh=grid, in_specs=in_specs, out_specs=P(SPOTS, "mp"), check_vma=False
        )(projected, *rest)

    return program
```

```python
import functools

import jax
import jax.numpy as jnp
from jax import lax
from jax.experimental import pallas as pl
from jax.experimental.pallas import tpu as pltpu
from jax.sharding import Mesh, PartitionSpec as P

GROUP = 128
BLK = 128
norm_eps = 1e-06

VMEM = pl.BlockSpec(memory_space=pltpu.VMEM)
SMEM = pl.BlockSpec(memory_space=pltpu.SMEM)
SPOTS = ("blk", "half")


def moved(block, pairs):
    return lax.ppermute(block, SPOTS, pairs)


def boundaries(seq_ref, t):
    def step(k, carry):
        end, first, second = carry
        end = end + seq_ref[k]
        return end, first | (t == end).astype(jnp.int32), second | (t - 1 == end).astype(jnp.int32)

    first = (t == 0).astype(jnp.int32)
    second = (t == 1).astype(jnp.int32)
    _, first, second = lax.fori_loop(0, seq_ref.shape[0], step, (jnp.int32(0), first, second), unroll=True)
    return first, first | second


def row_masks(seq_ref, start, m1_ref, m2_ref):
    rows = lax.broadcasted_iota(jnp.int32, (BLK, GROUP), 0)
    diagonal = rows == lax.broadcasted_iota(jnp.int32, (BLK, GROUP), 1)
    marks = boundaries(seq_ref, start + lax.broadcasted_iota(jnp.int32, (8, GROUP), 1))
    for mark, m_ref in zip(marks, (m1_ref, m2_ref)):
        keep = 1.0 - mark.astype(jnp.float32)[0:1]
        column = jnp.sum(jnp.where(diagonal, keep, 0.0), axis=1, keepdims=True)
        m_ref[...] = jnp.broadcast_to(column, (BLK, GROUP))


def counted(seq_ref, t):
    def step(k, carry):
        end, total = carry
        end = end + seq_ref[k]
        return end, total + (end <= t).astype(jnp.int32)

    _, total = lax.fori_loop(
        0, seq_ref.shape[0], step, (jnp.int32(0), jnp.zeros(t.shape, jnp.int32)), unroll=True
    )
    return jnp.where(t >= 0, total, -1)


def feature(x, x_ref, w, m1_ref, m2_ref):
    rows = x.shape[0]
    return (
        w[0:1] * x
        + w[1:2] * x_ref[7 : rows + 7, :] * m1_ref[...]
        + w[2:3] * x_ref[6 : rows + 6, :] * m2_ref[...]
    )


def products_kernel(seq_hbm, panels_hbm, w_hbm, kept_ref, *refs):
    *sent_refs, seq_ref, kv_ref, q_ref, w_ref, x_ref, m1_ref, m2_ref, sems = refs
    width = kept_ref.shape[1]
    rows = kv_ref.shape[2]
    pieces = kv_ref.shape[0]
    piece = kv_ref.shape[3]
    half = lax.axis_index("half")
    shard = lax.axis_index("blk") * 2 + half
    keep_at = pl.multiple_of(half * width, width)
    send_at = pl.multiple_of((1 - half) * width, width)

    loads = [pltpu.make_async_copy(seq_hbm, seq_ref, sems.at[0])]
    for p in range(pieces):
        at = keep_at if p < pieces // 2 else send_at
        lanes = pl.ds(pl.multiple_of(at + (p % (pieces // 2)) * piece, piece), piece)
        loads.append(pltpu.make_async_copy(panels_hbm.at[1:3, :, lanes], kv_ref.at[p], sems.at[1 + p]))
    loads.append(pltpu.make_async_copy(w_hbm, w_ref, sems.at[1 + pieces]))
    loads.append(pltpu.make_async_copy(panels_hbm.at[0, rows - 16 :, :], q_ref, sems.at[2 + pieces]))
    for load in loads:
        load.start()
    x_ref[:, 0:8, :] = jnp.zeros((x_ref.shape[0], 8, GROUP), jnp.float32)
    loads[0].wait()
    row_masks(seq_ref, shard * rows, m1_ref, m2_ref)
    loads[1 + pieces].wait()
    loads[2 + pieces].wait()
    for p in range(pieces):
        loads[1 + p].wait()
        out_ref, at = (kept_ref, keep_at) if p < pieces // 2 else (sent_refs[p - pieces // 2], send_at)
        for c in range(0, piece, GROUP):
            base = (p % (pieces // 2)) * piece + c
            there = slice(base, base + GROUP) if p < pieces // 2 else slice(c, c + GROUP)
            lanes = pl.ds(pl.multiple_of(at + base, GROUP), GROUP)
            slot = (c // GROUP) % (x_ref.shape[0] // 2) * 2
            raw, made = [], []
            for i in range(2):
                x = kv_ref[p, i, :, c : c + GROUP].astype(jnp.float32)
                x_ref[slot + i, 8:, :] = x
                made.append(feature(x, x_ref.at[slot + i], w_ref[1 + i, :, lanes], m1_ref, m2_ref))
                raw.append(x)
            product = made[0] * made[1]
            top = jnp.where(lax.broadcasted_iota(jnp.int32, (8, GROUP), 0) < 2, raw[0][:8], product[:8])
            out_ref[:rows, there] = jnp.concatenate([top, product[8:]], 0).astype(out_ref.dtype)
            tails = [x[rows - 2 :] for x in raw] + [q_ref[:, lanes].astype(jnp.float32)[14:]]
            out_ref[rows:, there] = jnp.concatenate([raw[1][0:2]] + tails, 0).astype(out_ref.dtype)


def edge_marks(seq_ref):
    t = (
        (lax.axis_index("blk") - 2) * (2 * BLK)
        + lax.broadcasted_iota(jnp.int32, (8, GROUP), 1) * BLK
        + lax.broadcasted_iota(jnp.int32, (8, GROUP), 0)
    )
    return [1.0 - mark.astype(jnp.float32) for mark in boundaries(seq_ref, t)]


def first_rows(now, ahead, w_ref, marks, spot, lanes=slice(None)):
    m1, m2 = [mark[:, spot : spot + 1] for mark in marks]
    top = lax.broadcasted_iota(jnp.int32, ahead.shape, 0) == 0
    made = []
    for i, x0 in enumerate((now[8:], now[:8])):
        x1 = jnp.where(top, pltpu.roll(ahead, 5 - 2 * i, 0), pltpu.roll(x0, 1, 0))
        x2 = pltpu.roll(ahead, 6 - 2 * i, 0)
        w = w_ref[1 + i, :, lanes]
        made.append(w[0:1] * x0 + w[1:2] * x1 * m1 + w[2:3] * x2 * m2)
    return made[0] * made[1]


def put_first_rows(win_ref, at, rows):
    old = win_ref[at : at + 16, :].astype(jnp.float32)
    new = jnp.concatenate([rows, rows], 0)
    first = lax.broadcasted_iota(jnp.int32, old.shape, 0) < 2
    win_ref[at : at + 16, :] = jnp.where(first, new, old).astype(win_ref.dtype)


def reaches_past(seq_ref, block):
    first = block * (2 * BLK)

    def step(k, carry):
        end, start = carry
        end = end + seq_ref[k]
        return end, jnp.where(end <= first, end, start)

    _, start = lax.fori_loop(0, seq_ref.shape[0], step, (jnp.int32(0), jnp.int32(0)), unroll=True)
    return first - 2 * BLK - start > BLK


def tables_kernel(seq_ref, taps_ref, w_ref, out_ref, next_ref, w_half_ref, rev_ref, m_ref):
    groups = out_ref.shape[0]
    taps = taps_ref.shape[1]
    span = out_ref.shape[3]
    half = lax.axis_index("half")
    start = lax.axis_index("blk") * (2 * BLK)
    width = w_half_ref.shape[2]
    w_half_ref[...] = w_ref[:, :, pl.ds(pl.multiple_of(half * width, width), width)]
    turn = lax.broadcasted_iota(jnp.int32, (taps, span), 0) + lax.broadcasted_iota(
        jnp.int32, (taps, span), 1
    )
    turn = (turn == taps).astype(jnp.bfloat16)
    rev_ref[...] = jnp.dot(taps_ref[...], turn, preferred_element_type=jnp.float32)
    seg_in = counted(seq_ref, start - taps + lax.broadcasted_iota(jnp.int32, (8, span), 1))[0:1]
    for part in range(3):
        t_out = start + part * BLK + lax.broadcasted_iota(jnp.int32, (BLK, GROUP), 0)
        seg_out = counted(seq_ref, t_out)[:, 0:1]
        if part < 2:
            m_ref[part] = (seg_in == seg_out).astype(jnp.float32)
        else:
            m_ref[2, :, : 2 * BLK] = (seg_in[:, 2 * BLK : 4 * BLK] == seg_out).astype(jnp.float32)

    def one(g, _):
        row = rev_ref[pl.ds(half * groups + g, 1), :]
        table = pltpu.roll(jnp.broadcast_to(row, (BLK, span)), 0, 1, stride=1, stride_axis=0)
        out_ref[g, 0] = (table * m_ref[0]).astype(out_ref.dtype)
        later = jnp.concatenate([table[:, span - BLK :], table[:, : span - BLK]], 1)
        out_ref[g, 1] = (later * m_ref[1]).astype(out_ref.dtype)
        next_ref[g] = (table[:, : 2 * BLK] * m_ref[2, :, : 2 * BLK]).astype(next_ref.dtype)
        return 0

    lax.fori_loop(0, groups, one, 0)


def fill(win_ref, extra_ref, spot, *pieces):
    at = 0
    for piece in pieces:
        lanes = slice(at, at + piece.shape[1])
        win_ref[pl.ds(pl.multiple_of(spot * BLK, BLK), BLK), lanes] = piece[:BLK]
        extra_ref[spot, :8, lanes] = piece[BLK:].astype(jnp.float32)
        extra_ref[spot, 8:, lanes] = piece[:16].astype(jnp.float32)[:8]
        at += piece.shape[1]


def relay_kernel(piece, seq_ref, next_ref, back_own_ref, back_pair_ref, w_ref, out_ref, win_ref, extra_ref):
    width = out_ref.shape[1]
    half = lax.axis_index("half")
    lanes = slice(piece * width, (piece + 1) * width)
    fill(win_ref, extra_ref, half, back_own_ref.at[:, lanes])
    fill(win_ref, extra_ref, 1 - half, back_pair_ref)
    marks = edge_marks(seq_ref)
    put_first_rows(win_ref, 0, first_rows(extra_ref[0], jnp.zeros((8, width), jnp.float32), w_ref, marks, 2, lanes))
    put_first_rows(win_ref, BLK, first_rows(extra_ref[1], extra_ref[0, :8], w_ref, marks, 3, lanes))
    out_ref[BLK:] = extra_ref[1, :8].astype(out_ref.dtype)
    summed = reaches_past(seq_ref, lax.axis_index("blk") + 1)

    @pl.when(summed)
    def _():
        for c in range(0, width, GROUP):
            total = jnp.dot(
                next_ref[(piece * width + c) // GROUP],
                win_ref[:, c : c + GROUP],
                preferred_element_type=jnp.float32,
            )
            out_ref[:BLK, c : c + GROUP] = total.astype(out_ref.dtype)

    @pl.when(jnp.logical_not(summed))
    def _():
        out_ref[:BLK] = win_ref[BLK:]


def gate_rows(seq_ref, raw_ref, tail, w_ref, part, q_ref, x_ref, m1_ref, m2_ref):
    width = raw_ref.shape[1]
    row_masks(seq_ref, lax.axis_index("blk") * (2 * BLK) + part * BLK, m1_ref, m2_ref)
    for c in range(0, width, GROUP):
        lanes = slice(c, c + GROUP)
        w = w_ref[0, :, lanes]
        x = raw_ref[:, lanes].astype(jnp.float32)
        slot = (c // GROUP) % 2
        x_ref[slot, 6:8, :] = tail(lanes)
        x_ref[slot, 8:, :] = x
        q_ref[:, lanes] = feature(x, x_ref.at[slot], w, m1_ref, m2_ref)


def near_kernel(
    seq_ref, table_ref, own_ref, back_own_ref, pair_a_ref, pair_b_ref, back_a_ref, back_b_ref, qkept_ref, w_ref, bias_ref,
    acc_ref, q_ref, marks_ref, win_ref, extra_ref, x_ref, m1_ref, m2_ref,
):
    groups = table_ref.shape[0]
    width = groups * GROUP
    half = lax.axis_index("half")
    block = lax.axis_index("blk")
    fill(win_ref, extra_ref, half, back_own_ref)
    fill(win_ref, extra_ref, 1 - half, back_a_ref, back_b_ref)
    fill(win_ref, extra_ref, 2 + half, own_ref)
    fill(win_ref, extra_ref, 3 - half, pair_a_ref, pair_b_ref)
    marks = edge_marks(seq_ref)
    marks_ref[0], marks_ref[1] = marks
    marks_ref[2] = jnp.full((8, GROUP), reaches_past(seq_ref, block).astype(jnp.float32))
    for spot in (1, 2, 3):
        rows = first_rows(extra_ref[spot], extra_ref[spot - 1, :8], w_ref, marks, spot + 2)
        put_first_rows(win_ref, spot * BLK, rows)
    for g in range(groups):
        lanes = slice(g * GROUP, (g + 1) * GROUP)
        bias = bias_ref[:, pl.ds(pl.multiple_of(half * width + g * GROUP, GROUP), GROUP)]
        for part in range(2):
            total = jnp.dot(
                table_ref[g, part, :, 3 * BLK : (5 + part) * BLK],
                win_ref[BLK : (3 + part) * BLK, lanes],
                preferred_element_type=jnp.float32,
            )
            here = win_ref[(2 + part) * BLK : (3 + part) * BLK, lanes].astype(jnp.float32)
            acc_ref[part * BLK : (part + 1) * BLK, lanes] = total + bias * here
    gate_rows(
        seq_ref, qkept_ref, lambda lanes: extra_ref[1 + half, 6:8, lanes], w_ref, half, q_ref, x_ref, m1_ref, m2_ref
    )


def pair_gate_kernel(seq_ref, raw_ref, own_ref, back_own_ref, w_ref, q_ref, x_ref, m1_ref, m2_ref):
    half = lax.axis_index("half")

    def tail(lanes):
        back = back_own_ref[BLK:, lanes].astype(jnp.float32)
        own = own_ref[BLK:, lanes].astype(jnp.float32)
        return jnp.where(half == 1, back, own)[6:8]

    gate_rows(seq_ref, raw_ref, tail, w_ref, 1 - half, q_ref, x_ref, m1_ref, m2_ref)


def far_kernel(short, table_ref, acc_ref, qown_ref, qpair_ref, w_ref, marks_ref, *refs):
    *messages, kept_ref, sent_ref, power_ref, win_ref, extra_ref = refs
    groups = table_ref.shape[0]
    width = groups * GROUP
    half = lax.axis_index("half")
    marks = [marks_ref[0], marks_ref[1]]
    back_own_ref, back_a_ref, back_b_ref, *far_refs = messages
    low = 1 if short else 0
    fill(win_ref, extra_ref, 2 + half, back_own_ref)
    fill(win_ref, extra_ref, 3 - half, back_a_ref, back_b_ref)
    if short:
        summed = marks_ref[2, 0:1, 0:1]
        fill(win_ref, extra_ref, 1, *far_refs)
        payload = win_ref[BLK : 2 * BLK, :].astype(jnp.float32)
        win_ref[BLK : 2 * BLK, :] = (payload * (1.0 - summed)).astype(win_ref.dtype)
    else:
        fill(win_ref, extra_ref, half, far_refs[0])
        fill(win_ref, extra_ref, 1 - half, far_refs[1], far_refs[2])
        ahead = far_refs[3][...].astype(jnp.float32)
        put_first_rows(win_ref, 0, first_rows(extra_ref[0], ahead, w_ref, marks, 0))
        rows = first_rows(extra_ref[1], extra_ref[0, :8], w_ref, marks, 1)
        put_first_rows(win_ref, BLK, rows)
    rows = first_rows(extra_ref[2], extra_ref[1, :8], w_ref, marks, 2)
    put_first_rows(win_ref, 2 * BLK, rows)
    for at, part, q_ref, out_ref in ((0, half, qown_ref, kept_ref), (BLK, 1 - half, qpair_ref, sent_ref)):
        squares = jnp.zeros((BLK, GROUP), jnp.float32)
        rows = pl.ds(pl.multiple_of(part * BLK, BLK), BLK)
        for g in range(groups):
            lanes = slice(g * GROUP, (g + 1) * GROUP)
            filtered = acc_ref[rows, lanes] + jnp.dot(
                table_ref[g, part, :, low * BLK : 3 * BLK],
                win_ref[low * BLK : 3 * BLK, lanes],
                preferred_element_type=jnp.float32,
            )
            if short:
                weight = summed * (part == 0).astype(jnp.float32)
                at_far = g * GROUP % far_refs[0].shape[1]
                far_ref = far_refs[g * GROUP // far_refs[0].shape[1]]
                filtered = filtered + weight * far_ref[:BLK, at_far : at_far + GROUP].astype(jnp.float32)
            gated = q_ref[:, lanes] * filtered
            squares = squares + gated * gated
            out_ref[:, lanes] = gated.astype(out_ref.dtype)
        power_ref[:, at : at + BLK] = lax.dot_general(
            jnp.ones((8, GROUP), jnp.float32),
            squares,
            (((1,), (1,)), ((), ())),
            precision=lax.Precision.HIGHEST,
            preferred_element_type=jnp.float32,
        )[0:1]


def norm_kernel(channels, power_ref, power_got_ref, kept_ref, got_ref, gain_ref, out_ref):
    half = lax.axis_index("half")
    width = kept_ref.shape[1]
    power = power_ref[:, :BLK] + power_got_ref[:, BLK:]
    scale = lax.rsqrt(power / channels + norm_eps)
    diagonal = lax.broadcasted_iota(jnp.int32, (BLK, BLK), 0) == lax.broadcasted_iota(
        jnp.int32, (BLK, BLK), 1
    )
    column = jnp.sum(jnp.where(diagonal, scale, 0.0), axis=1, keepdims=True)
    for which, part_ref in ((half, kept_ref), (1 - half, got_ref)):
        for c in range(0, width, GROUP):
            lanes = pl.ds(pl.multiple_of(which * width + c, GROUP), GROUP)
            out_ref[:, lanes] = (
                part_ref[:, c : c + GROUP].astype(jnp.float32) * column * gain_ref[:, lanes]
            ).astype(out_ref.dtype)


def kernel_call(body, outs, in_specs, scratch, flops, moved_bytes, vmem=24 << 20):
    return pl.pallas_call(
        body,
        out_shape=outs,
        in_specs=in_specs,
        out_specs=jax.tree.map(lambda _: VMEM, outs),
        scratch_shapes=scratch,
        compiler_params=pltpu.CompilerParams(vmem_limit_bytes=vmem),
        cost_estimate=pl.CostEstimate(flops=flops, bytes_accessed=moved_bytes, transcendentals=0),
    )


def shards(blocks, whole_tokens, channels, projected, short_weight, filter_taps, tap_blocks, skip_bias, norm_gain, seq_lengths):
    rows = projected.shape[0]
    width = projected.shape[2] // 2
    groups = width // GROUP
    taps = filter_taps.shape[1]
    shape = jax.ShapeDtypeStruct
    half_shape = shape((rows, width), jnp.bfloat16)
    half_wide = shape((rows, width), jnp.float32)

    spots = range(2 * blocks)
    to_pair = [(i, i ^ 1) for i in spots]
    ahead = [(i, (i + 2) % (2 * blocks)) for i in spots]

    panels = jnp.transpose(projected, (1, 0, 2))
    message = shape((rows + 8, width), jnp.bfloat16)
    small = shape((rows + 8, width // 2), jnp.bfloat16)
    hbm = pl.BlockSpec(memory_space=pltpu.HBM)
    pieces = 4
    row_mask = pltpu.VMEM((rows, GROUP), jnp.float32)

    kept, *sent = kernel_call(
        products_kernel,
        (message, small, small),
        [hbm] * 3,
        [
            pltpu.SMEM(seq_lengths.shape, jnp.int32),
            pltpu.VMEM((pieces, 2, rows, 2 * width // pieces), jnp.bfloat16),
            pltpu.VMEM((16, 2 * width), jnp.bfloat16),
            pltpu.VMEM(short_weight.shape, jnp.float32),
            pltpu.VMEM((4, rows + 8, GROUP), jnp.float32),
            row_mask,
            row_mask,
            pltpu.SemaphoreType.DMA((3 + pieces,)),
        ],
        40 * rows * width,
        16 * rows * width,
        60 << 20,
    )(seq_lengths, panels, short_weight)

    back_own = moved(kept, ahead)
    pair = [moved(piece, to_pair) for piece in sent]

    filter_taps, _ = lax.optimization_barrier((filter_taps, kept))
    scaled = (filter_taps * jnp.repeat(tap_blocks.astype(jnp.float32), BLK, axis=1)).astype(jnp.bfloat16)
    span = taps + 2 * BLK
    table, table_next, w_half = kernel_call(
        tables_kernel,
        (
            shape((groups, 2, BLK, span), jnp.bfloat16),
            shape((groups, BLK, 2 * BLK), jnp.bfloat16),
            shape((3, 3, width), jnp.float32),
        ),
        [SMEM, VMEM, VMEM],
        [pltpu.VMEM((2 * groups, span), jnp.float32), pltpu.VMEM((3, BLK, span), jnp.float32)],
        40 * groups * BLK * taps,
        8 * groups * BLK * taps,
    )(seq_lengths, scaled, short_weight)
    table, table_next, pair[0] = lax.optimization_barrier((table, table_next, pair[0]))

    half = lax.axis_index("half")
    query, _, back_own = lax.optimization_barrier((panels, pair[0], back_own))
    qkept = lax.dynamic_slice(query, (0, 0, half * width), (1, rows, width))[0]
    qsent = lax.dynamic_slice(query, (0, 0, (1 - half) * width), (1, rows, width))[0]
    qkept, qsent, pair[1] = lax.optimization_barrier((qkept, qsent, pair[1]))
    qgot = moved(qsent, to_pair)
    back_pair = [moved(piece, ahead) for piece in pair]

    window = pltpu.VMEM((4 * rows, width), jnp.bfloat16)
    extras = pltpu.VMEM((4, 16, width), jnp.float32)
    shifted = pltpu.VMEM((2, rows + 8, GROUP), jnp.float32)
    short = whole_tokens // 2 <= 4 * BLK
    if short:
        onward = [(i, i ^ 1 if i < 2 else i + 2 if i + 2 < 2 * blocks else 2 + i % 2) for i in spots]
        far = []
        for piece in range(2):
            relayed = kernel_call(
                functools.partial(relay_kernel, piece),
                small,
                [SMEM] + [VMEM] * 4,
                [pltpu.VMEM((2 * rows, width // 2), jnp.bfloat16), pltpu.VMEM((2, 16, width // 2), jnp.float32)],
                2 * rows * BLK * width,
                4 * rows * width,
            )(seq_lengths, table_next, back_own, back_pair[piece], w_half)
            far.append(moved(relayed, onward))
    else:
        across = jnp.concatenate([piece[rows:] for piece in sent], 1)
        across = moved(across, [(i, ((i ^ 1) + 6) % (2 * blocks)) for i in spots])
        straight = moved(kept[rows:], [(i, (i + 6) % (2 * blocks)) for i in spots])
        deep = jnp.where(half == 1, straight, across)
        far = [moved(piece, ahead) for piece in (back_own, *back_pair)] + [deep]

    acc, qown, marks = kernel_call(
        near_kernel,
        (shape((2 * rows, width), jnp.float32), half_wide, shape((3, 8, GROUP), jnp.float32)),
        [SMEM] + [VMEM] * 10,
        [window, extras, shifted, row_mask, row_mask],
        2 * 5 * rows * BLK * width,
        16 * rows * width,
    )(seq_lengths, table, kept, back_own, *pair, *back_pair, qkept, w_half, skip_bias.reshape(1, -1))

    qpair = kernel_call(
        pair_gate_kernel,
        half_wide,
        [SMEM] + [VMEM] * 4,
        [shifted, row_mask, row_mask],
        10 * rows * width,
        8 * rows * width,
    )(seq_lengths, qgot, kept, back_own, w_half)

    done, send, power = kernel_call(
        functools.partial(far_kernel, short),
        (half_wide, half_shape, shape((1, 2 * rows), jnp.float32)),
        [VMEM] * (9 + len(far)),
        [window, extras],
        2 * 5 * rows * BLK * width,
        24 * rows * width,
    )(table, acc, qown, qpair, w_half, marks, back_own, *back_pair, *far)

    back = moved(send, to_pair)
    peers = lax.axis_size("mp")
    shares = [lax.ppermute(power, "mp", [(i, i ^ k) for i in range(peers)]) for k in range(1, peers)]
    power = sum(shares, power)
    return kernel_call(
        functools.partial(norm_kernel, channels),
        shape((rows, 2 * width), jnp.bfloat16),
        [VMEM] * 5,
        [],
        8 * rows * width,
        10 * rows * width,
    )(power, moved(power, to_pair), done, back, norm_gain.reshape(1, -1))


def solution(mesh):
    blocks = mesh.shape["ctx"] // 2
    grid = Mesh(mesh.devices.reshape(blocks, 2, mesh.shape["mp"]), ("blk", "half", "mp"))
    in_specs = (
        P(SPOTS, None, "mp"),
        P(None, None, "mp"),
        P("mp", None),
        P("mp", None),
        P("mp"),
        P("mp"),
        P(),
    )

    def program(projected, *rest):
        body = functools.partial(shards, blocks, projected.shape[0], projected.shape[2])
        return jax.shard_map(
            body, mesh=grid, in_specs=in_specs, out_specs=P(SPOTS, "mp"), check_vma=False
        )(projected, *rest)

    return program
```

```python
import functools

import jax
import jax.numpy as jnp
from jax import lax
from jax.experimental import pallas as pl
from jax.experimental.pallas import tpu as pltpu
from jax.sharding import Mesh, PartitionSpec as P

GROUP = 128
BLK = 128
norm_eps = 1e-06

VMEM = pl.BlockSpec(memory_space=pltpu.VMEM)
SMEM = pl.BlockSpec(memory_space=pltpu.SMEM)
SPOTS = ("blk", "half")


def moved(block, pairs):
    return lax.ppermute(block, SPOTS, pairs)


def boundaries(seq_ref, t):
    def step(k, carry):
        end, first, second = carry
        end = end + seq_ref[k]
        return end, first | (t == end).astype(jnp.int32), second | (t - 1 == end).astype(jnp.int32)

    first = (t == 0).astype(jnp.int32)
    second = (t == 1).astype(jnp.int32)
    _, first, second = lax.fori_loop(0, seq_ref.shape[0], step, (jnp.int32(0), first, second), unroll=True)
    return first, first | second


def row_masks(seq_ref, start, m1_ref, m2_ref):
    rows = lax.broadcasted_iota(jnp.int32, (BLK, GROUP), 0)
    diagonal = rows == lax.broadcasted_iota(jnp.int32, (BLK, GROUP), 1)
    marks = boundaries(seq_ref, start + lax.broadcasted_iota(jnp.int32, (8, GROUP), 1))
    for mark, m_ref in zip(marks, (m1_ref, m2_ref)):
        keep = 1.0 - mark.astype(jnp.float32)[0:1]
        column = jnp.sum(jnp.where(diagonal, keep, 0.0), axis=1, keepdims=True)
        m_ref[...] = jnp.broadcast_to(column, (BLK, GROUP))


def counted(seq_ref, t):
    def step(k, carry):
        end, total = carry
        end = end + seq_ref[k]
        return end, total + (end <= t).astype(jnp.int32)

    _, total = lax.fori_loop(
        0, seq_ref.shape[0], step, (jnp.int32(0), jnp.zeros(t.shape, jnp.int32)), unroll=True
    )
    return jnp.where(t >= 0, total, -1)


def feature(x, x_ref, w, m1_ref, m2_ref):
    rows = x.shape[0]
    return (
        w[0:1] * x
        + w[1:2] * x_ref[7 : rows + 7, :] * m1_ref[...]
        + w[2:3] * x_ref[6 : rows + 6, :] * m2_ref[...]
    )


def products_kernel(seq_hbm, panels_hbm, w_hbm, kept_ref, *refs):
    *sent_refs, seq_ref, kv_ref, q_ref, w_ref, x_ref, m1_ref, m2_ref, sems = refs
    width = kept_ref.shape[1]
    rows = kv_ref.shape[2]
    pieces = kv_ref.shape[0]
    piece = kv_ref.shape[3]
    half = lax.axis_index("half")
    shard = lax.axis_index("blk") * 2 + half
    keep_at = pl.multiple_of(half * width, width)
    send_at = pl.multiple_of((1 - half) * width, width)

    loads = [pltpu.make_async_copy(seq_hbm, seq_ref, sems.at[0])]
    for p in range(pieces):
        at = keep_at if p < pieces // 2 else send_at
        lanes = pl.ds(pl.multiple_of(at + (p % (pieces // 2)) * piece, piece), piece)
        loads.append(pltpu.make_async_copy(panels_hbm.at[1:3, :, lanes], kv_ref.at[p], sems.at[1 + p]))
    loads.append(pltpu.make_async_copy(w_hbm, w_ref, sems.at[1 + pieces]))
    loads.append(pltpu.make_async_copy(panels_hbm.at[0, rows - 16 :, :], q_ref, sems.at[2 + pieces]))
    for load in loads:
        load.start()
    x_ref[:, 0:8, :] = jnp.zeros((x_ref.shape[0], 8, GROUP), jnp.float32)
    loads[0].wait()
    row_masks(seq_ref, shard * rows, m1_ref, m2_ref)
    loads[1 + pieces].wait()
    loads[2 + pieces].wait()
    for p in range(pieces):
        loads[1 + p].wait()
        out_ref, at = (kept_ref, keep_at) if p < pieces // 2 else (sent_refs[p - pieces // 2], send_at)
        for c in range(0, piece, GROUP):
            base = (p % (pieces // 2)) * piece + c
            there = slice(base, base + GROUP) if p < pieces // 2 else slice(c, c + GROUP)
            lanes = pl.ds(pl.multiple_of(at + base, GROUP), GROUP)
            slot = (c // GROUP) % (x_ref.shape[0] // 2) * 2
            raw, made = [], []
            for i in range(2):
                x = kv_ref[p, i, :, c : c + GROUP].astype(jnp.float32)
                x_ref[slot + i, 8:, :] = x
                made.append(feature(x, x_ref.at[slot + i], w_ref[1 + i, :, lanes], m1_ref, m2_ref))
                raw.append(x)
            product = made[0] * made[1]
            top = jnp.where(lax.broadcasted_iota(jnp.int32, (8, GROUP), 0) < 2, raw[0][:8], product[:8])
            out_ref[:rows, there] = jnp.concatenate([top, product[8:]], 0).astype(out_ref.dtype)
            tails = [x[rows - 2 :] for x in raw] + [q_ref[:, lanes].astype(jnp.float32)[14:]]
            out_ref[rows:, there] = jnp.concatenate([raw[1][0:2]] + tails, 0).astype(out_ref.dtype)


def edge_marks(seq_ref):
    t = (
        (lax.axis_index("blk") - 2) * (2 * BLK)
        + lax.broadcasted_iota(jnp.int32, (8, GROUP), 1) * BLK
        + lax.broadcasted_iota(jnp.int32, (8, GROUP), 0)
    )
    return [1.0 - mark.astype(jnp.float32) for mark in boundaries(seq_ref, t)]


def first_rows(now, ahead, w_ref, marks, spot, lanes=slice(None)):
    m1, m2 = [mark[:, spot : spot + 1] for mark in marks]
    top = lax.broadcasted_iota(jnp.int32, ahead.shape, 0) == 0
    made = []
    for i, x0 in enumerate((now[8:], now[:8])):
        x1 = jnp.where(top, pltpu.roll(ahead, 5 - 2 * i, 0), pltpu.roll(x0, 1, 0))
        x2 = pltpu.roll(ahead, 6 - 2 * i, 0)
        w = w_ref[1 + i, :, lanes]
        made.append(w[0:1] * x0 + w[1:2] * x1 * m1 + w[2:3] * x2 * m2)
    return made[0] * made[1]


def put_first_rows(win_ref, at, rows):
    old = win_ref[at : at + 16, :].astype(jnp.float32)
    new = jnp.concatenate([rows, rows], 0)
    first = lax.broadcasted_iota(jnp.int32, old.shape, 0) < 2
    win_ref[at : at + 16, :] = jnp.where(first, new, old).astype(win_ref.dtype)


def reaches_past(seq_ref, block):
    first = block * (2 * BLK)

    def step(k, carry):
        end, start = carry
        end = end + seq_ref[k]
        return end, jnp.where(end <= first, end, start)

    _, start = lax.fori_loop(0, seq_ref.shape[0], step, (jnp.int32(0), jnp.int32(0)), unroll=True)
    return first - 2 * BLK - start > BLK


def tables_kernel(seq_ref, taps_ref, w_ref, out_ref, next_ref, w_half_ref, rev_ref, m_ref):
    groups = out_ref.shape[0]
    taps = taps_ref.shape[1]
    span = out_ref.shape[3]
    half = lax.axis_index("half")
    start = lax.axis_index("blk") * (2 * BLK)
    width = w_half_ref.shape[2]
    w_half_ref[...] = w_ref[:, :, pl.ds(pl.multiple_of(half * width, width), width)]
    turn = lax.broadcasted_iota(jnp.int32, (taps, span), 0) + lax.broadcasted_iota(
        jnp.int32, (taps, span), 1
    )
    turn = (turn == taps).astype(jnp.bfloat16)
    rev_ref[...] = jnp.dot(taps_ref[...], turn, preferred_element_type=jnp.float32)
    seg_in = counted(seq_ref, start - taps + lax.broadcasted_iota(jnp.int32, (8, span), 1))[0:1]
    for part in range(3):
        t_out = start + part * BLK + lax.broadcasted_iota(jnp.int32, (BLK, GROUP), 0)
        seg_out = counted(seq_ref, t_out)[:, 0:1]
        if part < 2:
            m_ref[part] = (seg_in == seg_out).astype(jnp.float32)
        else:
            m_ref[2, :, : 2 * BLK] = (seg_in[:, 2 * BLK : 4 * BLK] == seg_out).astype(jnp.float32)

    def one(g, _):
        row = rev_ref[pl.ds(half * groups + g, 1), :]
        table = pltpu.roll(jnp.broadcast_to(row, (BLK, span)), 0, 1, stride=1, stride_axis=0)
        out_ref[g, 0] = (table * m_ref[0]).astype(out_ref.dtype)
        later = jnp.concatenate([table[:, span - BLK :], table[:, : span - BLK]], 1)
        out_ref[g, 1] = (later * m_ref[1]).astype(out_ref.dtype)
        next_ref[g] = (table[:, : 2 * BLK] * m_ref[2, :, : 2 * BLK]).astype(next_ref.dtype)
        return 0

    lax.fori_loop(0, groups, one, 0)


def fill(win_ref, extra_ref, spot, *pieces):
    at = 0
    for piece in pieces:
        lanes = slice(at, at + piece.shape[1])
        win_ref[pl.ds(pl.multiple_of(spot * BLK, BLK), BLK), lanes] = piece[:BLK]
        extra_ref[spot, :8, lanes] = piece[BLK:].astype(jnp.float32)
        extra_ref[spot, 8:, lanes] = piece[:16].astype(jnp.float32)[:8]
        at += piece.shape[1]


def relay_kernel(piece, seq_ref, next_ref, back_own_ref, back_pair_ref, w_ref, out_ref, win_ref, extra_ref):
    width = out_ref.shape[1]
    half = lax.axis_index("half")
    lanes = slice(piece * width, (piece + 1) * width)
    fill(win_ref, extra_ref, half, back_own_ref.at[:, lanes])
    fill(win_ref, extra_ref, 1 - half, back_pair_ref)
    marks = edge_marks(seq_ref)
    put_first_rows(win_ref, 0, first_rows(extra_ref[0], jnp.zeros((8, width), jnp.float32), w_ref, marks, 2, lanes))
    put_first_rows(win_ref, BLK, first_rows(extra_ref[1], extra_ref[0, :8], w_ref, marks, 3, lanes))
    out_ref[BLK:] = extra_ref[1, :8].astype(out_ref.dtype)
    summed = reaches_past(seq_ref, lax.axis_index("blk") + 1)

    @pl.when(summed)
    def _():
        for c in range(0, width, GROUP):
            total = jnp.dot(
                next_ref[(piece * width + c) // GROUP],
                win_ref[:, c : c + GROUP],
                preferred_element_type=jnp.float32,
            )
            out_ref[:BLK, c : c + GROUP] = total.astype(out_ref.dtype)

    @pl.when(jnp.logical_not(summed))
    def _():
        out_ref[:BLK] = win_ref[BLK:]


def gate_rows(seq_ref, raw_ref, tail, w_ref, part, q_ref, x_ref, m1_ref, m2_ref):
    width = raw_ref.shape[1]
    row_masks(seq_ref, lax.axis_index("blk") * (2 * BLK) + part * BLK, m1_ref, m2_ref)
    for c in range(0, width, GROUP):
        lanes = slice(c, c + GROUP)
        w = w_ref[0, :, lanes]
        x = raw_ref[:, lanes].astype(jnp.float32)
        slot = (c // GROUP) % 2
        x_ref[slot, 6:8, :] = tail(lanes)
        x_ref[slot, 8:, :] = x
        q_ref[:, lanes] = feature(x, x_ref.at[slot], w, m1_ref, m2_ref)


def near_kernel(
    seq_ref, table_ref, own_ref, back_own_ref, pair_a_ref, pair_b_ref, back_a_ref, back_b_ref, qkept_ref, w_ref, bias_ref,
    acc_ref, q_ref, marks_ref, win_ref, extra_ref, x_ref, m1_ref, m2_ref,
):
    groups = table_ref.shape[0]
    width = groups * GROUP
    half = lax.axis_index("half")
    block = lax.axis_index("blk")
    fill(win_ref, extra_ref, half, back_own_ref)
    fill(win_ref, extra_ref, 1 - half, back_a_ref, back_b_ref)
    fill(win_ref, extra_ref, 2 + half, own_ref)
    fill(win_ref, extra_ref, 3 - half, pair_a_ref, pair_b_ref)
    marks = edge_marks(seq_ref)
    marks_ref[0], marks_ref[1] = marks
    marks_ref[2] = jnp.full((8, GROUP), reaches_past(seq_ref, block).astype(jnp.float32))
    for spot in (1, 2, 3):
        rows = first_rows(extra_ref[spot], extra_ref[spot - 1, :8], w_ref, marks, spot + 2)
        put_first_rows(win_ref, spot * BLK, rows)
    for g in range(groups):
        lanes = slice(g * GROUP, (g + 1) * GROUP)
        bias = bias_ref[:, pl.ds(pl.multiple_of(half * width + g * GROUP, GROUP), GROUP)]
        for part in range(2):
            total = jnp.dot(
                table_ref[g, part, :, 3 * BLK : (5 + part) * BLK],
                win_ref[BLK : (3 + part) * BLK, lanes],
                preferred_element_type=jnp.float32,
            )
            here = win_ref[(2 + part) * BLK : (3 + part) * BLK, lanes].astype(jnp.float32)
            acc_ref[part * BLK : (part + 1) * BLK, lanes] = total + bias * here
    gate_rows(
        seq_ref, qkept_ref, lambda lanes: extra_ref[1 + half, 6:8, lanes], w_ref, half, q_ref, x_ref, m1_ref, m2_ref
    )


def pair_gate_kernel(seq_ref, raw_ref, own_ref, back_own_ref, w_ref, q_ref, x_ref, m1_ref, m2_ref):
    half = lax.axis_index("half")

    def tail(lanes):
        back = back_own_ref[BLK:, lanes].astype(jnp.float32)
        own = own_ref[BLK:, lanes].astype(jnp.float32)
        return jnp.where(half == 1, back, own)[6:8]

    gate_rows(seq_ref, raw_ref, tail, w_ref, 1 - half, q_ref, x_ref, m1_ref, m2_ref)


def far_kernel(short, table_ref, acc_ref, qown_ref, qpair_ref, w_ref, marks_ref, *refs):
    *messages, kept_ref, sent_ref, power_ref, win_ref, extra_ref = refs
    groups = table_ref.shape[0]
    width = groups * GROUP
    half = lax.axis_index("half")
    marks = [marks_ref[0], marks_ref[1]]
    back_own_ref, back_a_ref, back_b_ref, *far_refs = messages
    low = 1 if short else 0
    fill(win_ref, extra_ref, 2 + half, back_own_ref)
    fill(win_ref, extra_ref, 3 - half, back_a_ref, back_b_ref)
    if short:
        summed = marks_ref[2, 0:1, 0:1]
        fill(win_ref, extra_ref, 1, *far_refs)
        payload = win_ref[BLK : 2 * BLK, :].astype(jnp.float32)
        win_ref[BLK : 2 * BLK, :] = (payload * (1.0 - summed)).astype(win_ref.dtype)
    else:
        fill(win_ref, extra_ref, half, far_refs[0])
        fill(win_ref, extra_ref, 1 - half, far_refs[1], far_refs[2])
        ahead = far_refs[3][...].astype(jnp.float32)
        put_first_rows(win_ref, 0, first_rows(extra_ref[0], ahead, w_ref, marks, 0))
        rows = first_rows(extra_ref[1], extra_ref[0, :8], w_ref, marks, 1)
        put_first_rows(win_ref, BLK, rows)
    rows = first_rows(extra_ref[2], extra_ref[1, :8], w_ref, marks, 2)
    put_first_rows(win_ref, 2 * BLK, rows)
    for at, part, q_ref, out_ref in ((0, half, qown_ref, kept_ref), (BLK, 1 - half, qpair_ref, sent_ref)):
        squares = jnp.zeros((BLK, GROUP), jnp.float32)
        rows = pl.ds(pl.multiple_of(part * BLK, BLK), BLK)
        for g in range(groups):
            lanes = slice(g * GROUP, (g + 1) * GROUP)
            filtered = acc_ref[rows, lanes] + jnp.dot(
                table_ref[g, part, :, low * BLK : 3 * BLK],
                win_ref[low * BLK : 3 * BLK, lanes],
                preferred_element_type=jnp.float32,
            )
            if short:
                weight = summed * (part == 0).astype(jnp.float32)
                at_far = g * GROUP % far_refs[0].shape[1]
                far_ref = far_refs[g * GROUP // far_refs[0].shape[1]]
                filtered = filtered + weight * far_ref[:BLK, at_far : at_far + GROUP].astype(jnp.float32)
            gated = q_ref[:, lanes] * filtered
            squares = squares + gated * gated
            out_ref[:, lanes] = gated.astype(out_ref.dtype)
        power_ref[:, at : at + BLK] = lax.dot_general(
            jnp.ones((8, GROUP), jnp.float32),
            squares,
            (((1,), (1,)), ((), ())),
            precision=lax.Precision.HIGHEST,
            preferred_element_type=jnp.float32,
        )[0:1]


def norm_kernel(channels, power_ref, power_got_ref, kept_ref, got_ref, gain_ref, out_ref):
    half = lax.axis_index("half")
    width = kept_ref.shape[1]
    power = power_ref[:, :BLK] + power_got_ref[:, BLK:]
    scale = lax.rsqrt(power / channels + norm_eps)
    diagonal = lax.broadcasted_iota(jnp.int32, (BLK, BLK), 0) == lax.broadcasted_iota(
        jnp.int32, (BLK, BLK), 1
    )
    column = jnp.sum(jnp.where(diagonal, scale, 0.0), axis=1, keepdims=True)
    for which, part_ref in ((half, kept_ref), (1 - half, got_ref)):
        for c in range(0, width, GROUP):
            lanes = pl.ds(pl.multiple_of(which * width + c, GROUP), GROUP)
            out_ref[:, lanes] = (
                part_ref[:, c : c + GROUP].astype(jnp.float32) * column * gain_ref[:, lanes]
            ).astype(out_ref.dtype)


def kernel_call(body, outs, in_specs, scratch, flops, moved_bytes, vmem=24 << 20):
    return pl.pallas_call(
        body,
        out_shape=outs,
        in_specs=in_specs,
        out_specs=jax.tree.map(lambda _: VMEM, outs),
        scratch_shapes=scratch,
        compiler_params=pltpu.CompilerParams(vmem_limit_bytes=vmem),
        cost_estimate=pl.CostEstimate(flops=flops, bytes_accessed=moved_bytes, transcendentals=0),
    )


def shards(blocks, whole_tokens, channels, projected, short_weight, filter_taps, tap_blocks, skip_bias, norm_gain, seq_lengths):
    rows = projected.shape[0]
    width = projected.shape[2] // 2
    groups = width // GROUP
    taps = filter_taps.shape[1]
    shape = jax.ShapeDtypeStruct
    half_shape = shape((rows, width), jnp.bfloat16)
    half_wide = shape((rows, width), jnp.float32)

    spots = range(2 * blocks)
    to_pair = [(i, i ^ 1) for i in spots]
    ahead = [(i, (i + 2) % (2 * blocks)) for i in spots]

    panels = jnp.transpose(projected, (1, 0, 2))
    message = shape((rows + 8, width), jnp.bfloat16)
    small = shape((rows + 8, width // 2), jnp.bfloat16)
    hbm = pl.BlockSpec(memory_space=pltpu.HBM)
    pieces = 4
    row_mask = pltpu.VMEM((rows, GROUP), jnp.float32)

    kept, *sent = kernel_call(
        products_kernel,
        (message, small, small),
        [hbm] * 3,
        [
            pltpu.SMEM(seq_lengths.shape, jnp.int32),
            pltpu.VMEM((pieces, 2, rows, 2 * width // pieces), jnp.bfloat16),
            pltpu.VMEM((16, 2 * width), jnp.bfloat16),
            pltpu.VMEM(short_weight.shape, jnp.float32),
            pltpu.VMEM((4, rows + 8, GROUP), jnp.float32),
            row_mask,
            row_mask,
            pltpu.SemaphoreType.DMA((3 + pieces,)),
        ],
        40 * rows * width,
        16 * rows * width,
        60 << 20,
    )(seq_lengths, panels, short_weight)

    back_own = moved(kept, ahead)
    pair = [moved(piece, to_pair) for piece in sent]

    filter_taps, _ = lax.optimization_barrier((filter_taps, kept))
    scaled = (filter_taps * jnp.repeat(tap_blocks.astype(jnp.float32), BLK, axis=1)).astype(jnp.bfloat16)
    span = taps + 2 * BLK
    table, table_next, w_half = kernel_call(
        tables_kernel,
        (
            shape((groups, 2, BLK, span), jnp.bfloat16),
            shape((groups, BLK, 2 * BLK), jnp.bfloat16),
            shape((3, 3, width), jnp.float32),
        ),
        [SMEM, VMEM, VMEM],
        [pltpu.VMEM((2 * groups, span), jnp.float32), pltpu.VMEM((3, BLK, span), jnp.float32)],
        40 * groups * BLK * taps,
        8 * groups * BLK * taps,
    )(seq_lengths, scaled, short_weight)
    table, table_next, pair[0] = lax.optimization_barrier((table, table_next, pair[0]))

    half = lax.axis_index("half")
    query, _ = lax.optimization_barrier((panels, pair[0]))
    qkept = lax.dynamic_slice(query, (0, 0, half * width), (1, rows, width))[0]
    qsent = lax.dynamic_slice(query, (0, 0, (1 - half) * width), (1, rows, width))[0]
    qkept, qsent, pair[1] = lax.optimization_barrier((qkept, qsent, pair[1]))
    qgot = moved(qsent, to_pair)
    back_pair = [moved(piece, ahead) for piece in pair]

    window = pltpu.VMEM((4 * rows, width), jnp.bfloat16)
    extras = pltpu.VMEM((4, 16, width), jnp.float32)
    shifted = pltpu.VMEM((2, rows + 8, GROUP), jnp.float32)
    short = whole_tokens // 2 <= 4 * BLK
    if short:
        onward = [(i, i ^ 1 if i < 2 else i + 2 if i + 2 < 2 * blocks else 2 + i % 2) for i in spots]
        far = []
        for piece in range(2):
            relayed = kernel_call(
                functools.partial(relay_kernel, piece),
                small,
                [SMEM] + [VMEM] * 4,
                [pltpu.VMEM((2 * rows, width // 2), jnp.bfloat16), pltpu.VMEM((2, 16, width // 2), jnp.float32)],
                2 * rows * BLK * width,
                4 * rows * width,
            )(seq_lengths, table_next, back_own, back_pair[piece], w_half)
            far.append(moved(relayed, onward))
    else:
        across = jnp.concatenate([piece[rows:] for piece in sent], 1)
        across = moved(across, [(i, ((i ^ 1) + 6) % (2 * blocks)) for i in spots])
        straight = moved(kept[rows:], [(i, (i + 6) % (2 * blocks)) for i in spots])
        deep = jnp.where(half == 1, straight, across)
        far = [moved(piece, ahead) for piece in (back_own, *back_pair)] + [deep]

    acc, qown, marks = kernel_call(
        near_kernel,
        (shape((2 * rows, width), jnp.float32), half_wide, shape((3, 8, GROUP), jnp.float32)),
        [SMEM] + [VMEM] * 10,
        [window, extras, shifted, row_mask, row_mask],
        2 * 5 * rows * BLK * width,
        16 * rows * width,
    )(seq_lengths, table, kept, back_own, *pair, *back_pair, qkept, w_half, skip_bias.reshape(1, -1))

    qpair = kernel_call(
        pair_gate_kernel,
        half_wide,
        [SMEM] + [VMEM] * 4,
        [shifted, row_mask, row_mask],
        10 * rows * width,
        8 * rows * width,
    )(seq_lengths, qgot, kept, back_own, w_half)

    done, send, power = kernel_call(
        functools.partial(far_kernel, short),
        (half_wide, half_shape, shape((1, 2 * rows), jnp.float32)),
        [VMEM] * (9 + len(far)),
        [window, extras],
        2 * 5 * rows * BLK * width,
        24 * rows * width,
    )(table, acc, qown, qpair, w_half, marks, back_own, *back_pair, *far)

    back = moved(send, to_pair)
    peers = lax.axis_size("mp")
    shares = [lax.ppermute(power, "mp", [(i, i ^ k) for i in range(peers)]) for k in range(1, peers)]
    power = sum(shares, power)
    return kernel_call(
        functools.partial(norm_kernel, channels),
        shape((rows, 2 * width), jnp.bfloat16),
        [VMEM] * 5,
        [],
        8 * rows * width,
        10 * rows * width,
    )(power, moved(power, to_pair), done, back, norm_gain.reshape(1, -1))


def solution(mesh):
    blocks = mesh.shape["ctx"] // 2
    grid = Mesh(mesh.devices.reshape(blocks, 2, mesh.shape["mp"]), ("blk", "half", "mp"))
    in_specs = (
        P(SPOTS, None, "mp"),
        P(None, None, "mp"),
        P("mp", None),
        P("mp", None),
        P("mp"),
        P("mp"),
        P(),
    )

    def program(projected, *rest):
        body = functools.partial(shards, blocks, projected.shape[0], projected.shape[2])
        return jax.shard_map(
            body, mesh=grid, in_specs=in_specs, out_specs=P(SPOTS, "mp"), check_vma=False
        )(projected, *rest)

    return program
```

```python
import functools

import jax
import jax.numpy as jnp
from jax import lax
from jax.experimental import pallas as pl
from jax.experimental.pallas import tpu as pltpu
from jax.sharding import Mesh, PartitionSpec as P

GROUP = 128
BLK = 128
norm_eps = 1e-06

VMEM = pl.BlockSpec(memory_space=pltpu.VMEM)
SMEM = pl.BlockSpec(memory_space=pltpu.SMEM)
SPOTS = ("blk", "half")


def moved(block, pairs):
    return lax.ppermute(block, SPOTS, pairs)


def boundaries(seq_ref, t):
    def step(k, carry):
        end, first, second = carry
        end = end + seq_ref[k]
        return end, first | (t == end).astype(jnp.int32), second | (t - 1 == end).astype(jnp.int32)

    first = (t == 0).astype(jnp.int32)
    second = (t == 1).astype(jnp.int32)
    _, first, second = lax.fori_loop(0, seq_ref.shape[0], step, (jnp.int32(0), first, second), unroll=True)
    return first, first | second


def row_masks(seq_ref, start, m1_ref, m2_ref):
    rows = lax.broadcasted_iota(jnp.int32, (BLK, GROUP), 0)
    diagonal = rows == lax.broadcasted_iota(jnp.int32, (BLK, GROUP), 1)
    marks = boundaries(seq_ref, start + lax.broadcasted_iota(jnp.int32, (8, GROUP), 1))
    for mark, m_ref in zip(marks, (m1_ref, m2_ref)):
        keep = 1.0 - mark.astype(jnp.float32)[0:1]
        column = jnp.sum(jnp.where(diagonal, keep, 0.0), axis=1, keepdims=True)
        m_ref[...] = jnp.broadcast_to(column, (BLK, GROUP))


def counted(seq_ref, t):
    def step(k, carry):
        end, total = carry
        end = end + seq_ref[k]
        return end, total + (end <= t).astype(jnp.int32)

    _, total = lax.fori_loop(
        0, seq_ref.shape[0], step, (jnp.int32(0), jnp.zeros(t.shape, jnp.int32)), unroll=True
    )
    return jnp.where(t >= 0, total, -1)


def feature(x, x_ref, w, m1_ref, m2_ref):
    rows = x.shape[0]
    return (
        w[0:1] * x
        + w[1:2] * x_ref[7 : rows + 7, :] * m1_ref[...]
        + w[2:3] * x_ref[6 : rows + 6, :] * m2_ref[...]
    )


def products_kernel(seq_hbm, panels_hbm, w_hbm, kept_ref, *refs):
    *sent_refs, seq_ref, kv_ref, q_ref, w_ref, x_ref, m1_ref, m2_ref, sems = refs
    width = kept_ref.shape[1]
    rows = kv_ref.shape[2]
    pieces = kv_ref.shape[0]
    piece = kv_ref.shape[3]
    half = lax.axis_index("half")
    shard = lax.axis_index("blk") * 2 + half
    keep_at = pl.multiple_of(half * width, width)
    send_at = pl.multiple_of((1 - half) * width, width)

    loads = [pltpu.make_async_copy(seq_hbm, seq_ref, sems.at[0])]
    for p in range(pieces):
        at = keep_at if p < pieces // 2 else send_at
        lanes = pl.ds(pl.multiple_of(at + (p % (pieces // 2)) * piece, piece), piece)
        loads.append(pltpu.make_async_copy(panels_hbm.at[1:3, :, lanes], kv_ref.at[p], sems.at[1 + p]))
    loads.append(pltpu.make_async_copy(w_hbm, w_ref, sems.at[1 + pieces]))
    loads.append(pltpu.make_async_copy(panels_hbm.at[0, rows - 16 :, :], q_ref, sems.at[2 + pieces]))
    for load in loads:
        load.start()
    x_ref[:, 0:8, :] = jnp.zeros((x_ref.shape[0], 8, GROUP), jnp.float32)
    loads[0].wait()
    row_masks(seq_ref, shard * rows, m1_ref, m2_ref)
    loads[1 + pieces].wait()
    loads[2 + pieces].wait()
    for p in range(pieces):
        loads[1 + p].wait()
        out_ref, at = (kept_ref, keep_at) if p < pieces // 2 else (sent_refs[p - pieces // 2], send_at)
        for c in range(0, piece, GROUP):
            base = (p % (pieces // 2)) * piece + c
            there = slice(base, base + GROUP) if p < pieces // 2 else slice(c, c + GROUP)
            lanes = pl.ds(pl.multiple_of(at + base, GROUP), GROUP)
            slot = (c // GROUP) % (x_ref.shape[0] // 2) * 2
            raw, made = [], []
            for i in range(2):
                x = kv_ref[p, i, :, c : c + GROUP].astype(jnp.float32)
                x_ref[slot + i, 8:, :] = x
                made.append(feature(x, x_ref.at[slot + i], w_ref[1 + i, :, lanes], m1_ref, m2_ref))
                raw.append(x)
            product = made[0] * made[1]
            top = jnp.where(lax.broadcasted_iota(jnp.int32, (8, GROUP), 0) < 2, raw[0][:8], product[:8])
            out_ref[:rows, there] = jnp.concatenate([top, product[8:]], 0).astype(out_ref.dtype)
            tails = [x[rows - 2 :] for x in raw] + [q_ref[:, lanes].astype(jnp.float32)[14:]]
            out_ref[rows:, there] = jnp.concatenate([raw[1][0:2]] + tails, 0).astype(out_ref.dtype)


def edge_marks(seq_ref):
    t = (
        (lax.axis_index("blk") - 2) * (2 * BLK)
        + lax.broadcasted_iota(jnp.int32, (8, GROUP), 1) * BLK
        + lax.broadcasted_iota(jnp.int32, (8, GROUP), 0)
    )
    return [1.0 - mark.astype(jnp.float32) for mark in boundaries(seq_ref, t)]


def first_rows(now, ahead, w_ref, marks, spot, lanes=slice(None)):
    m1, m2 = [mark[:, spot : spot + 1] for mark in marks]
    top = lax.broadcasted_iota(jnp.int32, ahead.shape, 0) == 0
    made = []
    for i, x0 in enumerate((now[8:], now[:8])):
        x1 = jnp.where(top, pltpu.roll(ahead, 5 - 2 * i, 0), pltpu.roll(x0, 1, 0))
        x2 = pltpu.roll(ahead, 6 - 2 * i, 0)
        w = w_ref[1 + i, :, lanes]
        made.append(w[0:1] * x0 + w[1:2] * x1 * m1 + w[2:3] * x2 * m2)
    return made[0] * made[1]


def put_first_rows(win_ref, at, rows):
    old = win_ref[at : at + 16, :].astype(jnp.float32)
    new = jnp.concatenate([rows, rows], 0)
    first = lax.broadcasted_iota(jnp.int32, old.shape, 0) < 2
    win_ref[at : at + 16, :] = jnp.where(first, new, old).astype(win_ref.dtype)


def reaches_past(seq_ref, block):
    first = block * (2 * BLK)

    def step(k, carry):
        end, start = carry
        end = end + seq_ref[k]
        return end, jnp.where(end <= first, end, start)

    _, start = lax.fori_loop(0, seq_ref.shape[0], step, (jnp.int32(0), jnp.int32(0)), unroll=True)
    return first - 2 * BLK - start > BLK


def tables_kernel(seq_ref, taps_ref, w_ref, out_ref, next_ref, w_half_ref, rev_ref, m_ref):
    groups = out_ref.shape[0]
    taps = taps_ref.shape[1]
    span = out_ref.shape[3]
    half = lax.axis_index("half")
    start = lax.axis_index("blk") * (2 * BLK)
    width = w_half_ref.shape[2]
    w_half_ref[...] = w_ref[:, :, pl.ds(pl.multiple_of(half * width, width), width)]
    turn = lax.broadcasted_iota(jnp.int32, (taps, span), 0) + lax.broadcasted_iota(
        jnp.int32, (taps, span), 1
    )
    turn = (turn == taps).astype(jnp.bfloat16)
    rev_ref[...] = jnp.dot(taps_ref[...], turn, preferred_element_type=jnp.float32)
    seg_in = counted(seq_ref, start - taps + lax.broadcasted_iota(jnp.int32, (8, span), 1))[0:1]
    for part in range(3):
        t_out = start + part * BLK + lax.broadcasted_iota(jnp.int32, (BLK, GROUP), 0)
        seg_out = counted(seq_ref, t_out)[:, 0:1]
        if part < 2:
            m_ref[part] = (seg_in == seg_out).astype(jnp.float32)
        else:
            m_ref[2, :, : 2 * BLK] = (seg_in[:, 2 * BLK : 4 * BLK] == seg_out).astype(jnp.float32)

    def one(g, _):
        row = rev_ref[pl.ds(half * groups + g, 1), :]
        table = pltpu.roll(jnp.broadcast_to(row, (BLK, span)), 0, 1, stride=1, stride_axis=0)
        out_ref[g, 0] = (table * m_ref[0]).astype(out_ref.dtype)
        later = jnp.concatenate([table[:, span - BLK :], table[:, : span - BLK]], 1)
        out_ref[g, 1] = (later * m_ref[1]).astype(out_ref.dtype)
        next_ref[g] = (table[:, : 2 * BLK] * m_ref[2, :, : 2 * BLK]).astype(next_ref.dtype)
        return 0

    lax.fori_loop(0, groups, one, 0)


def fill(win_ref, extra_ref, spot, *pieces):
    at = 0
    for piece in pieces:
        lanes = slice(at, at + piece.shape[1])
        win_ref[pl.ds(pl.multiple_of(spot * BLK, BLK), BLK), lanes] = piece[:BLK]
        extra_ref[spot, :8, lanes] = piece[BLK:].astype(jnp.float32)
        extra_ref[spot, 8:, lanes] = piece[:16].astype(jnp.float32)[:8]
        at += piece.shape[1]


def relay_kernel(piece, seq_ref, next_ref, back_own_ref, back_pair_ref, w_ref, out_ref, win_ref, extra_ref):
    width = out_ref.shape[1]
    half = lax.axis_index("half")
    lanes = slice(piece * width, (piece + 1) * width)
    fill(win_ref, extra_ref, half, back_own_ref.at[:, lanes])
    fill(win_ref, extra_ref, 1 - half, back_pair_ref)
    marks = edge_marks(seq_ref)
    put_first_rows(win_ref, 0, first_rows(extra_ref[0], jnp.zeros((8, width), jnp.float32), w_ref, marks, 2, lanes))
    put_first_rows(win_ref, BLK, first_rows(extra_ref[1], extra_ref[0, :8], w_ref, marks, 3, lanes))
    out_ref[BLK:] = extra_ref[1, :8].astype(out_ref.dtype)
    summed = reaches_past(seq_ref, lax.axis_index("blk") + 1)

    @pl.when(summed)
    def _():
        for c in range(0, width, GROUP):
            total = jnp.dot(
                next_ref[(piece * width + c) // GROUP],
                win_ref[:, c : c + GROUP],
                preferred_element_type=jnp.float32,
            )
            out_ref[:BLK, c : c + GROUP] = total.astype(out_ref.dtype)

    @pl.when(jnp.logical_not(summed))
    def _():
        out_ref[:BLK] = win_ref[BLK:]


def gate_rows(seq_ref, raw_ref, tail, w_ref, part, q_ref, x_ref, m1_ref, m2_ref):
    width = raw_ref.shape[1]
    row_masks(seq_ref, lax.axis_index("blk") * (2 * BLK) + part * BLK, m1_ref, m2_ref)
    for c in range(0, width, GROUP):
        lanes = slice(c, c + GROUP)
        w = w_ref[0, :, lanes]
        x = raw_ref[:, lanes].astype(jnp.float32)
        slot = (c // GROUP) % 2
        x_ref[slot, 6:8, :] = tail(lanes)
        x_ref[slot, 8:, :] = x
        q_ref[:, lanes] = feature(x, x_ref.at[slot], w, m1_ref, m2_ref)


def near_kernel(
    seq_ref, table_ref, own_ref, back_own_ref, pair_a_ref, pair_b_ref, back_a_ref, back_b_ref, qkept_ref, w_ref, bias_ref,
    acc_ref, q_ref, marks_ref, win_ref, extra_ref, x_ref, m1_ref, m2_ref,
):
    groups = table_ref.shape[0]
    width = groups * GROUP
    half = lax.axis_index("half")
    block = lax.axis_index("blk")
    fill(win_ref, extra_ref, half, back_own_ref)
    fill(win_ref, extra_ref, 1 - half, back_a_ref, back_b_ref)
    fill(win_ref, extra_ref, 2 + half, own_ref)
    fill(win_ref, extra_ref, 3 - half, pair_a_ref, pair_b_ref)
    marks = edge_marks(seq_ref)
    marks_ref[0], marks_ref[1] = marks
    marks_ref[2] = jnp.full((8, GROUP), reaches_past(seq_ref, block).astype(jnp.float32))
    for spot in (1, 2, 3):
        rows = first_rows(extra_ref[spot], extra_ref[spot - 1, :8], w_ref, marks, spot + 2)
        put_first_rows(win_ref, spot * BLK, rows)
    for g in range(groups):
        lanes = slice(g * GROUP, (g + 1) * GROUP)
        bias = bias_ref[:, pl.ds(pl.multiple_of(half * width + g * GROUP, GROUP), GROUP)]
        for part in range(2):
            total = jnp.dot(
                table_ref[g, part, :, 3 * BLK : (5 + part) * BLK],
                win_ref[BLK : (3 + part) * BLK, lanes],
                preferred_element_type=jnp.float32,
            )
            here = win_ref[(2 + part) * BLK : (3 + part) * BLK, lanes].astype(jnp.float32)
            acc_ref[part * BLK : (part + 1) * BLK, lanes] = total + bias * here
    gate_rows(
        seq_ref, qkept_ref, lambda lanes: extra_ref[1 + half, 6:8, lanes], w_ref, half, q_ref, x_ref, m1_ref, m2_ref
    )


def pair_gate_kernel(seq_ref, raw_ref, own_ref, back_own_ref, w_ref, q_ref, x_ref, m1_ref, m2_ref):
    half = lax.axis_index("half")

    def tail(lanes):
        back = back_own_ref[BLK:, lanes].astype(jnp.float32)
        own = own_ref[BLK:, lanes].astype(jnp.float32)
        return jnp.where(half == 1, back, own)[6:8]

    gate_rows(seq_ref, raw_ref, tail, w_ref, 1 - half, q_ref, x_ref, m1_ref, m2_ref)


def far_kernel(short, table_ref, acc_ref, qown_ref, qpair_ref, w_ref, marks_ref, *refs):
    *messages, kept_ref, sent_ref, power_ref, win_ref, extra_ref = refs
    groups = table_ref.shape[0]
    width = groups * GROUP
    half = lax.axis_index("half")
    marks = [marks_ref[0], marks_ref[1]]
    back_own_ref, back_a_ref, back_b_ref, *far_refs = messages
    low = 1 if short else 0
    fill(win_ref, extra_ref, 2 + half, back_own_ref)
    fill(win_ref, extra_ref, 3 - half, back_a_ref, back_b_ref)
    if short:
        summed = marks_ref[2, 0:1, 0:1]
        fill(win_ref, extra_ref, 1, *far_refs)
        payload = win_ref[BLK : 2 * BLK, :].astype(jnp.float32)
        win_ref[BLK : 2 * BLK, :] = (payload * (1.0 - summed)).astype(win_ref.dtype)
    else:
        fill(win_ref, extra_ref, half, far_refs[0])
        fill(win_ref, extra_ref, 1 - half, far_refs[1], far_refs[2])
        ahead = far_refs[3][...].astype(jnp.float32)
        put_first_rows(win_ref, 0, first_rows(extra_ref[0], ahead, w_ref, marks, 0))
        rows = first_rows(extra_ref[1], extra_ref[0, :8], w_ref, marks, 1)
        put_first_rows(win_ref, BLK, rows)
    rows = first_rows(extra_ref[2], extra_ref[1, :8], w_ref, marks, 2)
    put_first_rows(win_ref, 2 * BLK, rows)
    for at, part, q_ref, out_ref in ((0, half, qown_ref, kept_ref), (BLK, 1 - half, qpair_ref, sent_ref)):
        squares = jnp.zeros((BLK, GROUP), jnp.float32)
        rows = pl.ds(pl.multiple_of(part * BLK, BLK), BLK)
        for g in range(groups):
            lanes = slice(g * GROUP, (g + 1) * GROUP)
            filtered = acc_ref[rows, lanes] + jnp.dot(
                table_ref[g, part, :, low * BLK : 3 * BLK],
                win_ref[low * BLK : 3 * BLK, lanes],
                preferred_element_type=jnp.float32,
            )
            if short:
                weight = summed * (part == 0).astype(jnp.float32)
                at_far = g * GROUP % far_refs[0].shape[1]
                far_ref = far_refs[g * GROUP // far_refs[0].shape[1]]
                filtered = filtered + weight * far_ref[:BLK, at_far : at_far + GROUP].astype(jnp.float32)
            gated = q_ref[:, lanes] * filtered
            squares = squares + gated * gated
            out_ref[:, lanes] = gated.astype(out_ref.dtype)
        power_ref[:, at : at + BLK] = lax.dot_general(
            jnp.ones((8, GROUP), jnp.float32),
            squares,
            (((1,), (1,)), ((), ())),
            precision=lax.Precision.HIGHEST,
            preferred_element_type=jnp.float32,
        )[0:1]


def norm_kernel(channels, power_ref, power_got_ref, kept_ref, got_ref, gain_ref, out_ref):
    half = lax.axis_index("half")
    width = kept_ref.shape[1]
    power = power_ref[:, :BLK] + power_got_ref[:, BLK:]
    scale = lax.rsqrt(power / channels + norm_eps)
    diagonal = lax.broadcasted_iota(jnp.int32, (BLK, BLK), 0) == lax.broadcasted_iota(
        jnp.int32, (BLK, BLK), 1
    )
    column = jnp.sum(jnp.where(diagonal, scale, 0.0), axis=1, keepdims=True)
    for which, part_ref in ((half, kept_ref), (1 - half, got_ref)):
        for c in range(0, width, GROUP):
            lanes = pl.ds(pl.multiple_of(which * width + c, GROUP), GROUP)
            out_ref[:, lanes] = (
                part_ref[:, c : c + GROUP].astype(jnp.float32) * column * gain_ref[:, lanes]
            ).astype(out_ref.dtype)


def kernel_call(body, outs, in_specs, scratch, flops, moved_bytes, vmem=24 << 20):
    return pl.pallas_call(
        body,
        out_shape=outs,
        in_specs=in_specs,
        out_specs=jax.tree.map(lambda _: VMEM, outs),
        scratch_shapes=scratch,
        compiler_params=pltpu.CompilerParams(vmem_limit_bytes=vmem),
        cost_estimate=pl.CostEstimate(flops=flops, bytes_accessed=moved_bytes, transcendentals=0),
    )


def shards(blocks, whole_tokens, channels, projected, short_weight, filter_taps, tap_blocks, skip_bias, norm_gain, seq_lengths):
    rows = projected.shape[0]
    width = projected.shape[2] // 2
    groups = width // GROUP
    taps = filter_taps.shape[1]
    shape = jax.ShapeDtypeStruct
    half_shape = shape((rows, width), jnp.bfloat16)
    half_wide = shape((rows, width), jnp.float32)

    spots = range(2 * blocks)
    to_pair = [(i, i ^ 1) for i in spots]
    ahead = [(i, (i + 2) % (2 * blocks)) for i in spots]

    panels = jnp.transpose(projected, (1, 0, 2))
    message = shape((rows + 8, width), jnp.bfloat16)
    small = shape((rows + 8, width // 2), jnp.bfloat16)
    hbm = pl.BlockSpec(memory_space=pltpu.HBM)
    pieces = 4
    row_mask = pltpu.VMEM((rows, GROUP), jnp.float32)

    kept, *sent = kernel_call(
        products_kernel,
        (message, small, small),
        [hbm] * 3,
        [
            pltpu.SMEM(seq_lengths.shape, jnp.int32),
            pltpu.VMEM((pieces, 2, rows, 2 * width // pieces), jnp.bfloat16),
            pltpu.VMEM((16, 2 * width), jnp.bfloat16),
            pltpu.VMEM(short_weight.shape, jnp.float32),
            pltpu.VMEM((4, rows + 8, GROUP), jnp.float32),
            row_mask,
            row_mask,
            pltpu.SemaphoreType.DMA((3 + pieces,)),
        ],
        40 * rows * width,
        16 * rows * width,
        60 << 20,
    )(seq_lengths, panels, short_weight)

    back_own = moved(kept, ahead)
    pair = [moved(sent[0], to_pair)]

    filter_taps, _ = lax.optimization_barrier((filter_taps, kept))
    scaled = (filter_taps * jnp.repeat(tap_blocks.astype(jnp.float32), BLK, axis=1)).astype(jnp.bfloat16)
    span = taps + 2 * BLK
    table, table_next, w_half = kernel_call(
        tables_kernel,
        (
            shape((groups, 2, BLK, span), jnp.bfloat16),
            shape((groups, BLK, 2 * BLK), jnp.bfloat16),
            shape((3, 3, width), jnp.float32),
        ),
        [SMEM, VMEM, VMEM],
        [pltpu.VMEM((2 * groups, span), jnp.float32), pltpu.VMEM((3, BLK, span), jnp.float32)],
        40 * groups * BLK * taps,
        8 * groups * BLK * taps,
    )(seq_lengths, scaled, short_weight)
    table, table_next, later = lax.optimization_barrier((table, table_next, sent[1]))
    pair.append(moved(later, to_pair))

    half = lax.axis_index("half")
    query, _, back_own = lax.optimization_barrier((panels, pair[0], back_own))
    qkept = lax.dynamic_slice(query, (0, 0, half * width), (1, rows, width))[0]
    qsent = lax.dynamic_slice(query, (0, 0, (1 - half) * width), (1, rows, width))[0]
    qkept, qsent, pair[1] = lax.optimization_barrier((qkept, qsent, pair[1]))
    qgot = moved(qsent, to_pair)
    back_pair = [moved(piece, ahead) for piece in pair]

    window = pltpu.VMEM((4 * rows, width), jnp.bfloat16)
    extras = pltpu.VMEM((4, 16, width), jnp.float32)
    shifted = pltpu.VMEM((2, rows + 8, GROUP), jnp.float32)
    short = whole_tokens // 2 <= 4 * BLK
    if short:
        onward = [(i, i ^ 1 if i < 2 else i + 2 if i + 2 < 2 * blocks else 2 + i % 2) for i in spots]
        far = []
        for piece in range(2):
            relayed = kernel_call(
                functools.partial(relay_kernel, piece),
                small,
                [SMEM] + [VMEM] * 4,
                [pltpu.VMEM((2 * rows, width // 2), jnp.bfloat16), pltpu.VMEM((2, 16, width // 2), jnp.float32)],
                2 * rows * BLK * width,
                4 * rows * width,
            )(seq_lengths, table_next, back_own, back_pair[piece], w_half)
            far.append(moved(relayed, onward))
    else:
        across = jnp.concatenate([piece[rows:] for piece in sent], 1)
        across = moved(across, [(i, ((i ^ 1) + 6) % (2 * blocks)) for i in spots])
        straight = moved(kept[rows:], [(i, (i + 6) % (2 * blocks)) for i in spots])
        deep = jnp.where(half == 1, straight, across)
        far = [moved(piece, ahead) for piece in (back_own, *back_pair)] + [deep]

    acc, qown, marks = kernel_call(
        near_kernel,
        (shape((2 * rows, width), jnp.float32), half_wide, shape((3, 8, GROUP), jnp.float32)),
        [SMEM] + [VMEM] * 10,
        [window, extras, shifted, row_mask, row_mask],
        2 * 5 * rows * BLK * width,
        16 * rows * width,
    )(seq_lengths, table, kept, back_own, *pair, *back_pair, qkept, w_half, skip_bias.reshape(1, -1))

    qpair = kernel_call(
        pair_gate_kernel,
        half_wide,
        [SMEM] + [VMEM] * 4,
        [shifted, row_mask, row_mask],
        10 * rows * width,
        8 * rows * width,
    )(seq_lengths, qgot, kept, back_own, w_half)

    done, send, power = kernel_call(
        functools.partial(far_kernel, short),
        (half_wide, half_shape, shape((1, 2 * rows), jnp.float32)),
        [VMEM] * (9 + len(far)),
        [window, extras],
        2 * 5 * rows * BLK * width,
        24 * rows * width,
    )(table, acc, qown, qpair, w_half, marks, back_own, *back_pair, *far)

    back = moved(send, to_pair)
    peers = lax.axis_size("mp")
    shares = [lax.ppermute(power, "mp", [(i, i ^ k) for i in range(peers)]) for k in range(1, peers)]
    power = sum(shares, power)
    return kernel_call(
        functools.partial(norm_kernel, channels),
        shape((rows, 2 * width), jnp.bfloat16),
        [VMEM] * 5,
        [],
        8 * rows * width,
        10 * rows * width,
    )(power, moved(power, to_pair), done, back, norm_gain.reshape(1, -1))


def solution(mesh):
    blocks = mesh.shape["ctx"] // 2
    grid = Mesh(mesh.devices.reshape(blocks, 2, mesh.shape["mp"]), ("blk", "half", "mp"))
    in_specs = (
        P(SPOTS, None, "mp"),
        P(None, None, "mp"),
        P("mp", None),
        P("mp", None),
        P("mp"),
        P("mp"),
        P(),
    )

    def program(projected, *rest):
        body = functools.partial(shards, blocks, projected.shape[0], projected.shape[2])
        return jax.shard_map(
            body, mesh=grid, in_specs=in_specs, out_specs=P(SPOTS, "mp"), check_vma=False
        )(projected, *rest)

    return program
```

```python
import functools

import jax
import jax.numpy as jnp
from jax import lax
from jax.experimental import pallas as pl
from jax.experimental.pallas import tpu as pltpu
from jax.sharding import Mesh, PartitionSpec as P

GROUP = 128
BLK = 128
norm_eps = 1e-06

VMEM = pl.BlockSpec(memory_space=pltpu.VMEM)
SMEM = pl.BlockSpec(memory_space=pltpu.SMEM)
SPOTS = ("blk", "half")


def moved(block, pairs):
    return lax.ppermute(block, SPOTS, pairs)


def boundaries(seq_ref, t):
    def step(k, carry):
        end, first, second = carry
        end = end + seq_ref[k]
        return end, first | (t == end).astype(jnp.int32), second | (t - 1 == end).astype(jnp.int32)

    first = (t == 0).astype(jnp.int32)
    second = (t == 1).astype(jnp.int32)
    _, first, second = lax.fori_loop(0, seq_ref.shape[0], step, (jnp.int32(0), first, second), unroll=True)
    return first, first | second


def row_masks(seq_ref, start, m1_ref, m2_ref):
    rows = lax.broadcasted_iota(jnp.int32, (BLK, GROUP), 0)
    diagonal = rows == lax.broadcasted_iota(jnp.int32, (BLK, GROUP), 1)
    marks = boundaries(seq_ref, start + lax.broadcasted_iota(jnp.int32, (8, GROUP), 1))
    for mark, m_ref in zip(marks, (m1_ref, m2_ref)):
        keep = 1.0 - mark.astype(jnp.float32)[0:1]
        column = jnp.sum(jnp.where(diagonal, keep, 0.0), axis=1, keepdims=True)
        m_ref[...] = jnp.broadcast_to(column, (BLK, GROUP))


def counted(seq_ref, t):
    def step(k, carry):
        end, total = carry
        end = end + seq_ref[k]
        return end, total + (end <= t).astype(jnp.int32)

    _, total = lax.fori_loop(
        0, seq_ref.shape[0], step, (jnp.int32(0), jnp.zeros(t.shape, jnp.int32)), unroll=True
    )
    return jnp.where(t >= 0, total, -1)


def feature(x, x_ref, w, m1_ref, m2_ref):
    rows = x.shape[0]
    return (
        w[0:1] * x
        + w[1:2] * x_ref[7 : rows + 7, :] * m1_ref[...]
        + w[2:3] * x_ref[6 : rows + 6, :] * m2_ref[...]
    )


def products_kernel(seq_hbm, panels_hbm, w_hbm, kept_ref, *refs):
    *sent_refs, seq_ref, kv_ref, q_ref, w_ref, x_ref, m1_ref, m2_ref, sems = refs
    width = kept_ref.shape[1]
    rows = kv_ref.shape[2]
    pieces = kv_ref.shape[0]
    piece = kv_ref.shape[3]
    half = lax.axis_index("half")
    shard = lax.axis_index("blk") * 2 + half
    keep_at = pl.multiple_of(half * width, width)
    send_at = pl.multiple_of((1 - half) * width, width)

    loads = [pltpu.make_async_copy(seq_hbm, seq_ref, sems.at[0])]
    for p in range(pieces):
        at = keep_at if p < pieces // 2 else send_at
        lanes = pl.ds(pl.multiple_of(at + (p % (pieces // 2)) * piece, piece), piece)
        loads.append(pltpu.make_async_copy(panels_hbm.at[1:3, :, lanes], kv_ref.at[p], sems.at[1 + p]))
    loads.append(pltpu.make_async_copy(w_hbm, w_ref, sems.at[1 + pieces]))
    loads.append(pltpu.make_async_copy(panels_hbm.at[0, rows - 16 :, :], q_ref, sems.at[2 + pieces]))
    for load in loads:
        load.start()
    x_ref[:, 0:8, :] = jnp.zeros((x_ref.shape[0], 8, GROUP), jnp.float32)
    loads[0].wait()
    row_masks(seq_ref, shard * rows, m1_ref, m2_ref)
    loads[1 + pieces].wait()
    loads[2 + pieces].wait()
    for p in range(pieces):
        loads[1 + p].wait()
        out_ref, at = (kept_ref, keep_at) if p < pieces // 2 else (sent_refs[p - pieces // 2], send_at)
        for c in range(0, piece, GROUP):
            base = (p % (pieces // 2)) * piece + c
            there = slice(base, base + GROUP) if p < pieces // 2 else slice(c, c + GROUP)
            lanes = pl.ds(pl.multiple_of(at + base, GROUP), GROUP)
            slot = (c // GROUP) % (x_ref.shape[0] // 2) * 2
            raw, made = [], []
            for i in range(2):
                x = kv_ref[p, i, :, c : c + GROUP].astype(jnp.float32)
                x_ref[slot + i, 8:, :] = x
                made.append(feature(x, x_ref.at[slot + i], w_ref[1 + i, :, lanes], m1_ref, m2_ref))
                raw.append(x)
            product = made[0] * made[1]
            top = jnp.where(lax.broadcasted_iota(jnp.int32, (8, GROUP), 0) < 2, raw[0][:8], product[:8])
            out_ref[:rows, there] = jnp.concatenate([top, product[8:]], 0).astype(out_ref.dtype)
            tails = [x[rows - 2 :] for x in raw] + [q_ref[:, lanes].astype(jnp.float32)[14:]]
            out_ref[rows:, there] = jnp.concatenate([raw[1][0:2]] + tails, 0).astype(out_ref.dtype)


def edge_marks(seq_ref):
    t = (
        (lax.axis_index("blk") - 2) * (2 * BLK)
        + lax.broadcasted_iota(jnp.int32, (8, GROUP), 1) * BLK
        + lax.broadcasted_iota(jnp.int32, (8, GROUP), 0)
    )
    return [1.0 - mark.astype(jnp.float32) for mark in boundaries(seq_ref, t)]


def first_rows(now, ahead, w_ref, marks, spot, lanes=slice(None)):
    m1, m2 = [mark[:, spot : spot + 1] for mark in marks]
    top = lax.broadcasted_iota(jnp.int32, ahead.shape, 0) == 0
    made = []
    for i, x0 in enumerate((now[8:], now[:8])):
        x1 = jnp.where(top, pltpu.roll(ahead, 5 - 2 * i, 0), pltpu.roll(x0, 1, 0))
        x2 = pltpu.roll(ahead, 6 - 2 * i, 0)
        w = w_ref[1 + i, :, lanes]
        made.append(w[0:1] * x0 + w[1:2] * x1 * m1 + w[2:3] * x2 * m2)
    return made[0] * made[1]


def put_first_rows(win_ref, at, rows):
    old = win_ref[at : at + 16, :].astype(jnp.float32)
    new = jnp.concatenate([rows, rows], 0)
    first = lax.broadcasted_iota(jnp.int32, old.shape, 0) < 2
    win_ref[at : at + 16, :] = jnp.where(first, new, old).astype(win_ref.dtype)


def reaches_past(seq_ref, block):
    first = block * (2 * BLK)

    def step(k, carry):
        end, start = carry
        end = end + seq_ref[k]
        return end, jnp.where(end <= first, end, start)

    _, start = lax.fori_loop(0, seq_ref.shape[0], step, (jnp.int32(0), jnp.int32(0)), unroll=True)
    return first - 2 * BLK - start > BLK


def tables_kernel(seq_ref, taps_ref, w_ref, out_ref, next_ref, w_half_ref, marks_ref, rev_ref, m_ref):
    groups = out_ref.shape[0]
    taps = taps_ref.shape[1]
    span = out_ref.shape[3]
    half = lax.axis_index("half")
    start = lax.axis_index("blk") * (2 * BLK)
    marks_ref[0], marks_ref[1] = edge_marks(seq_ref)
    for ahead in range(2):
        flag = reaches_past(seq_ref, lax.axis_index("blk") + ahead)
        marks_ref[2 + ahead] = jnp.full((8, GROUP), flag.astype(jnp.float32))
    width = w_half_ref.shape[2]
    w_half_ref[...] = w_ref[:, :, pl.ds(pl.multiple_of(half * width, width), width)]
    turn = lax.broadcasted_iota(jnp.int32, (taps, span), 0) + lax.broadcasted_iota(
        jnp.int32, (taps, span), 1
    )
    turn = (turn == taps).astype(jnp.bfloat16)
    rev_ref[...] = jnp.dot(taps_ref[...], turn, preferred_element_type=jnp.float32)
    seg_in = counted(seq_ref, start - taps + lax.broadcasted_iota(jnp.int32, (8, span), 1))[0:1]
    for part in range(3):
        t_out = start + part * BLK + lax.broadcasted_iota(jnp.int32, (BLK, GROUP), 0)
        seg_out = counted(seq_ref, t_out)[:, 0:1]
        if part < 2:
            m_ref[part] = (seg_in == seg_out).astype(jnp.float32)
        else:
            m_ref[2, :, : 2 * BLK] = (seg_in[:, 2 * BLK : 4 * BLK] == seg_out).astype(jnp.float32)

    def one(g, _):
        row = rev_ref[pl.ds(half * groups + g, 1), :]
        table = pltpu.roll(jnp.broadcast_to(row, (BLK, span)), 0, 1, stride=1, stride_axis=0)
        out_ref[g, 0] = (table * m_ref[0]).astype(out_ref.dtype)
        later = jnp.concatenate([table[:, span - BLK :], table[:, : span - BLK]], 1)
        out_ref[g, 1] = (later * m_ref[1]).astype(out_ref.dtype)
        next_ref[g] = (table[:, : 2 * BLK] * m_ref[2, :, : 2 * BLK]).astype(next_ref.dtype)
        return 0

    lax.fori_loop(0, groups, one, 0)


def fill(win_ref, extra_ref, spot, *pieces):
    at = 0
    for piece in pieces:
        lanes = slice(at, at + piece.shape[1])
        win_ref[pl.ds(pl.multiple_of(spot * BLK, BLK), BLK), lanes] = piece[:BLK]
        extra_ref[spot, :8, lanes] = piece[BLK:].astype(jnp.float32)
        extra_ref[spot, 8:, lanes] = piece[:16].astype(jnp.float32)[:8]
        at += piece.shape[1]


def relay_kernel(piece, marks_ref, next_ref, back_own_ref, back_pair_ref, w_ref, out_ref, win_ref, extra_ref):
    width = out_ref.shape[1]
    half = lax.axis_index("half")
    lanes = slice(piece * width, (piece + 1) * width)
    fill(win_ref, extra_ref, half, back_own_ref.at[:, lanes])
    fill(win_ref, extra_ref, 1 - half, back_pair_ref)
    marks = [marks_ref[0], marks_ref[1]]
    put_first_rows(win_ref, 0, first_rows(extra_ref[0], jnp.zeros((8, width), jnp.float32), w_ref, marks, 2, lanes))
    put_first_rows(win_ref, BLK, first_rows(extra_ref[1], extra_ref[0, :8], w_ref, marks, 3, lanes))
    out_ref[BLK:] = extra_ref[1, :8].astype(out_ref.dtype)
    summed = jnp.max(marks_ref[3]) > 0.5

    @pl.when(summed)
    def _():
        for c in range(0, width, GROUP):
            total = jnp.dot(
                next_ref[(piece * width + c) // GROUP],
                win_ref[:, c : c + GROUP],
                preferred_element_type=jnp.float32,
            )
            out_ref[:BLK, c : c + GROUP] = total.astype(out_ref.dtype)

    @pl.when(jnp.logical_not(summed))
    def _():
        out_ref[:BLK] = win_ref[BLK:]


def gate_rows(seq_ref, raw_ref, tail, w_ref, part, q_ref, x_ref, m1_ref, m2_ref):
    width = raw_ref.shape[1]
    row_masks(seq_ref, lax.axis_index("blk") * (2 * BLK) + part * BLK, m1_ref, m2_ref)
    for c in range(0, width, GROUP):
        lanes = slice(c, c + GROUP)
        w = w_ref[0, :, lanes]
        x = raw_ref[:, lanes].astype(jnp.float32)
        slot = (c // GROUP) % 2
        x_ref[slot, 6:8, :] = tail(lanes)
        x_ref[slot, 8:, :] = x
        q_ref[:, lanes] = feature(x, x_ref.at[slot], w, m1_ref, m2_ref)


def near_kernel(
    seq_ref, marks_ref, table_ref, own_ref, back_own_ref, pair_a_ref, pair_b_ref, back_a_ref, back_b_ref, qkept_ref, w_ref, bias_ref,
    acc_ref, q_ref, win_ref, extra_ref, x_ref, m1_ref, m2_ref,
):
    groups = table_ref.shape[0]
    width = groups * GROUP
    half = lax.axis_index("half")
    fill(win_ref, extra_ref, half, back_own_ref)
    fill(win_ref, extra_ref, 1 - half, back_a_ref, back_b_ref)
    fill(win_ref, extra_ref, 2 + half, own_ref)
    fill(win_ref, extra_ref, 3 - half, pair_a_ref, pair_b_ref)
    marks = [marks_ref[0], marks_ref[1]]
    for spot in (1, 2, 3):
        rows = first_rows(extra_ref[spot], extra_ref[spot - 1, :8], w_ref, marks, spot + 2)
        put_first_rows(win_ref, spot * BLK, rows)
    for g in range(groups):
        lanes = slice(g * GROUP, (g + 1) * GROUP)
        bias = bias_ref[:, pl.ds(pl.multiple_of(half * width + g * GROUP, GROUP), GROUP)]
        for part in range(2):
            total = jnp.dot(
                table_ref[g, part, :, 3 * BLK : (5 + part) * BLK],
                win_ref[BLK : (3 + part) * BLK, lanes],
                preferred_element_type=jnp.float32,
            )
            here = win_ref[(2 + part) * BLK : (3 + part) * BLK, lanes].astype(jnp.float32)
            acc_ref[part * BLK : (part + 1) * BLK, lanes] = total + bias * here
    gate_rows(
        seq_ref, qkept_ref, lambda lanes: extra_ref[1 + half, 6:8, lanes], w_ref, half, q_ref, x_ref, m1_ref, m2_ref
    )


def pair_gate_kernel(seq_ref, raw_ref, own_ref, back_own_ref, w_ref, q_ref, x_ref, m1_ref, m2_ref):
    half = lax.axis_index("half")

    def tail(lanes):
        back = back_own_ref[BLK:, lanes].astype(jnp.float32)
        own = own_ref[BLK:, lanes].astype(jnp.float32)
        return jnp.where(half == 1, back, own)[6:8]

    gate_rows(seq_ref, raw_ref, tail, w_ref, 1 - half, q_ref, x_ref, m1_ref, m2_ref)


def far_kernel(
    short, piece, table_ref, acc_ref, qown_ref, qpair_ref, w_ref, marks_ref, back_own_ref, back_pair_ref, *refs
):
    *refs, kept_ref, sent_ref, total_ref, win_ref, extra_ref = refs
    far_refs, before = refs[: len(refs) - 2 * piece], refs[len(refs) - 2 * piece :]
    width = kept_ref.shape[1]
    half = lax.axis_index("half")
    lanes = slice(piece * width, (piece + 1) * width)
    marks = [marks_ref[0], marks_ref[1]]
    low = 1 if short else 0

    @pl.when(half == 0)
    def _():
        fill(win_ref, extra_ref, 2, back_own_ref.at[:, lanes])

    @pl.when(half == 1)
    def _():
        fill(win_ref, extra_ref, 2, back_pair_ref)

    if short:
        summed = marks_ref[2, 0:1, 0:1]
        fill(win_ref, extra_ref, 1, far_refs[0])
        payload = win_ref[BLK : 2 * BLK, :].astype(jnp.float32)
        win_ref[BLK : 2 * BLK, :] = (payload * (1.0 - summed)).astype(win_ref.dtype)
    else:
        fill(win_ref, extra_ref, half, far_refs[0].at[:, lanes])
        fill(win_ref, extra_ref, 1 - half, far_refs[1 + piece])
        ahead = far_refs[3][:, lanes].astype(jnp.float32)
        put_first_rows(win_ref, 0, first_rows(extra_ref[0], ahead, w_ref, marks, 0, lanes))
        put_first_rows(win_ref, BLK, first_rows(extra_ref[1], extra_ref[0, :8], w_ref, marks, 1, lanes))
    put_first_rows(win_ref, 2 * BLK, first_rows(extra_ref[2], extra_ref[1, :8], w_ref, marks, 2, lanes))
    if before:
        sent_ref[:, :width] = before[1][...]
    for i, (part, q_ref, out_ref) in enumerate(((half, qown_ref, kept_ref), (1 - half, qpair_ref, sent_ref))):
        part_sent = i == 1
        squares = before[0][i] if before else jnp.zeros((BLK, GROUP), jnp.float32)
        rows = pl.ds(pl.multiple_of(part * BLK, BLK), BLK)
        for c in range(0, width, GROUP):
            here = slice(c, c + GROUP)
            whole = slice(piece * width + c, piece * width + c + GROUP)
            filtered = acc_ref[rows, whole] + jnp.dot(
                table_ref[(piece * width + c) // GROUP, part, :, low * BLK : 3 * BLK],
                win_ref[low * BLK : 3 * BLK, here],
                preferred_element_type=jnp.float32,
            )
            if short:
                weight = summed * (part == 0).astype(jnp.float32)
                filtered = filtered + weight * far_refs[0][:BLK, here].astype(jnp.float32)
            gated = q_ref[:, whole] * filtered
            squares = squares + gated * gated
            out_ref[:, whole if before and part_sent else here] = gated.astype(out_ref.dtype)
        if before:
            total_ref[:, i * BLK : (i + 1) * BLK] = lax.dot_general(
                jnp.ones((8, GROUP), jnp.float32),
                squares,
                (((1,), (1,)), ((), ())),
                precision=lax.Precision.HIGHEST,
                preferred_element_type=jnp.float32,
            )[0:1]
        else:
            total_ref[i] = squares


def norm_kernel(channels, power_ref, power_got_ref, *refs):
    *kept_refs, got_ref, gain_ref, out_ref = refs
    half = lax.axis_index("half")
    power = power_ref[:, :BLK] + power_got_ref[:, BLK:]
    scale = lax.rsqrt(power / channels + norm_eps)
    diagonal = lax.broadcasted_iota(jnp.int32, (BLK, BLK), 0) == lax.broadcasted_iota(
        jnp.int32, (BLK, BLK), 1
    )
    column = jnp.sum(jnp.where(diagonal, scale, 0.0), axis=1, keepdims=True)
    for at, refs in ((half, kept_refs), (1 - half, [got_ref])):
        at = at * got_ref.shape[1]
        for ref in refs:
            for c in range(0, ref.shape[1], GROUP):
                lanes = pl.ds(pl.multiple_of(at + c, GROUP), GROUP)
                part = ref[:, c : c + GROUP].astype(jnp.float32)
                out_ref[:, lanes] = (part * column * gain_ref[:, lanes]).astype(out_ref.dtype)
            at = at + ref.shape[1]


def kernel_call(body, outs, in_specs, scratch, flops, moved_bytes, vmem=24 << 20):
    return pl.pallas_call(
        body,
        out_shape=outs,
        in_specs=in_specs,
        out_specs=jax.tree.map(lambda _: VMEM, outs),
        scratch_shapes=scratch,
        compiler_params=pltpu.CompilerParams(vmem_limit_bytes=vmem),
        cost_estimate=pl.CostEstimate(flops=flops, bytes_accessed=moved_bytes, transcendentals=0),
    )


def shards(blocks, whole_tokens, channels, projected, short_weight, filter_taps, tap_blocks, skip_bias, norm_gain, seq_lengths):
    rows = projected.shape[0]
    width = projected.shape[2] // 2
    groups = width // GROUP
    taps = filter_taps.shape[1]
    shape = jax.ShapeDtypeStruct
    half_shape = shape((rows, width), jnp.bfloat16)
    half_wide = shape((rows, width), jnp.float32)

    spots = range(2 * blocks)
    to_pair = [(i, i ^ 1) for i in spots]
    ahead = [(i, (i + 2) % (2 * blocks)) for i in spots]

    panels = jnp.transpose(projected, (1, 0, 2))
    message = shape((rows + 8, width), jnp.bfloat16)
    small = shape((rows + 8, width // 2), jnp.bfloat16)
    hbm = pl.BlockSpec(memory_space=pltpu.HBM)
    pieces = 4
    row_mask = pltpu.VMEM((rows, GROUP), jnp.float32)

    kept, *sent = kernel_call(
        products_kernel,
        (message, small, small),
        [hbm] * 3,
        [
            pltpu.SMEM(seq_lengths.shape, jnp.int32),
            pltpu.VMEM((pieces, 2, rows, 2 * width // pieces), jnp.bfloat16),
            pltpu.VMEM((16, 2 * width), jnp.bfloat16),
            pltpu.VMEM(short_weight.shape, jnp.float32),
            pltpu.VMEM((4, rows + 8, GROUP), jnp.float32),
            row_mask,
            row_mask,
            pltpu.SemaphoreType.DMA((3 + pieces,)),
        ],
        40 * rows * width,
        16 * rows * width,
        60 << 20,
    )(seq_lengths, panels, short_weight)

    back_own = moved(kept, ahead)
    pair = [moved(piece, to_pair) for piece in sent]

    filter_taps, _ = lax.optimization_barrier((filter_taps, kept))
    scaled = (filter_taps * jnp.repeat(tap_blocks.astype(jnp.float32), BLK, axis=1)).astype(jnp.bfloat16)
    span = taps + 2 * BLK
    table, table_next, w_half, marks = kernel_call(
        tables_kernel,
        (
            shape((groups, 2, BLK, span), jnp.bfloat16),
            shape((groups, BLK, 2 * BLK), jnp.bfloat16),
            shape((3, 3, width), jnp.float32),
            shape((4, 8, GROUP), jnp.float32),
        ),
        [SMEM, VMEM, VMEM],
        [pltpu.VMEM((2 * groups, span), jnp.float32), pltpu.VMEM((3, BLK, span), jnp.float32)],
        40 * groups * BLK * taps,
        8 * groups * BLK * taps,
    )(seq_lengths, scaled, short_weight)
    table, table_next, pair[0] = lax.optimization_barrier((table, table_next, pair[0]))

    half = lax.axis_index("half")
    query, _ = lax.optimization_barrier((panels, pair[0]))
    qkept = lax.dynamic_slice(query, (0, 0, half * width), (1, rows, width))[0]
    qsent = lax.dynamic_slice(query, (0, 0, (1 - half) * width), (1, rows, width))[0]
    qkept, qsent, pair[1] = lax.optimization_barrier((qkept, qsent, pair[1]))
    qgot = moved(qsent, to_pair)
    back_pair = [moved(piece, ahead) for piece in pair]

    window = pltpu.VMEM((4 * rows, width), jnp.bfloat16)
    extras = pltpu.VMEM((4, 16, width), jnp.float32)
    shifted = pltpu.VMEM((2, rows + 8, GROUP), jnp.float32)
    short = whole_tokens // 2 <= 4 * BLK
    if short:
        onward = [(i, i ^ 1 if i < 2 else i + 2 if i + 2 < 2 * blocks else 2 + i % 2) for i in spots]
        far = []
        for piece in range(2):
            relayed = kernel_call(
                functools.partial(relay_kernel, piece),
                small,
                [VMEM] * 5,
                [pltpu.VMEM((2 * rows, width // 2), jnp.bfloat16), pltpu.VMEM((2, 16, width // 2), jnp.float32)],
                2 * rows * BLK * width,
                4 * rows * width,
            )(marks, table_next, back_own, back_pair[piece], w_half)
            far.append(moved(relayed, onward))
    else:
        across = jnp.concatenate([piece[rows:] for piece in sent], 1)
        across = moved(across, [(i, ((i ^ 1) + 6) % (2 * blocks)) for i in spots])
        straight = moved(kept[rows:], [(i, (i + 6) % (2 * blocks)) for i in spots])
        deep = jnp.where(half == 1, straight, across)
        far = [moved(piece, ahead) for piece in (back_own, *back_pair)] + [deep]

    acc, qown = kernel_call(
        near_kernel,
        (shape((2 * rows, width), jnp.float32), half_wide),
        [SMEM] + [VMEM] * 11,
        [window, extras, shifted, row_mask, row_mask],
        2 * 5 * rows * BLK * width,
        16 * rows * width,
    )(seq_lengths, marks, table, kept, back_own, *pair, *back_pair, qkept, w_half, skip_bias.reshape(1, -1))

    qpair = kernel_call(
        pair_gate_kernel,
        half_wide,
        [SMEM] + [VMEM] * 4,
        [shifted, row_mask, row_mask],
        10 * rows * width,
        8 * rows * width,
    )(seq_lengths, qgot, kept, back_own, w_half)

    done, power, send = [], None, None
    for piece in range(2):
        needed = far[piece : piece + 1] if short else far
        before = [power, send] if piece else []
        own, send, power = kernel_call(
            functools.partial(far_kernel, short, piece),
            (
                shape((rows, width // 2), jnp.float32),
                shape((rows, width if piece else width // 2), jnp.bfloat16),
                shape((1, 2 * rows) if piece else (2, rows, GROUP), jnp.float32),
            ),
            [VMEM] * (8 + len(needed) + len(before)),
            [pltpu.VMEM((3 * rows, width // 2), jnp.bfloat16), pltpu.VMEM((3, 16, width // 2), jnp.float32)],
            2 * 3 * rows * BLK * width,
            12 * rows * width,
        )(table, acc, qown, qpair, w_half, marks, back_own, back_pair[piece], *needed, *before)
        done.append(own)
    back = moved(send, to_pair)

    peers = lax.axis_size("mp")
    shares = [lax.ppermute(power, "mp", [(i, i ^ k) for i in range(peers)]) for k in range(1, peers)]
    power = sum(shares, power)
    return kernel_call(
        functools.partial(norm_kernel, channels),
        shape((rows, 2 * width), jnp.bfloat16),
        [VMEM] * 6,
        [],
        8 * rows * width,
        10 * rows * width,
    )(power, moved(power, to_pair), *done, back, norm_gain.reshape(1, -1))


def solution(mesh):
    blocks = mesh.shape["ctx"] // 2
    grid = Mesh(mesh.devices.reshape(blocks, 2, mesh.shape["mp"]), ("blk", "half", "mp"))
    in_specs = (
        P(SPOTS, None, "mp"),
        P(None, None, "mp"),
        P("mp", None),
        P("mp", None),
        P("mp"),
        P("mp"),
        P(),
    )

    def program(projected, *rest):
        body = functools.partial(shards, blocks, projected.shape[0], projected.shape[2])
        return jax.shard_map(
            body, mesh=grid, in_specs=in_specs, out_specs=P(SPOTS, "mp"), check_vma=False
        )(projected, *rest)

    return program
```

```python
import functools

import jax
import jax.numpy as jnp
from jax import lax
from jax.experimental import pallas as pl
from jax.experimental.pallas import tpu as pltpu
from jax.sharding import Mesh, PartitionSpec as P

GROUP = 128
BLK = 128
norm_eps = 1e-06

VMEM = pl.BlockSpec(memory_space=pltpu.VMEM)
SMEM = pl.BlockSpec(memory_space=pltpu.SMEM)
SPOTS = ("blk", "half")


def moved(block, pairs):
    return lax.ppermute(block, SPOTS, pairs)


def boundaries(seq_ref, t):
    def step(k, carry):
        end, first, second = carry
        end = end + seq_ref[k]
        return end, first | (t == end).astype(jnp.int32), second | (t - 1 == end).astype(jnp.int32)

    first = (t == 0).astype(jnp.int32)
    second = (t == 1).astype(jnp.int32)
    _, first, second = lax.fori_loop(0, seq_ref.shape[0], step, (jnp.int32(0), first, second), unroll=True)
    return first, first | second


def row_masks(lengths_ref, start, m1_ref, m2_ref):
    count = lengths_ref.shape[1]
    square = (count, count)
    upto = lax.broadcasted_iota(jnp.int32, square, 1) <= lax.broadcasted_iota(jnp.int32, square, 0)
    lengths = jnp.broadcast_to(lengths_ref[...].astype(jnp.float32), square)
    ends = jnp.sum(jnp.where(upto, lengths, 0.0), axis=1, keepdims=True)
    t = (start + lax.broadcasted_iota(jnp.int32, (count, BLK), 1)).astype(jnp.float32)
    opens = (t == ends) | (t == 0.0)
    after = opens | (t - 1.0 == ends) | (t == 1.0)
    diagonal = lax.broadcasted_iota(jnp.int32, (BLK, BLK), 0) == lax.broadcasted_iota(jnp.int32, (BLK, BLK), 1)
    for mark, m_ref in ((opens, m1_ref), (after, m2_ref)):
        keep = 1.0 - jnp.max(mark.astype(jnp.float32), axis=0, keepdims=True)
        column = jnp.sum(jnp.where(diagonal, keep, 0.0), axis=1, keepdims=True)
        m_ref[...] = jnp.broadcast_to(column, m_ref.shape)


def counted(seq_ref, t):
    def step(k, carry):
        end, total = carry
        end = end + seq_ref[k]
        return end, total + (end <= t).astype(jnp.int32)

    _, total = lax.fori_loop(
        0, seq_ref.shape[0], step, (jnp.int32(0), jnp.zeros(t.shape, jnp.int32)), unroll=True
    )
    return jnp.where(t >= 0, total, -1)


def feature(x, x_ref, w, m1_ref, m2_ref):
    rows = x.shape[0]
    return (
        w[0:1] * x
        + w[1:2] * x_ref[7 : rows + 7, :] * m1_ref[...]
        + w[2:3] * x_ref[6 : rows + 6, :] * m2_ref[...]
    )


def products_kernel(seq_hbm, panels_hbm, w_hbm, *refs):
    outs, (kept_ref, *sent_refs), refs = refs[:3], refs[3:6], refs[6:]
    seq_ref, kv_ref, q_ref, w_ref, x_ref, m1_ref, m2_ref, sems = refs
    width = kept_ref.shape[1]
    rows = kv_ref.shape[2]
    pieces = kv_ref.shape[0]
    piece = kv_ref.shape[3]
    half = lax.axis_index("half")
    shard = lax.axis_index("blk") * 2 + half
    keep_at = pl.multiple_of(half * width, width)
    send_at = pl.multiple_of((1 - half) * width, width)

    loads = [pltpu.make_async_copy(seq_hbm, seq_ref, sems.at[0])]
    for p in range(pieces):
        at = keep_at if p < pieces // 2 else send_at
        lanes = pl.ds(pl.multiple_of(at + (p % (pieces // 2)) * piece, piece), piece)
        loads.append(pltpu.make_async_copy(panels_hbm.at[1:3, :, lanes], kv_ref.at[p], sems.at[1 + p]))
    loads.append(pltpu.make_async_copy(w_hbm, w_ref, sems.at[1 + pieces]))
    loads.append(pltpu.make_async_copy(panels_hbm.at[0, rows - 16 :, :], q_ref, sems.at[2 + pieces]))
    for load in loads:
        load.start()
    x_ref[:, 0:8, :] = jnp.zeros((x_ref.shape[0], 8, GROUP), jnp.float32)
    loads[0].wait()
    row_masks(seq_ref, shard * rows, m1_ref, m2_ref)
    loads[1 + pieces].wait()
    loads[2 + pieces].wait()
    stores = []
    for p in range(pieces):
        loads[1 + p].wait()
        out_ref, at = (kept_ref, keep_at) if p < pieces // 2 else (sent_refs[p - pieces // 2], send_at)
        for c in range(0, piece, GROUP):
            base = (p % (pieces // 2)) * piece + c
            there = slice(base, base + GROUP) if p < pieces // 2 else slice(c, c + GROUP)
            lanes = pl.ds(pl.multiple_of(at + base, GROUP), GROUP)
            slot = (c // GROUP) % (x_ref.shape[0] // 2) * 2
            raw, made = [], []
            for i in range(2):
                x = kv_ref[p, i, :, c : c + GROUP].astype(jnp.float32)
                x_ref[slot + i, 8:, :] = x
                made.append(feature(x, x_ref.at[slot + i], w_ref[1 + i, :, lanes], m1_ref, m2_ref))
                raw.append(x)
            product = made[0] * made[1]
            top = jnp.where(lax.broadcasted_iota(jnp.int32, (8, GROUP), 0) < 2, raw[0][:8], product[:8])
            out_ref[:rows, there] = jnp.concatenate([top, product[8:]], 0).astype(out_ref.dtype)
            tails = [x[rows - 2 :] for x in raw] + [q_ref[:, lanes].astype(jnp.float32)[14:]]
            out_ref[rows:, there] = jnp.concatenate([raw[1][0:2]] + tails, 0).astype(out_ref.dtype)
        if p >= pieces // 2 - 1:
            done = p - pieces // 2 + 1
            stores.append(pltpu.make_async_copy(out_ref, outs[done], sems.at[3 + pieces + done]))
            stores[-1].start()
    for store in stores:
        store.wait()


def edge_marks(seq_ref):
    t = (
        (lax.axis_index("blk") - 2) * (2 * BLK)
        + lax.broadcasted_iota(jnp.int32, (8, GROUP), 1) * BLK
        + lax.broadcasted_iota(jnp.int32, (8, GROUP), 0)
    )
    return [1.0 - mark.astype(jnp.float32) for mark in boundaries(seq_ref, t)]


def first_rows(now, ahead, w_ref, marks, spot, lanes=slice(None)):
    m1, m2 = [mark[:, spot : spot + 1] for mark in marks]
    top = lax.broadcasted_iota(jnp.int32, ahead.shape, 0) == 0
    made = []
    for i, x0 in enumerate((now[8:], now[:8])):
        x1 = jnp.where(top, pltpu.roll(ahead, 5 - 2 * i, 0), pltpu.roll(x0, 1, 0))
        x2 = pltpu.roll(ahead, 6 - 2 * i, 0)
        w = w_ref[1 + i, :, lanes]
        made.append(w[0:1] * x0 + w[1:2] * x1 * m1 + w[2:3] * x2 * m2)
    return made[0] * made[1]


def put_first_rows(win_ref, at, rows):
    old = win_ref[at : at + 16, :].astype(jnp.float32)
    new = jnp.concatenate([rows, rows], 0)
    first = lax.broadcasted_iota(jnp.int32, old.shape, 0) < 2
    win_ref[at : at + 16, :] = jnp.where(first, new, old).astype(win_ref.dtype)


def reaches_past(seq_ref, block):
    first = block * (2 * BLK)

    def step(k, carry):
        end, start = carry
        end = end + seq_ref[k]
        return end, jnp.where(end <= first, end, start)

    _, start = lax.fori_loop(0, seq_ref.shape[0], step, (jnp.int32(0), jnp.int32(0)), unroll=True)
    return first - 2 * BLK - start > BLK


def tables_kernel(seq_ref, taps_ref, w_ref, out_ref, next_ref, w_half_ref, marks_ref, rev_ref, m_ref):
    groups = out_ref.shape[0]
    taps = taps_ref.shape[1]
    span = out_ref.shape[3]
    half = lax.axis_index("half")
    start = lax.axis_index("blk") * (2 * BLK)
    marks_ref[0], marks_ref[1] = edge_marks(seq_ref)
    for ahead in range(2):
        flag = reaches_past(seq_ref, lax.axis_index("blk") + ahead)
        marks_ref[2 + ahead] = jnp.full((8, GROUP), flag.astype(jnp.float32))
    width = w_half_ref.shape[2]
    w_half_ref[...] = w_ref[:, :, pl.ds(pl.multiple_of(half * width, width), width)]
    turn = lax.broadcasted_iota(jnp.int32, (taps, span), 0) + lax.broadcasted_iota(
        jnp.int32, (taps, span), 1
    )
    turn = (turn == taps).astype(jnp.bfloat16)
    rev_ref[...] = jnp.dot(taps_ref[...], turn, preferred_element_type=jnp.float32)
    seg_in = counted(seq_ref, start - taps + lax.broadcasted_iota(jnp.int32, (8, span), 1))[0:1]
    for part in range(3):
        t_out = start + part * BLK + lax.broadcasted_iota(jnp.int32, (BLK, GROUP), 0)
        seg_out = counted(seq_ref, t_out)[:, 0:1]
        if part < 2:
            m_ref[part] = (seg_in == seg_out).astype(jnp.float32)
        else:
            m_ref[2, :, : 2 * BLK] = (seg_in[:, 2 * BLK : 4 * BLK] == seg_out).astype(jnp.float32)

    def one(g, _):
        row = rev_ref[pl.ds(half * groups + g, 1), :]
        table = pltpu.roll(jnp.broadcast_to(row, (BLK, span)), 0, 1, stride=1, stride_axis=0)
        out_ref[g, 0] = (table * m_ref[0]).astype(out_ref.dtype)
        later = jnp.concatenate([table[:, span - BLK :], table[:, : span - BLK]], 1)
        out_ref[g, 1] = (later * m_ref[1]).astype(out_ref.dtype)
        next_ref[g] = (table[:, : 2 * BLK] * m_ref[2, :, : 2 * BLK]).astype(next_ref.dtype)
        return 0

    lax.fori_loop(0, groups, one, 0)


def fill(win_ref, extra_ref, spot, *pieces):
    at = 0
    for piece in pieces:
        lanes = slice(at, at + piece.shape[1])
        win_ref[pl.ds(pl.multiple_of(spot * BLK, BLK), BLK), lanes] = piece[:BLK]
        extra_ref[spot, :8, lanes] = piece[BLK:].astype(jnp.float32)
        extra_ref[spot, 8:, lanes] = piece[:16].astype(jnp.float32)[:8]
        at += piece.shape[1]


def relay_kernel(piece, marks_ref, next_ref, back_own_ref, back_pair_ref, w_ref, out_ref, win_ref, extra_ref):
    width = out_ref.shape[1]
    half = lax.axis_index("half")
    lanes = slice(piece * width, (piece + 1) * width)
    fill(win_ref, extra_ref, half, back_own_ref.at[:, lanes])
    fill(win_ref, extra_ref, 1 - half, back_pair_ref)
    marks = [marks_ref[0], marks_ref[1]]
    put_first_rows(win_ref, 0, first_rows(extra_ref[0], jnp.zeros((8, width), jnp.float32), w_ref, marks, 2, lanes))
    put_first_rows(win_ref, BLK, first_rows(extra_ref[1], extra_ref[0, :8], w_ref, marks, 3, lanes))
    out_ref[BLK:] = extra_ref[1, :8].astype(out_ref.dtype)
    summed = jnp.max(marks_ref[3]) > 0.5

    @pl.when(summed)
    def _():
        for c in range(0, width, GROUP):
            total = jnp.dot(
                next_ref[(piece * width + c) // GROUP],
                win_ref[:, c : c + GROUP],
                preferred_element_type=jnp.float32,
            )
            out_ref[:BLK, c : c + GROUP] = total.astype(out_ref.dtype)

    @pl.when(jnp.logical_not(summed))
    def _():
        out_ref[:BLK] = win_ref[BLK:]


def gate_rows(seq_ref, raw_ref, tail, w_ref, part, q_ref, x_ref, m1_ref, m2_ref):
    width = raw_ref.shape[1]
    row_masks(seq_ref, lax.axis_index("blk") * (2 * BLK) + part * BLK, m1_ref, m2_ref)
    for c in range(0, width, GROUP):
        lanes = slice(c, c + GROUP)
        w = w_ref[0, :, lanes]
        x = raw_ref[:, lanes].astype(jnp.float32)
        slot = (c // GROUP) % 2
        x_ref[slot, 6:8, :] = tail(lanes)
        x_ref[slot, 8:, :] = x
        q_ref[:, lanes] = feature(x, x_ref.at[slot], w, m1_ref, m2_ref)


def near_kernel(
    seq_ref, marks_ref, table_ref, own_ref, back_own_ref, pair_a_ref, pair_b_ref, back_a_ref, back_b_ref, qkept_ref, w_ref, bias_ref,
    acc_ref, q_ref, win_ref, extra_ref, x_ref, m1_ref, m2_ref,
):
    groups = table_ref.shape[0]
    width = groups * GROUP
    half = lax.axis_index("half")
    fill(win_ref, extra_ref, half, back_own_ref)
    fill(win_ref, extra_ref, 1 - half, back_a_ref, back_b_ref)
    fill(win_ref, extra_ref, 2 + half, own_ref)
    fill(win_ref, extra_ref, 3 - half, pair_a_ref, pair_b_ref)
    marks = [marks_ref[0], marks_ref[1]]
    for spot in (1, 2, 3):
        rows = first_rows(extra_ref[spot], extra_ref[spot - 1, :8], w_ref, marks, spot + 2)
        put_first_rows(win_ref, spot * BLK, rows)
    for g in range(groups):
        lanes = slice(g * GROUP, (g + 1) * GROUP)
        bias = bias_ref[:, pl.ds(pl.multiple_of(half * width + g * GROUP, GROUP), GROUP)]
        for part in range(2):
            total = jnp.dot(
                table_ref[g, part, :, 3 * BLK : (5 + part) * BLK],
                win_ref[BLK : (3 + part) * BLK, lanes],
                preferred_element_type=jnp.float32,
            )
            here = win_ref[(2 + part) * BLK : (3 + part) * BLK, lanes].astype(jnp.float32)
            acc_ref[part * BLK : (part + 1) * BLK, lanes] = total + bias * here
    gate_rows(
        seq_ref, qkept_ref, lambda lanes: extra_ref[1 + half, 6:8, lanes], w_ref, half, q_ref, x_ref, m1_ref, m2_ref
    )


def pair_gate_kernel(seq_ref, raw_ref, own_ref, back_own_ref, w_ref, q_ref, x_ref, m1_ref, m2_ref):
    half = lax.axis_index("half")

    def tail(lanes):
        back = back_own_ref[BLK:, lanes].astype(jnp.float32)
        own = own_ref[BLK:, lanes].astype(jnp.float32)
        return jnp.where(half == 1, back, own)[6:8]

    gate_rows(seq_ref, raw_ref, tail, w_ref, 1 - half, q_ref, x_ref, m1_ref, m2_ref)


def far_kernel(
    short, piece, table_ref, acc_ref, qown_ref, qpair_ref, w_ref, marks_ref, back_own_ref, back_pair_ref, *refs
):
    *refs, kept_ref, sent_ref, total_ref, win_ref, extra_ref = refs
    far_refs, before = refs[: len(refs) - 2 * piece], refs[len(refs) - 2 * piece :]
    width = kept_ref.shape[1]
    half = lax.axis_index("half")
    lanes = slice(piece * width, (piece + 1) * width)
    marks = [marks_ref[0], marks_ref[1]]
    low = 1 if short else 0

    @pl.when(half == 0)
    def _():
        fill(win_ref, extra_ref, 2, back_own_ref.at[:, lanes])

    @pl.when(half == 1)
    def _():
        fill(win_ref, extra_ref, 2, back_pair_ref)

    if short:
        summed = marks_ref[2, 0:1, 0:1]
        fill(win_ref, extra_ref, 1, far_refs[0])
        payload = win_ref[BLK : 2 * BLK, :].astype(jnp.float32)
        win_ref[BLK : 2 * BLK, :] = (payload * (1.0 - summed)).astype(win_ref.dtype)
    else:
        fill(win_ref, extra_ref, half, far_refs[0].at[:, lanes])
        fill(win_ref, extra_ref, 1 - half, far_refs[1 + piece])
        ahead = far_refs[3][:, lanes].astype(jnp.float32)
        put_first_rows(win_ref, 0, first_rows(extra_ref[0], ahead, w_ref, marks, 0, lanes))
        put_first_rows(win_ref, BLK, first_rows(extra_ref[1], extra_ref[0, :8], w_ref, marks, 1, lanes))
    put_first_rows(win_ref, 2 * BLK, first_rows(extra_ref[2], extra_ref[1, :8], w_ref, marks, 2, lanes))
    if before:
        sent_ref[:, :width] = before[1][...]
    for i, (part, q_ref, out_ref) in enumerate(((half, qown_ref, kept_ref), (1 - half, qpair_ref, sent_ref))):
        part_sent = i == 1
        squares = before[0][i] if before else jnp.zeros((BLK, GROUP), jnp.float32)
        rows = pl.ds(pl.multiple_of(part * BLK, BLK), BLK)
        for c in range(0, width, GROUP):
            here = slice(c, c + GROUP)
            whole = slice(piece * width + c, piece * width + c + GROUP)
            filtered = acc_ref[rows, whole] + jnp.dot(
                table_ref[(piece * width + c) // GROUP, part, :, low * BLK : 3 * BLK],
                win_ref[low * BLK : 3 * BLK, here],
                preferred_element_type=jnp.float32,
            )
            if short:
                weight = summed * (part == 0).astype(jnp.float32)
                filtered = filtered + weight * far_refs[0][:BLK, here].astype(jnp.float32)
            gated = q_ref[:, whole] * filtered
            squares = squares + gated * gated
            out_ref[:, whole if before and part_sent else here] = gated.astype(out_ref.dtype)
        if before:
            total_ref[:, i * BLK : (i + 1) * BLK] = lax.dot_general(
                jnp.ones((8, GROUP), jnp.float32),
                squares,
                (((1,), (1,)), ((), ())),
                precision=lax.Precision.HIGHEST,
                preferred_element_type=jnp.float32,
            )[0:1]
        else:
            total_ref[i] = squares


def norm_kernel(channels, power_ref, power_got_ref, *refs):
    *kept_refs, got_ref, gain_ref, out_ref = refs
    half = lax.axis_index("half")
    power = power_ref[:, :BLK] + power_got_ref[:, BLK:]
    scale = lax.rsqrt(power / channels + norm_eps)
    diagonal = lax.broadcasted_iota(jnp.int32, (BLK, BLK), 0) == lax.broadcasted_iota(
        jnp.int32, (BLK, BLK), 1
    )
    column = jnp.sum(jnp.where(diagonal, scale, 0.0), axis=1, keepdims=True)
    for at, refs in ((half, kept_refs), (1 - half, [got_ref])):
        at = at * got_ref.shape[1]
        for ref in refs:
            for c in range(0, ref.shape[1], GROUP):
                lanes = pl.ds(pl.multiple_of(at + c, GROUP), GROUP)
                part = ref[:, c : c + GROUP].astype(jnp.float32)
                out_ref[:, lanes] = (part * column * gain_ref[:, lanes]).astype(out_ref.dtype)
            at = at + ref.shape[1]


def kernel_call(body, outs, in_specs, scratch, flops, moved_bytes, vmem=24 << 20, out_space=VMEM):
    return pl.pallas_call(
        body,
        out_shape=outs,
        in_specs=in_specs,
        out_specs=jax.tree.map(lambda _: out_space, outs),
        scratch_shapes=scratch,
        compiler_params=pltpu.CompilerParams(vmem_limit_bytes=vmem),
        cost_estimate=pl.CostEstimate(flops=flops, bytes_accessed=moved_bytes, transcendentals=0),
    )


def shards(blocks, whole_tokens, channels, projected, short_weight, filter_taps, tap_blocks, skip_bias, norm_gain, seq_lengths):
    rows = projected.shape[0]
    width = projected.shape[2] // 2
    groups = width // GROUP
    taps = filter_taps.shape[1]
    shape = jax.ShapeDtypeStruct
    half_shape = shape((rows, width), jnp.bfloat16)
    half_wide = shape((rows, width), jnp.float32)

    spots = range(2 * blocks)
    to_pair = [(i, i ^ 1) for i in spots]
    ahead = [(i, (i + 2) % (2 * blocks)) for i in spots]

    panels = jnp.transpose(projected, (1, 0, 2))
    message = shape((rows + 8, width), jnp.bfloat16)
    small = shape((rows + 8, width // 2), jnp.bfloat16)
    hbm = pl.BlockSpec(memory_space=pltpu.HBM)
    pieces = 4
    lengths = seq_lengths.reshape(1, -1)
    row_mask = pltpu.VMEM((rows, GROUP), jnp.float32)

    kept, *sent = kernel_call(
        products_kernel,
        (message, small, small),
        [hbm] * 3,
        [
            pltpu.VMEM(message.shape, message.dtype),
            pltpu.VMEM(small.shape, small.dtype),
            pltpu.VMEM(small.shape, small.dtype),
            pltpu.VMEM(lengths.shape, jnp.int32),
            pltpu.VMEM((pieces, 2, rows, 2 * width // pieces), jnp.bfloat16),
            pltpu.VMEM((16, 2 * width), jnp.bfloat16),
            pltpu.VMEM(short_weight.shape, jnp.float32),
            pltpu.VMEM((4, rows + 8, GROUP), jnp.float32),
            row_mask,
            row_mask,
            pltpu.SemaphoreType.DMA((6 + pieces,)),
        ],
        40 * rows * width,
        16 * rows * width,
        60 << 20,
        hbm,
    )(lengths, panels, short_weight)

    back_own = moved(kept, ahead)
    pair = [moved(piece, to_pair) for piece in sent]

    filter_taps, _ = lax.optimization_barrier((filter_taps, kept))
    scaled = (filter_taps * jnp.repeat(tap_blocks.astype(jnp.float32), BLK, axis=1)).astype(jnp.bfloat16)
    span = taps + 2 * BLK
    table, table_next, w_half, marks = kernel_call(
        tables_kernel,
        (
            shape((groups, 2, BLK, span), jnp.bfloat16),
            shape((groups, BLK, 2 * BLK), jnp.bfloat16),
            shape((3, 3, width), jnp.float32),
            shape((4, 8, GROUP), jnp.float32),
        ),
        [SMEM, VMEM, VMEM],
        [pltpu.VMEM((2 * groups, span), jnp.float32), pltpu.VMEM((3, BLK, span), jnp.float32)],
        40 * groups * BLK * taps,
        8 * groups * BLK * taps,
    )(seq_lengths, scaled, short_weight)
    table, table_next, pair[0] = lax.optimization_barrier((table, table_next, pair[0]))

    half = lax.axis_index("half")
    query, _ = lax.optimization_barrier((panels, pair[0]))
    qkept = lax.dynamic_slice(query, (0, 0, half * width), (1, rows, width))[0]
    qsent = lax.dynamic_slice(query, (0, 0, (1 - half) * width), (1, rows, width))[0]
    qkept, qsent, pair[1] = lax.optimization_barrier((qkept, qsent, pair[1]))
    qgot = moved(qsent, to_pair)
    back_pair = [moved(piece, ahead) for piece in pair]

    window = pltpu.VMEM((4 * rows, width), jnp.bfloat16)
    extras = pltpu.VMEM((4, 16, width), jnp.float32)
    shifted = pltpu.VMEM((2, rows + 8, GROUP), jnp.float32)
    short = whole_tokens // 2 <= 4 * BLK
    if short:
        onward = [(i, i ^ 1 if i < 2 else i + 2 if i + 2 < 2 * blocks else 2 + i % 2) for i in spots]
        far = []
        for piece in range(2):
            relayed = kernel_call(
                functools.partial(relay_kernel, piece),
                small,
                [VMEM] * 5,
                [pltpu.VMEM((2 * rows, width // 2), jnp.bfloat16), pltpu.VMEM((2, 16, width // 2), jnp.float32)],
                2 * rows * BLK * width,
                4 * rows * width,
            )(marks, table_next, back_own, back_pair[piece], w_half)
            far.append(moved(relayed, onward))
    else:
        across = jnp.concatenate([piece[rows:] for piece in sent], 1)
        across = moved(across, [(i, ((i ^ 1) + 6) % (2 * blocks)) for i in spots])
        straight = moved(kept[rows:], [(i, (i + 6) % (2 * blocks)) for i in spots])
        deep = jnp.where(half == 1, straight, across)
        far = [moved(piece, ahead) for piece in (back_own, *back_pair)] + [deep]

    acc, qown = kernel_call(
        near_kernel,
        (shape((2 * rows, width), jnp.float32), half_wide),
        [VMEM] * 12,
        [window, extras, shifted, row_mask, row_mask],
        2 * 5 * rows * BLK * width,
        16 * rows * width,
    )(lengths, marks, table, kept, back_own, *pair, *back_pair, qkept, w_half, skip_bias.reshape(1, -1))

    qpair = kernel_call(
        pair_gate_kernel,
        half_wide,
        [VMEM] * 5,
        [shifted, row_mask, row_mask],
        10 * rows * width,
        8 * rows * width,
    )(lengths, qgot, kept, back_own, w_half)

    done, power, send = [], None, None
    for piece in range(2):
        needed = far[piece : piece + 1] if short else far
        before = [power, send] if piece else []
        own, send, power = kernel_call(
            functools.partial(far_kernel, short, piece),
            (
                shape((rows, width // 2), jnp.float32),
                shape((rows, width if piece else width // 2), jnp.bfloat16),
                shape((1, 2 * rows) if piece else (2, rows, GROUP), jnp.float32),
            ),
            [VMEM] * (8 + len(needed) + len(before)),
            [pltpu.VMEM((3 * rows, width // 2), jnp.bfloat16), pltpu.VMEM((3, 16, width // 2), jnp.float32)],
            2 * 3 * rows * BLK * width,
            12 * rows * width,
        )(table, acc, qown, qpair, w_half, marks, back_own, back_pair[piece], *needed, *before)
        done.append(own)
    back = moved(send, to_pair)

    peers = lax.axis_size("mp")
    shares = [lax.ppermute(power, "mp", [(i, i ^ k) for i in range(peers)]) for k in range(1, peers)]
    power = sum(shares, power)
    return kernel_call(
        functools.partial(norm_kernel, channels),
        shape((rows, 2 * width), jnp.bfloat16),
        [VMEM] * 6,
        [],
        8 * rows * width,
        10 * rows * width,
    )(power, moved(power, to_pair), *done, back, norm_gain.reshape(1, -1))


def solution(mesh):
    blocks = mesh.shape["ctx"] // 2
    grid = Mesh(mesh.devices.reshape(blocks, 2, mesh.shape["mp"]), ("blk", "half", "mp"))
    in_specs = (
        P(SPOTS, None, "mp"),
        P(None, None, "mp"),
        P("mp", None),
        P("mp", None),
        P("mp"),
        P("mp"),
        P(),
    )

    def program(projected, *rest):
        body = functools.partial(shards, blocks, projected.shape[0], projected.shape[2])
        return jax.shard_map(
            body, mesh=grid, in_specs=in_specs, out_specs=P(SPOTS, "mp"), check_vma=False
        )(projected, *rest)

    return program
```

```python
import functools

import jax
import jax.numpy as jnp
from jax import lax
from jax.experimental import pallas as pl
from jax.experimental.pallas import tpu as pltpu
from jax.sharding import Mesh, PartitionSpec as P

GROUP = 128
BLK = 128
norm_eps = 1e-06

VMEM = pl.BlockSpec(memory_space=pltpu.VMEM)
SMEM = pl.BlockSpec(memory_space=pltpu.SMEM)
SPOTS = ("blk", "half")


def moved(block, pairs):
    return lax.ppermute(block, SPOTS, pairs)


def boundaries(seq_ref, t):
    def step(k, carry):
        end, first, second = carry
        end = end + seq_ref[k]
        return end, first | (t == end).astype(jnp.int32), second | (t - 1 == end).astype(jnp.int32)

    first = (t == 0).astype(jnp.int32)
    second = (t == 1).astype(jnp.int32)
    _, first, second = lax.fori_loop(0, seq_ref.shape[0], step, (jnp.int32(0), first, second), unroll=True)
    return first, first | second


def mask_columns(lengths_ref, start):
    count = lengths_ref.shape[1]
    square = (count, count)
    upto = lax.broadcasted_iota(jnp.int32, square, 1) <= lax.broadcasted_iota(jnp.int32, square, 0)
    lengths = jnp.broadcast_to(lengths_ref[...].astype(jnp.float32), square)
    ends = jnp.sum(jnp.where(upto, lengths, 0.0), axis=1, keepdims=True)
    t = (start + lax.broadcasted_iota(jnp.int32, (count, BLK), 1)).astype(jnp.float32)
    opens = (t == ends) | (t == 0.0)
    after = opens | (t - 1.0 == ends) | (t == 1.0)
    diagonal = lax.broadcasted_iota(jnp.int32, (BLK, BLK), 0) == lax.broadcasted_iota(jnp.int32, (BLK, BLK), 1)
    columns = []
    for mark in (opens, after):
        keep = 1.0 - jnp.max(mark.astype(jnp.float32), axis=0, keepdims=True)
        columns.append(jnp.sum(jnp.where(diagonal, keep, 0.0), axis=1, keepdims=True))
    return columns


def row_masks(lengths_ref, start, m1_ref, m2_ref):
    for column, m_ref in zip(mask_columns(lengths_ref, start), (m1_ref, m2_ref)):
        m_ref[...] = jnp.broadcast_to(column, m_ref.shape)


def counted(seq_ref, t):
    def step(k, carry):
        end, total = carry
        end = end + seq_ref[k]
        return end, total + (end <= t).astype(jnp.int32)

    _, total = lax.fori_loop(
        0, seq_ref.shape[0], step, (jnp.int32(0), jnp.zeros(t.shape, jnp.int32)), unroll=True
    )
    return jnp.where(t >= 0, total, -1)


def feature(x, x_ref, w, m1_ref, m2_ref):
    rows = x.shape[0]
    return (
        w[0:1] * x
        + w[1:2] * x_ref[7 : rows + 7, :] * m1_ref[...]
        + w[2:3] * x_ref[6 : rows + 6, :] * m2_ref[...]
    )


def products_kernel(seq_hbm, panels_hbm, w_hbm, *refs):
    outs, (kept_ref, *sent_refs), refs = refs[:3], refs[3:6], refs[6:]
    seq_ref, kv_ref, q_ref, w_ref, shift_ref, sems = refs
    width = kept_ref.shape[1]
    rows = kv_ref.shape[2]
    pieces = kv_ref.shape[0]
    piece = kv_ref.shape[3]
    half = lax.axis_index("half")
    shard = lax.axis_index("blk") * 2 + half
    keep_at = pl.multiple_of(half * width, width)
    send_at = pl.multiple_of((1 - half) * width, width)

    loads = [pltpu.make_async_copy(seq_hbm, seq_ref, sems.at[0])]
    for p in range(pieces):
        at = keep_at if p < pieces // 2 else send_at
        lanes = pl.ds(pl.multiple_of(at + (p % (pieces // 2)) * piece, piece), piece)
        loads.append(pltpu.make_async_copy(panels_hbm.at[1:3, :, lanes], kv_ref.at[p], sems.at[1 + p]))
    loads.append(pltpu.make_async_copy(w_hbm, w_ref, sems.at[1 + pieces]))
    loads.append(pltpu.make_async_copy(panels_hbm.at[0, rows - 16 :, :], q_ref, sems.at[2 + pieces]))
    for load in loads:
        load.start()
    loads[0].wait()
    place = lax.broadcasted_iota(jnp.int32, (rows, rows), 0) - lax.broadcasted_iota(jnp.int32, (rows, rows), 1)
    for j, column in enumerate(mask_columns(seq_ref, shard * rows)):
        shift_ref[j * rows : (j + 1) * rows, :] = jnp.where(place == j + 1, column, 0.0).astype(shift_ref.dtype)
    loads[1 + pieces].wait()
    loads[2 + pieces].wait()
    stores = []
    for p in range(pieces):
        loads[1 + p].wait()
        out_ref, at = (kept_ref, keep_at) if p < pieces // 2 else (sent_refs[p - pieces // 2], send_at)
        step = 2 * GROUP
        for c in range(0, piece, step):
            base = (p % (pieces // 2)) * piece + c
            there = slice(base, base + step) if p < pieces // 2 else slice(c, c + step)
            lanes = pl.ds(pl.multiple_of(at + base, step), step)
            raw, made = [], []
            for i in range(2):
                x = kv_ref[p, i, :, c : c + step]
                moved_rows = jnp.dot(shift_ref[...], x, preferred_element_type=jnp.float32)
                w = w_ref[1 + i, :, lanes]
                x = x.astype(jnp.float32)
                made.append(w[0:1] * x + w[1:2] * moved_rows[:rows] + w[2:3] * moved_rows[rows:])
                raw.append(x)
            product = made[0] * made[1]
            top = jnp.where(lax.broadcasted_iota(jnp.int32, (8, step), 0) < 2, raw[0][:8], product[:8])
            out_ref[:rows, there] = jnp.concatenate([top, product[8:]], 0).astype(out_ref.dtype)
            tails = [x[rows - 2 :] for x in raw] + [q_ref[:, lanes].astype(jnp.float32)[14:]]
            out_ref[rows:, there] = jnp.concatenate([raw[1][0:2]] + tails, 0).astype(out_ref.dtype)
        if p >= pieces // 2 - 1:
            done = p - pieces // 2 + 1
            stores.append(pltpu.make_async_copy(out_ref, outs[done], sems.at[3 + pieces + done]))
            stores[-1].start()
    for store in stores:
        store.wait()


def edge_marks(seq_ref):
    t = (
        (lax.axis_index("blk") - 2) * (2 * BLK)
        + lax.broadcasted_iota(jnp.int32, (8, GROUP), 1) * BLK
        + lax.broadcasted_iota(jnp.int32, (8, GROUP), 0)
    )
    return [1.0 - mark.astype(jnp.float32) for mark in boundaries(seq_ref, t)]


def first_rows(now, ahead, w_ref, marks, spot, lanes=slice(None)):
    m1, m2 = [mark[:, spot : spot + 1] for mark in marks]
    top = lax.broadcasted_iota(jnp.int32, ahead.shape, 0) == 0
    made = []
    for i, x0 in enumerate((now[8:], now[:8])):
        x1 = jnp.where(top, pltpu.roll(ahead, 5 - 2 * i, 0), pltpu.roll(x0, 1, 0))
        x2 = pltpu.roll(ahead, 6 - 2 * i, 0)
        w = w_ref[1 + i, :, lanes]
        made.append(w[0:1] * x0 + w[1:2] * x1 * m1 + w[2:3] * x2 * m2)
    return made[0] * made[1]


def put_first_rows(win_ref, at, rows):
    old = win_ref[at : at + 16, :].astype(jnp.float32)
    new = jnp.concatenate([rows, rows], 0)
    first = lax.broadcasted_iota(jnp.int32, old.shape, 0) < 2
    win_ref[at : at + 16, :] = jnp.where(first, new, old).astype(win_ref.dtype)


def reaches_past(seq_ref, block):
    first = block * (2 * BLK)

    def step(k, carry):
        end, start = carry
        end = end + seq_ref[k]
        return end, jnp.where(end <= first, end, start)

    _, start = lax.fori_loop(0, seq_ref.shape[0], step, (jnp.int32(0), jnp.int32(0)), unroll=True)
    return first - 2 * BLK - start > BLK


def tables_kernel(seq_ref, taps_ref, w_ref, out_ref, next_ref, w_half_ref, marks_ref, rev_ref, m_ref):
    groups = out_ref.shape[0]
    taps = taps_ref.shape[1]
    span = out_ref.shape[3]
    half = lax.axis_index("half")
    start = lax.axis_index("blk") * (2 * BLK)
    marks_ref[0], marks_ref[1] = edge_marks(seq_ref)
    for ahead in range(2):
        flag = reaches_past(seq_ref, lax.axis_index("blk") + ahead)
        marks_ref[2 + ahead] = jnp.full((8, GROUP), flag.astype(jnp.float32))
    width = w_half_ref.shape[2]
    w_half_ref[...] = w_ref[:, :, pl.ds(pl.multiple_of(half * width, width), width)]
    turn = lax.broadcasted_iota(jnp.int32, (taps, span), 0) + lax.broadcasted_iota(
        jnp.int32, (taps, span), 1
    )
    turn = (turn == taps).astype(jnp.bfloat16)
    rev_ref[...] = jnp.dot(taps_ref[...], turn, preferred_element_type=jnp.float32)
    seg_in = counted(seq_ref, start - taps + lax.broadcasted_iota(jnp.int32, (8, span), 1))[0:1]
    for part in range(3):
        t_out = start + part * BLK + lax.broadcasted_iota(jnp.int32, (BLK, GROUP), 0)
        seg_out = counted(seq_ref, t_out)[:, 0:1]
        if part < 2:
            m_ref[part] = (seg_in == seg_out).astype(jnp.float32)
        else:
            m_ref[2, :, : 2 * BLK] = (seg_in[:, 2 * BLK : 4 * BLK] == seg_out).astype(jnp.float32)

    def one(g, _):
        row = rev_ref[pl.ds(half * groups + g, 1), :]
        table = pltpu.roll(jnp.broadcast_to(row, (BLK, span)), 0, 1, stride=1, stride_axis=0)
        out_ref[g, 0] = (table * m_ref[0]).astype(out_ref.dtype)
        later = jnp.concatenate([table[:, span - BLK :], table[:, : span - BLK]], 1)
        out_ref[g, 1] = (later * m_ref[1]).astype(out_ref.dtype)
        next_ref[g] = (table[:, : 2 * BLK] * m_ref[2, :, : 2 * BLK]).astype(next_ref.dtype)
        return 0

    lax.fori_loop(0, groups, one, 0)


def fill(win_ref, extra_ref, spot, *pieces):
    at = 0
    for piece in pieces:
        lanes = slice(at, at + piece.shape[1])
        win_ref[pl.ds(pl.multiple_of(spot * BLK, BLK), BLK), lanes] = piece[:BLK]
        extra_ref[spot, :8, lanes] = piece[BLK:].astype(jnp.float32)
        extra_ref[spot, 8:, lanes] = piece[:16].astype(jnp.float32)[:8]
        at += piece.shape[1]


def relay_kernel(piece, marks_ref, next_ref, back_own_ref, back_pair_ref, w_ref, out_ref, win_ref, extra_ref):
    width = out_ref.shape[1]
    half = lax.axis_index("half")
    lanes = slice(piece * width, (piece + 1) * width)
    fill(win_ref, extra_ref, half, back_own_ref.at[:, lanes])
    fill(win_ref, extra_ref, 1 - half, back_pair_ref)
    marks = [marks_ref[0], marks_ref[1]]
    put_first_rows(win_ref, 0, first_rows(extra_ref[0], jnp.zeros((8, width), jnp.float32), w_ref, marks, 2, lanes))
    put_first_rows(win_ref, BLK, first_rows(extra_ref[1], extra_ref[0, :8], w_ref, marks, 3, lanes))
    out_ref[BLK:] = extra_ref[1, :8].astype(out_ref.dtype)
    summed = jnp.max(marks_ref[3]) > 0.5

    @pl.when(summed)
    def _():
        for c in range(0, width, GROUP):
            total = jnp.dot(
                next_ref[(piece * width + c) // GROUP],
                win_ref[:, c : c + GROUP],
                preferred_element_type=jnp.float32,
            )
            out_ref[:BLK, c : c + GROUP] = total.astype(out_ref.dtype)

    @pl.when(jnp.logical_not(summed))
    def _():
        out_ref[:BLK] = win_ref[BLK:]


def gate_rows(seq_ref, raw_ref, tail, w_ref, part, q_ref, x_ref, m1_ref, m2_ref):
    width = raw_ref.shape[1]
    row_masks(seq_ref, lax.axis_index("blk") * (2 * BLK) + part * BLK, m1_ref, m2_ref)
    for c in range(0, width, GROUP):
        lanes = slice(c, c + GROUP)
        w = w_ref[0, :, lanes]
        x = raw_ref[:, lanes].astype(jnp.float32)
        slot = (c // GROUP) % 2
        x_ref[slot, 6:8, :] = tail(lanes)
        x_ref[slot, 8:, :] = x
        q_ref[:, lanes] = feature(x, x_ref.at[slot], w, m1_ref, m2_ref)


def near_kernel(
    seq_ref, marks_ref, table_ref, own_ref, back_own_ref, pair_a_ref, pair_b_ref, back_a_ref, back_b_ref, qkept_ref, w_ref, bias_ref,
    acc_ref, q_ref, win_ref, extra_ref, x_ref, m1_ref, m2_ref,
):
    groups = table_ref.shape[0]
    width = groups * GROUP
    half = lax.axis_index("half")
    fill(win_ref, extra_ref, half, back_own_ref)
    fill(win_ref, extra_ref, 1 - half, back_a_ref, back_b_ref)
    fill(win_ref, extra_ref, 2 + half, own_ref)
    fill(win_ref, extra_ref, 3 - half, pair_a_ref, pair_b_ref)
    marks = [marks_ref[0], marks_ref[1]]
    for spot in (1, 2, 3):
        rows = first_rows(extra_ref[spot], extra_ref[spot - 1, :8], w_ref, marks, spot + 2)
        put_first_rows(win_ref, spot * BLK, rows)
    for g in range(groups):
        lanes = slice(g * GROUP, (g + 1) * GROUP)
        bias = bias_ref[:, pl.ds(pl.multiple_of(half * width + g * GROUP, GROUP), GROUP)]
        for part in range(2):
            total = jnp.dot(
                table_ref[g, part, :, 3 * BLK : (5 + part) * BLK],
                win_ref[BLK : (3 + part) * BLK, lanes],
                preferred_element_type=jnp.float32,
            )
            here = win_ref[(2 + part) * BLK : (3 + part) * BLK, lanes].astype(jnp.float32)
            acc_ref[part * BLK : (part + 1) * BLK, lanes] = total + bias * here
    gate_rows(
        seq_ref, qkept_ref, lambda lanes: extra_ref[1 + half, 6:8, lanes], w_ref, half, q_ref, x_ref, m1_ref, m2_ref
    )


def pair_gate_kernel(seq_ref, raw_ref, own_ref, back_own_ref, w_ref, q_ref, x_ref, m1_ref, m2_ref):
    half = lax.axis_index("half")

    def tail(lanes):
        back = back_own_ref[BLK:, lanes].astype(jnp.float32)
        own = own_ref[BLK:, lanes].astype(jnp.float32)
        return jnp.where(half == 1, back, own)[6:8]

    gate_rows(seq_ref, raw_ref, tail, w_ref, 1 - half, q_ref, x_ref, m1_ref, m2_ref)


def far_kernel(
    short, piece, table_ref, acc_ref, qown_ref, qpair_ref, w_ref, marks_ref, back_own_ref, back_pair_ref, *refs
):
    *refs, kept_ref, sent_ref, total_ref, win_ref, extra_ref = refs
    far_refs, before = refs[: len(refs) - 2 * piece], refs[len(refs) - 2 * piece :]
    width = kept_ref.shape[1]
    half = lax.axis_index("half")
    lanes = slice(piece * width, (piece + 1) * width)
    marks = [marks_ref[0], marks_ref[1]]
    low = 1 if short else 0

    @pl.when(half == 0)
    def _():
        fill(win_ref, extra_ref, 2, back_own_ref.at[:, lanes])

    @pl.when(half == 1)
    def _():
        fill(win_ref, extra_ref, 2, back_pair_ref)

    if short:
        summed = marks_ref[2, 0:1, 0:1]
        fill(win_ref, extra_ref, 1, far_refs[0])
        payload = win_ref[BLK : 2 * BLK, :].astype(jnp.float32)
        win_ref[BLK : 2 * BLK, :] = (payload * (1.0 - summed)).astype(win_ref.dtype)
    else:
        fill(win_ref, extra_ref, half, far_refs[0].at[:, lanes])
        fill(win_ref, extra_ref, 1 - half, far_refs[1 + piece])
        ahead = far_refs[3][:, lanes].astype(jnp.float32)
        put_first_rows(win_ref, 0, first_rows(extra_ref[0], ahead, w_ref, marks, 0, lanes))
        put_first_rows(win_ref, BLK, first_rows(extra_ref[1], extra_ref[0, :8], w_ref, marks, 1, lanes))
    put_first_rows(win_ref, 2 * BLK, first_rows(extra_ref[2], extra_ref[1, :8], w_ref, marks, 2, lanes))
    if before:
        sent_ref[:, :width] = before[1][...]
    for i, (part, q_ref, out_ref) in enumerate(((half, qown_ref, kept_ref), (1 - half, qpair_ref, sent_ref))):
        part_sent = i == 1
        squares = before[0][i] if before else jnp.zeros((BLK, GROUP), jnp.float32)
        rows = pl.ds(pl.multiple_of(part * BLK, BLK), BLK)
        for c in range(0, width, GROUP):
            here = slice(c, c + GROUP)
            whole = slice(piece * width + c, piece * width + c + GROUP)
            filtered = acc_ref[rows, whole] + jnp.dot(
                table_ref[(piece * width + c) // GROUP, part, :, low * BLK : 3 * BLK],
                win_ref[low * BLK : 3 * BLK, here],
                preferred_element_type=jnp.float32,
            )
            if short:
                weight = summed * (part == 0).astype(jnp.float32)
                filtered = filtered + weight * far_refs[0][:BLK, here].astype(jnp.float32)
            gated = q_ref[:, whole] * filtered
            squares = squares + gated * gated
            out_ref[:, whole if before and part_sent else here] = gated.astype(out_ref.dtype)
        if before:
            total_ref[:, i * BLK : (i + 1) * BLK] = lax.dot_general(
                jnp.ones((8, GROUP), jnp.float32),
                squares,
                (((1,), (1,)), ((), ())),
                precision=lax.Precision.HIGHEST,
                preferred_element_type=jnp.float32,
            )[0:1]
        else:
            total_ref[i] = squares


def norm_kernel(channels, power_ref, power_got_ref, *refs):
    *kept_refs, got_ref, gain_ref, out_ref = refs
    half = lax.axis_index("half")
    power = power_ref[:, :BLK] + power_got_ref[:, BLK:]
    scale = lax.rsqrt(power / channels + norm_eps)
    diagonal = lax.broadcasted_iota(jnp.int32, (BLK, BLK), 0) == lax.broadcasted_iota(
        jnp.int32, (BLK, BLK), 1
    )
    column = jnp.sum(jnp.where(diagonal, scale, 0.0), axis=1, keepdims=True)
    for at, refs in ((half, kept_refs), (1 - half, [got_ref])):
        at = at * got_ref.shape[1]
        for ref in refs:
            for c in range(0, ref.shape[1], GROUP):
                lanes = pl.ds(pl.multiple_of(at + c, GROUP), GROUP)
                part = ref[:, c : c + GROUP].astype(jnp.float32)
                out_ref[:, lanes] = (part * column * gain_ref[:, lanes]).astype(out_ref.dtype)
            at = at + ref.shape[1]


def kernel_call(body, outs, in_specs, scratch, flops, moved_bytes, vmem=24 << 20, out_space=VMEM):
    return pl.pallas_call(
        body,
        out_shape=outs,
        in_specs=in_specs,
        out_specs=jax.tree.map(lambda _: out_space, outs),
        scratch_shapes=scratch,
        compiler_params=pltpu.CompilerParams(vmem_limit_bytes=vmem),
        cost_estimate=pl.CostEstimate(flops=flops, bytes_accessed=moved_bytes, transcendentals=0),
    )


def shards(blocks, whole_tokens, channels, projected, short_weight, filter_taps, tap_blocks, skip_bias, norm_gain, seq_lengths):
    rows = projected.shape[0]
    width = projected.shape[2] // 2
    groups = width // GROUP
    taps = filter_taps.shape[1]
    shape = jax.ShapeDtypeStruct
    half_shape = shape((rows, width), jnp.bfloat16)
    half_wide = shape((rows, width), jnp.float32)

    spots = range(2 * blocks)
    to_pair = [(i, i ^ 1) for i in spots]
    ahead = [(i, (i + 2) % (2 * blocks)) for i in spots]

    panels = jnp.transpose(projected, (1, 0, 2))
    message = shape((rows + 8, width), jnp.bfloat16)
    small = shape((rows + 8, width // 2), jnp.bfloat16)
    hbm = pl.BlockSpec(memory_space=pltpu.HBM)
    pieces = 4
    lengths = seq_lengths.reshape(1, -1)
    row_mask = pltpu.VMEM((rows, GROUP), jnp.float32)

    kept, *sent = kernel_call(
        products_kernel,
        (message, small, small),
        [hbm] * 3,
        [
            pltpu.VMEM(message.shape, message.dtype),
            pltpu.VMEM(small.shape, small.dtype),
            pltpu.VMEM(small.shape, small.dtype),
            pltpu.VMEM(lengths.shape, jnp.int32),
            pltpu.VMEM((pieces, 2, rows, 2 * width // pieces), jnp.bfloat16),
            pltpu.VMEM((16, 2 * width), jnp.bfloat16),
            pltpu.VMEM(short_weight.shape, jnp.float32),
            pltpu.VMEM((2 * rows, rows), jnp.bfloat16),
            pltpu.SemaphoreType.DMA((6 + pieces,)),
        ],
        40 * rows * width,
        16 * rows * width,
        60 << 20,
        hbm,
    )(lengths, panels, short_weight)

    back_own = moved(kept, ahead)
    pair = [moved(piece, to_pair) for piece in sent]

    filter_taps, _ = lax.optimization_barrier((filter_taps, kept))
    scaled = (filter_taps * jnp.repeat(tap_blocks.astype(jnp.float32), BLK, axis=1)).astype(jnp.bfloat16)
    span = taps + 2 * BLK
    table, table_next, w_half, marks = kernel_call(
        tables_kernel,
        (
            shape((groups, 2, BLK, span), jnp.bfloat16),
            shape((groups, BLK, 2 * BLK), jnp.bfloat16),
            shape((3, 3, width), jnp.float32),
            shape((4, 8, GROUP), jnp.float32),
        ),
        [SMEM, VMEM, VMEM],
        [pltpu.VMEM((2 * groups, span), jnp.float32), pltpu.VMEM((3, BLK, span), jnp.float32)],
        40 * groups * BLK * taps,
        8 * groups * BLK * taps,
    )(seq_lengths, scaled, short_weight)
    table, table_next, pair[0] = lax.optimization_barrier((table, table_next, pair[0]))

    half = lax.axis_index("half")
    query, _ = lax.optimization_barrier((panels, pair[0]))
    qkept = lax.dynamic_slice(query, (0, 0, half * width), (1, rows, width))[0]
    qsent = lax.dynamic_slice(query, (0, 0, (1 - half) * width), (1, rows, width))[0]
    qkept, qsent, pair[1] = lax.optimization_barrier((qkept, qsent, pair[1]))
    qgot = moved(qsent, to_pair)
    back_pair = [moved(piece, ahead) for piece in pair]

    window = pltpu.VMEM((4 * rows, width), jnp.bfloat16)
    extras = pltpu.VMEM((4, 16, width), jnp.float32)
    shifted = pltpu.VMEM((2, rows + 8, GROUP), jnp.float32)
    short = whole_tokens // 2 <= 4 * BLK
    if short:
        onward = [(i, i ^ 1 if i < 2 else i + 2 if i + 2 < 2 * blocks else 2 + i % 2) for i in spots]
        far = []
        for piece in range(2):
            relayed = kernel_call(
                functools.partial(relay_kernel, piece),
                small,
                [VMEM] * 5,
                [pltpu.VMEM((2 * rows, width // 2), jnp.bfloat16), pltpu.VMEM((2, 16, width // 2), jnp.float32)],
                2 * rows * BLK * width,
                4 * rows * width,
            )(marks, table_next, back_own, back_pair[piece], w_half)
            far.append(moved(relayed, onward))
    else:
        across = jnp.concatenate([piece[rows:] for piece in sent], 1)
        across = moved(across, [(i, ((i ^ 1) + 6) % (2 * blocks)) for i in spots])
        straight = moved(kept[rows:], [(i, (i + 6) % (2 * blocks)) for i in spots])
        deep = jnp.where(half == 1, straight, across)
        far = [moved(piece, ahead) for piece in (back_own, *back_pair)] + [deep]

    acc, qown = kernel_call(
        near_kernel,
        (shape((2 * rows, width), jnp.float32), half_wide),
        [VMEM] * 12,
        [window, extras, shifted, row_mask, row_mask],
        2 * 5 * rows * BLK * width,
        16 * rows * width,
    )(lengths, marks, table, kept, back_own, *pair, *back_pair, qkept, w_half, skip_bias.reshape(1, -1))

    qpair = kernel_call(
        pair_gate_kernel,
        half_wide,
        [VMEM] * 5,
        [shifted, row_mask, row_mask],
        10 * rows * width,
        8 * rows * width,
    )(lengths, qgot, kept, back_own, w_half)

    done, power, send = [], None, None
    for piece in range(2):
        needed = far[piece : piece + 1] if short else far
        before = [power, send] if piece else []
        own, send, power = kernel_call(
            functools.partial(far_kernel, short, piece),
            (
                shape((rows, width // 2), jnp.float32),
                shape((rows, width if piece else width // 2), jnp.bfloat16),
                shape((1, 2 * rows) if piece else (2, rows, GROUP), jnp.float32),
            ),
            [VMEM] * (8 + len(needed) + len(before)),
            [pltpu.VMEM((3 * rows, width // 2), jnp.bfloat16), pltpu.VMEM((3, 16, width // 2), jnp.float32)],
            2 * 3 * rows * BLK * width,
            12 * rows * width,
        )(table, acc, qown, qpair, w_half, marks, back_own, back_pair[piece], *needed, *before)
        done.append(own)
    back = moved(send, to_pair)

    peers = lax.axis_size("mp")
    shares = [lax.ppermute(power, "mp", [(i, i ^ k) for i in range(peers)]) for k in range(1, peers)]
    power = sum(shares, power)
    return kernel_call(
        functools.partial(norm_kernel, channels),
        shape((rows, 2 * width), jnp.bfloat16),
        [VMEM] * 6,
        [],
        8 * rows * width,
        10 * rows * width,
    )(power, moved(power, to_pair), *done, back, norm_gain.reshape(1, -1))


def solution(mesh):
    blocks = mesh.shape["ctx"] // 2
    grid = Mesh(mesh.devices.reshape(blocks, 2, mesh.shape["mp"]), ("blk", "half", "mp"))
    in_specs = (
        P(SPOTS, None, "mp"),
        P(None, None, "mp"),
        P("mp", None),
        P("mp", None),
        P("mp"),
        P("mp"),
        P(),
    )

    def program(projected, *rest):
        body = functools.partial(shards, blocks, projected.shape[0], projected.shape[2])
        return jax.shard_map(
            body, mesh=grid, in_specs=in_specs, out_specs=P(SPOTS, "mp"), check_vma=False
        )(projected, *rest)

    return program
```

```python
import functools

import jax
import jax.numpy as jnp
from jax import lax
from jax.experimental import pallas as pl
from jax.experimental.pallas import tpu as pltpu
from jax.sharding import Mesh, PartitionSpec as P

GROUP = 128
BLK = 128
norm_eps = 1e-06

VMEM = pl.BlockSpec(memory_space=pltpu.VMEM)
SMEM = pl.BlockSpec(memory_space=pltpu.SMEM)
SPOTS = ("blk", "half")


def moved(block, pairs):
    return lax.ppermute(block, SPOTS, pairs)


def boundaries(seq_ref, t):
    def step(k, carry):
        end, first, second = carry
        end = end + seq_ref[k]
        return end, first | (t == end).astype(jnp.int32), second | (t - 1 == end).astype(jnp.int32)

    first = (t == 0).astype(jnp.int32)
    second = (t == 1).astype(jnp.int32)
    _, first, second = lax.fori_loop(0, seq_ref.shape[0], step, (jnp.int32(0), first, second), unroll=True)
    return first, first | second


def row_masks(lengths_ref, start, m1_ref, m2_ref):
    count = lengths_ref.shape[1]
    square = (count, count)
    upto = lax.broadcasted_iota(jnp.int32, square, 1) <= lax.broadcasted_iota(jnp.int32, square, 0)
    lengths = jnp.broadcast_to(lengths_ref[...].astype(jnp.float32), square)
    ends = jnp.sum(jnp.where(upto, lengths, 0.0), axis=1, keepdims=True)
    t = (start + lax.broadcasted_iota(jnp.int32, (count, BLK), 1)).astype(jnp.float32)
    opens = (t == ends) | (t == 0.0)
    after = opens | (t - 1.0 == ends) | (t == 1.0)
    diagonal = lax.broadcasted_iota(jnp.int32, (BLK, BLK), 0) == lax.broadcasted_iota(jnp.int32, (BLK, BLK), 1)
    for mark, m_ref in ((opens, m1_ref), (after, m2_ref)):
        keep = 1.0 - jnp.max(mark.astype(jnp.float32), axis=0, keepdims=True)
        column = jnp.sum(jnp.where(diagonal, keep, 0.0), axis=1, keepdims=True)
        m_ref[...] = jnp.broadcast_to(column, m_ref.shape)


def counted(seq_ref, t):
    def step(k, carry):
        end, total = carry
        end = end + seq_ref[k]
        return end, total + (end <= t).astype(jnp.int32)

    _, total = lax.fori_loop(
        0, seq_ref.shape[0], step, (jnp.int32(0), jnp.zeros(t.shape, jnp.int32)), unroll=True
    )
    return jnp.where(t >= 0, total, -1)


def feature(x, x_ref, w, m1_ref, m2_ref):
    rows = x.shape[0]
    return (
        w[0:1] * x
        + w[1:2] * x_ref[7 : rows + 7, :] * m1_ref[...]
        + w[2:3] * x_ref[6 : rows + 6, :] * m2_ref[...]
    )


def products_kernel(seq_hbm, panels_hbm, w_hbm, *refs):
    (kept_ref, *sent_refs), refs = refs[:3], refs[3:]
    seq_ref, kv_ref, q_ref, w_ref, x_ref, m1_ref, m2_ref, sems = refs
    width = kept_ref.shape[1]
    rows = kv_ref.shape[2]
    pieces = kv_ref.shape[0]
    piece = kv_ref.shape[3]
    half = lax.axis_index("half")
    shard = lax.axis_index("blk") * 2 + half
    keep_at = pl.multiple_of(half * width, width)
    send_at = pl.multiple_of((1 - half) * width, width)

    loads = [pltpu.make_async_copy(seq_hbm, seq_ref, sems.at[0])]
    for p in range(pieces):
        at = keep_at if p < pieces // 2 else send_at
        lanes = pl.ds(pl.multiple_of(at + (p % (pieces // 2)) * piece, piece), piece)
        loads.append(pltpu.make_async_copy(panels_hbm.at[1:3, :, lanes], kv_ref.at[p], sems.at[1 + p]))
    loads.append(pltpu.make_async_copy(w_hbm, w_ref, sems.at[1 + pieces]))
    loads.append(pltpu.make_async_copy(panels_hbm.at[0, rows - 16 :, :], q_ref, sems.at[2 + pieces]))
    for load in loads:
        load.start()
    x_ref[:, 0:8, :] = jnp.zeros((x_ref.shape[0], 8, GROUP), jnp.float32)
    loads[0].wait()
    row_masks(seq_ref, shard * rows, m1_ref, m2_ref)
    loads[1 + pieces].wait()
    loads[2 + pieces].wait()
    for p in range(pieces):
        loads[1 + p].wait()
        out_ref, at = (kept_ref, keep_at) if p < pieces // 2 else (sent_refs[p - pieces // 2], send_at)
        for c in range(0, piece, GROUP):
            base = (p % (pieces // 2)) * piece + c
            there = slice(base, base + GROUP) if p < pieces // 2 else slice(c, c + GROUP)
            lanes = pl.ds(pl.multiple_of(at + base, GROUP), GROUP)
            slot = (c // GROUP) % (x_ref.shape[0] // 2) * 2
            raw, made = [], []
            for i in range(2):
                x = kv_ref[p, i, :, c : c + GROUP].astype(jnp.float32)
                x_ref[slot + i, 8:, :] = x
                made.append(feature(x, x_ref.at[slot + i], w_ref[1 + i, :, lanes], m1_ref, m2_ref))
                raw.append(x)
            product = made[0] * made[1]
            top = jnp.where(lax.broadcasted_iota(jnp.int32, (8, GROUP), 0) < 2, raw[0][:8], product[:8])
            out_ref[:rows, there] = jnp.concatenate([top, product[8:]], 0).astype(out_ref.dtype)
            tails = [x[rows - 2 :] for x in raw] + [q_ref[:, lanes].astype(jnp.float32)[14:]]
            out_ref[rows:, there] = jnp.concatenate([raw[1][0:2]] + tails, 0).astype(out_ref.dtype)


def edge_marks(seq_ref):
    t = (
        (lax.axis_index("blk") - 2) * (2 * BLK)
        + lax.broadcasted_iota(jnp.int32, (8, GROUP), 1) * BLK
        + lax.broadcasted_iota(jnp.int32, (8, GROUP), 0)
    )
    return [1.0 - mark.astype(jnp.float32) for mark in boundaries(seq_ref, t)]


def first_rows(now, ahead, w_ref, marks, spot, lanes=slice(None)):
    m1, m2 = [mark[:, spot : spot + 1] for mark in marks]
    top = lax.broadcasted_iota(jnp.int32, ahead.shape, 0) == 0
    made = []
    for i, x0 in enumerate((now[8:], now[:8])):
        x1 = jnp.where(top, pltpu.roll(ahead, 5 - 2 * i, 0), pltpu.roll(x0, 1, 0))
        x2 = pltpu.roll(ahead, 6 - 2 * i, 0)
        w = w_ref[1 + i, :, lanes]
        made.append(w[0:1] * x0 + w[1:2] * x1 * m1 + w[2:3] * x2 * m2)
    return made[0] * made[1]


def put_first_rows(win_ref, at, rows):
    old = win_ref[at : at + 16, :].astype(jnp.float32)
    new = jnp.concatenate([rows, rows], 0)
    first = lax.broadcasted_iota(jnp.int32, old.shape, 0) < 2
    win_ref[at : at + 16, :] = jnp.where(first, new, old).astype(win_ref.dtype)


def reaches_past(seq_ref, block):
    first = block * (2 * BLK)

    def step(k, carry):
        end, start = carry
        end = end + seq_ref[k]
        return end, jnp.where(end <= first, end, start)

    _, start = lax.fori_loop(0, seq_ref.shape[0], step, (jnp.int32(0), jnp.int32(0)), unroll=True)
    return first - 2 * BLK - start > BLK


def tables_kernel(seq_ref, taps_ref, w_ref, out_ref, next_ref, w_half_ref, marks_ref, rev_ref, m_ref):
    groups = out_ref.shape[0]
    taps = taps_ref.shape[1]
    span = out_ref.shape[3]
    half = lax.axis_index("half")
    start = lax.axis_index("blk") * (2 * BLK)
    marks_ref[0], marks_ref[1] = edge_marks(seq_ref)
    for ahead in range(2):
        flag = reaches_past(seq_ref, lax.axis_index("blk") + ahead)
        marks_ref[2 + ahead] = jnp.full((8, GROUP), flag.astype(jnp.float32))
    width = w_half_ref.shape[2]
    w_half_ref[...] = w_ref[:, :, pl.ds(pl.multiple_of(half * width, width), width)]
    turn = lax.broadcasted_iota(jnp.int32, (taps, span), 0) + lax.broadcasted_iota(
        jnp.int32, (taps, span), 1
    )
    turn = (turn == taps).astype(jnp.bfloat16)
    rev_ref[...] = jnp.dot(taps_ref[...], turn, preferred_element_type=jnp.float32)
    seg_in = counted(seq_ref, start - taps + lax.broadcasted_iota(jnp.int32, (8, span), 1))[0:1]
    for part in range(3):
        t_out = start + part * BLK + lax.broadcasted_iota(jnp.int32, (BLK, GROUP), 0)
        seg_out = counted(seq_ref, t_out)[:, 0:1]
        if part < 2:
            m_ref[part] = (seg_in == seg_out).astype(jnp.float32)
        else:
            m_ref[2, :, : 2 * BLK] = (seg_in[:, 2 * BLK : 4 * BLK] == seg_out).astype(jnp.float32)

    def one(g, _):
        row = rev_ref[pl.ds(half * groups + g, 1), :]
        table = pltpu.roll(jnp.broadcast_to(row, (BLK, span)), 0, 1, stride=1, stride_axis=0)
        out_ref[g, 0] = (table * m_ref[0]).astype(out_ref.dtype)
        later = jnp.concatenate([table[:, span - BLK :], table[:, : span - BLK]], 1)
        out_ref[g, 1] = (later * m_ref[1]).astype(out_ref.dtype)
        next_ref[g] = (table[:, : 2 * BLK] * m_ref[2, :, : 2 * BLK]).astype(next_ref.dtype)
        return 0

    lax.fori_loop(0, groups, one, 0)


def fill(win_ref, extra_ref, spot, *pieces):
    at = 0
    for piece in pieces:
        lanes = slice(at, at + piece.shape[1])
        win_ref[pl.ds(pl.multiple_of(spot * BLK, BLK), BLK), lanes] = piece[:BLK]
        extra_ref[spot, :8, lanes] = piece[BLK:].astype(jnp.float32)
        extra_ref[spot, 8:, lanes] = piece[:16].astype(jnp.float32)[:8]
        at += piece.shape[1]


def relay_kernel(piece, marks_ref, next_ref, back_own_ref, back_pair_ref, w_ref, out_ref, win_ref, extra_ref):
    width = out_ref.shape[1]
    half = lax.axis_index("half")
    lanes = slice(piece * width, (piece + 1) * width)
    fill(win_ref, extra_ref, half, back_own_ref.at[:, lanes])
    fill(win_ref, extra_ref, 1 - half, back_pair_ref)
    marks = [marks_ref[0], marks_ref[1]]
    put_first_rows(win_ref, 0, first_rows(extra_ref[0], jnp.zeros((8, width), jnp.float32), w_ref, marks, 2, lanes))
    put_first_rows(win_ref, BLK, first_rows(extra_ref[1], extra_ref[0, :8], w_ref, marks, 3, lanes))
    out_ref[BLK:] = extra_ref[1, :8].astype(out_ref.dtype)
    summed = jnp.max(marks_ref[3]) > 0.5

    @pl.when(summed)
    def _():
        for c in range(0, width, GROUP):
            total = jnp.dot(
                next_ref[(piece * width + c) // GROUP],
                win_ref[:, c : c + GROUP],
                preferred_element_type=jnp.float32,
            )
            out_ref[:BLK, c : c + GROUP] = total.astype(out_ref.dtype)

    @pl.when(jnp.logical_not(summed))
    def _():
        out_ref[:BLK] = win_ref[BLK:]


def gate_rows(seq_ref, raw_ref, tail, w_ref, part, q_ref, x_ref, m1_ref, m2_ref):
    width = raw_ref.shape[1]
    row_masks(seq_ref, lax.axis_index("blk") * (2 * BLK) + part * BLK, m1_ref, m2_ref)
    for c in range(0, width, GROUP):
        lanes = slice(c, c + GROUP)
        w = w_ref[0, :, lanes]
        x = raw_ref[:, lanes].astype(jnp.float32)
        slot = (c // GROUP) % 2
        x_ref[slot, 6:8, :] = tail(lanes)
        x_ref[slot, 8:, :] = x
        q_ref[:, lanes] = feature(x, x_ref.at[slot], w, m1_ref, m2_ref)


def near_kernel(
    seq_ref, marks_ref, table_ref, own_ref, back_own_ref, pair_a_ref, pair_b_ref, back_a_ref, back_b_ref, qkept_ref, w_ref, bias_ref,
    acc_ref, q_ref, win_ref, extra_ref, x_ref, m1_ref, m2_ref,
):
    groups = table_ref.shape[0]
    width = groups * GROUP
    half = lax.axis_index("half")
    fill(win_ref, extra_ref, half, back_own_ref)
    fill(win_ref, extra_ref, 1 - half, back_a_ref, back_b_ref)
    fill(win_ref, extra_ref, 2 + half, own_ref)
    fill(win_ref, extra_ref, 3 - half, pair_a_ref, pair_b_ref)
    marks = [marks_ref[0], marks_ref[1]]
    for spot in (1, 2, 3):
        rows = first_rows(extra_ref[spot], extra_ref[spot - 1, :8], w_ref, marks, spot + 2)
        put_first_rows(win_ref, spot * BLK, rows)
    for g in range(groups):
        lanes = slice(g * GROUP, (g + 1) * GROUP)
        bias = bias_ref[:, pl.ds(pl.multiple_of(half * width + g * GROUP, GROUP), GROUP)]
        for part in range(2):
            total = jnp.dot(
                table_ref[g, part, :, 3 * BLK : (5 + part) * BLK],
                win_ref[BLK : (3 + part) * BLK, lanes],
                preferred_element_type=jnp.float32,
            )
            here = win_ref[(2 + part) * BLK : (3 + part) * BLK, lanes].astype(jnp.float32)
            acc_ref[part * BLK : (part + 1) * BLK, lanes] = total + bias * here
    gate_rows(
        seq_ref, qkept_ref, lambda lanes: extra_ref[1 + half, 6:8, lanes], w_ref, half, q_ref, x_ref, m1_ref, m2_ref
    )


def pair_gate_kernel(seq_ref, raw_ref, own_ref, back_own_ref, w_ref, q_ref, x_ref, m1_ref, m2_ref):
    half = lax.axis_index("half")

    def tail(lanes):
        back = back_own_ref[BLK:, lanes].astype(jnp.float32)
        own = own_ref[BLK:, lanes].astype(jnp.float32)
        return jnp.where(half == 1, back, own)[6:8]

    gate_rows(seq_ref, raw_ref, tail, w_ref, 1 - half, q_ref, x_ref, m1_ref, m2_ref)


def far_kernel(
    short, piece, table_ref, acc_ref, qown_ref, qpair_ref, w_ref, marks_ref, back_own_ref, back_pair_ref, *refs
):
    *refs, kept_ref, sent_ref, total_ref, win_ref, extra_ref = refs
    far_refs, before = refs[: len(refs) - 2 * piece], refs[len(refs) - 2 * piece :]
    width = kept_ref.shape[1]
    half = lax.axis_index("half")
    lanes = slice(piece * width, (piece + 1) * width)
    marks = [marks_ref[0], marks_ref[1]]
    low = 1 if short else 0

    @pl.when(half == 0)
    def _():
        fill(win_ref, extra_ref, 2, back_own_ref.at[:, lanes])

    @pl.when(half == 1)
    def _():
        fill(win_ref, extra_ref, 2, back_pair_ref)

    if short:
        summed = marks_ref[2, 0:1, 0:1]
        fill(win_ref, extra_ref, 1, far_refs[0])
        payload = win_ref[BLK : 2 * BLK, :].astype(jnp.float32)
        win_ref[BLK : 2 * BLK, :] = (payload * (1.0 - summed)).astype(win_ref.dtype)
    else:
        fill(win_ref, extra_ref, half, far_refs[0].at[:, lanes])
        fill(win_ref, extra_ref, 1 - half, far_refs[1 + piece])
        ahead = far_refs[3][:, lanes].astype(jnp.float32)
        put_first_rows(win_ref, 0, first_rows(extra_ref[0], ahead, w_ref, marks, 0, lanes))
        put_first_rows(win_ref, BLK, first_rows(extra_ref[1], extra_ref[0, :8], w_ref, marks, 1, lanes))
    put_first_rows(win_ref, 2 * BLK, first_rows(extra_ref[2], extra_ref[1, :8], w_ref, marks, 2, lanes))
    if before:
        sent_ref[:, :width] = before[1][...]
    for i, (part, q_ref, out_ref) in enumerate(((half, qown_ref, kept_ref), (1 - half, qpair_ref, sent_ref))):
        part_sent = i == 1
        squares = before[0][i] if before else jnp.zeros((BLK, GROUP), jnp.float32)
        rows = pl.ds(pl.multiple_of(part * BLK, BLK), BLK)
        for c in range(0, width, GROUP):
            here = slice(c, c + GROUP)
            whole = slice(piece * width + c, piece * width + c + GROUP)
            filtered = acc_ref[rows, whole] + jnp.dot(
                table_ref[(piece * width + c) // GROUP, part, :, low * BLK : 3 * BLK],
                win_ref[low * BLK : 3 * BLK, here],
                preferred_element_type=jnp.float32,
            )
            if short:
                weight = summed * (part == 0).astype(jnp.float32)
                filtered = filtered + weight * far_refs[0][:BLK, here].astype(jnp.float32)
            gated = q_ref[:, whole] * filtered
            squares = squares + gated * gated
            out_ref[:, whole if before and part_sent else here] = gated.astype(out_ref.dtype)
        if before:
            total_ref[:, i * BLK : (i + 1) * BLK] = lax.dot_general(
                jnp.ones((8, GROUP), jnp.float32),
                squares,
                (((1,), (1,)), ((), ())),
                precision=lax.Precision.HIGHEST,
                preferred_element_type=jnp.float32,
            )[0:1]
        else:
            total_ref[i] = squares


def norm_kernel(channels, power_ref, power_got_ref, *refs):
    *kept_refs, got_ref, gain_ref, out_ref = refs
    half = lax.axis_index("half")
    power = power_ref[:, :BLK] + power_got_ref[:, BLK:]
    scale = lax.rsqrt(power / channels + norm_eps)
    diagonal = lax.broadcasted_iota(jnp.int32, (BLK, BLK), 0) == lax.broadcasted_iota(
        jnp.int32, (BLK, BLK), 1
    )
    column = jnp.sum(jnp.where(diagonal, scale, 0.0), axis=1, keepdims=True)
    for at, refs in ((half, kept_refs), (1 - half, [got_ref])):
        at = at * got_ref.shape[1]
        for ref in refs:
            for c in range(0, ref.shape[1], GROUP):
                lanes = pl.ds(pl.multiple_of(at + c, GROUP), GROUP)
                part = ref[:, c : c + GROUP].astype(jnp.float32)
                out_ref[:, lanes] = (part * column * gain_ref[:, lanes]).astype(out_ref.dtype)
            at = at + ref.shape[1]


def kernel_call(body, outs, in_specs, scratch, flops, moved_bytes):
    return pl.pallas_call(
        body,
        out_shape=outs,
        in_specs=in_specs,
        out_specs=jax.tree.map(lambda _: VMEM, outs),
        scratch_shapes=scratch,
        compiler_params=pltpu.CompilerParams(vmem_limit_bytes=24 << 20),
        cost_estimate=pl.CostEstimate(flops=flops, bytes_accessed=moved_bytes, transcendentals=0),
    )


def shards(blocks, whole_tokens, channels, projected, short_weight, filter_taps, tap_blocks, skip_bias, norm_gain, seq_lengths):
    rows = projected.shape[0]
    width = projected.shape[2] // 2
    groups = width // GROUP
    taps = filter_taps.shape[1]
    shape = jax.ShapeDtypeStruct
    half_shape = shape((rows, width), jnp.bfloat16)
    half_wide = shape((rows, width), jnp.float32)

    spots = range(2 * blocks)
    to_pair = [(i, i ^ 1) for i in spots]
    ahead = [(i, (i + 2) % (2 * blocks)) for i in spots]

    panels = jnp.transpose(projected, (1, 0, 2))
    message = shape((rows + 8, width), jnp.bfloat16)
    small = shape((rows + 8, width // 2), jnp.bfloat16)
    hbm = pl.BlockSpec(memory_space=pltpu.HBM)
    pieces = 4
    lengths = seq_lengths.reshape(1, -1)
    row_mask = pltpu.VMEM((rows, GROUP), jnp.float32)

    kept, *sent = kernel_call(
        products_kernel,
        (message, small, small),
        [hbm] * 3,
        [
            pltpu.VMEM(lengths.shape, jnp.int32),
            pltpu.VMEM((pieces, 2, rows, 2 * width // pieces), jnp.bfloat16),
            pltpu.VMEM((16, 2 * width), jnp.bfloat16),
            pltpu.VMEM(short_weight.shape, jnp.float32),
            pltpu.VMEM((4, rows + 8, GROUP), jnp.float32),
            row_mask,
            row_mask,
            pltpu.SemaphoreType.DMA((3 + pieces,)),
        ],
        40 * rows * width,
        16 * rows * width,
    )(*[pltpu.with_memory_space_constraint(a, pltpu.HBM) for a in (lengths, panels, short_weight)])

    back_own = moved(kept, ahead)
    pair = [moved(piece, to_pair) for piece in sent]

    filter_taps, _ = lax.optimization_barrier((filter_taps, kept))
    scaled = (filter_taps * jnp.repeat(tap_blocks.astype(jnp.float32), BLK, axis=1)).astype(jnp.bfloat16)
    span = taps + 2 * BLK
    table, table_next, w_half, marks = kernel_call(
        tables_kernel,
        (
            shape((groups, 2, BLK, span), jnp.bfloat16),
            shape((groups, BLK, 2 * BLK), jnp.bfloat16),
            shape((3, 3, width), jnp.float32),
            shape((4, 8, GROUP), jnp.float32),
        ),
        [SMEM, VMEM, VMEM],
        [pltpu.VMEM((2 * groups, span), jnp.float32), pltpu.VMEM((3, BLK, span), jnp.float32)],
        40 * groups * BLK * taps,
        8 * groups * BLK * taps,
    )(seq_lengths, scaled, short_weight)
    table, table_next, pair[0] = lax.optimization_barrier((table, table_next, pair[0]))

    half = lax.axis_index("half")
    query, _ = lax.optimization_barrier((panels, pair[0]))
    qkept = lax.dynamic_slice(query, (0, 0, half * width), (1, rows, width))[0]
    qsent = lax.dynamic_slice(query, (0, 0, (1 - half) * width), (1, rows, width))[0]
    qkept, qsent, pair[1] = lax.optimization_barrier((qkept, qsent, pair[1]))
    qgot = moved(qsent, to_pair)
    back_pair = [moved(piece, ahead) for piece in pair]

    window = pltpu.VMEM((4 * rows, width), jnp.bfloat16)
    extras = pltpu.VMEM((4, 16, width), jnp.float32)
    shifted = pltpu.VMEM((2, rows + 8, GROUP), jnp.float32)
    short = whole_tokens // 2 <= 4 * BLK
    if short:
        onward = [(i, i ^ 1 if i < 2 else i + 2 if i + 2 < 2 * blocks else 2 + i % 2) for i in spots]
        far = []
        for piece in range(2):
            relayed = kernel_call(
                functools.partial(relay_kernel, piece),
                small,
                [VMEM] * 5,
                [pltpu.VMEM((2 * rows, width // 2), jnp.bfloat16), pltpu.VMEM((2, 16, width // 2), jnp.float32)],
                2 * rows * BLK * width,
                4 * rows * width,
            )(marks, table_next, back_own, back_pair[piece], w_half)
            far.append(moved(relayed, onward))
    else:
        across = jnp.concatenate([piece[rows:] for piece in sent], 1)
        across = moved(across, [(i, ((i ^ 1) + 6) % (2 * blocks)) for i in spots])
        straight = moved(kept[rows:], [(i, (i + 6) % (2 * blocks)) for i in spots])
        deep = jnp.where(half == 1, straight, across)
        far = [moved(piece, ahead) for piece in (back_own, *back_pair)] + [deep]

    acc, qown = kernel_call(
        near_kernel,
        (shape((2 * rows, width), jnp.float32), half_wide),
        [VMEM] * 12,
        [window, extras, shifted, row_mask, row_mask],
        2 * 5 * rows * BLK * width,
        16 * rows * width,
    )(lengths, marks, table, kept, back_own, *pair, *back_pair, qkept, w_half, skip_bias.reshape(1, -1))

    qpair = kernel_call(
        pair_gate_kernel,
        half_wide,
        [VMEM] * 5,
        [shifted, row_mask, row_mask],
        10 * rows * width,
        8 * rows * width,
    )(lengths, qgot, kept, back_own, w_half)

    done, power, send = [], None, None
    for piece in range(2):
        needed = far[piece : piece + 1] if short else far
        before = [power, send] if piece else []
        own, send, power = kernel_call(
            functools.partial(far_kernel, short, piece),
            (
                shape((rows, width // 2), jnp.float32),
                shape((rows, width if piece else width // 2), jnp.bfloat16),
                shape((1, 2 * rows) if piece else (2, rows, GROUP), jnp.float32),
            ),
            [VMEM] * (8 + len(needed) + len(before)),
            [pltpu.VMEM((3 * rows, width // 2), jnp.bfloat16), pltpu.VMEM((3, 16, width // 2), jnp.float32)],
            2 * 3 * rows * BLK * width,
            12 * rows * width,
        )(table, acc, qown, qpair, w_half, marks, back_own, back_pair[piece], *needed, *before)
        done.append(own)
    back = moved(send, to_pair)

    peers = lax.axis_size("mp")
    shares = [lax.ppermute(power, "mp", [(i, i ^ k) for i in range(peers)]) for k in range(1, peers)]
    power = sum(shares, power)
    return kernel_call(
        functools.partial(norm_kernel, channels),
        shape((rows, 2 * width), jnp.bfloat16),
        [VMEM] * 6,
        [],
        8 * rows * width,
        10 * rows * width,
    )(power, moved(power, to_pair), *done, back, norm_gain.reshape(1, -1))


def solution(mesh):
    blocks = mesh.shape["ctx"] // 2
    grid = Mesh(mesh.devices.reshape(blocks, 2, mesh.shape["mp"]), ("blk", "half", "mp"))
    in_specs = (
        P(SPOTS, None, "mp"),
        P(None, None, "mp"),
        P("mp", None),
        P("mp", None),
        P("mp"),
        P("mp"),
        P(),
    )

    def program(projected, *rest):
        body = functools.partial(shards, blocks, projected.shape[0], projected.shape[2])
        return jax.shard_map(
            body, mesh=grid, in_specs=in_specs, out_specs=P(SPOTS, "mp"), check_vma=False
        )(projected, *rest)

    return program
```

```python
import functools

import jax
import jax.numpy as jnp
from jax import lax
from jax.experimental import pallas as pl
from jax.experimental.pallas import tpu as pltpu
from jax.sharding import Mesh, PartitionSpec as P

GROUP = 128
BLK = 128
norm_eps = 1e-06

VMEM = pl.BlockSpec(memory_space=pltpu.VMEM)
SMEM = pl.BlockSpec(memory_space=pltpu.SMEM)
SPOTS = ("blk", "half")


def moved(block, pairs):
    return lax.ppermute(block, SPOTS, pairs)


def boundaries(seq_ref, t):
    def step(k, carry):
        end, first, second = carry
        end = end + seq_ref[k]
        return end, first | (t == end).astype(jnp.int32), second | (t - 1 == end).astype(jnp.int32)

    first = (t == 0).astype(jnp.int32)
    second = (t == 1).astype(jnp.int32)
    _, first, second = lax.fori_loop(0, seq_ref.shape[0], step, (jnp.int32(0), first, second), unroll=True)
    return first, first | second


def row_masks(lengths_ref, start, m1_ref, m2_ref):
    count = lengths_ref.shape[1]
    square = (count, count)
    upto = lax.broadcasted_iota(jnp.int32, square, 1) <= lax.broadcasted_iota(jnp.int32, square, 0)
    lengths = jnp.broadcast_to(lengths_ref[...].astype(jnp.float32), square)
    ends = jnp.sum(jnp.where(upto, lengths, 0.0), axis=1, keepdims=True)
    t = (start + lax.broadcasted_iota(jnp.int32, (count, BLK), 1)).astype(jnp.float32)
    opens = (t == ends) | (t == 0.0)
    after = opens | (t - 1.0 == ends) | (t == 1.0)
    diagonal = lax.broadcasted_iota(jnp.int32, (BLK, BLK), 0) == lax.broadcasted_iota(jnp.int32, (BLK, BLK), 1)
    for mark, m_ref in ((opens, m1_ref), (after, m2_ref)):
        keep = 1.0 - jnp.max(mark.astype(jnp.float32), axis=0, keepdims=True)
        column = jnp.sum(jnp.where(diagonal, keep, 0.0), axis=1, keepdims=True)
        m_ref[...] = jnp.broadcast_to(column, m_ref.shape)


def counted(seq_ref, t):
    def step(k, carry):
        end, total = carry
        end = end + seq_ref[k]
        return end, total + (end <= t).astype(jnp.int32)

    _, total = lax.fori_loop(
        0, seq_ref.shape[0], step, (jnp.int32(0), jnp.zeros(t.shape, jnp.int32)), unroll=True
    )
    return jnp.where(t >= 0, total, -1)


def feature(x, x_ref, w, m1_ref, m2_ref):
    rows = x.shape[0]
    return (
        w[0:1] * x
        + w[1:2] * x_ref[7 : rows + 7, :] * m1_ref[...]
        + w[2:3] * x_ref[6 : rows + 6, :] * m2_ref[...]
    )


def products_kernel(seq_hbm, panels_hbm, w_hbm, *refs):
    (kept_ref, *sent_refs), refs = refs[:3], refs[3:]
    seq_ref, kv_ref, q_ref, w_ref, x_ref, m1_ref, m2_ref, sems = refs
    width = kept_ref.shape[1]
    rows = kv_ref.shape[2]
    pieces = kv_ref.shape[0]
    piece = kv_ref.shape[3]
    half = lax.axis_index("half")
    shard = lax.axis_index("blk") * 2 + half
    keep_at = pl.multiple_of(half * width, width)
    send_at = pl.multiple_of((1 - half) * width, width)

    loads = [pltpu.make_async_copy(seq_hbm, seq_ref, sems.at[0])]
    for p in range(pieces):
        at = keep_at if p < pieces // 2 else send_at
        lanes = pl.ds(pl.multiple_of(at + (p % (pieces // 2)) * piece, piece), piece)
        loads.append(pltpu.make_async_copy(panels_hbm.at[1:3, :, lanes], kv_ref.at[p], sems.at[1 + p]))
    loads.append(pltpu.make_async_copy(w_hbm, w_ref, sems.at[1 + pieces]))
    loads.append(pltpu.make_async_copy(panels_hbm.at[0, rows - 16 :, :], q_ref, sems.at[2 + pieces]))
    for load in loads:
        load.start()
    x_ref[:, 0:8, :] = jnp.zeros((x_ref.shape[0], 8, GROUP), jnp.float32)
    loads[0].wait()
    row_masks(seq_ref, shard * rows, m1_ref, m2_ref)
    loads[1 + pieces].wait()
    loads[2 + pieces].wait()
    for p in range(pieces):
        loads[1 + p].wait()
        out_ref, at = (kept_ref, keep_at) if p < pieces // 2 else (sent_refs[p - pieces // 2], send_at)
        for c in range(0, piece, GROUP):
            base = (p % (pieces // 2)) * piece + c
            there = slice(base, base + GROUP) if p < pieces // 2 else slice(c, c + GROUP)
            lanes = pl.ds(pl.multiple_of(at + base, GROUP), GROUP)
            slot = (c // GROUP) % (x_ref.shape[0] // 2) * 2
            raw, made = [], []
            for i in range(2):
                x = kv_ref[p, i, :, c : c + GROUP].astype(jnp.float32)
                x_ref[slot + i, 8:, :] = x
                made.append(feature(x, x_ref.at[slot + i], w_ref[1 + i, :, lanes], m1_ref, m2_ref))
                raw.append(x)
            product = made[0] * made[1]
            top = jnp.where(lax.broadcasted_iota(jnp.int32, (8, GROUP), 0) < 2, raw[0][:8], product[:8])
            out_ref[:rows, there] = jnp.concatenate([top, product[8:]], 0).astype(out_ref.dtype)
            tails = [x[rows - 2 :] for x in raw] + [q_ref[:, lanes].astype(jnp.float32)[14:]]
            out_ref[rows:, there] = jnp.concatenate([raw[1][0:2]] + tails, 0).astype(out_ref.dtype)


def edge_marks(seq_ref):
    t = (
        (lax.axis_index("blk") - 2) * (2 * BLK)
        + lax.broadcasted_iota(jnp.int32, (8, GROUP), 1) * BLK
        + lax.broadcasted_iota(jnp.int32, (8, GROUP), 0)
    )
    return [1.0 - mark.astype(jnp.float32) for mark in boundaries(seq_ref, t)]


def first_rows(now, ahead, w_ref, marks, spot, lanes=slice(None)):
    m1, m2 = [mark[:, spot : spot + 1] for mark in marks]
    top = lax.broadcasted_iota(jnp.int32, ahead.shape, 0) == 0
    made = []
    for i, x0 in enumerate((now[8:], now[:8])):
        x1 = jnp.where(top, pltpu.roll(ahead, 5 - 2 * i, 0), pltpu.roll(x0, 1, 0))
        x2 = pltpu.roll(ahead, 6 - 2 * i, 0)
        w = w_ref[1 + i, :, lanes]
        made.append(w[0:1] * x0 + w[1:2] * x1 * m1 + w[2:3] * x2 * m2)
    return made[0] * made[1]


def put_first_rows(win_ref, at, rows):
    old = win_ref[at : at + 16, :].astype(jnp.float32)
    new = jnp.concatenate([rows, rows], 0)
    first = lax.broadcasted_iota(jnp.int32, old.shape, 0) < 2
    win_ref[at : at + 16, :] = jnp.where(first, new, old).astype(win_ref.dtype)


def reaches_past(seq_ref, block):
    first = block * (2 * BLK)

    def step(k, carry):
        end, start = carry
        end = end + seq_ref[k]
        return end, jnp.where(end <= first, end, start)

    _, start = lax.fori_loop(0, seq_ref.shape[0], step, (jnp.int32(0), jnp.int32(0)), unroll=True)
    return first - 2 * BLK - start > BLK


def tables_kernel(seq_ref, taps_ref, w_ref, out_ref, next_ref, w_half_ref, marks_ref, rev_ref, m_ref):
    groups = out_ref.shape[0]
    taps = taps_ref.shape[1]
    span = out_ref.shape[3]
    half = lax.axis_index("half")
    start = lax.axis_index("blk") * (2 * BLK)
    marks_ref[0], marks_ref[1] = edge_marks(seq_ref)
    for ahead in range(2):
        flag = reaches_past(seq_ref, lax.axis_index("blk") + ahead)
        marks_ref[2 + ahead] = jnp.full((8, GROUP), flag.astype(jnp.float32))
    width = w_half_ref.shape[2]
    w_half_ref[...] = w_ref[:, :, pl.ds(pl.multiple_of(half * width, width), width)]
    turn = lax.broadcasted_iota(jnp.int32, (taps, span), 0) + lax.broadcasted_iota(
        jnp.int32, (taps, span), 1
    )
    turn = (turn == taps).astype(jnp.bfloat16)
    rev_ref[...] = jnp.dot(taps_ref[...], turn, preferred_element_type=jnp.float32)
    seg_in = counted(seq_ref, start - taps + lax.broadcasted_iota(jnp.int32, (8, span), 1))[0:1]
    for part in range(3):
        t_out = start + part * BLK + lax.broadcasted_iota(jnp.int32, (BLK, GROUP), 0)
        seg_out = counted(seq_ref, t_out)[:, 0:1]
        if part < 2:
            m_ref[part] = (seg_in == seg_out).astype(jnp.float32)
        else:
            m_ref[2, :, : 2 * BLK] = (seg_in[:, 2 * BLK : 4 * BLK] == seg_out).astype(jnp.float32)

    def one(g, _):
        row = rev_ref[pl.ds(half * groups + g, 1), :]
        table = pltpu.roll(jnp.broadcast_to(row, (BLK, span)), 0, 1, stride=1, stride_axis=0)
        out_ref[g, 0] = (table * m_ref[0]).astype(out_ref.dtype)
        later = jnp.concatenate([table[:, span - BLK :], table[:, : span - BLK]], 1)
        out_ref[g, 1] = (later * m_ref[1]).astype(out_ref.dtype)
        next_ref[g] = (table[:, : 2 * BLK] * m_ref[2, :, : 2 * BLK]).astype(next_ref.dtype)
        return 0

    lax.fori_loop(0, groups, one, 0)


def fill(win_ref, extra_ref, spot, *pieces):
    at = 0
    for piece in pieces:
        lanes = slice(at, at + piece.shape[1])
        win_ref[pl.ds(pl.multiple_of(spot * BLK, BLK), BLK), lanes] = piece[:BLK]
        extra_ref[spot, :8, lanes] = piece[BLK:].astype(jnp.float32)
        extra_ref[spot, 8:, lanes] = piece[:16].astype(jnp.float32)[:8]
        at += piece.shape[1]


def relay_kernel(piece, marks_ref, next_ref, back_own_ref, back_pair_ref, w_ref, out_ref, win_ref, extra_ref):
    width = out_ref.shape[1]
    half = lax.axis_index("half")
    lanes = slice(piece * width, (piece + 1) * width)
    fill(win_ref, extra_ref, half, back_own_ref.at[:, lanes])
    fill(win_ref, extra_ref, 1 - half, back_pair_ref)
    marks = [marks_ref[0], marks_ref[1]]
    put_first_rows(win_ref, 0, first_rows(extra_ref[0], jnp.zeros((8, width), jnp.float32), w_ref, marks, 2, lanes))
    put_first_rows(win_ref, BLK, first_rows(extra_ref[1], extra_ref[0, :8], w_ref, marks, 3, lanes))
    out_ref[BLK:] = extra_ref[1, :8].astype(out_ref.dtype)
    summed = jnp.max(marks_ref[3]) > 0.5

    @pl.when(summed)
    def _():
        for c in range(0, width, GROUP):
            total = jnp.dot(
                next_ref[(piece * width + c) // GROUP],
                win_ref[:, c : c + GROUP],
                preferred_element_type=jnp.float32,
            )
            out_ref[:BLK, c : c + GROUP] = total.astype(out_ref.dtype)

    @pl.when(jnp.logical_not(summed))
    def _():
        out_ref[:BLK] = win_ref[BLK:]


def gate_rows(seq_ref, raw_ref, tail, w_ref, part, q_ref, x_ref, m1_ref, m2_ref):
    width = raw_ref.shape[1]
    row_masks(seq_ref, lax.axis_index("blk") * (2 * BLK) + part * BLK, m1_ref, m2_ref)
    for c in range(0, width, GROUP):
        lanes = slice(c, c + GROUP)
        w = w_ref[0, :, lanes]
        x = raw_ref[:, lanes].astype(jnp.float32)
        slot = (c // GROUP) % 2
        x_ref[slot, 6:8, :] = tail(lanes)
        x_ref[slot, 8:, :] = x
        q_ref[:, lanes] = feature(x, x_ref.at[slot], w, m1_ref, m2_ref)


def near_kernel(
    seq_ref, marks_ref, table_ref, own_ref, back_own_ref, pair_a_ref, pair_b_ref, back_a_ref, back_b_ref, qkept_ref, w_ref, bias_ref,
    acc_ref, q_ref, win_ref, extra_ref, x_ref, m1_ref, m2_ref,
):
    groups = table_ref.shape[0]
    width = groups * GROUP
    half = lax.axis_index("half")
    fill(win_ref, extra_ref, half, back_own_ref)
    fill(win_ref, extra_ref, 1 - half, back_a_ref, back_b_ref)
    fill(win_ref, extra_ref, 2 + half, own_ref)
    fill(win_ref, extra_ref, 3 - half, pair_a_ref, pair_b_ref)
    marks = [marks_ref[0], marks_ref[1]]
    for spot in (1, 2, 3):
        rows = first_rows(extra_ref[spot], extra_ref[spot - 1, :8], w_ref, marks, spot + 2)
        put_first_rows(win_ref, spot * BLK, rows)
    for g in range(groups):
        lanes = slice(g * GROUP, (g + 1) * GROUP)
        bias = bias_ref[:, pl.ds(pl.multiple_of(half * width + g * GROUP, GROUP), GROUP)]
        for part in range(2):
            total = jnp.dot(
                table_ref[g, part, :, 3 * BLK : (5 + part) * BLK],
                win_ref[BLK : (3 + part) * BLK, lanes],
                preferred_element_type=jnp.float32,
            )
            here = win_ref[(2 + part) * BLK : (3 + part) * BLK, lanes].astype(jnp.float32)
            acc_ref[part * BLK : (part + 1) * BLK, lanes] = total + bias * here
    gate_rows(
        seq_ref, qkept_ref, lambda lanes: extra_ref[1 + half, 6:8, lanes], w_ref, half, q_ref, x_ref, m1_ref, m2_ref
    )


def pair_gate_kernel(seq_ref, raw_ref, own_ref, back_own_ref, w_ref, q_ref, x_ref, m1_ref, m2_ref):
    half = lax.axis_index("half")

    def tail(lanes):
        back = back_own_ref[BLK:, lanes].astype(jnp.float32)
        own = own_ref[BLK:, lanes].astype(jnp.float32)
        return jnp.where(half == 1, back, own)[6:8]

    gate_rows(seq_ref, raw_ref, tail, w_ref, 1 - half, q_ref, x_ref, m1_ref, m2_ref)


def far_kernel(
    short, piece, table_ref, acc_ref, qown_ref, qpair_ref, w_ref, marks_ref, back_own_ref, back_pair_ref, *refs
):
    *refs, kept_ref, sent_ref, total_ref, win_ref, extra_ref = refs
    far_refs, before = refs[: len(refs) - 2 * piece], refs[len(refs) - 2 * piece :]
    width = kept_ref.shape[1]
    half = lax.axis_index("half")
    lanes = slice(piece * width, (piece + 1) * width)
    marks = [marks_ref[0], marks_ref[1]]
    low = 1 if short else 0

    @pl.when(half == 0)
    def _():
        fill(win_ref, extra_ref, 2, back_own_ref.at[:, lanes])

    @pl.when(half == 1)
    def _():
        fill(win_ref, extra_ref, 2, back_pair_ref)

    if short:
        summed = marks_ref[2, 0:1, 0:1]
        fill(win_ref, extra_ref, 1, far_refs[0])
        payload = win_ref[BLK : 2 * BLK, :].astype(jnp.float32)
        win_ref[BLK : 2 * BLK, :] = (payload * (1.0 - summed)).astype(win_ref.dtype)
    else:
        fill(win_ref, extra_ref, half, far_refs[0].at[:, lanes])
        fill(win_ref, extra_ref, 1 - half, far_refs[1 + piece])
        ahead = far_refs[3][:, lanes].astype(jnp.float32)
        put_first_rows(win_ref, 0, first_rows(extra_ref[0], ahead, w_ref, marks, 0, lanes))
        put_first_rows(win_ref, BLK, first_rows(extra_ref[1], extra_ref[0, :8], w_ref, marks, 1, lanes))
    put_first_rows(win_ref, 2 * BLK, first_rows(extra_ref[2], extra_ref[1, :8], w_ref, marks, 2, lanes))
    if before:
        sent_ref[:, :width] = before[1][...]
    for i, (part, q_ref, out_ref) in enumerate(((half, qown_ref, kept_ref), (1 - half, qpair_ref, sent_ref))):
        part_sent = i == 1
        squares = before[0][i] if before else jnp.zeros((BLK, GROUP), jnp.float32)
        rows = pl.ds(pl.multiple_of(part * BLK, BLK), BLK)
        for c in range(0, width, GROUP):
            here = slice(c, c + GROUP)
            whole = slice(piece * width + c, piece * width + c + GROUP)
            filtered = acc_ref[rows, whole] + jnp.dot(
                table_ref[(piece * width + c) // GROUP, part, :, low * BLK : 3 * BLK],
                win_ref[low * BLK : 3 * BLK, here],
                preferred_element_type=jnp.float32,
            )
            if short:
                weight = summed * (part == 0).astype(jnp.float32)
                filtered = filtered + weight * far_refs[0][:BLK, here].astype(jnp.float32)
            gated = q_ref[:, whole] * filtered
            squares = squares + gated * gated
            out_ref[:, whole if before and part_sent else here] = gated.astype(out_ref.dtype)
        if before:
            total_ref[:, i * BLK : (i + 1) * BLK] = lax.dot_general(
                jnp.ones((8, GROUP), jnp.float32),
                squares,
                (((1,), (1,)), ((), ())),
                precision=lax.Precision.HIGHEST,
                preferred_element_type=jnp.float32,
            )[0:1]
        else:
            total_ref[i] = squares


def norm_kernel(channels, power_ref, power_got_ref, *refs):
    *kept_refs, got_ref, gain_ref, out_ref = refs
    half = lax.axis_index("half")
    power = power_ref[:, :BLK] + power_got_ref[:, BLK:]
    scale = lax.rsqrt(power / channels + norm_eps)
    diagonal = lax.broadcasted_iota(jnp.int32, (BLK, BLK), 0) == lax.broadcasted_iota(
        jnp.int32, (BLK, BLK), 1
    )
    column = jnp.sum(jnp.where(diagonal, scale, 0.0), axis=1, keepdims=True)
    for at, refs in ((half, kept_refs), (1 - half, [got_ref])):
        at = at * got_ref.shape[1]
        for ref in refs:
            for c in range(0, ref.shape[1], GROUP):
                lanes = pl.ds(pl.multiple_of(at + c, GROUP), GROUP)
                part = ref[:, c : c + GROUP].astype(jnp.float32)
                out_ref[:, lanes] = (part * column * gain_ref[:, lanes]).astype(out_ref.dtype)
            at = at + ref.shape[1]


def kernel_call(body, outs, in_specs, scratch, flops, moved_bytes):
    return pl.pallas_call(
        body,
        out_shape=outs,
        in_specs=in_specs,
        out_specs=jax.tree.map(lambda _: VMEM, outs),
        scratch_shapes=scratch,
        compiler_params=pltpu.CompilerParams(vmem_limit_bytes=24 << 20),
        cost_estimate=pl.CostEstimate(flops=flops, bytes_accessed=moved_bytes, transcendentals=0),
    )


def shards(blocks, whole_tokens, channels, projected, short_weight, filter_taps, tap_blocks, skip_bias, norm_gain, seq_lengths):
    rows = projected.shape[0]
    width = projected.shape[2] // 2
    groups = width // GROUP
    taps = filter_taps.shape[1]
    shape = jax.ShapeDtypeStruct
    half_shape = shape((rows, width), jnp.bfloat16)
    half_wide = shape((rows, width), jnp.float32)

    spots = range(2 * blocks)
    to_pair = [(i, i ^ 1) for i in spots]
    ahead = [(i, (i + 2) % (2 * blocks)) for i in spots]

    panels = jnp.transpose(projected, (1, 0, 2))
    message = shape((rows + 8, width), jnp.bfloat16)
    small = shape((rows + 8, width // 2), jnp.bfloat16)
    hbm = pl.BlockSpec(memory_space=pltpu.HBM)
    pieces = 4
    lengths = seq_lengths.reshape(1, -1)
    row_mask = pltpu.VMEM((rows, GROUP), jnp.float32)

    kept, *sent = kernel_call(
        products_kernel,
        (message, small, small),
        [hbm] * 3,
        [
            pltpu.VMEM(lengths.shape, jnp.int32),
            pltpu.VMEM((pieces, 2, rows, 2 * width // pieces), jnp.bfloat16),
            pltpu.VMEM((16, 2 * width), jnp.bfloat16),
            pltpu.VMEM(short_weight.shape, jnp.float32),
            pltpu.VMEM((4, rows + 8, GROUP), jnp.float32),
            row_mask,
            row_mask,
            pltpu.SemaphoreType.DMA((3 + pieces,)),
        ],
        40 * rows * width,
        16 * rows * width,
    )(*[pltpu.with_memory_space_constraint(a, pltpu.HBM) for a in (lengths, panels, short_weight)])

    back_own = moved(kept, ahead)
    pair = [moved(piece, to_pair) for piece in sent]

    filter_taps, _ = lax.optimization_barrier((filter_taps, kept))
    scaled = (filter_taps * jnp.repeat(tap_blocks.astype(jnp.float32), BLK, axis=1)).astype(jnp.bfloat16)
    span = taps + 2 * BLK
    table, table_next, w_half, marks = kernel_call(
        tables_kernel,
        (
            shape((groups, 2, BLK, span), jnp.bfloat16),
            shape((groups, BLK, 2 * BLK), jnp.bfloat16),
            shape((3, 3, width), jnp.float32),
            shape((4, 8, GROUP), jnp.float32),
        ),
        [SMEM, VMEM, VMEM],
        [pltpu.VMEM((2 * groups, span), jnp.float32), pltpu.VMEM((3, BLK, span), jnp.float32)],
        40 * groups * BLK * taps,
        8 * groups * BLK * taps,
    )(seq_lengths, scaled, short_weight)
    table, table_next, pair[0] = lax.optimization_barrier((table, table_next, pair[0]))

    half = lax.axis_index("half")
    query, _ = lax.optimization_barrier((panels, pair[0]))
    qkept = lax.dynamic_slice(query, (0, 0, half * width), (1, rows, width))[0]
    qsent = lax.dynamic_slice(query, (0, 0, (1 - half) * width), (1, rows, width))[0]
    qkept, qsent, pair[1] = lax.optimization_barrier((qkept, qsent, pair[1]))
    qgot = moved(qsent, to_pair)
    back_pair = [moved(pair[0], ahead), moved(pair[1], [(i, j) for i, j in ahead if i < j])]

    window = pltpu.VMEM((4 * rows, width), jnp.bfloat16)
    extras = pltpu.VMEM((4, 16, width), jnp.float32)
    shifted = pltpu.VMEM((2, rows + 8, GROUP), jnp.float32)
    short = whole_tokens // 2 <= 4 * BLK
    if short:
        onward = [(i, i ^ 1 if i < 2 else i + 2 if i + 2 < 2 * blocks else 2 + i % 2) for i in spots]
        far = []
        for piece in range(2):
            relayed = kernel_call(
                functools.partial(relay_kernel, piece),
                small,
                [VMEM] * 5,
                [pltpu.VMEM((2 * rows, width // 2), jnp.bfloat16), pltpu.VMEM((2, 16, width // 2), jnp.float32)],
                2 * rows * BLK * width,
                4 * rows * width,
            )(marks, table_next, back_own, back_pair[piece], w_half)
            far.append(moved(relayed, onward))
    else:
        across = jnp.concatenate([piece[rows:] for piece in sent], 1)
        across = moved(across, [(i, ((i ^ 1) + 6) % (2 * blocks)) for i in spots])
        straight = moved(kept[rows:], [(i, (i + 6) % (2 * blocks)) for i in spots])
        deep = jnp.where(half == 1, straight, across)
        far = [moved(piece, ahead) for piece in (back_own, *back_pair)] + [deep]

    acc, qown = kernel_call(
        near_kernel,
        (shape((2 * rows, width), jnp.float32), half_wide),
        [VMEM] * 12,
        [window, extras, shifted, row_mask, row_mask],
        2 * 5 * rows * BLK * width,
        16 * rows * width,
    )(lengths, marks, table, kept, back_own, *pair, *back_pair, qkept, w_half, skip_bias.reshape(1, -1))

    qpair = kernel_call(
        pair_gate_kernel,
        half_wide,
        [VMEM] * 5,
        [shifted, row_mask, row_mask],
        10 * rows * width,
        8 * rows * width,
    )(lengths, qgot, kept, back_own, w_half)

    done, power, send = [], None, None
    for piece in range(2):
        needed = far[piece : piece + 1] if short else far
        before = [power, send] if piece else []
        own, send, power = kernel_call(
            functools.partial(far_kernel, short, piece),
            (
                shape((rows, width // 2), jnp.float32),
                shape((rows, width if piece else width // 2), jnp.bfloat16),
                shape((1, 2 * rows) if piece else (2, rows, GROUP), jnp.float32),
            ),
            [VMEM] * (8 + len(needed) + len(before)),
            [pltpu.VMEM((3 * rows, width // 2), jnp.bfloat16), pltpu.VMEM((3, 16, width // 2), jnp.float32)],
            2 * 3 * rows * BLK * width,
            12 * rows * width,
        )(table, acc, qown, qpair, w_half, marks, back_own, back_pair[piece], *needed, *before)
        done.append(own)
    back = moved(send, to_pair)

    peers = lax.axis_size("mp")
    shares = [lax.ppermute(power, "mp", [(i, i ^ k) for i in range(peers)]) for k in range(1, peers)]
    power = sum(shares, power)
    return kernel_call(
        functools.partial(norm_kernel, channels),
        shape((rows, 2 * width), jnp.bfloat16),
        [VMEM] * 6,
        [],
        8 * rows * width,
        10 * rows * width,
    )(power, moved(power, to_pair), *done, back, norm_gain.reshape(1, -1))


def solution(mesh):
    blocks = mesh.shape["ctx"] // 2
    grid = Mesh(mesh.devices.reshape(blocks, 2, mesh.shape["mp"]), ("blk", "half", "mp"))
    in_specs = (
        P(SPOTS, None, "mp"),
        P(None, None, "mp"),
        P("mp", None),
        P("mp", None),
        P("mp"),
        P("mp"),
        P(),
    )

    def program(projected, *rest):
        body = functools.partial(shards, blocks, projected.shape[0], projected.shape[2])
        return jax.shard_map(
            body, mesh=grid, in_specs=in_specs, out_specs=P(SPOTS, "mp"), check_vma=False
        )(projected, *rest)

    return program
```

```python
import functools

import jax
import jax.numpy as jnp
from jax import lax
from jax.experimental import pallas as pl
from jax.experimental.pallas import tpu as pltpu
from jax.sharding import Mesh, PartitionSpec as P

GROUP = 128
BLK = 128
norm_eps = 1e-06

VMEM = pl.BlockSpec(memory_space=pltpu.VMEM)
SMEM = pl.BlockSpec(memory_space=pltpu.SMEM)
SPOTS = ("blk", "half")


def moved(block, pairs):
    return lax.ppermute(block, SPOTS, pairs)


def boundaries(seq_ref, t):
    def step(k, carry):
        end, first, second = carry
        end = end + seq_ref[k]
        return end, first | (t == end).astype(jnp.int32), second | (t - 1 == end).astype(jnp.int32)

    first = (t == 0).astype(jnp.int32)
    second = (t == 1).astype(jnp.int32)
    _, first, second = lax.fori_loop(0, seq_ref.shape[0], step, (jnp.int32(0), first, second), unroll=True)
    return first, first | second


def row_masks(lengths_ref, start, m1_ref, m2_ref):
    count = lengths_ref.shape[1]
    square = (count, count)
    upto = lax.broadcasted_iota(jnp.int32, square, 1) <= lax.broadcasted_iota(jnp.int32, square, 0)
    lengths = jnp.broadcast_to(lengths_ref[...].astype(jnp.float32), square)
    ends = jnp.sum(jnp.where(upto, lengths, 0.0), axis=1, keepdims=True)
    t = (start + lax.broadcasted_iota(jnp.int32, (count, BLK), 1)).astype(jnp.float32)
    opens = (t == ends) | (t == 0.0)
    after = opens | (t - 1.0 == ends) | (t == 1.0)
    diagonal = lax.broadcasted_iota(jnp.int32, (BLK, BLK), 0) == lax.broadcasted_iota(jnp.int32, (BLK, BLK), 1)
    for mark, m_ref in ((opens, m1_ref), (after, m2_ref)):
        keep = 1.0 - jnp.max(mark.astype(jnp.float32), axis=0, keepdims=True)
        column = jnp.sum(jnp.where(diagonal, keep, 0.0), axis=1, keepdims=True)
        m_ref[...] = jnp.broadcast_to(column, m_ref.shape)


def counted(seq_ref, t):
    def step(k, carry):
        end, total = carry
        end = end + seq_ref[k]
        return end, total + (end <= t).astype(jnp.int32)

    _, total = lax.fori_loop(
        0, seq_ref.shape[0], step, (jnp.int32(0), jnp.zeros(t.shape, jnp.int32)), unroll=True
    )
    return jnp.where(t >= 0, total, -1)


def feature(x, x_ref, w, m1_ref, m2_ref):
    rows = x.shape[0]
    return (
        w[0:1] * x
        + w[1:2] * x_ref[7 : rows + 7, :] * m1_ref[...]
        + w[2:3] * x_ref[6 : rows + 6, :] * m2_ref[...]
    )


def products_kernel(seq_hbm, panels_hbm, w_hbm, *refs):
    (kept_ref, *sent_refs), refs = refs[:3], refs[3:]
    seq_ref, kv_ref, q_ref, w_ref, x_ref, m1_ref, m2_ref, sems = refs
    width = kept_ref.shape[1]
    rows = kv_ref.shape[2]
    pieces = kv_ref.shape[0]
    piece = kv_ref.shape[3]
    half = lax.axis_index("half")
    shard = lax.axis_index("blk") * 2 + half
    keep_at = pl.multiple_of(half * width, width)
    send_at = pl.multiple_of((1 - half) * width, width)

    loads = [pltpu.make_async_copy(seq_hbm, seq_ref, sems.at[0])]
    for p in range(pieces):
        at = keep_at if p < pieces // 2 else send_at
        lanes = pl.ds(pl.multiple_of(at + (p % (pieces // 2)) * piece, piece), piece)
        loads.append(pltpu.make_async_copy(panels_hbm.at[1:3, :, lanes], kv_ref.at[p], sems.at[1 + p]))
    loads.append(pltpu.make_async_copy(w_hbm, w_ref, sems.at[1 + pieces]))
    loads.append(pltpu.make_async_copy(panels_hbm.at[0, rows - 16 :, :], q_ref, sems.at[2 + pieces]))
    for load in loads:
        load.start()
    x_ref[:, 0:8, :] = jnp.zeros((x_ref.shape[0], 8, GROUP), jnp.float32)
    loads[0].wait()
    row_masks(seq_ref, shard * rows, m1_ref, m2_ref)
    loads[1 + pieces].wait()
    loads[2 + pieces].wait()
    for p in range(pieces):
        loads[1 + p].wait()
        out_ref, at = (kept_ref, keep_at) if p < pieces // 2 else (sent_refs[p - pieces // 2], send_at)
        for c in range(0, piece, GROUP):
            base = (p % (pieces // 2)) * piece + c
            there = slice(base, base + GROUP) if p < pieces // 2 else slice(c, c + GROUP)
            lanes = pl.ds(pl.multiple_of(at + base, GROUP), GROUP)
            slot = (c // GROUP) % (x_ref.shape[0] // 2) * 2
            raw, made = [], []
            for i in range(2):
                x = kv_ref[p, i, :, c : c + GROUP].astype(jnp.float32)
                x_ref[slot + i, 8:, :] = x
                made.append(feature(x, x_ref.at[slot + i], w_ref[1 + i, :, lanes], m1_ref, m2_ref))
                raw.append(x)
            product = made[0] * made[1]
            top = jnp.where(lax.broadcasted_iota(jnp.int32, (8, GROUP), 0) < 2, raw[0][:8], product[:8])
            out_ref[:rows, there] = jnp.concatenate([top, product[8:]], 0).astype(out_ref.dtype)
            tails = [x[rows - 2 :] for x in raw] + [q_ref[:, lanes].astype(jnp.float32)[14:]]
            out_ref[rows:, there] = jnp.concatenate([raw[1][0:2]] + tails, 0).astype(out_ref.dtype)


def edge_marks(seq_ref):
    t = (
        (lax.axis_index("blk") - 2) * (2 * BLK)
        + lax.broadcasted_iota(jnp.int32, (8, GROUP), 1) * BLK
        + lax.broadcasted_iota(jnp.int32, (8, GROUP), 0)
    )
    return [1.0 - mark.astype(jnp.float32) for mark in boundaries(seq_ref, t)]


def first_rows(now, ahead, w_ref, marks, spot, lanes=slice(None)):
    m1, m2 = [mark[:, spot : spot + 1] for mark in marks]
    top = lax.broadcasted_iota(jnp.int32, ahead.shape, 0) == 0
    made = []
    for i, x0 in enumerate((now[8:], now[:8])):
        x1 = jnp.where(top, pltpu.roll(ahead, 5 - 2 * i, 0), pltpu.roll(x0, 1, 0))
        x2 = pltpu.roll(ahead, 6 - 2 * i, 0)
        w = w_ref[1 + i, :, lanes]
        made.append(w[0:1] * x0 + w[1:2] * x1 * m1 + w[2:3] * x2 * m2)
    return made[0] * made[1]


def put_first_rows(win_ref, at, rows):
    old = win_ref[at : at + 16, :].astype(jnp.float32)
    new = jnp.concatenate([rows, rows], 0)
    first = lax.broadcasted_iota(jnp.int32, old.shape, 0) < 2
    win_ref[at : at + 16, :] = jnp.where(first, new, old).astype(win_ref.dtype)


def reaches_past(seq_ref, block):
    first = block * (2 * BLK)

    def step(k, carry):
        end, start = carry
        end = end + seq_ref[k]
        return end, jnp.where(end <= first, end, start)

    _, start = lax.fori_loop(0, seq_ref.shape[0], step, (jnp.int32(0), jnp.int32(0)), unroll=True)
    return first - 2 * BLK - start > BLK


def tables_kernel(seq_ref, taps_ref, w_ref, out_ref, next_ref, w_half_ref, marks_ref, rev_ref, m_ref):
    groups = out_ref.shape[0]
    taps = taps_ref.shape[1]
    span = out_ref.shape[3]
    half = lax.axis_index("half")
    start = lax.axis_index("blk") * (2 * BLK)
    marks_ref[0], marks_ref[1] = edge_marks(seq_ref)
    for ahead in range(2):
        flag = reaches_past(seq_ref, lax.axis_index("blk") + ahead)
        marks_ref[2 + ahead] = jnp.full((8, GROUP), flag.astype(jnp.float32))
    width = w_half_ref.shape[2]
    w_half_ref[...] = w_ref[:, :, pl.ds(pl.multiple_of(half * width, width), width)]
    turn = lax.broadcasted_iota(jnp.int32, (taps, span), 0) + lax.broadcasted_iota(
        jnp.int32, (taps, span), 1
    )
    turn = (turn == taps).astype(jnp.bfloat16)
    rev_ref[...] = jnp.dot(taps_ref[...], turn, preferred_element_type=jnp.float32)
    seg_in = counted(seq_ref, start - taps + lax.broadcasted_iota(jnp.int32, (8, span), 1))[0:1]
    for part in range(3):
        t_out = start + part * BLK + lax.broadcasted_iota(jnp.int32, (BLK, GROUP), 0)
        seg_out = counted(seq_ref, t_out)[:, 0:1]
        if part < 2:
            m_ref[part] = (seg_in == seg_out).astype(jnp.float32)
        else:
            m_ref[2, :, : 2 * BLK] = (seg_in[:, 2 * BLK : 4 * BLK] == seg_out).astype(jnp.float32)

    def one(g, _):
        row = rev_ref[pl.ds(half * groups + g, 1), :]
        table = pltpu.roll(jnp.broadcast_to(row, (BLK, span)), 0, 1, stride=1, stride_axis=0)
        out_ref[g, 0] = (table * m_ref[0]).astype(out_ref.dtype)
        later = jnp.concatenate([table[:, span - BLK :], table[:, : span - BLK]], 1)
        out_ref[g, 1] = (later * m_ref[1]).astype(out_ref.dtype)
        next_ref[g] = (table[:, : 2 * BLK] * m_ref[2, :, : 2 * BLK]).astype(next_ref.dtype)
        return 0

    lax.fori_loop(0, groups, one, 0)


def fill(win_ref, extra_ref, spot, *pieces):
    at = 0
    for piece in pieces:
        lanes = slice(at, at + piece.shape[1])
        win_ref[pl.ds(pl.multiple_of(spot * BLK, BLK), BLK), lanes] = piece[:BLK]
        extra_ref[spot, :8, lanes] = piece[BLK:].astype(jnp.float32)
        extra_ref[spot, 8:, lanes] = piece[:16].astype(jnp.float32)[:8]
        at += piece.shape[1]


def relay_kernel(piece, marks_ref, next_ref, back_own_ref, w_ref, *refs):
    *ways, out_ref, back_pair_ref, win_ref, extra_ref = refs
    for i, way in enumerate(ways):
        @pl.when((lax.axis_index("blk") + i) % len(ways) == 0)
        def _():
            back_pair_ref[...] = way[...]

    width = out_ref.shape[1]
    half = lax.axis_index("half")
    lanes = slice(piece * width, (piece + 1) * width)
    fill(win_ref, extra_ref, half, back_own_ref.at[:, lanes])
    fill(win_ref, extra_ref, 1 - half, back_pair_ref)
    marks = [marks_ref[0], marks_ref[1]]
    put_first_rows(win_ref, 0, first_rows(extra_ref[0], jnp.zeros((8, width), jnp.float32), w_ref, marks, 2, lanes))
    put_first_rows(win_ref, BLK, first_rows(extra_ref[1], extra_ref[0, :8], w_ref, marks, 3, lanes))
    out_ref[BLK:] = extra_ref[1, :8].astype(out_ref.dtype)
    summed = jnp.max(marks_ref[3]) > 0.5

    @pl.when(summed)
    def _():
        for c in range(0, width, GROUP):
            total = jnp.dot(
                next_ref[(piece * width + c) // GROUP],
                win_ref[:, c : c + GROUP],
                preferred_element_type=jnp.float32,
            )
            out_ref[:BLK, c : c + GROUP] = total.astype(out_ref.dtype)

    @pl.when(jnp.logical_not(summed))
    def _():
        out_ref[:BLK] = win_ref[BLK:]


def gate_rows(seq_ref, raw_ref, tail, w_ref, part, q_ref, x_ref, m1_ref, m2_ref):
    width = raw_ref.shape[1]
    row_masks(seq_ref, lax.axis_index("blk") * (2 * BLK) + part * BLK, m1_ref, m2_ref)
    for c in range(0, width, GROUP):
        lanes = slice(c, c + GROUP)
        w = w_ref[0, :, lanes]
        x = raw_ref[:, lanes].astype(jnp.float32)
        slot = (c // GROUP) % 2
        x_ref[slot, 6:8, :] = tail(lanes)
        x_ref[slot, 8:, :] = x
        q_ref[:, lanes] = feature(x, x_ref.at[slot], w, m1_ref, m2_ref)


def near_kernel(
    seq_ref, marks_ref, table_ref, own_ref, back_own_ref, pair_a_ref, pair_b_ref, back_a_ref, back_b_ref, qkept_ref, w_ref, bias_ref,
    acc_ref, q_ref, win_ref, extra_ref, x_ref, m1_ref, m2_ref,
):
    groups = table_ref.shape[0]
    width = groups * GROUP
    half = lax.axis_index("half")
    fill(win_ref, extra_ref, half, back_own_ref)
    fill(win_ref, extra_ref, 1 - half, back_a_ref, back_b_ref)
    fill(win_ref, extra_ref, 2 + half, own_ref)
    fill(win_ref, extra_ref, 3 - half, pair_a_ref, pair_b_ref)
    marks = [marks_ref[0], marks_ref[1]]
    for spot in (1, 2, 3):
        rows = first_rows(extra_ref[spot], extra_ref[spot - 1, :8], w_ref, marks, spot + 2)
        put_first_rows(win_ref, spot * BLK, rows)
    for g in range(groups):
        lanes = slice(g * GROUP, (g + 1) * GROUP)
        bias = bias_ref[:, pl.ds(pl.multiple_of(half * width + g * GROUP, GROUP), GROUP)]
        for part in range(2):
            total = jnp.dot(
                table_ref[g, part, :, 3 * BLK : (5 + part) * BLK],
                win_ref[BLK : (3 + part) * BLK, lanes],
                preferred_element_type=jnp.float32,
            )
            here = win_ref[(2 + part) * BLK : (3 + part) * BLK, lanes].astype(jnp.float32)
            acc_ref[part * BLK : (part + 1) * BLK, lanes] = total + bias * here
    gate_rows(
        seq_ref, qkept_ref, lambda lanes: extra_ref[1 + half, 6:8, lanes], w_ref, half, q_ref, x_ref, m1_ref, m2_ref
    )


def pair_gate_kernel(seq_ref, raw_ref, own_ref, back_own_ref, w_ref, q_ref, x_ref, m1_ref, m2_ref):
    half = lax.axis_index("half")

    def tail(lanes):
        back = back_own_ref[BLK:, lanes].astype(jnp.float32)
        own = own_ref[BLK:, lanes].astype(jnp.float32)
        return jnp.where(half == 1, back, own)[6:8]

    gate_rows(seq_ref, raw_ref, tail, w_ref, 1 - half, q_ref, x_ref, m1_ref, m2_ref)


def far_kernel(
    short, piece, table_ref, acc_ref, qown_ref, qpair_ref, w_ref, marks_ref, back_own_ref, back_pair_ref, *refs
):
    *refs, kept_ref, sent_ref, total_ref, win_ref, extra_ref = refs
    far_refs, before = refs[: len(refs) - 2 * piece], refs[len(refs) - 2 * piece :]
    width = kept_ref.shape[1]
    half = lax.axis_index("half")
    lanes = slice(piece * width, (piece + 1) * width)
    marks = [marks_ref[0], marks_ref[1]]
    low = 1 if short else 0

    @pl.when(half == 0)
    def _():
        fill(win_ref, extra_ref, 2, back_own_ref.at[:, lanes])

    @pl.when(half == 1)
    def _():
        fill(win_ref, extra_ref, 2, back_pair_ref)

    if short:
        summed = marks_ref[2, 0:1, 0:1]
        fill(win_ref, extra_ref, 1, far_refs[0])
        payload = win_ref[BLK : 2 * BLK, :].astype(jnp.float32)
        win_ref[BLK : 2 * BLK, :] = (payload * (1.0 - summed)).astype(win_ref.dtype)
    else:
        fill(win_ref, extra_ref, half, far_refs[0].at[:, lanes])
        fill(win_ref, extra_ref, 1 - half, far_refs[1 + piece])
        ahead = far_refs[3][:, lanes].astype(jnp.float32)
        put_first_rows(win_ref, 0, first_rows(extra_ref[0], ahead, w_ref, marks, 0, lanes))
        put_first_rows(win_ref, BLK, first_rows(extra_ref[1], extra_ref[0, :8], w_ref, marks, 1, lanes))
    put_first_rows(win_ref, 2 * BLK, first_rows(extra_ref[2], extra_ref[1, :8], w_ref, marks, 2, lanes))
    if before:
        sent_ref[:, :width] = before[1][...]
    for i, (part, q_ref, out_ref) in enumerate(((half, qown_ref, kept_ref), (1 - half, qpair_ref, sent_ref))):
        part_sent = i == 1
        squares = before[0][i] if before else jnp.zeros((BLK, GROUP), jnp.float32)
        rows = pl.ds(pl.multiple_of(part * BLK, BLK), BLK)
        for c in range(0, width, GROUP):
            here = slice(c, c + GROUP)
            whole = slice(piece * width + c, piece * width + c + GROUP)
            filtered = acc_ref[rows, whole] + jnp.dot(
                table_ref[(piece * width + c) // GROUP, part, :, low * BLK : 3 * BLK],
                win_ref[low * BLK : 3 * BLK, here],
                preferred_element_type=jnp.float32,
            )
            if short:
                weight = summed * (part == 0).astype(jnp.float32)
                filtered = filtered + weight * far_refs[0][:BLK, here].astype(jnp.float32)
            gated = q_ref[:, whole] * filtered
            squares = squares + gated * gated
            out_ref[:, whole if before and part_sent else here] = gated.astype(out_ref.dtype)
        if before:
            total_ref[:, i * BLK : (i + 1) * BLK] = lax.dot_general(
                jnp.ones((8, GROUP), jnp.float32),
                squares,
                (((1,), (1,)), ((), ())),
                precision=lax.Precision.HIGHEST,
                preferred_element_type=jnp.float32,
            )[0:1]
        else:
            total_ref[i] = squares


def norm_kernel(channels, power_ref, power_got_ref, *refs):
    *kept_refs, got_ref, gain_ref, out_ref = refs
    half = lax.axis_index("half")
    power = power_ref[:, :BLK] + power_got_ref[:, BLK:]
    scale = lax.rsqrt(power / channels + norm_eps)
    diagonal = lax.broadcasted_iota(jnp.int32, (BLK, BLK), 0) == lax.broadcasted_iota(
        jnp.int32, (BLK, BLK), 1
    )
    column = jnp.sum(jnp.where(diagonal, scale, 0.0), axis=1, keepdims=True)
    for at, refs in ((half, kept_refs), (1 - half, [got_ref])):
        at = at * got_ref.shape[1]
        for ref in refs:
            for c in range(0, ref.shape[1], GROUP):
                lanes = pl.ds(pl.multiple_of(at + c, GROUP), GROUP)
                part = ref[:, c : c + GROUP].astype(jnp.float32)
                out_ref[:, lanes] = (part * column * gain_ref[:, lanes]).astype(out_ref.dtype)
            at = at + ref.shape[1]


def kernel_call(body, outs, in_specs, scratch, flops, moved_bytes):
    return pl.pallas_call(
        body,
        out_shape=outs,
        in_specs=in_specs,
        out_specs=jax.tree.map(lambda _: VMEM, outs),
        scratch_shapes=scratch,
        compiler_params=pltpu.CompilerParams(vmem_limit_bytes=24 << 20),
        cost_estimate=pl.CostEstimate(flops=flops, bytes_accessed=moved_bytes, transcendentals=0),
    )


def matching(blocks, first):
    pairs = []
    for i in range(2 * blocks):
        block = i // 2
        partner = block + 1 if (block - first) % 2 == 0 else block - 1
        pairs.append((i, 2 * partner + i % 2 if 0 <= partner < blocks else i ^ 1))
    return pairs


def shards(blocks, whole_tokens, channels, projected, short_weight, filter_taps, tap_blocks, skip_bias, norm_gain, seq_lengths):
    rows = projected.shape[0]
    width = projected.shape[2] // 2
    groups = width // GROUP
    taps = filter_taps.shape[1]
    shape = jax.ShapeDtypeStruct
    half_shape = shape((rows, width), jnp.bfloat16)
    half_wide = shape((rows, width), jnp.float32)

    spots = range(2 * blocks)
    to_pair = [(i, i ^ 1) for i in spots]
    ahead = [(i, (i + 2) % (2 * blocks)) for i in spots]

    panels = jnp.transpose(projected, (1, 0, 2))
    message = shape((rows + 8, width), jnp.bfloat16)
    small = shape((rows + 8, width // 2), jnp.bfloat16)
    hbm = pl.BlockSpec(memory_space=pltpu.HBM)
    pieces = 4
    lengths = seq_lengths.reshape(1, -1)
    row_mask = pltpu.VMEM((rows, GROUP), jnp.float32)

    kept, *sent = kernel_call(
        products_kernel,
        (message, small, small),
        [hbm] * 3,
        [
            pltpu.VMEM(lengths.shape, jnp.int32),
            pltpu.VMEM((pieces, 2, rows, 2 * width // pieces), jnp.bfloat16),
            pltpu.VMEM((16, 2 * width), jnp.bfloat16),
            pltpu.VMEM(short_weight.shape, jnp.float32),
            pltpu.VMEM((4, rows + 8, GROUP), jnp.float32),
            row_mask,
            row_mask,
            pltpu.SemaphoreType.DMA((3 + pieces,)),
        ],
        40 * rows * width,
        16 * rows * width,
    )(*[pltpu.with_memory_space_constraint(a, pltpu.HBM) for a in (lengths, panels, short_weight)])

    back_own = moved(kept, ahead)
    pair = [moved(piece, to_pair) for piece in sent]

    filter_taps, _ = lax.optimization_barrier((filter_taps, kept))
    scaled = (filter_taps * jnp.repeat(tap_blocks.astype(jnp.float32), BLK, axis=1)).astype(jnp.bfloat16)
    span = taps + 2 * BLK
    table, table_next, w_half, marks = kernel_call(
        tables_kernel,
        (
            shape((groups, 2, BLK, span), jnp.bfloat16),
            shape((groups, BLK, 2 * BLK), jnp.bfloat16),
            shape((3, 3, width), jnp.float32),
            shape((4, 8, GROUP), jnp.float32),
        ),
        [SMEM, VMEM, VMEM],
        [pltpu.VMEM((2 * groups, span), jnp.float32), pltpu.VMEM((3, BLK, span), jnp.float32)],
        40 * groups * BLK * taps,
        8 * groups * BLK * taps,
    )(seq_lengths, scaled, short_weight)
    table, table_next, pair[0] = lax.optimization_barrier((table, table_next, pair[0]))

    half = lax.axis_index("half")
    query, _ = lax.optimization_barrier((panels, pair[0]))
    qkept = lax.dynamic_slice(query, (0, 0, half * width), (1, rows, width))[0]
    qsent = lax.dynamic_slice(query, (0, 0, (1 - half) * width), (1, rows, width))[0]
    qkept, qsent, pair[1] = lax.optimization_barrier((qkept, qsent, pair[1]))
    qgot = moved(qsent, to_pair)
    back_pair = [[moved(pair[0], ahead)], [moved(pair[1], matching(blocks, first)) for first in (1, 0)]]

    window = pltpu.VMEM((4 * rows, width), jnp.bfloat16)
    extras = pltpu.VMEM((4, 16, width), jnp.float32)
    shifted = pltpu.VMEM((2, rows + 8, GROUP), jnp.float32)
    short = whole_tokens // 2 <= 4 * BLK
    if short:
        onward = [(i, i ^ 1 if i < 2 else i + 2 if i + 2 < 2 * blocks else 2 + i % 2) for i in spots]
        far = []
        for piece in range(2):
            relayed, back_pair[piece] = kernel_call(
                functools.partial(relay_kernel, piece),
                (small, small),
                [VMEM] * (4 + len(back_pair[piece])),
                [pltpu.VMEM((2 * rows, width // 2), jnp.bfloat16), pltpu.VMEM((2, 16, width // 2), jnp.float32)],
                2 * rows * BLK * width,
                4 * rows * width,
            )(marks, table_next, back_own, w_half, *back_pair[piece])
            far.append(moved(relayed, onward))
    else:
        back_pair = [moved(piece, ahead) for piece in pair]
        across = jnp.concatenate([piece[rows:] for piece in sent], 1)
        across = moved(across, [(i, ((i ^ 1) + 6) % (2 * blocks)) for i in spots])
        straight = moved(kept[rows:], [(i, (i + 6) % (2 * blocks)) for i in spots])
        deep = jnp.where(half == 1, straight, across)
        far = [moved(piece, ahead) for piece in (back_own, *back_pair)] + [deep]

    acc, qown = kernel_call(
        near_kernel,
        (shape((2 * rows, width), jnp.float32), half_wide),
        [VMEM] * 12,
        [window, extras, shifted, row_mask, row_mask],
        2 * 5 * rows * BLK * width,
        16 * rows * width,
    )(lengths, marks, table, kept, back_own, *pair, *back_pair, qkept, w_half, skip_bias.reshape(1, -1))

    qpair = kernel_call(
        pair_gate_kernel,
        half_wide,
        [VMEM] * 5,
        [shifted, row_mask, row_mask],
        10 * rows * width,
        8 * rows * width,
    )(lengths, qgot, kept, back_own, w_half)

    done, power, send = [], None, None
    for piece in range(2):
        needed = far[piece : piece + 1] if short else far
        before = [power, send] if piece else []
        own, send, power = kernel_call(
            functools.partial(far_kernel, short, piece),
            (
                shape((rows, width // 2), jnp.float32),
                shape((rows, width if piece else width // 2), jnp.bfloat16),
                shape((1, 2 * rows) if piece else (2, rows, GROUP), jnp.float32),
            ),
            [VMEM] * (8 + len(needed) + len(before)),
            [pltpu.VMEM((3 * rows, width // 2), jnp.bfloat16), pltpu.VMEM((3, 16, width // 2), jnp.float32)],
            2 * 3 * rows * BLK * width,
            12 * rows * width,
        )(table, acc, qown, qpair, w_half, marks, back_own, back_pair[piece], *needed, *before)
        done.append(own)
    back = moved(send, to_pair)

    peers = lax.axis_size("mp")
    shares = [lax.ppermute(power, "mp", [(i, i ^ k) for i in range(peers)]) for k in range(1, peers)]
    power = sum(shares, power)
    return kernel_call(
        functools.partial(norm_kernel, channels),
        shape((rows, 2 * width), jnp.bfloat16),
        [VMEM] * 6,
        [],
        8 * rows * width,
        10 * rows * width,
    )(power, moved(power, to_pair), *done, back, norm_gain.reshape(1, -1))


def solution(mesh):
    blocks = mesh.shape["ctx"] // 2
    grid = Mesh(mesh.devices.reshape(blocks, 2, mesh.shape["mp"]), ("blk", "half", "mp"))
    in_specs = (
        P(SPOTS, None, "mp"),
        P(None, None, "mp"),
        P("mp", None),
        P("mp", None),
        P("mp"),
        P("mp"),
        P(),
    )

    def program(projected, *rest):
        body = functools.partial(shards, blocks, projected.shape[0], projected.shape[2])
        return jax.shard_map(
            body, mesh=grid, in_specs=in_specs, out_specs=P(SPOTS, "mp"), check_vma=False
        )(projected, *rest)

    return program
```

```python
import functools

import jax
import jax.numpy as jnp
from jax import lax
from jax.experimental import pallas as pl
from jax.experimental.pallas import tpu as pltpu
from jax.sharding import Mesh, PartitionSpec as P

GROUP = 128
BLK = 128
norm_eps = 1e-06

VMEM = pl.BlockSpec(memory_space=pltpu.VMEM)
SMEM = pl.BlockSpec(memory_space=pltpu.SMEM)
SPOTS = ("blk", "half")


def moved(block, pairs):
    peers = lax.axis_size("mp")
    whole = [(i * peers + m, j * peers + (m if i != j else m ^ 1)) for i, j in pairs for m in range(peers)]
    return lax.ppermute(block, SPOTS + ("mp",), whole)


def boundaries(seq_ref, t):
    def step(k, carry):
        end, first, second = carry
        end = end + seq_ref[k]
        return end, first | (t == end).astype(jnp.int32), second | (t - 1 == end).astype(jnp.int32)

    first = (t == 0).astype(jnp.int32)
    second = (t == 1).astype(jnp.int32)
    _, first, second = lax.fori_loop(0, seq_ref.shape[0], step, (jnp.int32(0), first, second), unroll=True)
    return first, first | second


def row_masks(lengths_ref, start, m1_ref, m2_ref):
    count = lengths_ref.shape[1]
    square = (count, count)
    upto = lax.broadcasted_iota(jnp.int32, square, 1) <= lax.broadcasted_iota(jnp.int32, square, 0)
    lengths = jnp.broadcast_to(lengths_ref[...].astype(jnp.float32), square)
    ends = jnp.sum(jnp.where(upto, lengths, 0.0), axis=1, keepdims=True)
    t = (start + lax.broadcasted_iota(jnp.int32, (count, BLK), 1)).astype(jnp.float32)
    opens = (t == ends) | (t == 0.0)
    after = opens | (t - 1.0 == ends) | (t == 1.0)
    diagonal = lax.broadcasted_iota(jnp.int32, (BLK, BLK), 0) == lax.broadcasted_iota(jnp.int32, (BLK, BLK), 1)
    for mark, m_ref in ((opens, m1_ref), (after, m2_ref)):
        keep = 1.0 - jnp.max(mark.astype(jnp.float32), axis=0, keepdims=True)
        column = jnp.sum(jnp.where(diagonal, keep, 0.0), axis=1, keepdims=True)
        m_ref[...] = jnp.broadcast_to(column, m_ref.shape)


def counted(seq_ref, t):
    def step(k, carry):
        end, total = carry
        end = end + seq_ref[k]
        return end, total + (end <= t).astype(jnp.int32)

    _, total = lax.fori_loop(
        0, seq_ref.shape[0], step, (jnp.int32(0), jnp.zeros(t.shape, jnp.int32)), unroll=True
    )
    return jnp.where(t >= 0, total, -1)


def feature(x, x_ref, w, m1_ref, m2_ref):
    rows = x.shape[0]
    return (
        w[0:1] * x
        + w[1:2] * x_ref[7 : rows + 7, :] * m1_ref[...]
        + w[2:3] * x_ref[6 : rows + 6, :] * m2_ref[...]
    )


def products_kernel(seq_hbm, panels_hbm, w_hbm, *refs):
    (kept_ref, *sent_refs), refs = refs[:3], refs[3:]
    seq_ref, kv_ref, q_ref, w_ref, x_ref, m1_ref, m2_ref, sems = refs
    width = kept_ref.shape[1]
    rows = kv_ref.shape[2]
    pieces = kv_ref.shape[0]
    piece = kv_ref.shape[3]
    half = lax.axis_index("half")
    shard = lax.axis_index("blk") * 2 + half
    keep_at = pl.multiple_of(half * width, width)
    send_at = pl.multiple_of((1 - half) * width, width)

    loads = [pltpu.make_async_copy(seq_hbm, seq_ref, sems.at[0])]
    for p in range(pieces):
        at = keep_at if p < pieces // 2 else send_at
        lanes = pl.ds(pl.multiple_of(at + (p % (pieces // 2)) * piece, piece), piece)
        loads.append(pltpu.make_async_copy(panels_hbm.at[1:3, :, lanes], kv_ref.at[p], sems.at[1 + p]))
    loads.append(pltpu.make_async_copy(w_hbm, w_ref, sems.at[1 + pieces]))
    loads.append(pltpu.make_async_copy(panels_hbm.at[0, rows - 16 :, :], q_ref, sems.at[2 + pieces]))
    for load in loads:
        load.start()
    x_ref[:, 0:8, :] = jnp.zeros((x_ref.shape[0], 8, GROUP), jnp.float32)
    loads[0].wait()
    row_masks(seq_ref, shard * rows, m1_ref, m2_ref)
    loads[1 + pieces].wait()
    loads[2 + pieces].wait()
    for p in range(pieces):
        loads[1 + p].wait()
        out_ref, at = (kept_ref, keep_at) if p < pieces // 2 else (sent_refs[p - pieces // 2], send_at)
        for c in range(0, piece, GROUP):
            base = (p % (pieces // 2)) * piece + c
            there = slice(base, base + GROUP) if p < pieces // 2 else slice(c, c + GROUP)
            lanes = pl.ds(pl.multiple_of(at + base, GROUP), GROUP)
            slot = (c // GROUP) % (x_ref.shape[0] // 2) * 2
            raw, made = [], []
            for i in range(2):
                x = kv_ref[p, i, :, c : c + GROUP].astype(jnp.float32)
                x_ref[slot + i, 8:, :] = x
                made.append(feature(x, x_ref.at[slot + i], w_ref[1 + i, :, lanes], m1_ref, m2_ref))
                raw.append(x)
            product = made[0] * made[1]
            top = jnp.where(lax.broadcasted_iota(jnp.int32, (8, GROUP), 0) < 2, raw[0][:8], product[:8])
            out_ref[:rows, there] = jnp.concatenate([top, product[8:]], 0).astype(out_ref.dtype)
            tails = [x[rows - 2 :] for x in raw] + [q_ref[:, lanes].astype(jnp.float32)[14:]]
            out_ref[rows:, there] = jnp.concatenate([raw[1][0:2]] + tails, 0).astype(out_ref.dtype)


def edge_marks(seq_ref):
    t = (
        (lax.axis_index("blk") - 2) * (2 * BLK)
        + lax.broadcasted_iota(jnp.int32, (8, GROUP), 1) * BLK
        + lax.broadcasted_iota(jnp.int32, (8, GROUP), 0)
    )
    return [1.0 - mark.astype(jnp.float32) for mark in boundaries(seq_ref, t)]


def first_rows(now, ahead, w_ref, marks, spot, lanes=slice(None)):
    m1, m2 = [mark[:, spot : spot + 1] for mark in marks]
    top = lax.broadcasted_iota(jnp.int32, ahead.shape, 0) == 0
    made = []
    for i, x0 in enumerate((now[8:], now[:8])):
        x1 = jnp.where(top, pltpu.roll(ahead, 5 - 2 * i, 0), pltpu.roll(x0, 1, 0))
        x2 = pltpu.roll(ahead, 6 - 2 * i, 0)
        w = w_ref[1 + i, :, lanes]
        made.append(w[0:1] * x0 + w[1:2] * x1 * m1 + w[2:3] * x2 * m2)
    return made[0] * made[1]


def put_first_rows(win_ref, at, rows):
    old = win_ref[at : at + 16, :].astype(jnp.float32)
    new = jnp.concatenate([rows, rows], 0)
    first = lax.broadcasted_iota(jnp.int32, old.shape, 0) < 2
    win_ref[at : at + 16, :] = jnp.where(first, new, old).astype(win_ref.dtype)


def reaches_past(seq_ref, block):
    first = block * (2 * BLK)

    def step(k, carry):
        end, start = carry
        end = end + seq_ref[k]
        return end, jnp.where(end <= first, end, start)

    _, start = lax.fori_loop(0, seq_ref.shape[0], step, (jnp.int32(0), jnp.int32(0)), unroll=True)
    return first - 2 * BLK - start > BLK


def tables_kernel(seq_ref, taps_ref, w_ref, out_ref, next_ref, w_half_ref, marks_ref, rev_ref, m_ref):
    groups = out_ref.shape[0]
    taps = taps_ref.shape[1]
    span = out_ref.shape[3]
    half = lax.axis_index("half")
    start = lax.axis_index("blk") * (2 * BLK)
    marks_ref[0], marks_ref[1] = edge_marks(seq_ref)
    for ahead in range(2):
        flag = reaches_past(seq_ref, lax.axis_index("blk") + ahead)
        marks_ref[2 + ahead] = jnp.full((8, GROUP), flag.astype(jnp.float32))
    width = w_half_ref.shape[2]
    w_half_ref[...] = w_ref[:, :, pl.ds(pl.multiple_of(half * width, width), width)]
    turn = lax.broadcasted_iota(jnp.int32, (taps, span), 0) + lax.broadcasted_iota(
        jnp.int32, (taps, span), 1
    )
    turn = (turn == taps).astype(jnp.bfloat16)
    rev_ref[...] = jnp.dot(taps_ref[...], turn, preferred_element_type=jnp.float32)
    seg_in = counted(seq_ref, start - taps + lax.broadcasted_iota(jnp.int32, (8, span), 1))[0:1]
    for part in range(3):
        t_out = start + part * BLK + lax.broadcasted_iota(jnp.int32, (BLK, GROUP), 0)
        seg_out = counted(seq_ref, t_out)[:, 0:1]
        if part < 2:
            m_ref[part] = (seg_in == seg_out).astype(jnp.float32)
        else:
            m_ref[2, :, : 2 * BLK] = (seg_in[:, 2 * BLK : 4 * BLK] == seg_out).astype(jnp.float32)

    def one(g, _):
        row = rev_ref[pl.ds(half * groups + g, 1), :]
        table = pltpu.roll(jnp.broadcast_to(row, (BLK, span)), 0, 1, stride=1, stride_axis=0)
        out_ref[g, 0] = (table * m_ref[0]).astype(out_ref.dtype)
        later = jnp.concatenate([table[:, span - BLK :], table[:, : span - BLK]], 1)
        out_ref[g, 1] = (later * m_ref[1]).astype(out_ref.dtype)
        next_ref[g] = (table[:, : 2 * BLK] * m_ref[2, :, : 2 * BLK]).astype(next_ref.dtype)
        return 0

    lax.fori_loop(0, groups, one, 0)


def fill(win_ref, extra_ref, spot, *pieces):
    at = 0
    for piece in pieces:
        lanes = slice(at, at + piece.shape[1])
        win_ref[pl.ds(pl.multiple_of(spot * BLK, BLK), BLK), lanes] = piece[:BLK]
        extra_ref[spot, :8, lanes] = piece[BLK:].astype(jnp.float32)
        extra_ref[spot, 8:, lanes] = piece[:16].astype(jnp.float32)[:8]
        at += piece.shape[1]


def relay_kernel(piece, marks_ref, next_ref, back_own_ref, w_ref, *refs):
    *ways, out_ref, back_pair_ref, win_ref, extra_ref = refs
    for i, way in enumerate(ways):
        @pl.when((lax.axis_index("blk") + i) % len(ways) == 0)
        def _():
            back_pair_ref[...] = way[...]

    width = out_ref.shape[1]
    half = lax.axis_index("half")
    lanes = slice(piece * width, (piece + 1) * width)
    fill(win_ref, extra_ref, half, back_own_ref.at[:, lanes])
    fill(win_ref, extra_ref, 1 - half, back_pair_ref)
    marks = [marks_ref[0], marks_ref[1]]
    put_first_rows(win_ref, 0, first_rows(extra_ref[0], jnp.zeros((8, width), jnp.float32), w_ref, marks, 2, lanes))
    put_first_rows(win_ref, BLK, first_rows(extra_ref[1], extra_ref[0, :8], w_ref, marks, 3, lanes))
    out_ref[BLK:] = extra_ref[1, :8].astype(out_ref.dtype)
    summed = jnp.max(marks_ref[3]) > 0.5

    @pl.when(summed)
    def _():
        for c in range(0, width, GROUP):
            total = jnp.dot(
                next_ref[(piece * width + c) // GROUP],
                win_ref[:, c : c + GROUP],
                preferred_element_type=jnp.float32,
            )
            out_ref[:BLK, c : c + GROUP] = total.astype(out_ref.dtype)

    @pl.when(jnp.logical_not(summed))
    def _():
        out_ref[:BLK] = win_ref[BLK:]


def gate_rows(seq_ref, raw_ref, tail, w_ref, part, q_ref, x_ref, m1_ref, m2_ref):
    width = raw_ref.shape[1]
    row_masks(seq_ref, lax.axis_index("blk") * (2 * BLK) + part * BLK, m1_ref, m2_ref)
    for c in range(0, width, GROUP):
        lanes = slice(c, c + GROUP)
        w = w_ref[0, :, lanes]
        x = raw_ref[:, lanes].astype(jnp.float32)
        slot = (c // GROUP) % 2
        x_ref[slot, 6:8, :] = tail(lanes)
        x_ref[slot, 8:, :] = x
        q_ref[:, lanes] = feature(x, x_ref.at[slot], w, m1_ref, m2_ref)


def near_kernel(
    seq_ref, marks_ref, table_ref, own_ref, back_own_ref, pair_a_ref, pair_b_ref, back_a_ref, back_b_ref, qkept_ref, w_ref, bias_ref,
    acc_ref, q_ref, win_ref, extra_ref, x_ref, m1_ref, m2_ref,
):
    groups = table_ref.shape[0]
    width = groups * GROUP
    half = lax.axis_index("half")
    fill(win_ref, extra_ref, half, back_own_ref)
    fill(win_ref, extra_ref, 1 - half, back_a_ref, back_b_ref)
    fill(win_ref, extra_ref, 2 + half, own_ref)
    fill(win_ref, extra_ref, 3 - half, pair_a_ref, pair_b_ref)
    marks = [marks_ref[0], marks_ref[1]]
    for spot in (1, 2, 3):
        rows = first_rows(extra_ref[spot], extra_ref[spot - 1, :8], w_ref, marks, spot + 2)
        put_first_rows(win_ref, spot * BLK, rows)
    for g in range(groups):
        lanes = slice(g * GROUP, (g + 1) * GROUP)
        bias = bias_ref[:, pl.ds(pl.multiple_of(half * width + g * GROUP, GROUP), GROUP)]
        for part in range(2):
            total = jnp.dot(
                table_ref[g, part, :, 3 * BLK : (5 + part) * BLK],
                win_ref[BLK : (3 + part) * BLK, lanes],
                preferred_element_type=jnp.float32,
            )
            here = win_ref[(2 + part) * BLK : (3 + part) * BLK, lanes].astype(jnp.float32)
            acc_ref[part * BLK : (part + 1) * BLK, lanes] = total + bias * here
    gate_rows(
        seq_ref, qkept_ref, lambda lanes: extra_ref[1 + half, 6:8, lanes], w_ref, half, q_ref, x_ref, m1_ref, m2_ref
    )


def pair_gate_kernel(seq_ref, raw_ref, own_ref, back_own_ref, w_ref, q_ref, x_ref, m1_ref, m2_ref):
    half = lax.axis_index("half")

    def tail(lanes):
        back = back_own_ref[BLK:, lanes].astype(jnp.float32)
        own = own_ref[BLK:, lanes].astype(jnp.float32)
        return jnp.where(half == 1, back, own)[6:8]

    gate_rows(seq_ref, raw_ref, tail, w_ref, 1 - half, q_ref, x_ref, m1_ref, m2_ref)


def far_kernel(
    short, piece, table_ref, acc_ref, qown_ref, qpair_ref, w_ref, marks_ref, back_own_ref, back_pair_ref, *refs
):
    *refs, kept_ref, sent_ref, total_ref, win_ref, extra_ref = refs
    far_refs, before = refs[: len(refs) - 2 * piece], refs[len(refs) - 2 * piece :]
    width = kept_ref.shape[1]
    half = lax.axis_index("half")
    lanes = slice(piece * width, (piece + 1) * width)
    marks = [marks_ref[0], marks_ref[1]]
    low = 1 if short else 0

    @pl.when(half == 0)
    def _():
        fill(win_ref, extra_ref, 2, back_own_ref.at[:, lanes])

    @pl.when(half == 1)
    def _():
        fill(win_ref, extra_ref, 2, back_pair_ref)

    if short:
        summed = marks_ref[2, 0:1, 0:1]
        fill(win_ref, extra_ref, 1, far_refs[0])
        payload = win_ref[BLK : 2 * BLK, :].astype(jnp.float32)
        win_ref[BLK : 2 * BLK, :] = (payload * (1.0 - summed)).astype(win_ref.dtype)
    else:
        fill(win_ref, extra_ref, half, far_refs[0].at[:, lanes])
        fill(win_ref, extra_ref, 1 - half, far_refs[1 + piece])
        ahead = far_refs[3][:, lanes].astype(jnp.float32)
        put_first_rows(win_ref, 0, first_rows(extra_ref[0], ahead, w_ref, marks, 0, lanes))
        put_first_rows(win_ref, BLK, first_rows(extra_ref[1], extra_ref[0, :8], w_ref, marks, 1, lanes))
    put_first_rows(win_ref, 2 * BLK, first_rows(extra_ref[2], extra_ref[1, :8], w_ref, marks, 2, lanes))
    if before:
        sent_ref[:, :width] = before[1][...]
    for i, (part, q_ref, out_ref) in enumerate(((half, qown_ref, kept_ref), (1 - half, qpair_ref, sent_ref))):
        part_sent = i == 1
        squares = before[0][i] if before else jnp.zeros((BLK, GROUP), jnp.float32)
        rows = pl.ds(pl.multiple_of(part * BLK, BLK), BLK)
        for c in range(0, width, GROUP):
            here = slice(c, c + GROUP)
            whole = slice(piece * width + c, piece * width + c + GROUP)
            filtered = acc_ref[rows, whole] + jnp.dot(
                table_ref[(piece * width + c) // GROUP, part, :, low * BLK : 3 * BLK],
                win_ref[low * BLK : 3 * BLK, here],
                preferred_element_type=jnp.float32,
            )
            if short:
                weight = summed * (part == 0).astype(jnp.float32)
                filtered = filtered + weight * far_refs[0][:BLK, here].astype(jnp.float32)
            gated = q_ref[:, whole] * filtered
            squares = squares + gated * gated
            out_ref[:, whole if before and part_sent else here] = gated.astype(out_ref.dtype)
        if before:
            total_ref[:, i * BLK : (i + 1) * BLK] = lax.dot_general(
                jnp.ones((8, GROUP), jnp.float32),
                squares,
                (((1,), (1,)), ((), ())),
                precision=lax.Precision.HIGHEST,
                preferred_element_type=jnp.float32,
            )[0:1]
        else:
            total_ref[i] = squares


def norm_kernel(channels, power_ref, power_got_ref, *refs):
    *kept_refs, got_ref, gain_ref, out_ref = refs
    half = lax.axis_index("half")
    power = power_ref[:, :BLK] + power_got_ref[:, BLK:]
    scale = lax.rsqrt(power / channels + norm_eps)
    diagonal = lax.broadcasted_iota(jnp.int32, (BLK, BLK), 0) == lax.broadcasted_iota(
        jnp.int32, (BLK, BLK), 1
    )
    column = jnp.sum(jnp.where(diagonal, scale, 0.0), axis=1, keepdims=True)
    for at, refs in ((half, kept_refs), (1 - half, [got_ref])):
        at = at * got_ref.shape[1]
        for ref in refs:
            for c in range(0, ref.shape[1], GROUP):
                lanes = pl.ds(pl.multiple_of(at + c, GROUP), GROUP)
                part = ref[:, c : c + GROUP].astype(jnp.float32)
                out_ref[:, lanes] = (part * column * gain_ref[:, lanes]).astype(out_ref.dtype)
            at = at + ref.shape[1]


def kernel_call(body, outs, in_specs, scratch, flops, moved_bytes):
    return pl.pallas_call(
        body,
        out_shape=outs,
        in_specs=in_specs,
        out_specs=jax.tree.map(lambda _: VMEM, outs),
        scratch_shapes=scratch,
        compiler_params=pltpu.CompilerParams(vmem_limit_bytes=24 << 20),
        cost_estimate=pl.CostEstimate(flops=flops, bytes_accessed=moved_bytes, transcendentals=0),
    )


def matching(blocks, first):
    pairs = []
    for i in range(2 * blocks):
        block = i // 2
        partner = block + 1 if (block - first) % 2 == 0 else block - 1
        pairs.append((i, 2 * partner + i % 2 if 0 <= partner < blocks else i))
    return pairs


def shards(blocks, whole_tokens, channels, projected, short_weight, filter_taps, tap_blocks, skip_bias, norm_gain, seq_lengths):
    rows = projected.shape[0]
    width = projected.shape[2] // 2
    groups = width // GROUP
    taps = filter_taps.shape[1]
    shape = jax.ShapeDtypeStruct
    half_shape = shape((rows, width), jnp.bfloat16)
    half_wide = shape((rows, width), jnp.float32)

    spots = range(2 * blocks)
    to_pair = [(i, i ^ 1) for i in spots]
    ahead = [(i, (i + 2) % (2 * blocks)) for i in spots]

    panels = jnp.transpose(projected, (1, 0, 2))
    message = shape((rows + 8, width), jnp.bfloat16)
    small = shape((rows + 8, width // 2), jnp.bfloat16)
    hbm = pl.BlockSpec(memory_space=pltpu.HBM)
    pieces = 4
    lengths = seq_lengths.reshape(1, -1)
    row_mask = pltpu.VMEM((rows, GROUP), jnp.float32)

    kept, *sent = kernel_call(
        products_kernel,
        (message, small, small),
        [hbm] * 3,
        [
            pltpu.VMEM(lengths.shape, jnp.int32),
            pltpu.VMEM((pieces, 2, rows, 2 * width // pieces), jnp.bfloat16),
            pltpu.VMEM((16, 2 * width), jnp.bfloat16),
            pltpu.VMEM(short_weight.shape, jnp.float32),
            pltpu.VMEM((4, rows + 8, GROUP), jnp.float32),
            row_mask,
            row_mask,
            pltpu.SemaphoreType.DMA((3 + pieces,)),
        ],
        40 * rows * width,
        16 * rows * width,
    )(*[pltpu.with_memory_space_constraint(a, pltpu.HBM) for a in (lengths, panels, short_weight)])

    back_own = moved(kept, ahead)
    pair = [moved(piece, to_pair) for piece in sent]

    filter_taps, _ = lax.optimization_barrier((filter_taps, kept))
    scaled = (filter_taps * jnp.repeat(tap_blocks.astype(jnp.float32), BLK, axis=1)).astype(jnp.bfloat16)
    span = taps + 2 * BLK
    table, table_next, w_half, marks = kernel_call(
        tables_kernel,
        (
            shape((groups, 2, BLK, span), jnp.bfloat16),
            shape((groups, BLK, 2 * BLK), jnp.bfloat16),
            shape((3, 3, width), jnp.float32),
            shape((4, 8, GROUP), jnp.float32),
        ),
        [SMEM, VMEM, VMEM],
        [pltpu.VMEM((2 * groups, span), jnp.float32), pltpu.VMEM((3, BLK, span), jnp.float32)],
        40 * groups * BLK * taps,
        8 * groups * BLK * taps,
    )(seq_lengths, scaled, short_weight)
    table, table_next, pair[0] = lax.optimization_barrier((table, table_next, pair[0]))

    half = lax.axis_index("half")
    query, _ = lax.optimization_barrier((panels, pair[0]))
    qkept = lax.dynamic_slice(query, (0, 0, half * width), (1, rows, width))[0]
    qsent = lax.dynamic_slice(query, (0, 0, (1 - half) * width), (1, rows, width))[0]
    qkept, qsent, pair[1] = lax.optimization_barrier((qkept, qsent, pair[1]))
    qgot = moved(qsent, to_pair)
    back_pair = [[moved(pair[0], ahead)], [moved(pair[1], matching(blocks, first)) for first in (1, 0)]]

    window = pltpu.VMEM((4 * rows, width), jnp.bfloat16)
    extras = pltpu.VMEM((4, 16, width), jnp.float32)
    shifted = pltpu.VMEM((2, rows + 8, GROUP), jnp.float32)
    short = whole_tokens // 2 <= 4 * BLK
    if short:
        onward = [(i, i if i < 2 else i + 2 if i + 2 < 2 * blocks else 2 + i % 2) for i in spots]
        far = []
        for piece in range(2):
            relayed, back_pair[piece] = kernel_call(
                functools.partial(relay_kernel, piece),
                (small, small),
                [VMEM] * (4 + len(back_pair[piece])),
                [pltpu.VMEM((2 * rows, width // 2), jnp.bfloat16), pltpu.VMEM((2, 16, width // 2), jnp.float32)],
                2 * rows * BLK * width,
                4 * rows * width,
            )(marks, table_next, back_own, w_half, *back_pair[piece])
            far.append(moved(relayed, onward))
    else:
        back_pair = [moved(piece, ahead) for piece in pair]
        across = jnp.concatenate([piece[rows:] for piece in sent], 1)
        across = moved(across, [(i, ((i ^ 1) + 6) % (2 * blocks)) for i in spots])
        straight = moved(kept[rows:], [(i, (i + 6) % (2 * blocks)) for i in spots])
        deep = jnp.where(half == 1, straight, across)
        far = [moved(piece, ahead) for piece in (back_own, *back_pair)] + [deep]

    acc, qown = kernel_call(
        near_kernel,
        (shape((2 * rows, width), jnp.float32), half_wide),
        [VMEM] * 12,
        [window, extras, shifted, row_mask, row_mask],
        2 * 5 * rows * BLK * width,
        16 * rows * width,
    )(lengths, marks, table, kept, back_own, *pair, *back_pair, qkept, w_half, skip_bias.reshape(1, -1))

    qpair = kernel_call(
        pair_gate_kernel,
        half_wide,
        [VMEM] * 5,
        [shifted, row_mask, row_mask],
        10 * rows * width,
        8 * rows * width,
    )(lengths, qgot, kept, back_own, w_half)

    done, power, send = [], None, None
    for piece in range(2):
        needed = far[piece : piece + 1] if short else far
        before = [power, send] if piece else []
        own, send, power = kernel_call(
            functools.partial(far_kernel, short, piece),
            (
                shape((rows, width // 2), jnp.float32),
                shape((rows, width if piece else width // 2), jnp.bfloat16),
                shape((1, 2 * rows) if piece else (2, rows, GROUP), jnp.float32),
            ),
            [VMEM] * (8 + len(needed) + len(before)),
            [pltpu.VMEM((3 * rows, width // 2), jnp.bfloat16), pltpu.VMEM((3, 16, width // 2), jnp.float32)],
            2 * 3 * rows * BLK * width,
            12 * rows * width,
        )(table, acc, qown, qpair, w_half, marks, back_own, back_pair[piece], *needed, *before)
        done.append(own)
    back = moved(send, to_pair)

    peers = lax.axis_size("mp")
    shares = [lax.ppermute(power, "mp", [(i, i ^ k) for i in range(peers)]) for k in range(1, peers)]
    power = sum(shares, power)
    return kernel_call(
        functools.partial(norm_kernel, channels),
        shape((rows, 2 * width), jnp.bfloat16),
        [VMEM] * 6,
        [],
        8 * rows * width,
        10 * rows * width,
    )(power, moved(power, to_pair), *done, back, norm_gain.reshape(1, -1))


def solution(mesh):
    blocks = mesh.shape["ctx"] // 2
    grid = Mesh(mesh.devices.reshape(blocks, 2, mesh.shape["mp"]), ("blk", "half", "mp"))
    in_specs = (
        P(SPOTS, None, "mp"),
        P(None, None, "mp"),
        P("mp", None),
        P("mp", None),
        P("mp"),
        P("mp"),
        P(),
    )

    def program(projected, *rest):
        body = functools.partial(shards, blocks, projected.shape[0], projected.shape[2])
        return jax.shard_map(
            body, mesh=grid, in_specs=in_specs, out_specs=P(SPOTS, "mp"), check_vma=False
        )(projected, *rest)

    return program
```

```python
import functools

import jax
import jax.numpy as jnp
from jax import lax
from jax.experimental import pallas as pl
from jax.experimental.pallas import tpu as pltpu
from jax.sharding import Mesh, PartitionSpec as P

GROUP = 128
BLK = 128
norm_eps = 1e-06

VMEM = pl.BlockSpec(memory_space=pltpu.VMEM)
SMEM = pl.BlockSpec(memory_space=pltpu.SMEM)
SPOTS = ("blk", "half")


def moved(block, pairs):
    peers = lax.axis_size("mp")
    whole = [(i * peers + m, j * peers + (m if i != j else m ^ 1)) for i, j in pairs for m in range(peers)]
    return lax.ppermute(block, SPOTS + ("mp",), whole)


def boundaries(seq_ref, t):
    def step(k, carry):
        end, first, second = carry
        end = end + seq_ref[k]
        return end, first | (t == end).astype(jnp.int32), second | (t - 1 == end).astype(jnp.int32)

    first = (t == 0).astype(jnp.int32)
    second = (t == 1).astype(jnp.int32)
    _, first, second = lax.fori_loop(0, seq_ref.shape[0], step, (jnp.int32(0), first, second), unroll=True)
    return first, first | second


def row_masks(lengths_ref, start, m1_ref, m2_ref):
    count = lengths_ref.shape[1]
    square = (count, count)
    upto = lax.broadcasted_iota(jnp.int32, square, 1) <= lax.broadcasted_iota(jnp.int32, square, 0)
    lengths = jnp.broadcast_to(lengths_ref[...].astype(jnp.float32), square)
    ends = jnp.sum(jnp.where(upto, lengths, 0.0), axis=1, keepdims=True)
    t = (start + lax.broadcasted_iota(jnp.int32, (count, BLK), 1)).astype(jnp.float32)
    opens = (t == ends) | (t == 0.0)
    after = opens | (t - 1.0 == ends) | (t == 1.0)
    diagonal = lax.broadcasted_iota(jnp.int32, (BLK, BLK), 0) == lax.broadcasted_iota(jnp.int32, (BLK, BLK), 1)
    for mark, m_ref in ((opens, m1_ref), (after, m2_ref)):
        keep = 1.0 - jnp.max(mark.astype(jnp.float32), axis=0, keepdims=True)
        column = jnp.sum(jnp.where(diagonal, keep, 0.0), axis=1, keepdims=True)
        m_ref[...] = jnp.broadcast_to(column, m_ref.shape)


def counted(seq_ref, t):
    def step(k, carry):
        end, total = carry
        end = end + seq_ref[k]
        return end, total + (end <= t).astype(jnp.int32)

    _, total = lax.fori_loop(
        0, seq_ref.shape[0], step, (jnp.int32(0), jnp.zeros(t.shape, jnp.int32)), unroll=True
    )
    return jnp.where(t >= 0, total, -1)


def feature(x, x_ref, w, m1_ref, m2_ref):
    rows = x.shape[0]
    return (
        w[0:1] * x
        + w[1:2] * x_ref[7 : rows + 7, :] * m1_ref[...]
        + w[2:3] * x_ref[6 : rows + 6, :] * m2_ref[...]
    )


def products_kernel(seq_hbm, panels_hbm, w_hbm, *refs):
    (kept_ref, *sent_refs), refs = refs[:3], refs[3:]
    seq_ref, kv_ref, q_ref, w_ref, x_ref, m1_ref, m2_ref, sems = refs
    width = kept_ref.shape[1]
    rows = kv_ref.shape[2]
    pieces = kv_ref.shape[0]
    piece = kv_ref.shape[3]
    half = lax.axis_index("half")
    shard = lax.axis_index("blk") * 2 + half
    keep_at = pl.multiple_of(half * width, width)
    send_at = pl.multiple_of((1 - half) * width, width)

    loads = [pltpu.make_async_copy(seq_hbm, seq_ref, sems.at[0])]
    for p in range(pieces):
        at = keep_at if p < pieces // 2 else send_at
        lanes = pl.ds(pl.multiple_of(at + (p % (pieces // 2)) * piece, piece), piece)
        loads.append(pltpu.make_async_copy(panels_hbm.at[1:3, :, lanes], kv_ref.at[p], sems.at[1 + p]))
    loads.append(pltpu.make_async_copy(w_hbm, w_ref, sems.at[1 + pieces]))
    loads.append(pltpu.make_async_copy(panels_hbm.at[0, rows - 16 :, :], q_ref, sems.at[2 + pieces]))
    for load in loads:
        load.start()
    x_ref[:, 0:8, :] = jnp.zeros((x_ref.shape[0], 8, GROUP), jnp.float32)
    loads[0].wait()
    row_masks(seq_ref, shard * rows, m1_ref, m2_ref)
    loads[1 + pieces].wait()
    loads[2 + pieces].wait()
    for p in range(pieces):
        loads[1 + p].wait()
        out_ref, at = (kept_ref, keep_at) if p < pieces // 2 else (sent_refs[p - pieces // 2], send_at)
        for c in range(0, piece, GROUP):
            base = (p % (pieces // 2)) * piece + c
            there = slice(base, base + GROUP) if p < pieces // 2 else slice(c, c + GROUP)
            lanes = pl.ds(pl.multiple_of(at + base, GROUP), GROUP)
            slot = (c // GROUP) % (x_ref.shape[0] // 2) * 2
            raw, made = [], []
            for i in range(2):
                x = kv_ref[p, i, :, c : c + GROUP].astype(jnp.float32)
                x_ref[slot + i, 8:, :] = x
                made.append(feature(x, x_ref.at[slot + i], w_ref[1 + i, :, lanes], m1_ref, m2_ref))
                raw.append(x)
            product = made[0] * made[1]
            top = jnp.where(lax.broadcasted_iota(jnp.int32, (8, GROUP), 0) < 2, raw[0][:8], product[:8])
            out_ref[:rows, there] = jnp.concatenate([top, product[8:]], 0).astype(out_ref.dtype)
            tails = [x[rows - 2 :] for x in raw] + [q_ref[:, lanes].astype(jnp.float32)[14:]]
            out_ref[rows:, there] = jnp.concatenate([raw[1][0:2]] + tails, 0).astype(out_ref.dtype)


def edge_marks(seq_ref):
    t = (
        (lax.axis_index("blk") - 2) * (2 * BLK)
        + lax.broadcasted_iota(jnp.int32, (8, GROUP), 1) * BLK
        + lax.broadcasted_iota(jnp.int32, (8, GROUP), 0)
    )
    return [1.0 - mark.astype(jnp.float32) for mark in boundaries(seq_ref, t)]


def first_rows(now, ahead, w_ref, marks, spot, lanes=slice(None)):
    m1, m2 = [mark[:, spot : spot + 1] for mark in marks]
    top = lax.broadcasted_iota(jnp.int32, ahead.shape, 0) == 0
    made = []
    for i, x0 in enumerate((now[8:], now[:8])):
        x1 = jnp.where(top, pltpu.roll(ahead, 5 - 2 * i, 0), pltpu.roll(x0, 1, 0))
        x2 = pltpu.roll(ahead, 6 - 2 * i, 0)
        w = w_ref[1 + i, :, lanes]
        made.append(w[0:1] * x0 + w[1:2] * x1 * m1 + w[2:3] * x2 * m2)
    return made[0] * made[1]


def put_first_rows(win_ref, at, rows):
    old = win_ref[at : at + 16, :].astype(jnp.float32)
    new = jnp.concatenate([rows, rows], 0)
    first = lax.broadcasted_iota(jnp.int32, old.shape, 0) < 2
    win_ref[at : at + 16, :] = jnp.where(first, new, old).astype(win_ref.dtype)


def reaches_past(seq_ref, block):
    first = block * (2 * BLK)

    def step(k, carry):
        end, start = carry
        end = end + seq_ref[k]
        return end, jnp.where(end <= first, end, start)

    _, start = lax.fori_loop(0, seq_ref.shape[0], step, (jnp.int32(0), jnp.int32(0)), unroll=True)
    return first - 2 * BLK - start > BLK


def tables_kernel(seq_ref, taps_ref, w_ref, out_ref, next_ref, w_half_ref, marks_ref, rev_ref, m_ref):
    groups = out_ref.shape[0]
    taps = taps_ref.shape[1]
    span = out_ref.shape[3]
    half = lax.axis_index("half")
    start = lax.axis_index("blk") * (2 * BLK)
    marks_ref[0], marks_ref[1] = edge_marks(seq_ref)
    for ahead in range(2):
        flag = reaches_past(seq_ref, lax.axis_index("blk") + ahead)
        marks_ref[2 + ahead] = jnp.full((8, GROUP), flag.astype(jnp.float32))
    width = w_half_ref.shape[2]
    w_half_ref[...] = w_ref[:, :, pl.ds(pl.multiple_of(half * width, width), width)]
    turn = lax.broadcasted_iota(jnp.int32, (taps, span), 0) + lax.broadcasted_iota(
        jnp.int32, (taps, span), 1
    )
    turn = (turn == taps).astype(jnp.bfloat16)
    rev_ref[...] = jnp.dot(taps_ref[...], turn, preferred_element_type=jnp.float32)
    seg_in = counted(seq_ref, start - taps + lax.broadcasted_iota(jnp.int32, (8, span), 1))[0:1]
    for part in range(3):
        t_out = start + part * BLK + lax.broadcasted_iota(jnp.int32, (BLK, GROUP), 0)
        seg_out = counted(seq_ref, t_out)[:, 0:1]
        if part < 2:
            m_ref[part] = (seg_in == seg_out).astype(jnp.float32)
        else:
            m_ref[2, :, : 2 * BLK] = (seg_in[:, 2 * BLK : 4 * BLK] == seg_out).astype(jnp.float32)

    def one(g, _):
        row = rev_ref[pl.ds(half * groups + g, 1), :]
        table = pltpu.roll(jnp.broadcast_to(row, (BLK, span)), 0, 1, stride=1, stride_axis=0)
        out_ref[g, 0] = (table * m_ref[0]).astype(out_ref.dtype)
        later = jnp.concatenate([table[:, span - BLK :], table[:, : span - BLK]], 1)
        out_ref[g, 1] = (later * m_ref[1]).astype(out_ref.dtype)
        next_ref[g] = (table[:, : 2 * BLK] * m_ref[2, :, : 2 * BLK]).astype(next_ref.dtype)
        return 0

    lax.fori_loop(0, groups, one, 0)


def fill(win_ref, extra_ref, spot, *pieces):
    at = 0
    for piece in pieces:
        lanes = slice(at, at + piece.shape[1])
        win_ref[pl.ds(pl.multiple_of(spot * BLK, BLK), BLK), lanes] = piece[:BLK]
        extra_ref[spot, :8, lanes] = piece[BLK:].astype(jnp.float32)
        extra_ref[spot, 8:, lanes] = piece[:16].astype(jnp.float32)[:8]
        at += piece.shape[1]


def relay_kernel(piece, marks_ref, next_ref, back_own_ref, w_ref, *refs):
    *ways, out_ref, back_pair_ref, win_ref, extra_ref = refs
    for i, way in enumerate(ways):
        @pl.when((lax.axis_index("blk") + i) % len(ways) == 0)
        def _():
            back_pair_ref[...] = way[...]

    width = out_ref.shape[1]
    half = lax.axis_index("half")
    lanes = slice(piece * width, (piece + 1) * width)
    fill(win_ref, extra_ref, half, back_own_ref.at[:, lanes])
    fill(win_ref, extra_ref, 1 - half, back_pair_ref)
    marks = [marks_ref[0], marks_ref[1]]
    put_first_rows(win_ref, 0, first_rows(extra_ref[0], jnp.zeros((8, width), jnp.float32), w_ref, marks, 2, lanes))
    put_first_rows(win_ref, BLK, first_rows(extra_ref[1], extra_ref[0, :8], w_ref, marks, 3, lanes))
    out_ref[BLK:] = extra_ref[1, :8].astype(out_ref.dtype)
    summed = jnp.max(marks_ref[3]) > 0.5

    @pl.when(summed)
    def _():
        for c in range(0, width, GROUP):
            total = jnp.dot(
                next_ref[(piece * width + c) // GROUP],
                win_ref[:, c : c + GROUP],
                preferred_element_type=jnp.float32,
            )
            out_ref[:BLK, c : c + GROUP] = total.astype(out_ref.dtype)

    @pl.when(jnp.logical_not(summed))
    def _():
        out_ref[:BLK] = win_ref[BLK:]


def gate_rows(seq_ref, raw_ref, tail, w_ref, part, q_ref, x_ref, m1_ref, m2_ref):
    width = raw_ref.shape[1]
    row_masks(seq_ref, lax.axis_index("blk") * (2 * BLK) + part * BLK, m1_ref, m2_ref)
    for c in range(0, width, GROUP):
        lanes = slice(c, c + GROUP)
        w = w_ref[0, :, lanes]
        x = raw_ref[:, lanes].astype(jnp.float32)
        slot = (c // GROUP) % 2
        x_ref[slot, 6:8, :] = tail(lanes)
        x_ref[slot, 8:, :] = x
        q_ref[:, lanes] = feature(x, x_ref.at[slot], w, m1_ref, m2_ref)


def near_kernel(
    seq_ref, marks_ref, table_ref, own_ref, back_own_ref, pair_a_ref, pair_b_ref, back_a_ref, back_b_ref, qkept_ref, w_ref, bias_ref,
    acc_ref, q_ref, win_ref, extra_ref, x_ref, m1_ref, m2_ref,
):
    groups = table_ref.shape[0]
    width = groups * GROUP
    half = lax.axis_index("half")
    fill(win_ref, extra_ref, half, back_own_ref)
    fill(win_ref, extra_ref, 1 - half, back_a_ref, back_b_ref)
    fill(win_ref, extra_ref, 2 + half, own_ref)
    fill(win_ref, extra_ref, 3 - half, pair_a_ref, pair_b_ref)
    marks = [marks_ref[0], marks_ref[1]]
    for spot in (1, 2, 3):
        rows = first_rows(extra_ref[spot], extra_ref[spot - 1, :8], w_ref, marks, spot + 2)
        put_first_rows(win_ref, spot * BLK, rows)
    for g in range(groups):
        lanes = slice(g * GROUP, (g + 1) * GROUP)
        bias = bias_ref[:, pl.ds(pl.multiple_of(half * width + g * GROUP, GROUP), GROUP)]
        for part in range(2):
            total = jnp.dot(
                table_ref[g, part, :, 3 * BLK : (5 + part) * BLK],
                win_ref[BLK : (3 + part) * BLK, lanes],
                preferred_element_type=jnp.float32,
            )
            here = win_ref[(2 + part) * BLK : (3 + part) * BLK, lanes].astype(jnp.float32)
            acc_ref[part * BLK : (part + 1) * BLK, lanes] = total + bias * here
    gate_rows(
        seq_ref, qkept_ref, lambda lanes: extra_ref[1 + half, 6:8, lanes], w_ref, half, q_ref, x_ref, m1_ref, m2_ref
    )


def pair_gate_kernel(seq_ref, raw_ref, own_ref, back_own_ref, w_ref, q_ref, x_ref, m1_ref, m2_ref):
    half = lax.axis_index("half")

    def tail(lanes):
        back = back_own_ref[BLK:, lanes].astype(jnp.float32)
        own = own_ref[BLK:, lanes].astype(jnp.float32)
        return jnp.where(half == 1, back, own)[6:8]

    gate_rows(seq_ref, raw_ref, tail, w_ref, 1 - half, q_ref, x_ref, m1_ref, m2_ref)


def far_kernel(
    short, piece, table_ref, acc_ref, qown_ref, qpair_ref, w_ref, marks_ref, back_own_ref, back_pair_ref, *refs
):
    *refs, kept_ref, sent_ref, total_ref, win_ref, extra_ref = refs
    far_refs, before = refs[: len(refs) - 2 * piece], refs[len(refs) - 2 * piece :]
    width = kept_ref.shape[1]
    half = lax.axis_index("half")
    lanes = slice(piece * width, (piece + 1) * width)
    marks = [marks_ref[0], marks_ref[1]]
    low = 1 if short else 0

    @pl.when(half == 0)
    def _():
        fill(win_ref, extra_ref, 2, back_own_ref.at[:, lanes])

    @pl.when(half == 1)
    def _():
        fill(win_ref, extra_ref, 2, back_pair_ref)

    if short:
        summed = marks_ref[2, 0:1, 0:1]
        for i, way in enumerate(far_refs):
            @pl.when((lax.axis_index("blk") + i) % len(far_refs) == 0)
            def _():
                fill(win_ref, extra_ref, 1, way)

        payload = win_ref[BLK : 2 * BLK, :].astype(jnp.float32)
        win_ref[:BLK, :] = (payload * summed).astype(win_ref.dtype)
        win_ref[BLK : 2 * BLK, :] = (payload * (1.0 - summed)).astype(win_ref.dtype)
    else:
        fill(win_ref, extra_ref, half, far_refs[0].at[:, lanes])
        fill(win_ref, extra_ref, 1 - half, far_refs[1 + piece])
        ahead = far_refs[3][:, lanes].astype(jnp.float32)
        put_first_rows(win_ref, 0, first_rows(extra_ref[0], ahead, w_ref, marks, 0, lanes))
        put_first_rows(win_ref, BLK, first_rows(extra_ref[1], extra_ref[0, :8], w_ref, marks, 1, lanes))
    put_first_rows(win_ref, 2 * BLK, first_rows(extra_ref[2], extra_ref[1, :8], w_ref, marks, 2, lanes))
    if before:
        sent_ref[:, :width] = before[1][...]
    for i, (part, q_ref, out_ref) in enumerate(((half, qown_ref, kept_ref), (1 - half, qpair_ref, sent_ref))):
        part_sent = i == 1
        squares = before[0][i] if before else jnp.zeros((BLK, GROUP), jnp.float32)
        rows = pl.ds(pl.multiple_of(part * BLK, BLK), BLK)
        for c in range(0, width, GROUP):
            here = slice(c, c + GROUP)
            whole = slice(piece * width + c, piece * width + c + GROUP)
            filtered = acc_ref[rows, whole] + jnp.dot(
                table_ref[(piece * width + c) // GROUP, part, :, low * BLK : 3 * BLK],
                win_ref[low * BLK : 3 * BLK, here],
                preferred_element_type=jnp.float32,
            )
            if short:
                weight = (part == 0).astype(jnp.float32)
                filtered = filtered + weight * win_ref[:BLK, here].astype(jnp.float32)
            gated = q_ref[:, whole] * filtered
            squares = squares + gated * gated
            out_ref[:, whole if before and part_sent else here] = gated.astype(out_ref.dtype)
        if before:
            total_ref[:, i * BLK : (i + 1) * BLK] = lax.dot_general(
                jnp.ones((8, GROUP), jnp.float32),
                squares,
                (((1,), (1,)), ((), ())),
                precision=lax.Precision.HIGHEST,
                preferred_element_type=jnp.float32,
            )[0:1]
        else:
            total_ref[i] = squares


def norm_kernel(channels, power_ref, power_got_ref, *refs):
    *kept_refs, got_ref, gain_ref, out_ref = refs
    half = lax.axis_index("half")
    power = power_ref[:, :BLK] + power_got_ref[:, BLK:]
    scale = lax.rsqrt(power / channels + norm_eps)
    diagonal = lax.broadcasted_iota(jnp.int32, (BLK, BLK), 0) == lax.broadcasted_iota(
        jnp.int32, (BLK, BLK), 1
    )
    column = jnp.sum(jnp.where(diagonal, scale, 0.0), axis=1, keepdims=True)
    for at, refs in ((half, kept_refs), (1 - half, [got_ref])):
        at = at * got_ref.shape[1]
        for ref in refs:
            for c in range(0, ref.shape[1], GROUP):
                lanes = pl.ds(pl.multiple_of(at + c, GROUP), GROUP)
                part = ref[:, c : c + GROUP].astype(jnp.float32)
                out_ref[:, lanes] = (part * column * gain_ref[:, lanes]).astype(out_ref.dtype)
            at = at + ref.shape[1]


def kernel_call(body, outs, in_specs, scratch, flops, moved_bytes):
    return pl.pallas_call(
        body,
        out_shape=outs,
        in_specs=in_specs,
        out_specs=jax.tree.map(lambda _: VMEM, outs),
        scratch_shapes=scratch,
        compiler_params=pltpu.CompilerParams(vmem_limit_bytes=24 << 20),
        cost_estimate=pl.CostEstimate(flops=flops, bytes_accessed=moved_bytes, transcendentals=0),
    )


def matching(blocks, first):
    pairs = []
    for i in range(2 * blocks):
        block = i // 2
        partner = block + 1 if (block - first) % 2 == 0 else block - 1
        pairs.append((i, 2 * partner + i % 2 if 0 <= partner < blocks else i))
    return pairs


def shards(blocks, whole_tokens, channels, projected, short_weight, filter_taps, tap_blocks, skip_bias, norm_gain, seq_lengths):
    rows = projected.shape[0]
    width = projected.shape[2] // 2
    groups = width // GROUP
    taps = filter_taps.shape[1]
    shape = jax.ShapeDtypeStruct
    half_shape = shape((rows, width), jnp.bfloat16)
    half_wide = shape((rows, width), jnp.float32)

    spots = range(2 * blocks)
    to_pair = [(i, i ^ 1) for i in spots]
    ahead = [(i, (i + 2) % (2 * blocks)) for i in spots]

    panels = jnp.transpose(projected, (1, 0, 2))
    message = shape((rows + 8, width), jnp.bfloat16)
    small = shape((rows + 8, width // 2), jnp.bfloat16)
    hbm = pl.BlockSpec(memory_space=pltpu.HBM)
    pieces = 4
    lengths = seq_lengths.reshape(1, -1)
    row_mask = pltpu.VMEM((rows, GROUP), jnp.float32)

    kept, *sent = kernel_call(
        products_kernel,
        (message, small, small),
        [hbm] * 3,
        [
            pltpu.VMEM(lengths.shape, jnp.int32),
            pltpu.VMEM((pieces, 2, rows, 2 * width // pieces), jnp.bfloat16),
            pltpu.VMEM((16, 2 * width), jnp.bfloat16),
            pltpu.VMEM(short_weight.shape, jnp.float32),
            pltpu.VMEM((4, rows + 8, GROUP), jnp.float32),
            row_mask,
            row_mask,
            pltpu.SemaphoreType.DMA((3 + pieces,)),
        ],
        40 * rows * width,
        16 * rows * width,
    )(*[pltpu.with_memory_space_constraint(a, pltpu.HBM) for a in (lengths, panels, short_weight)])

    back_own = moved(kept, ahead)
    pair = [moved(piece, to_pair) for piece in sent]

    filter_taps, _ = lax.optimization_barrier((filter_taps, kept))
    scaled = (filter_taps * jnp.repeat(tap_blocks.astype(jnp.float32), BLK, axis=1)).astype(jnp.bfloat16)
    span = taps + 2 * BLK
    table, table_next, w_half, marks = kernel_call(
        tables_kernel,
        (
            shape((groups, 2, BLK, span), jnp.bfloat16),
            shape((groups, BLK, 2 * BLK), jnp.bfloat16),
            shape((3, 3, width), jnp.float32),
            shape((4, 8, GROUP), jnp.float32),
        ),
        [SMEM, VMEM, VMEM],
        [pltpu.VMEM((2 * groups, span), jnp.float32), pltpu.VMEM((3, BLK, span), jnp.float32)],
        40 * groups * BLK * taps,
        8 * groups * BLK * taps,
    )(seq_lengths, scaled, short_weight)
    table, table_next, pair[0] = lax.optimization_barrier((table, table_next, pair[0]))

    half = lax.axis_index("half")
    query, _ = lax.optimization_barrier((panels, pair[0]))
    qkept = lax.dynamic_slice(query, (0, 0, half * width), (1, rows, width))[0]
    qsent = lax.dynamic_slice(query, (0, 0, (1 - half) * width), (1, rows, width))[0]
    qkept, qsent, pair[1] = lax.optimization_barrier((qkept, qsent, pair[1]))
    qgot = moved(qsent, to_pair)
    back_pair = [[moved(pair[0], ahead)], [moved(pair[1], matching(blocks, first)) for first in (1, 0)]]

    window = pltpu.VMEM((4 * rows, width), jnp.bfloat16)
    extras = pltpu.VMEM((4, 16, width), jnp.float32)
    shifted = pltpu.VMEM((2, rows + 8, GROUP), jnp.float32)
    short = whole_tokens // 2 <= 4 * BLK
    if short:
        onward = [(i, i if i < 2 else i + 2 if i + 2 < 2 * blocks else 2 + i % 2) for i in spots]
        linked = [[(i, j if min(i, j) >= 2 else i) for i, j in matching(blocks, first)] for first in (1, 0)]
        far = []
        for piece in range(2):
            relayed, back_pair[piece] = kernel_call(
                functools.partial(relay_kernel, piece),
                (small, small),
                [VMEM] * (4 + len(back_pair[piece])),
                [pltpu.VMEM((2 * rows, width // 2), jnp.bfloat16), pltpu.VMEM((2, 16, width // 2), jnp.float32)],
                2 * rows * BLK * width,
                4 * rows * width,
            )(marks, table_next, back_own, w_half, *back_pair[piece])
            far.append([moved(relayed, way) for way in (linked if piece else [onward])])
    else:
        back_pair = [moved(piece, ahead) for piece in pair]
        across = jnp.concatenate([piece[rows:] for piece in sent], 1)
        across = moved(across, [(i, ((i ^ 1) + 6) % (2 * blocks)) for i in spots])
        straight = moved(kept[rows:], [(i, (i + 6) % (2 * blocks)) for i in spots])
        deep = jnp.where(half == 1, straight, across)
        far = [moved(piece, ahead) for piece in (back_own, *back_pair)] + [deep]

    acc, qown = kernel_call(
        near_kernel,
        (shape((2 * rows, width), jnp.float32), half_wide),
        [VMEM] * 12,
        [window, extras, shifted, row_mask, row_mask],
        2 * 5 * rows * BLK * width,
        16 * rows * width,
    )(lengths, marks, table, kept, back_own, *pair, *back_pair, qkept, w_half, skip_bias.reshape(1, -1))

    qpair = kernel_call(
        pair_gate_kernel,
        half_wide,
        [VMEM] * 5,
        [shifted, row_mask, row_mask],
        10 * rows * width,
        8 * rows * width,
    )(lengths, qgot, kept, back_own, w_half)

    done, power, send = [], None, None
    for piece in range(2):
        needed = far[piece] if short else far
        before = [power, send] if piece else []
        own, send, power = kernel_call(
            functools.partial(far_kernel, short, piece),
            (
                shape((rows, width // 2), jnp.float32),
                shape((rows, width if piece else width // 2), jnp.bfloat16),
                shape((1, 2 * rows) if piece else (2, rows, GROUP), jnp.float32),
            ),
            [VMEM] * (8 + len(needed) + len(before)),
            [pltpu.VMEM((3 * rows, width // 2), jnp.bfloat16), pltpu.VMEM((3, 16, width // 2), jnp.float32)],
            2 * 3 * rows * BLK * width,
            12 * rows * width,
        )(table, acc, qown, qpair, w_half, marks, back_own, back_pair[piece], *needed, *before)
        done.append(own)
    back = moved(send, to_pair)

    peers = lax.axis_size("mp")
    shares = [lax.ppermute(power, "mp", [(i, i ^ k) for i in range(peers)]) for k in range(1, peers)]
    power = sum(shares, power)
    return kernel_call(
        functools.partial(norm_kernel, channels),
        shape((rows, 2 * width), jnp.bfloat16),
        [VMEM] * 6,
        [],
        8 * rows * width,
        10 * rows * width,
    )(power, moved(power, to_pair), *done, back, norm_gain.reshape(1, -1))


def solution(mesh):
    blocks = mesh.shape["ctx"] // 2
    grid = Mesh(mesh.devices.reshape(blocks, 2, mesh.shape["mp"]), ("blk", "half", "mp"))
    in_specs = (
        P(SPOTS, None, "mp"),
        P(None, None, "mp"),
        P("mp", None),
        P("mp", None),
        P("mp"),
        P("mp"),
        P(),
    )

    def program(projected, *rest):
        body = functools.partial(shards, blocks, projected.shape[0], projected.shape[2])
        return jax.shard_map(
            body, mesh=grid, in_specs=in_specs, out_specs=P(SPOTS, "mp"), check_vma=False
        )(projected, *rest)

    return program
```

```python
import functools

import jax
import jax.numpy as jnp
from jax import lax
from jax.experimental import pallas as pl
from jax.experimental.pallas import tpu as pltpu
from jax.sharding import Mesh, PartitionSpec as P

GROUP = 128
BLK = 128
norm_eps = 1e-06

VMEM = pl.BlockSpec(memory_space=pltpu.VMEM)
SMEM = pl.BlockSpec(memory_space=pltpu.SMEM)
SPOTS = ("blk", "half")


def moved(block, pairs):
    peers = lax.axis_size("mp")
    whole = [(i * peers + m, j * peers + (m if i != j else m ^ 1)) for i, j in pairs for m in range(peers)]
    return lax.ppermute(block, SPOTS + ("mp",), whole)


def boundaries(seq_ref, t):
    def step(k, carry):
        end, first, second = carry
        end = end + seq_ref[k]
        return end, first | (t == end).astype(jnp.int32), second | (t - 1 == end).astype(jnp.int32)

    first = (t == 0).astype(jnp.int32)
    second = (t == 1).astype(jnp.int32)
    _, first, second = lax.fori_loop(0, seq_ref.shape[0], step, (jnp.int32(0), first, second), unroll=True)
    return first, first | second


def row_masks(lengths_ref, start, m1_ref, m2_ref):
    count = lengths_ref.shape[1]
    square = (count, count)
    upto = lax.broadcasted_iota(jnp.int32, square, 1) <= lax.broadcasted_iota(jnp.int32, square, 0)
    lengths = jnp.broadcast_to(lengths_ref[...].astype(jnp.float32), square)
    ends = jnp.sum(jnp.where(upto, lengths, 0.0), axis=1, keepdims=True)
    t = (start + lax.broadcasted_iota(jnp.int32, (count, BLK), 1)).astype(jnp.float32)
    opens = (t == ends) | (t == 0.0)
    after = opens | (t - 1.0 == ends) | (t == 1.0)
    diagonal = lax.broadcasted_iota(jnp.int32, (BLK, BLK), 0) == lax.broadcasted_iota(jnp.int32, (BLK, BLK), 1)
    for mark, m_ref in ((opens, m1_ref), (after, m2_ref)):
        keep = 1.0 - jnp.max(mark.astype(jnp.float32), axis=0, keepdims=True)
        column = jnp.sum(jnp.where(diagonal, keep, 0.0), axis=1, keepdims=True)
        m_ref[...] = jnp.broadcast_to(column, m_ref.shape)


def counted(seq_ref, t):
    def step(k, carry):
        end, total = carry
        end = end + seq_ref[k]
        return end, total + (end <= t).astype(jnp.int32)

    _, total = lax.fori_loop(
        0, seq_ref.shape[0], step, (jnp.int32(0), jnp.zeros(t.shape, jnp.int32)), unroll=True
    )
    return jnp.where(t >= 0, total, -1)


def feature(x, x_ref, w, m1_ref, m2_ref):
    rows = x.shape[0]
    return (
        w[0:1] * x
        + w[1:2] * x_ref[7 : rows + 7, :] * m1_ref[...]
        + w[2:3] * x_ref[6 : rows + 6, :] * m2_ref[...]
    )


def products_kernel(seq_hbm, panels_hbm, w_hbm, *refs):
    (kept_ref, *sent_refs), refs = refs[:3], refs[3:]
    seq_ref, kv_ref, q_ref, w_ref, x_ref, m1_ref, m2_ref, sems = refs
    width = kept_ref.shape[1]
    rows = kv_ref.shape[2]
    pieces = kv_ref.shape[0]
    piece = kv_ref.shape[3]
    half = lax.axis_index("half")
    shard = lax.axis_index("blk") * 2 + half
    keep_at = pl.multiple_of(half * width, width)
    send_at = pl.multiple_of((1 - half) * width, width)

    loads = [pltpu.make_async_copy(seq_hbm, seq_ref, sems.at[0])]
    for p in range(pieces):
        at = keep_at if p < pieces // 2 else send_at
        lanes = pl.ds(pl.multiple_of(at + (p % (pieces // 2)) * piece, piece), piece)
        loads.append(pltpu.make_async_copy(panels_hbm.at[1:3, :, lanes], kv_ref.at[p], sems.at[1 + p]))
    loads.append(pltpu.make_async_copy(w_hbm, w_ref, sems.at[1 + pieces]))
    loads.append(pltpu.make_async_copy(panels_hbm.at[0, rows - 16 :, :], q_ref, sems.at[2 + pieces]))
    for load in loads:
        load.start()
    x_ref[:, 0:8, :] = jnp.zeros((x_ref.shape[0], 8, GROUP), jnp.float32)
    loads[0].wait()
    row_masks(seq_ref, shard * rows, m1_ref, m2_ref)
    loads[1 + pieces].wait()
    loads[2 + pieces].wait()
    for p in range(pieces):
        loads[1 + p].wait()
        out_ref, at = (kept_ref, keep_at) if p < pieces // 2 else (sent_refs[p - pieces // 2], send_at)
        for c in range(0, piece, GROUP):
            base = (p % (pieces // 2)) * piece + c
            there = slice(base, base + GROUP) if p < pieces // 2 else slice(c, c + GROUP)
            lanes = pl.ds(pl.multiple_of(at + base, GROUP), GROUP)
            slot = (c // GROUP) % (x_ref.shape[0] // 2) * 2
            raw, made = [], []
            for i in range(2):
                x = kv_ref[p, i, :, c : c + GROUP].astype(jnp.float32)
                x_ref[slot + i, 8:, :] = x
                made.append(feature(x, x_ref.at[slot + i], w_ref[1 + i, :, lanes], m1_ref, m2_ref))
                raw.append(x)
            product = made[0] * made[1]
            top = jnp.where(lax.broadcasted_iota(jnp.int32, (8, GROUP), 0) < 2, raw[0][:8], product[:8])
            out_ref[:rows, there] = jnp.concatenate([top, product[8:]], 0).astype(out_ref.dtype)
            tails = [x[rows - 2 :] for x in raw] + [q_ref[:, lanes].astype(jnp.float32)[14:]]
            out_ref[rows:, there] = jnp.concatenate([raw[1][0:2]] + tails, 0).astype(out_ref.dtype)


def edge_marks(seq_ref):
    t = (
        (lax.axis_index("blk") - 2) * (2 * BLK)
        + lax.broadcasted_iota(jnp.int32, (8, GROUP), 1) * BLK
        + lax.broadcasted_iota(jnp.int32, (8, GROUP), 0)
    )
    return [1.0 - mark.astype(jnp.float32) for mark in boundaries(seq_ref, t)]


def first_rows(now, ahead, w_ref, marks, spot, lanes=slice(None)):
    m1, m2 = [mark[:, spot : spot + 1] for mark in marks]
    top = lax.broadcasted_iota(jnp.int32, ahead.shape, 0) == 0
    made = []
    for i, x0 in enumerate((now[8:], now[:8])):
        x1 = jnp.where(top, pltpu.roll(ahead, 5 - 2 * i, 0), pltpu.roll(x0, 1, 0))
        x2 = pltpu.roll(ahead, 6 - 2 * i, 0)
        w = w_ref[1 + i, :, lanes]
        made.append(w[0:1] * x0 + w[1:2] * x1 * m1 + w[2:3] * x2 * m2)
    return made[0] * made[1]


def put_first_rows(win_ref, at, rows):
    old = win_ref[at : at + 16, :].astype(jnp.float32)
    new = jnp.concatenate([rows, rows], 0)
    first = lax.broadcasted_iota(jnp.int32, old.shape, 0) < 2
    win_ref[at : at + 16, :] = jnp.where(first, new, old).astype(win_ref.dtype)


def reaches_past(seq_ref, block):
    first = block * (2 * BLK)

    def step(k, carry):
        end, start = carry
        end = end + seq_ref[k]
        return end, jnp.where(end <= first, end, start)

    _, start = lax.fori_loop(0, seq_ref.shape[0], step, (jnp.int32(0), jnp.int32(0)), unroll=True)
    return first - 2 * BLK - start > BLK


def tables_kernel(seq_ref, taps_ref, w_ref, out_ref, next_ref, w_half_ref, marks_ref, rev_ref, m_ref):
    groups = out_ref.shape[0]
    taps = taps_ref.shape[1]
    span = out_ref.shape[3]
    half = lax.axis_index("half")
    start = lax.axis_index("blk") * (2 * BLK)
    marks_ref[0], marks_ref[1] = edge_marks(seq_ref)
    for ahead in range(2):
        flag = reaches_past(seq_ref, lax.axis_index("blk") + ahead)
        marks_ref[2 + ahead] = jnp.full((8, GROUP), flag.astype(jnp.float32))
    width = w_half_ref.shape[2]
    w_half_ref[...] = w_ref[:, :, pl.ds(pl.multiple_of(half * width, width), width)]
    turn = lax.broadcasted_iota(jnp.int32, (taps, span), 0) + lax.broadcasted_iota(
        jnp.int32, (taps, span), 1
    )
    turn = (turn == taps).astype(jnp.bfloat16)
    rev_ref[...] = jnp.dot(taps_ref[...], turn, preferred_element_type=jnp.float32)
    seg_in = counted(seq_ref, start - taps + lax.broadcasted_iota(jnp.int32, (8, span), 1))[0:1]
    for part in range(3):
        t_out = start + part * BLK + lax.broadcasted_iota(jnp.int32, (BLK, GROUP), 0)
        seg_out = counted(seq_ref, t_out)[:, 0:1]
        if part < 2:
            m_ref[part] = (seg_in == seg_out).astype(jnp.float32)
        else:
            m_ref[2, :, : 2 * BLK] = (seg_in[:, 2 * BLK : 4 * BLK] == seg_out).astype(jnp.float32)

    def one(g, _):
        row = rev_ref[pl.ds(half * groups + g, 1), :]
        table = pltpu.roll(jnp.broadcast_to(row, (BLK, span)), 0, 1, stride=1, stride_axis=0)
        out_ref[g, 0] = (table * m_ref[0]).astype(out_ref.dtype)
        later = jnp.concatenate([table[:, span - BLK :], table[:, : span - BLK]], 1)
        out_ref[g, 1] = (later * m_ref[1]).astype(out_ref.dtype)
        next_ref[g] = (table[:, : 2 * BLK] * m_ref[2, :, : 2 * BLK]).astype(next_ref.dtype)
        return 0

    lax.fori_loop(0, groups, one, 0)


def fill(win_ref, extra_ref, spot, *pieces):
    at = 0
    for piece in pieces:
        lanes = slice(at, at + piece.shape[1])
        win_ref[pl.ds(pl.multiple_of(spot * BLK, BLK), BLK), lanes] = piece[:BLK]
        extra_ref[spot, :8, lanes] = piece[BLK:].astype(jnp.float32)
        extra_ref[spot, 8:, lanes] = piece[:16].astype(jnp.float32)[:8]
        at += piece.shape[1]


def relay_kernel(piece, marks_ref, next_ref, back_own_ref, w_ref, *refs):
    *ways, out_ref, back_pair_ref, win_ref, extra_ref = refs
    for i, way in enumerate(ways):
        @pl.when((lax.axis_index("blk") + i) % len(ways) == 0)
        def _():
            back_pair_ref[...] = way[...]

    width = out_ref.shape[1]
    half = lax.axis_index("half")
    lanes = slice(piece * width, (piece + 1) * width)
    fill(win_ref, extra_ref, half, back_own_ref.at[:, lanes])
    fill(win_ref, extra_ref, 1 - half, back_pair_ref)
    marks = [marks_ref[0], marks_ref[1]]
    put_first_rows(win_ref, 0, first_rows(extra_ref[0], jnp.zeros((8, width), jnp.float32), w_ref, marks, 2, lanes))
    put_first_rows(win_ref, BLK, first_rows(extra_ref[1], extra_ref[0, :8], w_ref, marks, 3, lanes))
    out_ref[BLK:] = extra_ref[1, :8].astype(out_ref.dtype)
    summed = jnp.max(marks_ref[3]) > 0.5

    @pl.when(summed)
    def _():
        for c in range(0, width, GROUP):
            total = jnp.dot(
                next_ref[(piece * width + c) // GROUP],
                win_ref[:, c : c + GROUP],
                preferred_element_type=jnp.float32,
            )
            out_ref[:BLK, c : c + GROUP] = total.astype(out_ref.dtype)

    @pl.when(jnp.logical_not(summed))
    def _():
        out_ref[:BLK] = win_ref[BLK:]


def gate_rows(seq_ref, raw_ref, tail, w_ref, part, q_ref, x_ref, m1_ref, m2_ref):
    width = raw_ref.shape[1]
    row_masks(seq_ref, lax.axis_index("blk") * (2 * BLK) + part * BLK, m1_ref, m2_ref)
    for c in range(0, width, GROUP):
        lanes = slice(c, c + GROUP)
        w = w_ref[0, :, lanes]
        x = raw_ref[:, lanes].astype(jnp.float32)
        slot = (c // GROUP) % 2
        x_ref[slot, 6:8, :] = tail(lanes)
        x_ref[slot, 8:, :] = x
        q_ref[:, lanes] = feature(x, x_ref.at[slot], w, m1_ref, m2_ref)


def near_kernel(
    seq_ref, marks_ref, table_ref, own_ref, back_own_ref, pair_a_ref, pair_b_ref, back_a_ref, back_b_ref, qkept_ref, w_ref, bias_ref,
    acc_ref, q_ref, win_ref, extra_ref, x_ref, m1_ref, m2_ref,
):
    groups = table_ref.shape[0]
    width = groups * GROUP
    half = lax.axis_index("half")
    fill(win_ref, extra_ref, half, back_own_ref)
    fill(win_ref, extra_ref, 1 - half, back_a_ref, back_b_ref)
    fill(win_ref, extra_ref, 2 + half, own_ref)
    fill(win_ref, extra_ref, 3 - half, pair_a_ref, pair_b_ref)
    marks = [marks_ref[0], marks_ref[1]]
    for spot in (1, 2, 3):
        rows = first_rows(extra_ref[spot], extra_ref[spot - 1, :8], w_ref, marks, spot + 2)
        put_first_rows(win_ref, spot * BLK, rows)
    for g in range(groups):
        lanes = slice(g * GROUP, (g + 1) * GROUP)
        bias = bias_ref[:, pl.ds(pl.multiple_of(half * width + g * GROUP, GROUP), GROUP)]
        for part in range(2):
            total = jnp.dot(
                table_ref[g, part, :, 3 * BLK : (5 + part) * BLK],
                win_ref[BLK : (3 + part) * BLK, lanes],
                preferred_element_type=jnp.float32,
            )
            here = win_ref[(2 + part) * BLK : (3 + part) * BLK, lanes].astype(jnp.float32)
            acc_ref[part * BLK : (part + 1) * BLK, lanes] = total + bias * here
    gate_rows(
        seq_ref, qkept_ref, lambda lanes: extra_ref[1 + half, 6:8, lanes], w_ref, half, q_ref, x_ref, m1_ref, m2_ref
    )


def pair_gate_kernel(seq_ref, raw_ref, own_ref, back_own_ref, w_ref, q_ref, x_ref, m1_ref, m2_ref):
    half = lax.axis_index("half")

    def tail(lanes):
        back = back_own_ref[BLK:, lanes].astype(jnp.float32)
        own = own_ref[BLK:, lanes].astype(jnp.float32)
        return jnp.where(half == 1, back, own)[6:8]

    gate_rows(seq_ref, raw_ref, tail, w_ref, 1 - half, q_ref, x_ref, m1_ref, m2_ref)


def far_kernel(
    short, piece, table_ref, acc_ref, qown_ref, qpair_ref, w_ref, marks_ref, back_own_ref, back_pair_ref, *refs
):
    *refs, kept_ref, sent_ref, total_ref, win_ref, extra_ref = refs
    far_refs, before = refs[: len(refs) - 2 * piece], refs[len(refs) - 2 * piece :]
    width = kept_ref.shape[1]
    half = lax.axis_index("half")
    lanes = slice(piece * width, (piece + 1) * width)
    marks = [marks_ref[0], marks_ref[1]]
    low = 1 if short else 0

    @pl.when(half == 0)
    def _():
        fill(win_ref, extra_ref, 2, back_own_ref.at[:, lanes])

    @pl.when(half == 1)
    def _():
        fill(win_ref, extra_ref, 2, back_pair_ref)

    if short:
        summed = marks_ref[2, 0:1, 0:1]
        fill(win_ref, extra_ref, 1, far_refs[0])
        payload = win_ref[BLK : 2 * BLK, :].astype(jnp.float32)
        win_ref[BLK : 2 * BLK, :] = (payload * (1.0 - summed)).astype(win_ref.dtype)
    else:
        fill(win_ref, extra_ref, half, far_refs[0].at[:, lanes])
        fill(win_ref, extra_ref, 1 - half, far_refs[1 + piece])
        ahead = far_refs[3][:, lanes].astype(jnp.float32)
        put_first_rows(win_ref, 0, first_rows(extra_ref[0], ahead, w_ref, marks, 0, lanes))
        put_first_rows(win_ref, BLK, first_rows(extra_ref[1], extra_ref[0, :8], w_ref, marks, 1, lanes))
    put_first_rows(win_ref, 2 * BLK, first_rows(extra_ref[2], extra_ref[1, :8], w_ref, marks, 2, lanes))
    if before:
        sent_ref[:, :width] = before[1][...]
    for i, (part, q_ref, out_ref) in enumerate(((half, qown_ref, kept_ref), (1 - half, qpair_ref, sent_ref))):
        part_sent = i == 1
        squares = before[0][i] if before else jnp.zeros((BLK, GROUP), jnp.float32)
        rows = pl.ds(pl.multiple_of(part * BLK, BLK), BLK)
        for c in range(0, width, GROUP):
            here = slice(c, c + GROUP)
            whole = slice(piece * width + c, piece * width + c + GROUP)
            filtered = acc_ref[rows, whole] + jnp.dot(
                table_ref[(piece * width + c) // GROUP, part, :, low * BLK : 3 * BLK],
                win_ref[low * BLK : 3 * BLK, here],
                preferred_element_type=jnp.float32,
            )
            if short:
                weight = summed * (part == 0).astype(jnp.float32)
                filtered = filtered + weight * far_refs[0][:BLK, here].astype(jnp.float32)
            gated = q_ref[:, whole] * filtered
            squares = squares + gated * gated
            out_ref[:, whole if before and part_sent else here] = gated.astype(out_ref.dtype)
        if before:
            place = lax.broadcasted_iota(jnp.int32, (BLK, BLK), 0) - lax.broadcasted_iota(jnp.int32, (BLK, BLK), 1)
            column = jnp.sum(squares, axis=1, keepdims=True)
            total_ref[:, i * BLK : (i + 1) * BLK] = jnp.sum(
                jnp.where(place == 0, column, 0.0), axis=0, keepdims=True
            )
        else:
            total_ref[i] = squares


def norm_kernel(channels, power_ref, power_got_ref, *refs):
    *kept_refs, got_ref, gain_ref, out_hbm, out_ref, sems = refs
    half = lax.axis_index("half")
    power = power_ref[:, :BLK] + power_got_ref[:, BLK:]
    scale = lax.rsqrt(power / channels + norm_eps)
    diagonal = lax.broadcasted_iota(jnp.int32, (BLK, BLK), 0) == lax.broadcasted_iota(
        jnp.int32, (BLK, BLK), 1
    )
    column = jnp.sum(jnp.where(diagonal, scale, 0.0), axis=1, keepdims=True)
    piece = kept_refs[0].shape[1]
    stores = []
    for at, refs in ((half, kept_refs), (1 - half, [got_ref])):
        at = at * got_ref.shape[1]
        for ref in refs:
            for c in range(0, ref.shape[1], GROUP):
                lanes = pl.ds(pl.multiple_of(at + c, GROUP), GROUP)
                part = ref[:, c : c + GROUP].astype(jnp.float32)
                out_ref[:, lanes] = (part * column * gain_ref[:, lanes]).astype(out_ref.dtype)
                if (c + GROUP) % piece == 0:
                    ready = pl.ds(pl.multiple_of(at + c + GROUP - piece, piece), piece)
                    stores.append(
                        pltpu.make_async_copy(out_ref.at[:, ready], out_hbm.at[:, ready], sems.at[len(stores)])
                    )
                    stores[-1].start()
            at = at + ref.shape[1]
    for store in stores:
        store.wait()


def kernel_call(body, outs, in_specs, scratch, flops, moved_bytes, out_space=VMEM):
    return pl.pallas_call(
        body,
        out_shape=outs,
        in_specs=in_specs,
        out_specs=jax.tree.map(lambda _: out_space, outs),
        scratch_shapes=scratch,
        compiler_params=pltpu.CompilerParams(vmem_limit_bytes=24 << 20),
        cost_estimate=pl.CostEstimate(flops=flops, bytes_accessed=moved_bytes, transcendentals=0),
    )


def matching(blocks, first):
    pairs = []
    for i in range(2 * blocks):
        block = i // 2
        partner = block + 1 if (block - first) % 2 == 0 else block - 1
        pairs.append((i, 2 * partner + i % 2 if 0 <= partner < blocks else i))
    return pairs


def shards(blocks, whole_tokens, channels, projected, short_weight, filter_taps, tap_blocks, skip_bias, norm_gain, seq_lengths):
    rows = projected.shape[0]
    width = projected.shape[2] // 2
    groups = width // GROUP
    taps = filter_taps.shape[1]
    shape = jax.ShapeDtypeStruct
    half_shape = shape((rows, width), jnp.bfloat16)
    half_wide = shape((rows, width), jnp.float32)

    spots = range(2 * blocks)
    to_pair = [(i, i ^ 1) for i in spots]
    ahead = [(i, (i + 2) % (2 * blocks)) for i in spots]

    panels = jnp.transpose(projected, (1, 0, 2))
    message = shape((rows + 8, width), jnp.bfloat16)
    small = shape((rows + 8, width // 2), jnp.bfloat16)
    hbm = pl.BlockSpec(memory_space=pltpu.HBM)
    pieces = 4
    lengths = seq_lengths.reshape(1, -1)
    row_mask = pltpu.VMEM((rows, GROUP), jnp.float32)

    kept, *sent = kernel_call(
        products_kernel,
        (message, small, small),
        [hbm] * 3,
        [
            pltpu.VMEM(lengths.shape, jnp.int32),
            pltpu.VMEM((pieces, 2, rows, 2 * width // pieces), jnp.bfloat16),
            pltpu.VMEM((16, 2 * width), jnp.bfloat16),
            pltpu.VMEM(short_weight.shape, jnp.float32),
            pltpu.VMEM((4, rows + 8, GROUP), jnp.float32),
            row_mask,
            row_mask,
            pltpu.SemaphoreType.DMA((3 + pieces,)),
        ],
        40 * rows * width,
        16 * rows * width,
    )(*[pltpu.with_memory_space_constraint(a, pltpu.HBM) for a in (lengths, panels, short_weight)])

    back_own = moved(kept, ahead)
    pair = [moved(piece, to_pair) for piece in sent]

    filter_taps, _ = lax.optimization_barrier((filter_taps, kept))
    scaled = (filter_taps * jnp.repeat(tap_blocks.astype(jnp.float32), BLK, axis=1)).astype(jnp.bfloat16)
    span = taps + 2 * BLK
    table, table_next, w_half, marks = kernel_call(
        tables_kernel,
        (
            shape((groups, 2, BLK, span), jnp.bfloat16),
            shape((groups, BLK, 2 * BLK), jnp.bfloat16),
            shape((3, 3, width), jnp.float32),
            shape((4, 8, GROUP), jnp.float32),
        ),
        [SMEM, VMEM, VMEM],
        [pltpu.VMEM((2 * groups, span), jnp.float32), pltpu.VMEM((3, BLK, span), jnp.float32)],
        40 * groups * BLK * taps,
        8 * groups * BLK * taps,
    )(seq_lengths, scaled, short_weight)
    table, table_next, pair[0] = lax.optimization_barrier((table, table_next, pair[0]))

    half = lax.axis_index("half")
    query, _ = lax.optimization_barrier((panels, pair[0]))
    qkept = lax.dynamic_slice(query, (0, 0, half * width), (1, rows, width))[0]
    qsent = lax.dynamic_slice(query, (0, 0, (1 - half) * width), (1, rows, width))[0]
    qkept, qsent, pair[1] = lax.optimization_barrier((qkept, qsent, pair[1]))
    qgot = moved(qsent, to_pair)
    back_pair = [[moved(pair[0], ahead)], [moved(pair[1], matching(blocks, first)) for first in (1, 0)]]

    window = pltpu.VMEM((4 * rows, width), jnp.bfloat16)
    extras = pltpu.VMEM((4, 16, width), jnp.float32)
    shifted = pltpu.VMEM((2, rows + 8, GROUP), jnp.float32)
    short = whole_tokens // 2 <= 4 * BLK
    if short:
        onward = [(i, i if i < 2 else i + 2 if i + 2 < 2 * blocks else 2 + i % 2) for i in spots]
        far = []
        for piece in range(2):
            relayed, back_pair[piece] = kernel_call(
                functools.partial(relay_kernel, piece),
                (small, small),
                [VMEM] * (4 + len(back_pair[piece])),
                [pltpu.VMEM((2 * rows, width // 2), jnp.bfloat16), pltpu.VMEM((2, 16, width // 2), jnp.float32)],
                2 * rows * BLK * width,
                4 * rows * width,
            )(marks, table_next, back_own, w_half, *back_pair[piece])
            far.append(moved(relayed, onward))
    else:
        back_pair = [moved(piece, ahead) for piece in pair]
        across = jnp.concatenate([piece[rows:] for piece in sent], 1)
        across = moved(across, [(i, ((i ^ 1) + 6) % (2 * blocks)) for i in spots])
        straight = moved(kept[rows:], [(i, (i + 6) % (2 * blocks)) for i in spots])
        deep = jnp.where(half == 1, straight, across)
        far = [moved(piece, ahead) for piece in (back_own, *back_pair)] + [deep]

    acc, qown = kernel_call(
        near_kernel,
        (shape((2 * rows, width), jnp.float32), half_wide),
        [VMEM] * 12,
        [window, extras, shifted, row_mask, row_mask],
        2 * 5 * rows * BLK * width,
        16 * rows * width,
    )(lengths, marks, table, kept, back_own, *pair, *back_pair, qkept, w_half, skip_bias.reshape(1, -1))

    qpair = kernel_call(
        pair_gate_kernel,
        half_wide,
        [VMEM] * 5,
        [shifted, row_mask, row_mask],
        10 * rows * width,
        8 * rows * width,
    )(lengths, qgot, kept, back_own, w_half)

    done, power, send = [], None, None
    for piece in range(2):
        needed = far[piece : piece + 1] if short else far
        before = [power, send] if piece else []
        own, send, power = kernel_call(
            functools.partial(far_kernel, short, piece),
            (
                shape((rows, width // 2), jnp.float32),
                shape((rows, width if piece else width // 2), jnp.bfloat16),
                shape((1, 2 * rows) if piece else (2, rows, GROUP), jnp.float32),
            ),
            [VMEM] * (8 + len(needed) + len(before)),
            [pltpu.VMEM((3 * rows, width // 2), jnp.bfloat16), pltpu.VMEM((3, 16, width // 2), jnp.float32)],
            2 * 3 * rows * BLK * width,
            12 * rows * width,
        )(table, acc, qown, qpair, w_half, marks, back_own, back_pair[piece], *needed, *before)
        done.append(own)
    back = moved(send, to_pair)

    peers = lax.axis_size("mp")
    shares = [lax.ppermute(power, "mp", [(i, i ^ k) for i in range(peers)]) for k in range(1, peers)]
    power = sum(shares, power)
    return kernel_call(
        functools.partial(norm_kernel, channels),
        shape((rows, 2 * width), jnp.bfloat16),
        [VMEM] * 6,
        [pltpu.VMEM((rows, 2 * width), jnp.bfloat16), pltpu.SemaphoreType.DMA((4,))],
        8 * rows * width,
        10 * rows * width,
        hbm,
    )(power, moved(power, to_pair), *done, back, norm_gain.reshape(1, -1))


def solution(mesh):
    blocks = mesh.shape["ctx"] // 2
    grid = Mesh(mesh.devices.reshape(blocks, 2, mesh.shape["mp"]), ("blk", "half", "mp"))
    in_specs = (
        P(SPOTS, None, "mp"),
        P(None, None, "mp"),
        P("mp", None),
        P("mp", None),
        P("mp"),
        P("mp"),
        P(),
    )

    def program(projected, *rest):
        body = functools.partial(shards, blocks, projected.shape[0], projected.shape[2])
        return jax.shard_map(
            body, mesh=grid, in_specs=in_specs, out_specs=P(SPOTS, "mp"), check_vma=False
        )(projected, *rest)

    return program
```

```python
import functools

import jax
import jax.numpy as jnp
from jax import lax
from jax.experimental import pallas as pl
from jax.experimental.pallas import tpu as pltpu
from jax.sharding import Mesh, PartitionSpec as P

GROUP = 128
BLK = 128
norm_eps = 1e-06

VMEM = pl.BlockSpec(memory_space=pltpu.VMEM)
SMEM = pl.BlockSpec(memory_space=pltpu.SMEM)
SPOTS = ("blk", "half")


def moved(block, pairs):
    peers = lax.axis_size("mp")
    whole = [(i * peers + m, j * peers + (m if i != j else m ^ 1)) for i, j in pairs for m in range(peers)]
    return lax.ppermute(block, SPOTS + ("mp",), whole)


def boundaries(seq_ref, t):
    def step(k, carry):
        end, first, second = carry
        end = end + seq_ref[k]
        return end, first | (t == end).astype(jnp.int32), second | (t - 1 == end).astype(jnp.int32)

    first = (t == 0).astype(jnp.int32)
    second = (t == 1).astype(jnp.int32)
    _, first, second = lax.fori_loop(0, seq_ref.shape[0], step, (jnp.int32(0), first, second), unroll=True)
    return first, first | second


def row_masks(lengths_ref, start, m1_ref, m2_ref):
    count = lengths_ref.shape[1]
    square = (count, count)
    upto = lax.broadcasted_iota(jnp.int32, square, 1) <= lax.broadcasted_iota(jnp.int32, square, 0)
    lengths = jnp.broadcast_to(lengths_ref[...].astype(jnp.float32), square)
    ends = jnp.sum(jnp.where(upto, lengths, 0.0), axis=1, keepdims=True)
    t = (start + lax.broadcasted_iota(jnp.int32, (count, BLK), 1)).astype(jnp.float32)
    opens = (t == ends) | (t == 0.0)
    after = opens | (t - 1.0 == ends) | (t == 1.0)
    diagonal = lax.broadcasted_iota(jnp.int32, (BLK, BLK), 0) == lax.broadcasted_iota(jnp.int32, (BLK, BLK), 1)
    for mark, m_ref in ((opens, m1_ref), (after, m2_ref)):
        keep = 1.0 - jnp.max(mark.astype(jnp.float32), axis=0, keepdims=True)
        column = jnp.sum(jnp.where(diagonal, keep, 0.0), axis=1, keepdims=True)
        m_ref[...] = jnp.broadcast_to(column, m_ref.shape)


def counted(seq_ref, t):
    def step(k, carry):
        end, total = carry
        end = end + seq_ref[k]
        return end, total + (end <= t).astype(jnp.int32)

    _, total = lax.fori_loop(
        0, seq_ref.shape[0], step, (jnp.int32(0), jnp.zeros(t.shape, jnp.int32)), unroll=True
    )
    return jnp.where(t >= 0, total, -1)


def feature(x, x_ref, w, m1_ref, m2_ref):
    rows = x.shape[0]
    return (
        w[0:1] * x
        + w[1:2] * x_ref[7 : rows + 7, :] * m1_ref[...]
        + w[2:3] * x_ref[6 : rows + 6, :] * m2_ref[...]
    )


def products_kernel(seq_hbm, panels_hbm, w_hbm, *refs):
    (kept_ref, *sent_refs), refs = refs[:3], refs[3:]
    seq_ref, kv_ref, q_ref, w_ref, x_ref, m1_ref, m2_ref, sems = refs
    width = kept_ref.shape[1]
    rows = kv_ref.shape[2]
    pieces = kv_ref.shape[0]
    piece = kv_ref.shape[3]
    half = lax.axis_index("half")
    shard = lax.axis_index("blk") * 2 + half
    keep_at = pl.multiple_of(half * width, width)
    send_at = pl.multiple_of((1 - half) * width, width)

    loads = [pltpu.make_async_copy(seq_hbm, seq_ref, sems.at[0])]
    for p in range(pieces):
        at = keep_at if p < pieces // 2 else send_at
        lanes = pl.ds(pl.multiple_of(at + (p % (pieces // 2)) * piece, piece), piece)
        loads.append(pltpu.make_async_copy(panels_hbm.at[1:3, :, lanes], kv_ref.at[p], sems.at[1 + p]))
    loads.append(pltpu.make_async_copy(w_hbm, w_ref, sems.at[1 + pieces]))
    loads.append(pltpu.make_async_copy(panels_hbm.at[0, rows - 16 :, :], q_ref, sems.at[2 + pieces]))
    for load in loads:
        load.start()
    x_ref[:, 0:8, :] = jnp.zeros((x_ref.shape[0], 8, GROUP), jnp.float32)
    loads[0].wait()
    row_masks(seq_ref, shard * rows, m1_ref, m2_ref)
    loads[1 + pieces].wait()
    loads[2 + pieces].wait()
    for p in range(pieces):
        loads[1 + p].wait()
        out_ref, at = (kept_ref, keep_at) if p < pieces // 2 else (sent_refs[p - pieces // 2], send_at)
        for c in range(0, piece, GROUP):
            base = (p % (pieces // 2)) * piece + c
            there = slice(base, base + GROUP) if p < pieces // 2 else slice(c, c + GROUP)
            lanes = pl.ds(pl.multiple_of(at + base, GROUP), GROUP)
            slot = (c // GROUP) % (x_ref.shape[0] // 2) * 2
            raw, made = [], []
            for i in range(2):
                x = kv_ref[p, i, :, c : c + GROUP].astype(jnp.float32)
                x_ref[slot + i, 8:, :] = x
                made.append(feature(x, x_ref.at[slot + i], w_ref[1 + i, :, lanes], m1_ref, m2_ref))
                raw.append(x)
            product = made[0] * made[1]
            top = jnp.where(lax.broadcasted_iota(jnp.int32, (8, GROUP), 0) < 2, raw[0][:8], product[:8])
            out_ref[:rows, there] = jnp.concatenate([top, product[8:]], 0).astype(out_ref.dtype)
            tails = [x[rows - 2 :] for x in raw] + [q_ref[:, lanes].astype(jnp.float32)[14:]]
            out_ref[rows:, there] = jnp.concatenate([raw[1][0:2]] + tails, 0).astype(out_ref.dtype)


def edge_marks(seq_ref):
    t = (
        (lax.axis_index("blk") - 2) * (2 * BLK)
        + lax.broadcasted_iota(jnp.int32, (8, GROUP), 1) * BLK
        + lax.broadcasted_iota(jnp.int32, (8, GROUP), 0)
    )
    return [1.0 - mark.astype(jnp.float32) for mark in boundaries(seq_ref, t)]


def first_rows(now, ahead, w_ref, marks, spot, lanes=slice(None)):
    m1, m2 = [mark[:, spot : spot + 1] for mark in marks]
    top = lax.broadcasted_iota(jnp.int32, ahead.shape, 0) == 0
    made = []
    for i, x0 in enumerate((now[8:], now[:8])):
        x1 = jnp.where(top, pltpu.roll(ahead, 5 - 2 * i, 0), pltpu.roll(x0, 1, 0))
        x2 = pltpu.roll(ahead, 6 - 2 * i, 0)
        w = w_ref[1 + i, :, lanes]
        made.append(w[0:1] * x0 + w[1:2] * x1 * m1 + w[2:3] * x2 * m2)
    return made[0] * made[1]


def put_first_rows(win_ref, at, rows):
    old = win_ref[at : at + 16, :].astype(jnp.float32)
    new = jnp.concatenate([rows, rows], 0)
    first = lax.broadcasted_iota(jnp.int32, old.shape, 0) < 2
    win_ref[at : at + 16, :] = jnp.where(first, new, old).astype(win_ref.dtype)


def reaches_past(seq_ref, block):
    first = block * (2 * BLK)

    def step(k, carry):
        end, start = carry
        end = end + seq_ref[k]
        return end, jnp.where(end <= first, end, start)

    _, start = lax.fori_loop(0, seq_ref.shape[0], step, (jnp.int32(0), jnp.int32(0)), unroll=True)
    return first - 2 * BLK - start > BLK


def tables_kernel(seq_ref, taps_ref, w_ref, out_ref, next_ref, w_half_ref, marks_ref, rev_ref, m_ref):
    groups = out_ref.shape[0]
    taps = taps_ref.shape[1]
    span = out_ref.shape[3]
    half = lax.axis_index("half")
    start = lax.axis_index("blk") * (2 * BLK)
    marks_ref[0], marks_ref[1] = edge_marks(seq_ref)
    for ahead in range(2):
        flag = reaches_past(seq_ref, lax.axis_index("blk") + ahead)
        marks_ref[2 + ahead] = jnp.full((8, GROUP), flag.astype(jnp.float32))
    width = w_half_ref.shape[2]
    w_half_ref[...] = w_ref[:, :, pl.ds(pl.multiple_of(half * width, width), width)]
    turn = lax.broadcasted_iota(jnp.int32, (taps, span), 0) + lax.broadcasted_iota(
        jnp.int32, (taps, span), 1
    )
    turn = (turn == taps).astype(jnp.bfloat16)
    rev_ref[...] = jnp.dot(taps_ref[...], turn, preferred_element_type=jnp.float32)
    seg_in = counted(seq_ref, start - taps + lax.broadcasted_iota(jnp.int32, (8, span), 1))[0:1]
    for part in range(3):
        t_out = start + part * BLK + lax.broadcasted_iota(jnp.int32, (BLK, GROUP), 0)
        seg_out = counted(seq_ref, t_out)[:, 0:1]
        if part < 2:
            m_ref[part] = (seg_in == seg_out).astype(jnp.float32)
        else:
            m_ref[2, :, : 2 * BLK] = (seg_in[:, 2 * BLK : 4 * BLK] == seg_out).astype(jnp.float32)

    def one(g, _):
        row = rev_ref[pl.ds(half * groups + g, 1), :]
        table = pltpu.roll(jnp.broadcast_to(row, (BLK, span)), 0, 1, stride=1, stride_axis=0)
        out_ref[g, 0] = (table * m_ref[0]).astype(out_ref.dtype)
        later = jnp.concatenate([table[:, span - BLK :], table[:, : span - BLK]], 1)
        out_ref[g, 1] = (later * m_ref[1]).astype(out_ref.dtype)
        next_ref[g] = (table[:, : 2 * BLK] * m_ref[2, :, : 2 * BLK]).astype(next_ref.dtype)
        return 0

    lax.fori_loop(0, groups, one, 0)


def fill(win_ref, extra_ref, spot, *pieces):
    at = 0
    for piece in pieces:
        lanes = slice(at, at + piece.shape[1])
        win_ref[pl.ds(pl.multiple_of(spot * BLK, BLK), BLK), lanes] = piece[:BLK]
        extra_ref[spot, :8, lanes] = piece[BLK:].astype(jnp.float32)
        extra_ref[spot, 8:, lanes] = piece[:16].astype(jnp.float32)[:8]
        at += piece.shape[1]


def relay_kernel(piece, marks_ref, next_ref, back_own_ref, w_ref, *refs):
    *ways, out_ref, back_pair_ref, win_ref, extra_ref = refs
    for i, way in enumerate(ways):
        @pl.when((lax.axis_index("blk") + i) % len(ways) == len(ways) - 1)
        def _():
            back_pair_ref[...] = way[...]

    width = out_ref.shape[1]
    half = lax.axis_index("half")
    lanes = slice(piece * width, (piece + 1) * width)
    fill(win_ref, extra_ref, half, back_own_ref.at[:, lanes])
    fill(win_ref, extra_ref, 1 - half, back_pair_ref)
    marks = [marks_ref[0], marks_ref[1]]
    put_first_rows(win_ref, 0, first_rows(extra_ref[0], jnp.zeros((8, width), jnp.float32), w_ref, marks, 2, lanes))
    put_first_rows(win_ref, BLK, first_rows(extra_ref[1], extra_ref[0, :8], w_ref, marks, 3, lanes))
    out_ref[BLK:] = extra_ref[1, :8].astype(out_ref.dtype)
    summed = jnp.max(marks_ref[3]) > 0.5

    @pl.when(summed)
    def _():
        for c in range(0, width, GROUP):
            total = jnp.dot(
                next_ref[(piece * width + c) // GROUP],
                win_ref[:, c : c + GROUP],
                preferred_element_type=jnp.float32,
            )
            out_ref[:BLK, c : c + GROUP] = total.astype(out_ref.dtype)

    @pl.when(jnp.logical_not(summed))
    def _():
        out_ref[:BLK] = win_ref[BLK:]


def gate_rows(seq_ref, raw_ref, tail, w_ref, part, q_ref, x_ref, m1_ref, m2_ref):
    width = raw_ref.shape[1]
    row_masks(seq_ref, lax.axis_index("blk") * (2 * BLK) + part * BLK, m1_ref, m2_ref)
    for c in range(0, width, GROUP):
        lanes = slice(c, c + GROUP)
        w = w_ref[0, :, lanes]
        x = raw_ref[:, lanes].astype(jnp.float32)
        slot = (c // GROUP) % 2
        x_ref[slot, 6:8, :] = tail(lanes)
        x_ref[slot, 8:, :] = x
        q_ref[:, lanes] = feature(x, x_ref.at[slot], w, m1_ref, m2_ref)


def near_kernel(
    seq_ref, marks_ref, table_ref, own_ref, back_own_ref, pair_a_ref, pair_b_ref, back_a_ref, back_b_ref, qkept_ref, w_ref, bias_ref,
    acc_ref, q_ref, win_ref, extra_ref, x_ref, m1_ref, m2_ref,
):
    groups = table_ref.shape[0]
    width = groups * GROUP
    half = lax.axis_index("half")
    fill(win_ref, extra_ref, half, back_own_ref)
    fill(win_ref, extra_ref, 1 - half, back_a_ref, back_b_ref)
    fill(win_ref, extra_ref, 2 + half, own_ref)
    fill(win_ref, extra_ref, 3 - half, pair_a_ref, pair_b_ref)
    marks = [marks_ref[0], marks_ref[1]]
    for spot in (1, 2, 3):
        rows = first_rows(extra_ref[spot], extra_ref[spot - 1, :8], w_ref, marks, spot + 2)
        put_first_rows(win_ref, spot * BLK, rows)
    for g in range(groups):
        lanes = slice(g * GROUP, (g + 1) * GROUP)
        bias = bias_ref[:, pl.ds(pl.multiple_of(half * width + g * GROUP, GROUP), GROUP)]
        for part in range(2):
            total = jnp.dot(
                table_ref[g, part, :, 3 * BLK : (5 + part) * BLK],
                win_ref[BLK : (3 + part) * BLK, lanes],
                preferred_element_type=jnp.float32,
            )
            here = win_ref[(2 + part) * BLK : (3 + part) * BLK, lanes].astype(jnp.float32)
            acc_ref[part * BLK : (part + 1) * BLK, lanes] = total + bias * here
    gate_rows(
        seq_ref, qkept_ref, lambda lanes: extra_ref[1 + half, 6:8, lanes], w_ref, half, q_ref, x_ref, m1_ref, m2_ref
    )


def pair_gate_kernel(seq_ref, raw_ref, own_ref, back_own_ref, w_ref, q_ref, x_ref, m1_ref, m2_ref):
    half = lax.axis_index("half")

    def tail(lanes):
        back = back_own_ref[BLK:, lanes].astype(jnp.float32)
        own = own_ref[BLK:, lanes].astype(jnp.float32)
        return jnp.where(half == 1, back, own)[6:8]

    gate_rows(seq_ref, raw_ref, tail, w_ref, 1 - half, q_ref, x_ref, m1_ref, m2_ref)


def far_kernel(
    short, piece, table_ref, acc_ref, qown_ref, qpair_ref, w_ref, marks_ref, back_own_ref, back_pair_ref, *refs
):
    *refs, kept_ref, sent_ref, total_ref, win_ref, extra_ref = refs
    far_refs, before = refs[: len(refs) - 2 * piece], refs[len(refs) - 2 * piece :]
    width = kept_ref.shape[1]
    half = lax.axis_index("half")
    lanes = slice(piece * width, (piece + 1) * width)
    marks = [marks_ref[0], marks_ref[1]]
    low = 1 if short else 0

    @pl.when(half == 0)
    def _():
        fill(win_ref, extra_ref, 2, back_own_ref.at[:, lanes])

    @pl.when(half == 1)
    def _():
        fill(win_ref, extra_ref, 2, back_pair_ref)

    if short:
        summed = marks_ref[2, 0:1, 0:1]
        fill(win_ref, extra_ref, 1, far_refs[0])
        payload = win_ref[BLK : 2 * BLK, :].astype(jnp.float32)
        win_ref[BLK : 2 * BLK, :] = (payload * (1.0 - summed)).astype(win_ref.dtype)
    else:
        fill(win_ref, extra_ref, half, far_refs[0].at[:, lanes])
        fill(win_ref, extra_ref, 1 - half, far_refs[1 + piece])
        ahead = far_refs[3][:, lanes].astype(jnp.float32)
        put_first_rows(win_ref, 0, first_rows(extra_ref[0], ahead, w_ref, marks, 0, lanes))
        put_first_rows(win_ref, BLK, first_rows(extra_ref[1], extra_ref[0, :8], w_ref, marks, 1, lanes))
    put_first_rows(win_ref, 2 * BLK, first_rows(extra_ref[2], extra_ref[1, :8], w_ref, marks, 2, lanes))
    if before:
        sent_ref[:, :width] = before[1][...]
    for i, (part, q_ref, out_ref) in enumerate(((half, qown_ref, kept_ref), (1 - half, qpair_ref, sent_ref))):
        part_sent = i == 1
        squares = before[0][i] if before else jnp.zeros((BLK, GROUP), jnp.float32)
        rows = pl.ds(pl.multiple_of(part * BLK, BLK), BLK)
        for c in range(0, width, GROUP):
            here = slice(c, c + GROUP)
            whole = slice(piece * width + c, piece * width + c + GROUP)
            filtered = acc_ref[rows, whole] + jnp.dot(
                table_ref[(piece * width + c) // GROUP, part, :, low * BLK : 3 * BLK],
                win_ref[low * BLK : 3 * BLK, here],
                preferred_element_type=jnp.float32,
            )
            if short:
                weight = summed * (part == 0).astype(jnp.float32)
                filtered = filtered + weight * far_refs[0][:BLK, here].astype(jnp.float32)
            gated = q_ref[:, whole] * filtered
            squares = squares + gated * gated
            out_ref[:, whole if before and part_sent else here] = gated.astype(out_ref.dtype)
        if before:
            place = lax.broadcasted_iota(jnp.int32, (BLK, BLK), 0) - lax.broadcasted_iota(jnp.int32, (BLK, BLK), 1)
            column = jnp.sum(squares, axis=1, keepdims=True)
            total_ref[:, i * BLK : (i + 1) * BLK] = jnp.sum(
                jnp.where(place == 0, column, 0.0), axis=0, keepdims=True
            )
        else:
            total_ref[i] = squares


def norm_kernel(channels, power_ref, power_got_ref, *refs):
    *kept_refs, got_ref, gain_ref, out_hbm, out_ref, sems = refs
    half = lax.axis_index("half")
    power = power_ref[:, :BLK] + power_got_ref[:, BLK:]
    scale = lax.rsqrt(power / channels + norm_eps)
    diagonal = lax.broadcasted_iota(jnp.int32, (BLK, BLK), 0) == lax.broadcasted_iota(
        jnp.int32, (BLK, BLK), 1
    )
    column = jnp.sum(jnp.where(diagonal, scale, 0.0), axis=1, keepdims=True)
    piece = kept_refs[0].shape[1]
    stores = []
    for at, refs in ((half, kept_refs), (1 - half, [got_ref])):
        at = at * got_ref.shape[1]
        for ref in refs:
            for c in range(0, ref.shape[1], GROUP):
                lanes = pl.ds(pl.multiple_of(at + c, GROUP), GROUP)
                part = ref[:, c : c + GROUP].astype(jnp.float32)
                out_ref[:, lanes] = (part * column * gain_ref[:, lanes]).astype(out_ref.dtype)
                if (c + GROUP) % piece == 0:
                    ready = pl.ds(pl.multiple_of(at + c + GROUP - piece, piece), piece)
                    stores.append(
                        pltpu.make_async_copy(out_ref.at[:, ready], out_hbm.at[:, ready], sems.at[len(stores)])
                    )
                    stores[-1].start()
            at = at + ref.shape[1]
    for store in stores:
        store.wait()


def kernel_call(body, outs, in_specs, scratch, flops, moved_bytes, out_space=VMEM):
    return pl.pallas_call(
        body,
        out_shape=outs,
        in_specs=in_specs,
        out_specs=jax.tree.map(lambda _: out_space, outs),
        scratch_shapes=scratch,
        compiler_params=pltpu.CompilerParams(vmem_limit_bytes=24 << 20),
        cost_estimate=pl.CostEstimate(flops=flops, bytes_accessed=moved_bytes, transcendentals=0),
    )


def matching(blocks, first):
    pairs = []
    for i in range(2 * blocks):
        block = i // 2
        partner = block + 1 if (block - first) % 2 == 0 else block - 1
        pairs.append((i, 2 * partner + i % 2 if 0 <= partner < blocks else i))
    return pairs


def shards(blocks, whole_tokens, channels, projected, short_weight, filter_taps, tap_blocks, skip_bias, norm_gain, seq_lengths):
    rows = projected.shape[0]
    width = projected.shape[2] // 2
    groups = width // GROUP
    taps = filter_taps.shape[1]
    shape = jax.ShapeDtypeStruct
    half_shape = shape((rows, width), jnp.bfloat16)
    half_wide = shape((rows, width), jnp.float32)

    spots = range(2 * blocks)
    to_pair = [(i, i ^ 1) for i in spots]
    ahead = [(i, (i + 2) % (2 * blocks)) for i in spots]

    panels = jnp.transpose(projected, (1, 0, 2))
    message = shape((rows + 8, width), jnp.bfloat16)
    small = shape((rows + 8, width // 2), jnp.bfloat16)
    hbm = pl.BlockSpec(memory_space=pltpu.HBM)
    pieces = 4
    lengths = seq_lengths.reshape(1, -1)
    row_mask = pltpu.VMEM((rows, GROUP), jnp.float32)

    kept, *sent = kernel_call(
        products_kernel,
        (message, small, small),
        [hbm] * 3,
        [
            pltpu.VMEM(lengths.shape, jnp.int32),
            pltpu.VMEM((pieces, 2, rows, 2 * width // pieces), jnp.bfloat16),
            pltpu.VMEM((16, 2 * width), jnp.bfloat16),
            pltpu.VMEM(short_weight.shape, jnp.float32),
            pltpu.VMEM((4, rows + 8, GROUP), jnp.float32),
            row_mask,
            row_mask,
            pltpu.SemaphoreType.DMA((3 + pieces,)),
        ],
        40 * rows * width,
        16 * rows * width,
    )(*[pltpu.with_memory_space_constraint(a, pltpu.HBM) for a in (lengths, panels, short_weight)])

    back_own = moved(kept, ahead)
    pair = [moved(piece, to_pair) for piece in sent]

    filter_taps, _ = lax.optimization_barrier((filter_taps, kept))
    scaled = (filter_taps * jnp.repeat(tap_blocks.astype(jnp.float32), BLK, axis=1)).astype(jnp.bfloat16)
    span = taps + 2 * BLK
    table, table_next, w_half, marks = kernel_call(
        tables_kernel,
        (
            shape((groups, 2, BLK, span), jnp.bfloat16),
            shape((groups, BLK, 2 * BLK), jnp.bfloat16),
            shape((3, 3, width), jnp.float32),
            shape((4, 8, GROUP), jnp.float32),
        ),
        [SMEM, VMEM, VMEM],
        [pltpu.VMEM((2 * groups, span), jnp.float32), pltpu.VMEM((3, BLK, span), jnp.float32)],
        40 * groups * BLK * taps,
        8 * groups * BLK * taps,
    )(seq_lengths, scaled, short_weight)
    table, table_next, pair[0] = lax.optimization_barrier((table, table_next, pair[0]))

    half = lax.axis_index("half")
    query, _ = lax.optimization_barrier((panels, pair[0]))
    qkept = lax.dynamic_slice(query, (0, 0, half * width), (1, rows, width))[0]
    qsent = lax.dynamic_slice(query, (0, 0, (1 - half) * width), (1, rows, width))[0]
    qkept, qsent, pair[1] = lax.optimization_barrier((qkept, qsent, pair[1]))
    qgot = moved(qsent, to_pair)
    by_odd = moved(pair[1], matching(blocks, 0))
    back_pair = [[moved(pair[0], ahead)], [by_odd, moved(pair[1], matching(blocks, 1))]]

    window = pltpu.VMEM((4 * rows, width), jnp.bfloat16)
    extras = pltpu.VMEM((4, 16, width), jnp.float32)
    shifted = pltpu.VMEM((2, rows + 8, GROUP), jnp.float32)
    short = whole_tokens // 2 <= 4 * BLK
    if short:
        onward = [(i, i if i < 2 else i + 2 if i + 2 < 2 * blocks else 2 + i % 2) for i in spots]
        far = []
        for piece in range(2):
            relayed, back_pair[piece] = kernel_call(
                functools.partial(relay_kernel, piece),
                (small, small),
                [VMEM] * (4 + len(back_pair[piece])),
                [pltpu.VMEM((2 * rows, width // 2), jnp.bfloat16), pltpu.VMEM((2, 16, width // 2), jnp.float32)],
                2 * rows * BLK * width,
                4 * rows * width,
            )(marks, table_next, back_own, w_half, *back_pair[piece])
            far.append(moved(relayed, onward))
    else:
        back_pair = [moved(piece, ahead) for piece in pair]
        across = jnp.concatenate([piece[rows:] for piece in sent], 1)
        across = moved(across, [(i, ((i ^ 1) + 6) % (2 * blocks)) for i in spots])
        straight = moved(kept[rows:], [(i, (i + 6) % (2 * blocks)) for i in spots])
        deep = jnp.where(half == 1, straight, across)
        far = [moved(piece, ahead) for piece in (back_own, *back_pair)] + [deep]

    acc, qown = kernel_call(
        near_kernel,
        (shape((2 * rows, width), jnp.float32), half_wide),
        [VMEM] * 12,
        [window, extras, shifted, row_mask, row_mask],
        2 * 5 * rows * BLK * width,
        16 * rows * width,
    )(lengths, marks, table, kept, back_own, *pair, *back_pair, qkept, w_half, skip_bias.reshape(1, -1))

    qpair = kernel_call(
        pair_gate_kernel,
        half_wide,
        [VMEM] * 5,
        [shifted, row_mask, row_mask],
        10 * rows * width,
        8 * rows * width,
    )(lengths, qgot, kept, back_own, w_half)

    done, power, send = [], None, None
    for piece in range(2):
        needed = far[piece : piece + 1] if short else far
        before = [power, send] if piece else []
        own, send, power = kernel_call(
            functools.partial(far_kernel, short, piece),
            (
                shape((rows, width // 2), jnp.float32),
                shape((rows, width if piece else width // 2), jnp.bfloat16),
                shape((1, 2 * rows) if piece else (2, rows, GROUP), jnp.float32),
            ),
            [VMEM] * (8 + len(needed) + len(before)),
            [pltpu.VMEM((3 * rows, width // 2), jnp.bfloat16), pltpu.VMEM((3, 16, width // 2), jnp.float32)],
            2 * 3 * rows * BLK * width,
            12 * rows * width,
        )(table, acc, qown, qpair, w_half, marks, back_own, back_pair[piece], *needed, *before)
        done.append(own)
    back = moved(send, to_pair)

    peers = lax.axis_size("mp")
    shares = [lax.ppermute(power, "mp", [(i, i ^ k) for i in range(peers)]) for k in range(1, peers)]
    power = sum(shares, power)
    return kernel_call(
        functools.partial(norm_kernel, channels),
        shape((rows, 2 * width), jnp.bfloat16),
        [VMEM] * 6,
        [pltpu.VMEM((rows, 2 * width), jnp.bfloat16), pltpu.SemaphoreType.DMA((4,))],
        8 * rows * width,
        10 * rows * width,
        hbm,
    )(power, moved(power, to_pair), *done, back, norm_gain.reshape(1, -1))


def solution(mesh):
    blocks = mesh.shape["ctx"] // 2
    grid = Mesh(mesh.devices.reshape(blocks, 2, mesh.shape["mp"]), ("blk", "half", "mp"))
    in_specs = (
        P(SPOTS, None, "mp"),
        P(None, None, "mp"),
        P("mp", None),
        P("mp", None),
        P("mp"),
        P("mp"),
        P(),
    )

    def program(projected, *rest):
        body = functools.partial(shards, blocks, projected.shape[0], projected.shape[2])
        return jax.shard_map(
            body, mesh=grid, in_specs=in_specs, out_specs=P(SPOTS, "mp"), check_vma=False
        )(projected, *rest)

    return program
```

```python
import functools

import jax
import jax.numpy as jnp
from jax import lax
from jax.experimental import pallas as pl
from jax.experimental.pallas import tpu as pltpu
from jax.sharding import Mesh, PartitionSpec as P

GROUP = 128
BLK = 128
norm_eps = 1e-06

VMEM = pl.BlockSpec(memory_space=pltpu.VMEM)
SMEM = pl.BlockSpec(memory_space=pltpu.SMEM)
SPOTS = ("blk", "half")


def moved(block, pairs):
    peers = lax.axis_size("mp")
    whole = [(i * peers + m, j * peers + (m if i != j else m ^ 1)) for i, j in pairs for m in range(peers)]
    return lax.ppermute(block, SPOTS + ("mp",), whole)


def boundaries(seq_ref, t):
    def step(k, carry):
        end, first, second = carry
        end = end + seq_ref[k]
        return end, first | (t == end).astype(jnp.int32), second | (t - 1 == end).astype(jnp.int32)

    first = (t == 0).astype(jnp.int32)
    second = (t == 1).astype(jnp.int32)
    _, first, second = lax.fori_loop(0, seq_ref.shape[0], step, (jnp.int32(0), first, second), unroll=True)
    return first, first | second


def row_masks(lengths_ref, start, m1_ref, m2_ref):
    count = lengths_ref.shape[1]
    square = (count, count)
    upto = lax.broadcasted_iota(jnp.int32, square, 1) <= lax.broadcasted_iota(jnp.int32, square, 0)
    lengths = jnp.broadcast_to(lengths_ref[...].astype(jnp.float32), square)
    ends = jnp.sum(jnp.where(upto, lengths, 0.0), axis=1, keepdims=True)
    t = (start + lax.broadcasted_iota(jnp.int32, (count, BLK), 1)).astype(jnp.float32)
    opens = (t == ends) | (t == 0.0)
    after = opens | (t - 1.0 == ends) | (t == 1.0)
    diagonal = lax.broadcasted_iota(jnp.int32, (BLK, BLK), 0) == lax.broadcasted_iota(jnp.int32, (BLK, BLK), 1)
    for mark, m_ref in ((opens, m1_ref), (after, m2_ref)):
        keep = 1.0 - jnp.max(mark.astype(jnp.float32), axis=0, keepdims=True)
        column = jnp.sum(jnp.where(diagonal, keep, 0.0), axis=1, keepdims=True)
        m_ref[...] = jnp.broadcast_to(column, m_ref.shape)


def counted(seq_ref, t):
    def step(k, carry):
        end, total = carry
        end = end + seq_ref[k]
        return end, total + (end <= t).astype(jnp.int32)

    _, total = lax.fori_loop(
        0, seq_ref.shape[0], step, (jnp.int32(0), jnp.zeros(t.shape, jnp.int32)), unroll=True
    )
    return jnp.where(t >= 0, total, -1)


def feature(x, x_ref, w, m1_ref, m2_ref):
    rows = x.shape[0]
    return (
        w[0:1] * x
        + w[1:2] * x_ref[7 : rows + 7, :] * m1_ref[...]
        + w[2:3] * x_ref[6 : rows + 6, :] * m2_ref[...]
    )


def products_kernel(seq_hbm, panels_hbm, w_hbm, *refs):
    (kept_ref, *sent_refs), refs = refs[:3], refs[3:]
    seq_ref, kv_ref, q_ref, w_ref, x_ref, m1_ref, m2_ref, sems = refs
    width = kept_ref.shape[1]
    rows = kv_ref.shape[2]
    pieces = kv_ref.shape[0]
    piece = kv_ref.shape[3]
    half = lax.axis_index("half")
    shard = lax.axis_index("blk") * 2 + half
    keep_at = pl.multiple_of(half * width, width)
    send_at = pl.multiple_of((1 - half) * width, width)

    loads = [pltpu.make_async_copy(seq_hbm, seq_ref, sems.at[0])]
    for p in range(pieces):
        at = keep_at if p < pieces // 2 else send_at
        lanes = pl.ds(pl.multiple_of(at + (p % (pieces // 2)) * piece, piece), piece)
        loads.append(pltpu.make_async_copy(panels_hbm.at[1:3, :, lanes], kv_ref.at[p], sems.at[1 + p]))
    loads.append(pltpu.make_async_copy(w_hbm, w_ref, sems.at[1 + pieces]))
    loads.append(pltpu.make_async_copy(panels_hbm.at[0, rows - 16 :, :], q_ref, sems.at[2 + pieces]))
    for load in loads:
        load.start()
    x_ref[:, 0:8, :] = jnp.zeros((x_ref.shape[0], 8, GROUP), jnp.float32)
    loads[0].wait()
    row_masks(seq_ref, shard * rows, m1_ref, m2_ref)
    loads[1 + pieces].wait()
    loads[2 + pieces].wait()
    for p in range(pieces):
        loads[1 + p].wait()
        out_ref, at = (kept_ref, keep_at) if p < pieces // 2 else (sent_refs[p - pieces // 2], send_at)
        for c in range(0, piece, GROUP):
            base = (p % (pieces // 2)) * piece + c
            there = slice(base, base + GROUP) if p < pieces // 2 else slice(c, c + GROUP)
            lanes = pl.ds(pl.multiple_of(at + base, GROUP), GROUP)
            slot = (c // GROUP) % (x_ref.shape[0] // 2) * 2
            raw, made = [], []
            for i in range(2):
                x = kv_ref[p, i, :, c : c + GROUP].astype(jnp.float32)
                x_ref[slot + i, 8:, :] = x
                made.append(feature(x, x_ref.at[slot + i], w_ref[1 + i, :, lanes], m1_ref, m2_ref))
                raw.append(x)
            product = made[0] * made[1]
            top = jnp.where(lax.broadcasted_iota(jnp.int32, (8, GROUP), 0) < 2, raw[0][:8], product[:8])
            out_ref[:rows, there] = jnp.concatenate([top, product[8:]], 0).astype(out_ref.dtype)
            tails = [x[rows - 2 :] for x in raw] + [q_ref[:, lanes].astype(jnp.float32)[14:]]
            out_ref[rows:, there] = jnp.concatenate([raw[1][0:2]] + tails, 0).astype(out_ref.dtype)


def edge_marks(seq_ref):
    t = (
        (lax.axis_index("blk") - 2) * (2 * BLK)
        + lax.broadcasted_iota(jnp.int32, (8, GROUP), 1) * BLK
        + lax.broadcasted_iota(jnp.int32, (8, GROUP), 0)
    )
    return [1.0 - mark.astype(jnp.float32) for mark in boundaries(seq_ref, t)]


def first_rows(now, ahead, w_ref, marks, spot, lanes=slice(None)):
    m1, m2 = [mark[:, spot : spot + 1] for mark in marks]
    top = lax.broadcasted_iota(jnp.int32, ahead.shape, 0) == 0
    made = []
    for i, x0 in enumerate((now[8:], now[:8])):
        x1 = jnp.where(top, pltpu.roll(ahead, 5 - 2 * i, 0), pltpu.roll(x0, 1, 0))
        x2 = pltpu.roll(ahead, 6 - 2 * i, 0)
        w = w_ref[1 + i, :, lanes]
        made.append(w[0:1] * x0 + w[1:2] * x1 * m1 + w[2:3] * x2 * m2)
    return made[0] * made[1]


def put_first_rows(win_ref, at, rows):
    old = win_ref[at : at + 16, :].astype(jnp.float32)
    new = jnp.concatenate([rows, rows], 0)
    first = lax.broadcasted_iota(jnp.int32, old.shape, 0) < 2
    win_ref[at : at + 16, :] = jnp.where(first, new, old).astype(win_ref.dtype)


def reaches_past(seq_ref, block):
    first = block * (2 * BLK)

    def step(k, carry):
        end, start = carry
        end = end + seq_ref[k]
        return end, jnp.where(end <= first, end, start)

    _, start = lax.fori_loop(0, seq_ref.shape[0], step, (jnp.int32(0), jnp.int32(0)), unroll=True)
    return first - 2 * BLK - start > BLK


def tables_kernel(seq_ref, taps_ref, w_ref, out_ref, next_ref, w_half_ref, marks_ref, rev_ref, m_ref):
    groups = out_ref.shape[0]
    taps = taps_ref.shape[1]
    span = out_ref.shape[3]
    half = lax.axis_index("half")
    start = lax.axis_index("blk") * (2 * BLK)
    marks_ref[0], marks_ref[1] = edge_marks(seq_ref)
    for ahead in range(2):
        flag = reaches_past(seq_ref, lax.axis_index("blk") + ahead)
        marks_ref[2 + ahead] = jnp.full((8, GROUP), flag.astype(jnp.float32))
    width = w_half_ref.shape[2]
    w_half_ref[...] = w_ref[:, :, pl.ds(pl.multiple_of(half * width, width), width)]
    turn = lax.broadcasted_iota(jnp.int32, (taps, span), 0) + lax.broadcasted_iota(
        jnp.int32, (taps, span), 1
    )
    turn = (turn == taps).astype(jnp.bfloat16)
    rev_ref[...] = jnp.dot(taps_ref[...], turn, preferred_element_type=jnp.float32)
    seg_in = counted(seq_ref, start - taps + lax.broadcasted_iota(jnp.int32, (8, span), 1))[0:1]
    for part in range(3):
        t_out = start + part * BLK + lax.broadcasted_iota(jnp.int32, (BLK, GROUP), 0)
        seg_out = counted(seq_ref, t_out)[:, 0:1]
        if part < 2:
            m_ref[part] = (seg_in == seg_out).astype(jnp.float32)
        else:
            m_ref[2, :, : 2 * BLK] = (seg_in[:, 2 * BLK : 4 * BLK] == seg_out).astype(jnp.float32)

    def one(g, _):
        row = rev_ref[pl.ds(half * groups + g, 1), :]
        table = pltpu.roll(jnp.broadcast_to(row, (BLK, span)), 0, 1, stride=1, stride_axis=0)
        out_ref[g, 0] = (table * m_ref[0]).astype(out_ref.dtype)
        later = jnp.concatenate([table[:, span - BLK :], table[:, : span - BLK]], 1)
        out_ref[g, 1] = (later * m_ref[1]).astype(out_ref.dtype)
        next_ref[g] = (table[:, : 2 * BLK] * m_ref[2, :, : 2 * BLK]).astype(next_ref.dtype)
        return 0

    lax.fori_loop(0, groups, one, 0)


def fill(win_ref, extra_ref, spot, *pieces):
    at = 0
    for piece in pieces:
        lanes = slice(at, at + piece.shape[1])
        win_ref[pl.ds(pl.multiple_of(spot * BLK, BLK), BLK), lanes] = piece[:BLK]
        extra_ref[spot, :8, lanes] = piece[BLK:].astype(jnp.float32)
        extra_ref[spot, 8:, lanes] = piece[:16].astype(jnp.float32)[:8]
        at += piece.shape[1]


def relay_kernel(piece, marks_ref, next_ref, back_own_ref, w_ref, *refs):
    *ways, out_ref, back_pair_ref, win_ref, extra_ref = refs
    for i, way in enumerate(ways):
        @pl.when((lax.axis_index("blk") + i) % len(ways) == 0)
        def _():
            back_pair_ref[...] = way[...]

    width = out_ref.shape[1]
    half = lax.axis_index("half")
    lanes = slice(piece * width, (piece + 1) * width)
    fill(win_ref, extra_ref, half, back_own_ref.at[:, lanes])
    fill(win_ref, extra_ref, 1 - half, back_pair_ref)
    marks = [marks_ref[0], marks_ref[1]]
    put_first_rows(win_ref, 0, first_rows(extra_ref[0], jnp.zeros((8, width), jnp.float32), w_ref, marks, 2, lanes))
    put_first_rows(win_ref, BLK, first_rows(extra_ref[1], extra_ref[0, :8], w_ref, marks, 3, lanes))
    out_ref[BLK:] = extra_ref[1, :8].astype(out_ref.dtype)
    summed = jnp.max(marks_ref[3]) > 0.5

    @pl.when(summed)
    def _():
        for c in range(0, width, GROUP):
            total = jnp.dot(
                next_ref[(piece * width + c) // GROUP],
                win_ref[:, c : c + GROUP],
                preferred_element_type=jnp.float32,
            )
            out_ref[:BLK, c : c + GROUP] = total.astype(out_ref.dtype)

    @pl.when(jnp.logical_not(summed))
    def _():
        out_ref[:BLK] = win_ref[BLK:]


def gate_rows(seq_ref, raw_ref, tail, w_ref, part, q_ref, x_ref, m1_ref, m2_ref):
    width = raw_ref.shape[1]
    row_masks(seq_ref, lax.axis_index("blk") * (2 * BLK) + part * BLK, m1_ref, m2_ref)
    for c in range(0, width, GROUP):
        lanes = slice(c, c + GROUP)
        w = w_ref[0, :, lanes]
        x = raw_ref[:, lanes].astype(jnp.float32)
        slot = (c // GROUP) % 2
        x_ref[slot, 6:8, :] = tail(lanes)
        x_ref[slot, 8:, :] = x
        q_ref[:, lanes] = feature(x, x_ref.at[slot], w, m1_ref, m2_ref)


def near_kernel(
    seq_ref, marks_ref, table_ref, own_ref, back_own_ref, pair_a_ref, pair_b_ref, back_a_ref, back_b_ref, qkept_ref, w_ref, bias_ref,
    acc_ref, q_ref, win_ref, extra_ref, x_ref, m1_ref, m2_ref,
):
    groups = table_ref.shape[0]
    width = groups * GROUP
    half = lax.axis_index("half")
    fill(win_ref, extra_ref, half, back_own_ref)
    fill(win_ref, extra_ref, 1 - half, back_a_ref, back_b_ref)
    fill(win_ref, extra_ref, 2 + half, own_ref)
    fill(win_ref, extra_ref, 3 - half, pair_a_ref, pair_b_ref)
    marks = [marks_ref[0], marks_ref[1]]
    for spot in (1, 2, 3):
        rows = first_rows(extra_ref[spot], extra_ref[spot - 1, :8], w_ref, marks, spot + 2)
        put_first_rows(win_ref, spot * BLK, rows)
    for g in range(groups):
        lanes = slice(g * GROUP, (g + 1) * GROUP)
        bias = bias_ref[:, pl.ds(pl.multiple_of(half * width + g * GROUP, GROUP), GROUP)]
        for part in range(2):
            total = jnp.dot(
                table_ref[g, part, :, 3 * BLK : (5 + part) * BLK],
                win_ref[BLK : (3 + part) * BLK, lanes],
                preferred_element_type=jnp.float32,
            )
            here = win_ref[(2 + part) * BLK : (3 + part) * BLK, lanes].astype(jnp.float32)
            acc_ref[part * BLK : (part + 1) * BLK, lanes] = total + bias * here
    gate_rows(
        seq_ref, qkept_ref, lambda lanes: extra_ref[1 + half, 6:8, lanes], w_ref, half, q_ref, x_ref, m1_ref, m2_ref
    )


def pair_gate_kernel(seq_ref, raw_ref, own_ref, back_own_ref, w_ref, q_ref, x_ref, m1_ref, m2_ref):
    half = lax.axis_index("half")

    def tail(lanes):
        back = back_own_ref[BLK:, lanes].astype(jnp.float32)
        own = own_ref[BLK:, lanes].astype(jnp.float32)
        return jnp.where(half == 1, back, own)[6:8]

    gate_rows(seq_ref, raw_ref, tail, w_ref, 1 - half, q_ref, x_ref, m1_ref, m2_ref)


def far_kernel(
    short, piece, table_ref, acc_ref, qown_ref, qpair_ref, w_ref, marks_ref, back_own_ref, back_pair_ref, *refs
):
    *refs, kept_ref, sent_ref, total_ref, win_ref, extra_ref = refs
    far_refs, before = refs[: len(refs) - 2 * piece], refs[len(refs) - 2 * piece :]
    width = kept_ref.shape[1]
    half = lax.axis_index("half")
    lanes = slice(piece * width, (piece + 1) * width)
    marks = [marks_ref[0], marks_ref[1]]
    low = 1 if short else 0

    @pl.when(half == 0)
    def _():
        fill(win_ref, extra_ref, 2, back_own_ref.at[:, lanes])

    @pl.when(half == 1)
    def _():
        fill(win_ref, extra_ref, 2, back_pair_ref)

    if short:
        summed = marks_ref[2, 0:1, 0:1]
        fill(win_ref, extra_ref, 1, far_refs[0])
        payload = win_ref[BLK : 2 * BLK, :].astype(jnp.float32)
        win_ref[BLK : 2 * BLK, :] = (payload * (1.0 - summed)).astype(win_ref.dtype)
    else:
        fill(win_ref, extra_ref, half, far_refs[0].at[:, lanes])
        fill(win_ref, extra_ref, 1 - half, far_refs[1 + piece])
        ahead = far_refs[3][:, lanes].astype(jnp.float32)
        put_first_rows(win_ref, 0, first_rows(extra_ref[0], ahead, w_ref, marks, 0, lanes))
        put_first_rows(win_ref, BLK, first_rows(extra_ref[1], extra_ref[0, :8], w_ref, marks, 1, lanes))
    put_first_rows(win_ref, 2 * BLK, first_rows(extra_ref[2], extra_ref[1, :8], w_ref, marks, 2, lanes))
    if before:
        sent_ref[:, :width] = before[1][...]
    for i, (part, q_ref, out_ref) in enumerate(((half, qown_ref, kept_ref), (1 - half, qpair_ref, sent_ref))):
        part_sent = i == 1
        squares = before[0][i] if before else jnp.zeros((BLK, GROUP), jnp.float32)
        rows = pl.ds(pl.multiple_of(part * BLK, BLK), BLK)
        for c in range(0, width, GROUP):
            here = slice(c, c + GROUP)
            whole = slice(piece * width + c, piece * width + c + GROUP)
            filtered = acc_ref[rows, whole] + jnp.dot(
                table_ref[(piece * width + c) // GROUP, part, :, low * BLK : 3 * BLK],
                win_ref[low * BLK : 3 * BLK, here],
                preferred_element_type=jnp.float32,
            )
            if short:
                weight = summed * (part == 0).astype(jnp.float32)
                filtered = filtered + weight * far_refs[0][:BLK, here].astype(jnp.float32)
            gated = q_ref[:, whole] * filtered
            squares = squares + gated * gated
            out_ref[:, whole if before and part_sent else here] = gated.astype(out_ref.dtype)
        if before:
            place = lax.broadcasted_iota(jnp.int32, (BLK, BLK), 0) - lax.broadcasted_iota(jnp.int32, (BLK, BLK), 1)
            column = jnp.sum(squares, axis=1, keepdims=True)
            total_ref[:, i * BLK : (i + 1) * BLK] = jnp.sum(
                jnp.where(place == 0, column, 0.0), axis=0, keepdims=True
            )
        else:
            total_ref[i] = squares


def norm_kernel(channels, power_ref, power_got_ref, *refs):
    *kept_refs, got_ref, gain_ref, out_hbm, out_ref, sems = refs
    half = lax.axis_index("half")
    power = power_ref[:, :BLK] + power_got_ref[:, BLK:]
    scale = lax.rsqrt(power / channels + norm_eps)
    diagonal = lax.broadcasted_iota(jnp.int32, (BLK, BLK), 0) == lax.broadcasted_iota(
        jnp.int32, (BLK, BLK), 1
    )
    column = jnp.sum(jnp.where(diagonal, scale, 0.0), axis=1, keepdims=True)
    piece = kept_refs[0].shape[1]
    stores = []
    for at, refs in ((half, kept_refs), (1 - half, [got_ref])):
        at = at * got_ref.shape[1]
        for ref in refs:
            for c in range(0, ref.shape[1], GROUP):
                lanes = pl.ds(pl.multiple_of(at + c, GROUP), GROUP)
                part = ref[:, c : c + GROUP].astype(jnp.float32)
                out_ref[:, lanes] = (part * column * gain_ref[:, lanes]).astype(out_ref.dtype)
                if (c + GROUP) % piece == 0:
                    ready = pl.ds(pl.multiple_of(at + c + GROUP - piece, piece), piece)
                    stores.append(
                        pltpu.make_async_copy(out_ref.at[:, ready], out_hbm.at[:, ready], sems.at[len(stores)])
                    )
                    stores[-1].start()
            at = at + ref.shape[1]
    for store in stores:
        store.wait()


def kernel_call(body, outs, in_specs, scratch, flops, moved_bytes, out_space=VMEM):
    return pl.pallas_call(
        body,
        out_shape=outs,
        in_specs=in_specs,
        out_specs=jax.tree.map(lambda _: out_space, outs),
        scratch_shapes=scratch,
        compiler_params=pltpu.CompilerParams(vmem_limit_bytes=24 << 20),
        cost_estimate=pl.CostEstimate(flops=flops, bytes_accessed=moved_bytes, transcendentals=0),
    )


def matching(blocks, first):
    pairs = []
    for i in range(2 * blocks):
        block = i // 2
        partner = block + 1 if (block - first) % 2 == 0 else block - 1
        pairs.append((i, 2 * partner + i % 2 if 0 <= partner < blocks else i))
    return pairs


def shards(blocks, whole_tokens, channels, projected, short_weight, filter_taps, tap_blocks, skip_bias, norm_gain, seq_lengths):
    rows = projected.shape[0]
    width = projected.shape[2] // 2
    groups = width // GROUP
    taps = filter_taps.shape[1]
    shape = jax.ShapeDtypeStruct
    half_shape = shape((rows, width), jnp.bfloat16)
    half_wide = shape((rows, width), jnp.float32)

    spots = range(2 * blocks)
    to_pair = [(i, i ^ 1) for i in spots]
    ahead = [(i, (i + 2) % (2 * blocks)) for i in spots]

    panels = jnp.transpose(projected, (1, 0, 2))
    message = shape((rows + 8, width), jnp.bfloat16)
    small = shape((rows + 8, width // 2), jnp.bfloat16)
    hbm = pl.BlockSpec(memory_space=pltpu.HBM)
    pieces = 4
    lengths = seq_lengths.reshape(1, -1)
    row_mask = pltpu.VMEM((rows, GROUP), jnp.float32)

    kept, *sent = kernel_call(
        products_kernel,
        (message, small, small),
        [hbm] * 3,
        [
            pltpu.VMEM(lengths.shape, jnp.int32),
            pltpu.VMEM((pieces, 2, rows, 2 * width // pieces), jnp.bfloat16),
            pltpu.VMEM((16, 2 * width), jnp.bfloat16),
            pltpu.VMEM(short_weight.shape, jnp.float32),
            pltpu.VMEM((4, rows + 8, GROUP), jnp.float32),
            row_mask,
            row_mask,
            pltpu.SemaphoreType.DMA((3 + pieces,)),
        ],
        40 * rows * width,
        16 * rows * width,
    )(*[pltpu.with_memory_space_constraint(a, pltpu.HBM) for a in (lengths, panels, short_weight)])

    back_own = moved(kept, ahead)
    pair = [moved(piece, to_pair) for piece in sent]

    filter_taps, _ = lax.optimization_barrier((filter_taps, kept))
    scaled = (filter_taps * jnp.repeat(tap_blocks.astype(jnp.float32), BLK, axis=1)).astype(jnp.bfloat16)
    span = taps + 2 * BLK
    table, table_next, w_half, marks = kernel_call(
        tables_kernel,
        (
            shape((groups, 2, BLK, span), jnp.bfloat16),
            shape((groups, BLK, 2 * BLK), jnp.bfloat16),
            shape((3, 3, width), jnp.float32),
            shape((4, 8, GROUP), jnp.float32),
        ),
        [SMEM, VMEM, VMEM],
        [pltpu.VMEM((2 * groups, span), jnp.float32), pltpu.VMEM((3, BLK, span), jnp.float32)],
        40 * groups * BLK * taps,
        8 * groups * BLK * taps,
    )(seq_lengths, scaled, short_weight)
    table, table_next, pair[0] = lax.optimization_barrier((table, table_next, pair[0]))

    half = lax.axis_index("half")
    query, _ = lax.optimization_barrier((panels, kept))
    qkept = lax.dynamic_slice(query, (0, 0, half * width), (1, rows, width))[0]
    qsent = lax.dynamic_slice(query, (0, 0, (1 - half) * width), (1, rows, width))[0]
    table_next, qkept, qsent = lax.optimization_barrier((table_next, qkept, qsent))
    qgot = moved(qsent, to_pair)
    back_pair = [[moved(pair[0], ahead)], [moved(pair[1], matching(blocks, first)) for first in (1, 0)]]

    window = pltpu.VMEM((4 * rows, width), jnp.bfloat16)
    extras = pltpu.VMEM((4, 16, width), jnp.float32)
    shifted = pltpu.VMEM((2, rows + 8, GROUP), jnp.float32)
    short = whole_tokens // 2 <= 4 * BLK
    if short:
        onward = [(i, i if i < 2 else i + 2 if i + 2 < 2 * blocks else 2 + i % 2) for i in spots]
        far = []
        for piece in range(2):
            relayed, back_pair[piece] = kernel_call(
                functools.partial(relay_kernel, piece),
                (small, small),
                [VMEM] * (4 + len(back_pair[piece])),
                [pltpu.VMEM((2 * rows, width // 2), jnp.bfloat16), pltpu.VMEM((2, 16, width // 2), jnp.float32)],
                2 * rows * BLK * width,
                4 * rows * width,
            )(marks, table_next, back_own, w_half, *back_pair[piece])
            far.append(moved(relayed, onward))
    else:
        back_pair = [moved(piece, ahead) for piece in pair]
        across = jnp.concatenate([piece[rows:] for piece in sent], 1)
        across = moved(across, [(i, ((i ^ 1) + 6) % (2 * blocks)) for i in spots])
        straight = moved(kept[rows:], [(i, (i + 6) % (2 * blocks)) for i in spots])
        deep = jnp.where(half == 1, straight, across)
        far = [moved(piece, ahead) for piece in (back_own, *back_pair)] + [deep]

    acc, qown = kernel_call(
        near_kernel,
        (shape((2 * rows, width), jnp.float32), half_wide),
        [VMEM] * 12,
        [window, extras, shifted, row_mask, row_mask],
        2 * 5 * rows * BLK * width,
        16 * rows * width,
    )(lengths, marks, table, kept, back_own, *pair, *back_pair, qkept, w_half, skip_bias.reshape(1, -1))

    qpair = kernel_call(
        pair_gate_kernel,
        half_wide,
        [VMEM] * 5,
        [shifted, row_mask, row_mask],
        10 * rows * width,
        8 * rows * width,
    )(lengths, qgot, kept, back_own, w_half)

    done, power, send = [], None, None
    for piece in range(2):
        needed = far[piece : piece + 1] if short else far
        before = [power, send] if piece else []
        own, send, power = kernel_call(
            functools.partial(far_kernel, short, piece),
            (
                shape((rows, width // 2), jnp.float32),
                shape((rows, width if piece else width // 2), jnp.bfloat16),
                shape((1, 2 * rows) if piece else (2, rows, GROUP), jnp.float32),
            ),
            [VMEM] * (8 + len(needed) + len(before)),
            [pltpu.VMEM((3 * rows, width // 2), jnp.bfloat16), pltpu.VMEM((3, 16, width // 2), jnp.float32)],
            2 * 3 * rows * BLK * width,
            12 * rows * width,
        )(table, acc, qown, qpair, w_half, marks, back_own, back_pair[piece], *needed, *before)
        done.append(own)
    back = moved(send, to_pair)

    peers = lax.axis_size("mp")
    shares = [lax.ppermute(power, "mp", [(i, i ^ k) for i in range(peers)]) for k in range(1, peers)]
    power = sum(shares, power)
    return kernel_call(
        functools.partial(norm_kernel, channels),
        shape((rows, 2 * width), jnp.bfloat16),
        [VMEM] * 6,
        [pltpu.VMEM((rows, 2 * width), jnp.bfloat16), pltpu.SemaphoreType.DMA((4,))],
        8 * rows * width,
        10 * rows * width,
        hbm,
    )(power, moved(power, to_pair), *done, back, norm_gain.reshape(1, -1))


def solution(mesh):
    blocks = mesh.shape["ctx"] // 2
    grid = Mesh(mesh.devices.reshape(blocks, 2, mesh.shape["mp"]), ("blk", "half", "mp"))
    in_specs = (
        P(SPOTS, None, "mp"),
        P(None, None, "mp"),
        P("mp", None),
        P("mp", None),
        P("mp"),
        P("mp"),
        P(),
    )

    def program(projected, *rest):
        body = functools.partial(shards, blocks, projected.shape[0], projected.shape[2])
        return jax.shard_map(
            body, mesh=grid, in_specs=in_specs, out_specs=P(SPOTS, "mp"), check_vma=False
        )(projected, *rest)

    return program
```
